32 devices in a mesh: seq: 8 (over z, y), roll: 4 (over x, core).
Axes of the slice: x: 2, y: 2, z: 4, core: 2. Of those that a mesh axis runs over, the one named last changes fastest.
Arguments:
- tokens: int32 [4, 3968], P('roll', 'seq'), may hold values from 0 to 29
- breaks: int32 [4, 3968], P('roll', 'seq'), may hold values 0 or 1
- lengths: int32 [4], P('roll'), may hold values from 1984 to 3968, as said below
- embed_table: float32 [30, 1280], replicated, may hold values from -6 to 6
- break_vec: float32 [1280], replicated, may hold values from -6 to 6
- gain_in: float32 [2, 1280], replicated, may hold values from 0.25 to 1.75
- gain_mid: float32 [2, 640], replicated, may hold values from 0.25 to 1.75
- gain_out: float32 [2, 640], replicated, may hold values from 0.25 to 1.75
- w_in: bfloat16 [2, 1280, 640], P(None, 'roll'), may hold values from -0.15625 to 0.15625
- convolution_weight: bfloat16 [2, 640, 3200], P(None, 'roll'), may hold values from -0.109375 to 0.109375
- w_out: bfloat16 [2, 640, 1280], P(None, 'roll'), may hold values from -0.25 to 0.25
Outputs:
- encoded: bfloat16 [4, 3968, 1280], P('roll', 'seq')
The draws below stay inside these ranges and needn't reach their ends.
Inputs may be any that keep to these rules, and one draw needn't show every extreme that they name: `lengths`: some complex has all 3968 residues valid in every draw.
All inputs are finite; a program needn't handle non-finite values. No bound on the sum of `breaks` on one device may be relied on, other than what follows from the above.
Results may differ from the reference program's by a relative error of at most 0.014.
Values may be sent and summed in bfloat16 or wider, within the bound.
No kernel may reach another device: no remote copies, remote signals or barrier semaphores. Data moves between devices by JAX's collectives and lax.ppermute only.
A program may use at most 64 MiB of HBM per device.

```python
import jax
import jax.numpy as jnp
from jax import lax

D = 1280
H = 640
KERNEL = 5
VOCAB = 30
BLOCKS = 2
BASE_DILATION = 64
LENGTH = 3968
COMPLEXES = 4


def draw_lengths(key, part):
    sampled = jax.random.randint(key, (COMPLEXES,), LENGTH // 2, LENGTH + 1)
    return sampled.at[0].set(LENGTH).astype(jnp.int32)


def touch_ends(array, key, least, top_value):
    extent = array.shape
    index_at = [jax.random.randint(jax.random.fold_in(key, axis), (), 0, extent[axis]) for axis in range(len(extent))]
    array = array.at[tuple(index_at)].set(least)
    longest = extent.index(max(extent))
    index_at[longest] = (index_at[longest] + 1) % extent[longest]
    return array.at[tuple(index_at)].set(top_value)


def steps_of(stream_key, extent, cuts, least, top_value):
    level = 1.0
    for axis_at, shards_of in cuts:
        steps = jax.random.uniform(jax.random.fold_in(jax.random.fold_in(stream_key, 6), axis_at), (shards_of,), jnp.float32, least / len(cuts), top_value / len(cuts))
        level = level * jnp.repeat(jnp.exp(steps), extent[axis_at] // shards_of).reshape((-1,) + (1,) * (len(extent) - 1 - axis_at))
    return level


def bell_draw(own_key, dims, deviation, most, shards=(), held_as=jnp.bfloat16):
    array = deviation * jax.random.normal(own_key, dims, jnp.float32)
    if shards:
        array = array * steps_of(own_key, dims, shards, -0.22, 0.18)
    return jnp.clip(array, -most, most).astype(held_as)


def setup_inputs(seed: int = 0) -> dict:
    keys = jax.random.split(jax.random.key(seed), 12)
    return {
        "tokens": touch_ends(jax.random.randint(keys[0], (COMPLEXES, LENGTH), 0, VOCAB), jax.random.fold_in(keys[0], 1), 0, VOCAB - 1).astype(jnp.int32),
        "breaks": touch_ends((jax.random.randint(keys[1], (COMPLEXES, LENGTH), 0, 32) < 1).astype(jnp.int32), jax.random.fold_in(keys[1], 1), 0, 1),
        "lengths": draw_lengths(jax.random.fold_in(keys[11], 71), 0),
        "embed_table": bell_draw(keys[3], (VOCAB, D), 1.0, 6.0, (), jnp.float32),
        "break_vec": bell_draw(keys[4], (D,), 1.0, 6.0, (), jnp.float32),
        "gain_in": jnp.clip(1.0 + 0.15 * jax.random.normal(keys[5], (BLOCKS, D), jnp.float32), 0.25, 1.75),
        "gain_mid": jnp.clip(1.0 + 0.15 * jax.random.normal(keys[6], (BLOCKS, H), jnp.float32), 0.25, 1.75),
        "gain_out": jnp.clip(1.0 + 0.15 * jax.random.normal(keys[7], (BLOCKS, H), jnp.float32), 0.25, 1.75),
        "w_in": bell_draw(keys[8], (BLOCKS, D, H), D ** -0.5, 0.15625, ((1, 4),)),
        "convolution_weight": bell_draw(keys[9], (BLOCKS, H, KERNEL * H), (KERNEL * H) ** -0.5, 0.109375, ((1, 4),)),
        "w_out": bell_draw(keys[10], (BLOCKS, H, D), H ** -0.5, 0.25, ((1, 4),)),
    }


def layer_norm(values, gain):
    center = lax.optimization_barrier(jnp.mean(values, axis=-1, keepdims=True))
    spread = lax.optimization_barrier(jnp.mean((values - center) ** 2, axis=-1, keepdims=True))
    return (values - center) * lax.rsqrt(spread + 1e-05) * gain

def reference(tokens, breaks, lengths, embed_table, break_vec, gain_in, gain_mid, gain_out, w_in, convolution_weight, w_out):

    def score_complex(items):
        token_row, boundary_row, length = items
        onehot = (token_row[:, None] == jnp.arange(VOCAB, dtype=jnp.int32)[None, :]).astype(jnp.float32)
        hidden_state = jnp.dot(onehot, embed_table, precision=lax.Precision.HIGHEST, preferred_element_type=jnp.float32)
        hidden_state = (hidden_state + boundary_row[:, None].astype(jnp.float32) * break_vec[None, :]).astype(jnp.bfloat16)
        position = jnp.arange(LENGTH, dtype=jnp.int32)
        valid_rows = (position < length).astype(jnp.float32)[:, None]
        for block_number in range(BLOCKS):
            dilation_step = BASE_DILATION * 2 ** block_number
            reach_rows = KERNEL // 2 * dilation_step
            normed = jax.nn.gelu(layer_norm(hidden_state.astype(jnp.float32), gain_in[block_number]), approximate=False).astype(jnp.bfloat16)
            padded_hidden = jnp.dot(normed, w_in[block_number], preferred_element_type=jnp.float32)
            conv_input = (jax.nn.gelu(layer_norm(padded_hidden, gain_mid[block_number]), approximate=False) * valid_rows).astype(jnp.bfloat16)
            padded = jnp.pad(conv_input, ((reach_rows, reach_rows), (0, 0)))
            taps_weight = convolution_weight[block_number].reshape(H, KERNEL, H)
            mixed = jnp.zeros((LENGTH, H), jnp.float32)
            for tap in range(KERNEL):
                window = padded[tap * dilation_step:tap * dilation_step + LENGTH]
                mixed = mixed + jnp.dot(window, taps_weight[:, tap, :], preferred_element_type=jnp.float32)
            activated = jax.nn.gelu(layer_norm(mixed, gain_out[block_number]), approximate=False).astype(jnp.bfloat16)
            hidden_state = (hidden_state.astype(jnp.float32) + jnp.dot(activated, w_out[block_number], preferred_element_type=jnp.float32)).astype(jnp.bfloat16)
        return hidden_state
    return lax.map(score_complex, (tokens, breaks, lengths))
```

```python
import functools

import jax
import jax.numpy as jnp
from jax import lax
from jax.experimental import pallas as pl
from jax.experimental.pallas import tpu as pltpu
from jax.sharding import PartitionSpec as P

H = 640
KERNEL = 5
VOCAB = 30
SLOT = 32
CODES = 2 * SLOT
BASE_DILATION = 64
DIL0 = BASE_DILATION
DIL1 = 2 * BASE_DILATION
HALF = KERNEL // 2
EDGE = HALF * DIL1
REACH = EDGE + HALF * DIL0
VMEM_LIMIT = 48 * 1024 * 1024
BF = jnp.bfloat16
F32 = jnp.float32
VMEM = pl.BlockSpec(memory_space=pltpu.VMEM)
SMEM = pl.BlockSpec(memory_space=pltpu.SMEM)
ANY = pl.BlockSpec(memory_space=pl.ANY)


def params():
    return pltpu.CompilerParams(vmem_limit_bytes=VMEM_LIMIT)


def gelu(x):
    u = jnp.abs(x)
    t = 1.0 / (1.0 + (0.3275911 * 0.5**0.5) * u)
    q = 0.5 * 1.061405429
    for a in (-1.453152027, 1.421413741, -0.284496736, 0.254829592):
        q = q * t + 0.5 * a
    q = q * t * jnp.exp(-0.5 * u * u)
    return jnp.maximum(x, 0.0) - u * q


def norm(x, gain):
    center = jnp.mean(x, axis=-1, keepdims=True)
    d = x - center
    spread = jnp.mean(d * d, axis=-1, keepdims=True)
    return d * lax.rsqrt(spread + 1e-5) * gain


def dot(a, b):
    return jnp.dot(a, b, preferred_element_type=F32)


def pick(rows, columns, start):
    i = lax.broadcasted_iota(jnp.int32, (rows, columns), 0)
    j = lax.broadcasted_iota(jnp.int32, (rows, columns), 1)
    return jnp.where(i == j + start, 1.0, 0.0).astype(BF)


def embed_kernel(at, embed, brk, gain, w, table, part, scratch):
    scratch[...] = jnp.zeros_like(scratch)
    scratch[0:VOCAB] = embed[...]
    scratch[SLOT : SLOT + VOCAB] = embed[...] + brk[...]
    hidden = scratch[...].astype(BF)
    table[...] = hidden
    normed = gelu(norm(hidden.astype(F32), gain[0:1])).astype(BF)
    rows = w.shape[0]
    mine = dot(normed, pick(normed.shape[1], rows, at[0] * rows)).astype(BF)
    part[...] = dot(mine, w[...])


def table_kernel(at, own, other, gain, w, out):
    wide = own[...] + other[...].astype(F32)
    t = gelu(norm(wide, gain[0:1])).astype(BF)
    rows = w.shape[0]
    mine = dot(t, pick(t.shape[1], rows, at[0] * rows)).astype(BF)
    out[...] = dot(mine, w[...]).astype(out.dtype)


def rows_kernel(at, hot5, hot1, table, taps, gain_out, gain_in, gain_mid, w_out, w_in, ci, hid, tw):
    @pl.when(pl.program_id(0) == 0)
    def _():
        for k in range(KERNEL):
            tw[k * CODES : (k + 1) * CODES] = taps[:, k * H : (k + 1) * H]

    mixed = dot(hot5[...], tw[...])
    act = gelu(norm(mixed, gain_out[0:1])).astype(BF)
    hidden = (dot(hot1[...], table[...]) + dot(act, w_out[...])).astype(BF)
    hid[...] = hidden
    normed = gelu(norm(hidden.astype(F32), gain_in[1:2])).astype(BF)
    wide = dot(normed, w_in[...])
    rows = wide.shape[0]
    pos = at[0] + pl.program_id(0) * rows + lax.broadcasted_iota(jnp.int32, (rows, 1), 0)
    valid = jnp.where((pos >= 0) & (pos < at[1]), 1.0, 0.0)
    ci[...] = (gelu(norm(wide, gain_mid[1:2])) * valid).astype(BF)


def last_kernel(ci, hid, gain_out, w_conv, w_out, out):
    rows = out.shape[0]
    mixed = dot(ci[0:rows], w_conv[:, 0:H])
    for k in range(1, KERNEL):
        mixed += dot(ci[k * DIL1 : k * DIL1 + rows], w_conv[:, k * H : (k + 1) * H])
    act = gelu(norm(mixed, gain_out[1:2])).astype(BF)
    out[...] = (hid[EDGE : EDGE + rows].astype(F32) + dot(act, w_out[...])).astype(BF)


def per_device(tokens, breaks, lengths, embed_table, break_vec, gain_in, gain_mid, gain_out, w_in, conv_w, w_out):
    rows = tokens.shape[1]
    width = embed_table.shape[1]
    roll_at = lax.axis_index("roll")
    seq_at = lax.axis_index("seq")
    rolls = lax.axis_size("roll")
    seqs = lax.axis_size("seq")
    at = roll_at.astype(jnp.int32).reshape(1)

    codes = tokens + SLOT * breaks
    all_codes = lax.all_gather(codes[0], "seq").reshape(-1)
    out0 = lax.all_gather(w_out[0], "roll", axis=0, tiled=True)
    in1 = lax.all_gather(w_in[1], "roll", axis=0, tiled=True)
    conv1 = lax.all_gather(conv_w[1], "roll", axis=0, tiled=True)
    out1 = lax.all_gather(w_out[1], "roll", axis=0, tiled=True)

    table, part = pl.pallas_call(
        embed_kernel,
        out_shape=(
            jax.ShapeDtypeStruct((CODES, width), BF),
            jax.ShapeDtypeStruct((CODES, H), F32),
        ),
        in_specs=[SMEM, VMEM, VMEM, VMEM, VMEM],
        out_specs=(VMEM, VMEM),
        scratch_shapes=[pltpu.VMEM((CODES, width), F32)],
        compiler_params=params(),
    )(at, embed_table, break_vec[None], gain_in, w_in[0])

    def swap(x, step):
        return lax.ppermute(x, "roll", [(i, i ^ step) for i in range(rolls)])

    special = rolls == 4
    if special:
        own = part + swap(part, 1)
        other = swap(own.astype(BF), 2)
    else:
        own = lax.psum(part, "roll")
        other = jnp.zeros((CODES, H), BF)
    taps = pl.pallas_call(
        table_kernel,
        out_shape=jax.ShapeDtypeStruct((CODES, KERNEL * H), BF),
        in_specs=[SMEM, VMEM, VMEM, VMEM, VMEM],
        out_specs=VMEM,
        compiler_params=params(),
    )(at, own, other, gain_mid, conv_w[0])
    if special:
        core = roll_at % 2
        mine = lax.dynamic_slice_in_dim(taps, core * SLOT, SLOT, axis=0)
        theirs = lax.dynamic_slice_in_dim(taps, (1 - core) * SLOT, SLOT, axis=0)
        mine = mine.astype(F32) + swap(theirs, 1).astype(F32)
        mine = (mine + swap(mine.astype(BF), 2).astype(F32)).astype(BF)
        theirs = swap(mine, 1)
        first = core == 0
        taps = jnp.concatenate([jnp.where(first, mine, theirs), jnp.where(first, theirs, mine)], axis=0)
    else:
        taps = lax.psum(taps.astype(F32), "roll").astype(BF)

    start = seq_at * rows
    padded = jnp.pad(all_codes, (REACH, REACH))
    near = lax.dynamic_slice_in_dim(padded, start, rows + 2 * REACH)
    pos = start - REACH + jnp.arange(rows + 2 * REACH, dtype=jnp.int32)
    near_valid = jnp.where((pos >= 0) & (pos < lengths[0]), near, -1)
    wide_rows = rows + 2 * EDGE
    lanes = jnp.arange(CODES, dtype=jnp.int32)
    tap_codes = jnp.stack([near_valid[k * DIL0 : k * DIL0 + wide_rows] for k in range(KERNEL)], axis=1)
    hot5 = (tap_codes[:, :, None] == lanes).astype(BF).reshape(wide_rows, KERNEL * CODES)
    center = near[HALF * DIL0 : HALF * DIL0 + wide_rows]
    hot1 = (center[:, None] == lanes).astype(BF)

    span = jnp.stack([start.astype(jnp.int32) - EDGE, lengths[0]])
    steps = 3
    block = wide_rows // steps
    row_block = lambda n: pl.BlockSpec((block, n), lambda i: (i, 0))
    whole = lambda x: pl.BlockSpec(x.shape, lambda i: (0,) * x.ndim, pipeline_mode=pl.Buffered(1))
    ci, hid = pl.pallas_call(
        rows_kernel,
        grid=(steps,),
        out_shape=(
            jax.ShapeDtypeStruct((wide_rows, H), BF),
            jax.ShapeDtypeStruct((wide_rows, width), BF),
        ),
        in_specs=[SMEM, row_block(KERNEL * CODES), row_block(CODES)]
        + [whole(x) for x in (table, taps, gain_out, gain_in, gain_mid, out0, in1)],
        out_specs=(row_block(H), row_block(width)),
        scratch_shapes=[pltpu.VMEM((KERNEL * CODES, H), BF)],
        compiler_params=params(),
    )(span, hot5, hot1, table, taps, gain_out, gain_in, gain_mid, out0, in1)

    out = pl.pallas_call(
        last_kernel,
        out_shape=jax.ShapeDtypeStruct((rows, width), BF),
        in_specs=[VMEM] * 5,
        out_specs=VMEM,
        compiler_params=params(),
    )(ci, hid, gain_out, conv1, out1)
    return out[None]


def solution(mesh):
    placed = (
        P("roll", "seq"),
        P("roll", "seq"),
        P("roll"),
        P(),
        P(),
        P(),
        P(),
        P(),
        P(None, "roll", None),
        P(None, "roll", None),
        P(None, "roll", None),
    )
    return jax.shard_map(
        per_device, mesh=mesh, in_specs=placed, out_specs=P("roll", "seq", None), check_vma=False
    )
```

```python
import functools

import jax
import jax.numpy as jnp
from jax import lax
from jax.experimental import pallas as pl
from jax.experimental.pallas import tpu as pltpu
from jax.sharding import PartitionSpec as P

H = 640
KERNEL = 5
VOCAB = 30
SLOT = 32
CODES = 2 * SLOT
BASE_DILATION = 64
DIL0 = BASE_DILATION
DIL1 = 2 * BASE_DILATION
HALF = KERNEL // 2
EDGE = HALF * DIL1
REACH = EDGE + HALF * DIL0
VMEM_LIMIT = 44 * 1024 * 1024
BF = jnp.bfloat16
F32 = jnp.float32
VMEM = pl.BlockSpec(memory_space=pltpu.VMEM)
SMEM = pl.BlockSpec(memory_space=pltpu.SMEM)
ANY = pl.BlockSpec(memory_space=pl.ANY)
CUT_A = 18 * 128
CUT_B = 17 * 128


def params():
    return pltpu.CompilerParams(vmem_limit_bytes=VMEM_LIMIT)


def gelu(x):
    return (0.5 * x) * (1.0 + lax.erf(x * 0.5**0.5))


def norm(x, gain):
    center = jnp.mean(x, axis=-1, keepdims=True)
    d = x - center
    spread = jnp.mean(d * d, axis=-1, keepdims=True)
    return d * lax.rsqrt(spread + 1e-5) * gain


def dot(a, b):
    return jnp.dot(a, b, preferred_element_type=F32)


def place():
    roll, seq = lax.axis_index("roll"), lax.axis_index("seq")
    return lax.div(roll, 2), lax.rem(roll, 2), lax.rem(seq, 2), lax.rem(lax.div(seq, 2), 2)


def start(copies):
    for c in copies:
        c.start()


def wait(copies):
    for c in copies:
        c.wait()


def pick(rows, columns, first):
    i = lax.broadcasted_iota(jnp.int32, (rows, columns), 0)
    j = lax.broadcasted_iota(jnp.int32, (rows, columns), 1)
    return jnp.where(i == j + first, 1.0, 0.0).astype(BF)


def part_kernel(w_in, conv_w, w_out, a, b, sem):
    _, _, y, z = place()
    n = a.shape[0]
    r = pl.multiple_of(z * n, 16)
    r2 = pl.multiple_of(z * 2 * n, 16)
    rest = conv_w.shape[2] - CUT_B

    def go(pairs):
        copies = [pltpu.make_async_copy(s, d, sem) for s, d in pairs]
        start(copies)
        wait(copies)

    @pl.when(y == 0)
    def _():
        go([
            (w_out.at[0, pl.ds(r, n)], a),
            (conv_w.at[1, pl.ds(r, n), 0:CUT_A], b),
        ])

    @pl.when(y == 1)
    def _():
        go([
            (w_in.at[1, pl.ds(r2, n)], a.at[:, 0:H]),
            (w_in.at[1, pl.ds(r2 + n, n)], a.at[:, H : 2 * H]),
            (conv_w.at[1, pl.ds(r, n), CUT_B:], b.at[:, 0:rest]),
            (w_out.at[1, pl.ds(r, n)], b.at[:, rest:]),
        ])


def embed_kernel(embed, brk, gain, w_all, table, part, scratch, w, sem):
    copy = pltpu.make_async_copy(w_all.at[0], w, sem)
    copy.start()
    scratch[...] = jnp.zeros_like(scratch)
    scratch[0:VOCAB] = embed[...]
    scratch[SLOT : SLOT + VOCAB] = embed[...] + brk[...]
    hidden = scratch[...].astype(BF)
    table[...] = hidden
    normed = gelu(norm(hidden.astype(F32), gain[0:1])).astype(BF)
    rows = w.shape[0]
    mine = dot(normed, pick(normed.shape[1], rows, lax.axis_index("roll") * rows)).astype(BF)
    copy.wait()
    part[...] = dot(mine, w[...])


def table_kernel(own, other, gain, w_all, out, w, sem):
    copy = pltpu.make_async_copy(w_all.at[0], w, sem)
    copy.start()
    wide = own[...] + other[...].astype(F32)
    t = gelu(norm(wide, gain[0:1])).astype(BF)
    rows = w.shape[0]
    mine = dot(t, pick(t.shape[1], rows, lax.axis_index("roll") * rows)).astype(BF)
    copy.wait()
    out[...] = dot(mine, w[...]).astype(out.dtype)


def rows_kernel(split, span, hot5, hot1, table, taps, gain_out, gain_in, gain_mid, *rest):
    *w, ci, hid, tw, wo, wi, sem = rest
    depth = wo.shape[0] - CODES
    first = [
        pltpu.make_async_copy(taps.at[:, k * H : (k + 1) * H], tw.at[k * CODES : (k + 1) * CODES], sem.at[0])
        for k in range(KERNEL)
    ]
    first.append(pltpu.make_async_copy(table, wo.at[depth:], sem.at[0]))
    start(first)
    if not split:
        out_copies = [pltpu.make_async_copy(w[0], wo.at[0:depth], sem.at[1])]
        in_copies = [pltpu.make_async_copy(w[1], wi, sem.at[2])]
        start(out_copies + in_copies)
    else:
        w_out, w_in, near_out, near_in = w[:4]
        parts, near_parts = w[4:8], w[8:12]
        x, core, y, z = place()
        n = w_out.shape[1]
        m = w_in.shape[1]
        half = n // 2
        out_copies, in_copies = [], []
        for c, o, i in ((core, w_out, w_in), (1 - core, near_out, near_in)):
            at = 2 * x + c
            out_copies.append(pltpu.make_async_copy(o.at[0], wo.at[pl.ds(pl.multiple_of(at * n, 16), n)], sem.at[1]))
            in_copies.append(pltpu.make_async_copy(i.at[1], wi.at[pl.ds(pl.multiple_of(at * m, 16), m)], sem.at[2]))

        def far(outs, ins):
            out, into = [], []
            for c, of in ((core, parts), (1 - core, near_parts)):
                at = 2 * (1 - x) + c
                for p, zz in zip(outs, (z, 1 - z)):
                    row = pl.multiple_of(at * n + zz * half, 16)
                    out.append(pltpu.make_async_copy(of[p], wo.at[pl.ds(row, half)], sem.at[1]))
                for p, zz in zip(ins, (z, 1 - z)):
                    for j in range(2):
                        row = pl.multiple_of(at * m + zz * n + j * half, 16)
                        into.append(
                            pltpu.make_async_copy(of[p].at[:, j * H : (j + 1) * H], wi.at[pl.ds(row, half)], sem.at[2])
                        )
            return out, into

        start(out_copies + in_copies)
        far0, far1 = far((0, 2), (1, 3)), far((1, 3), (0, 2))

        @pl.when(y == 0)
        def _():
            start(far0[0] + far0[1])

        @pl.when(y == 1)
        def _():
            start(far1[0] + far1[1])

        out_copies += far0[0]
        in_copies += far0[1]

    wait(first)
    mixed = dot(hot5[...], tw[...])
    act = gelu(norm(mixed, gain_out[0:1])).astype(BF)
    wait(out_copies)
    hidden = dot(jnp.concatenate([act, hot1[...]], axis=1), wo[...]).astype(BF)
    rows = hidden.shape[0]
    hid[...] = hidden[EDGE : rows - EDGE]
    normed = gelu(norm(hidden.astype(F32), gain_in[1:2])).astype(BF)
    wait(in_copies)
    wide = dot(normed, wi[...])
    pos = span[0] + lax.broadcasted_iota(jnp.int32, (rows, 1), 0)
    valid = jnp.where((pos >= 0) & (pos < span[1]), 1.0, 0.0)
    ci[...] = (gelu(norm(wide, gain_mid[1:2])) * valid).astype(BF)


def last_kernel(split, ci, hid, gain_out, *rest):
    *w, out, wt, wo, sem = rest

    def conv(src, col, width, row, n):
        copies = []
        done = 0
        while done < width:
            tap, inner = divmod(col + done, H)
            step = min(H - inner, width - done)
            copies.append(
                pltpu.make_async_copy(
                    src.at[:, done : done + step],
                    wt.at[pl.ds(tap * H + row, n), inner : inner + step],
                    sem.at[0],
                )
            )
            done += step
        return copies

    if not split:
        conv_copies = conv(w[0], 0, KERNEL * H, 0, H)
        out_copies = [pltpu.make_async_copy(w[1], wo, sem.at[1])]
        start(conv_copies + out_copies)
    else:
        w_conv, w_out, near_conv, near_out = w[:4]
        parts, near_parts = w[4:8], w[8:12]
        x, core, y, z = place()
        n = w_out.shape[1]
        half = n // 2
        rest_cols = KERNEL * H - CUT_B
        conv_copies, out_copies = [], []
        for c, v, o in ((core, w_conv, w_out), (1 - core, near_conv, near_out)):
            row = pl.multiple_of((2 * x + c) * n, 16)
            conv_copies += conv(v.at[1], 0, KERNEL * H, row, n)
            out_copies.append(pltpu.make_async_copy(o.at[1], wo.at[pl.ds(row, n)], sem.at[1]))

        def far(head, tail):
            cv, out = [], []
            for c, of in ((core, parts), (1 - core, near_parts)):
                for p, zz in zip(head, (z, 1 - z)):
                    row = pl.multiple_of((2 * (1 - x) + c) * n + zz * half, 16)
                    cv += conv(of[p], 0, CUT_A, row, half)
                for p, zz in zip(tail, (z, 1 - z)):
                    row = pl.multiple_of((2 * (1 - x) + c) * n + zz * half, 16)
                    skip = CUT_A - CUT_B
                    cv += conv(of[p].at[:, skip:rest_cols], CUT_A, rest_cols - skip, row, half)
                    out.append(pltpu.make_async_copy(of[p].at[:, rest_cols:], wo.at[pl.ds(row, half)], sem.at[1]))
            return cv, out

        start(conv_copies + out_copies)
        far0, far1 = far((0, 2), (1, 3)), far((1, 3), (0, 2))

        @pl.when(y == 0)
        def _():
            start(far0[0] + far0[1])

        @pl.when(y == 1)
        def _():
            start(far1[0] + far1[1])

        conv_copies += far0[0]
        out_copies += far0[1]

    rows = out.shape[0]
    blocks = [0, 16 * (rows // 32), rows]
    for b in range(2):
        lo, hi = blocks[b], blocks[b + 1]
        lhs = jnp.concatenate([ci[lo + k * DIL1 : hi + k * DIL1] for k in range(KERNEL)], axis=1)
        if b == 0:
            wait(conv_copies)
        mixed = dot(lhs, wt[...])
        act = gelu(norm(mixed, gain_out[1:2])).astype(BF)
        if b == 0:
            wait(out_copies)
        out[lo:hi] = (hid[lo:hi].astype(F32) + dot(act, wo[...])).astype(BF)


def after(x, *deps):
    return lax.optimization_barrier((x, *deps))[0]


def per_device(tokens, breaks, lengths, embed_table, break_vec, gain_in, gain_mid, gain_out, w_in, conv_w, w_out):
    rows = tokens.shape[1]
    width = embed_table.shape[1]
    roll_at = lax.axis_index("roll")
    seq_at = lax.axis_index("seq")
    rolls = lax.axis_size("roll")
    seqs = lax.axis_size("seq")
    split = rolls == 4 and seqs % 4 == 0

    def core_swap(x):
        return lax.ppermute(x, "roll", [(i, i ^ 1) for i in range(rolls)])

    def x_swap(x):
        return lax.ppermute(x, "roll", [(i, i ^ 2) for i in range(rolls)])

    def seq_swap(x, bits):
        return lax.ppermute(x, "seq", [(i, i ^ bits) for i in range(seqs)])

    if split:
        shard = w_out.shape[1] // 2
        part_a, part_b = pl.pallas_call(
            part_kernel,
            out_shape=(jax.ShapeDtypeStruct((shard, width), BF), jax.ShapeDtypeStruct((shard, CUT_A), BF)),
            in_specs=[ANY] * 3,
            out_specs=(ANY, ANY),
            scratch_shapes=[pltpu.SemaphoreType.DMA],
            compiler_params=params(),
        )(w_in, conv_w, w_out)
        far_a = x_swap(part_a)
        near_in, near_conv, near_out = core_swap(w_in), core_swap(conv_w), core_swap(w_out)
    else:
        out0 = lax.all_gather(w_out[0], "roll", axis=0, tiled=True)
        in1 = lax.all_gather(w_in[1], "roll", axis=0, tiled=True)
        conv1 = lax.all_gather(conv_w[1], "roll", axis=0, tiled=True)
        out1 = lax.all_gather(w_out[1], "roll", axis=0, tiled=True)

    table, part = pl.pallas_call(
        embed_kernel,
        out_shape=(
            jax.ShapeDtypeStruct((CODES, width), BF),
            jax.ShapeDtypeStruct((CODES, H), F32),
        ),
        in_specs=[VMEM, VMEM, VMEM, ANY],
        out_specs=(VMEM, VMEM),
        scratch_shapes=[
            pltpu.VMEM((CODES, width), F32),
            pltpu.VMEM(w_in.shape[1:], BF),
            pltpu.SemaphoreType.DMA,
        ],
        compiler_params=params(),
    )(embed_table, break_vec[None], gain_in, w_in)

    if split:
        own = part + core_swap(part)
        other = x_swap(own.astype(BF))
    else:
        own = lax.psum(part, "roll")
        other = jnp.zeros((CODES, H), BF)

    codes = tokens[0] + SLOT * breaks[0]
    if split:
        codes = after(codes, own)
    up = [(i, i + 1) for i in range(seqs - 1)]
    down = [(i + 1, i) for i in range(seqs - 1)]
    near = jnp.concatenate(
        [lax.ppermute(codes[rows - REACH :], "seq", up), codes, lax.ppermute(codes[:REACH], "seq", down)]
    )
    if split:
        far_b = x_swap(after(part_b, own))

    taps = pl.pallas_call(
        table_kernel,
        out_shape=jax.ShapeDtypeStruct((CODES, KERNEL * H), BF),
        in_specs=[VMEM, VMEM, VMEM, ANY],
        out_specs=VMEM,
        scratch_shapes=[pltpu.VMEM(conv_w.shape[1:], BF), pltpu.SemaphoreType.DMA],
        compiler_params=params(),
    )(own, other, gain_mid, conv_w)
    if split:
        core = roll_at % 2
        mine = lax.dynamic_slice_in_dim(taps, core * SLOT, SLOT, axis=0)
        theirs = lax.dynamic_slice_in_dim(taps, (1 - core) * SLOT, SLOT, axis=0)
        mine = mine.astype(F32) + core_swap(theirs).astype(F32)
        sent = mine.astype(BF)
        relay = after(far_a, sent)
        parts_a = [far_a] + [seq_swap(relay, b) for b in (1, 2, 3)]
        mine = (mine + x_swap(sent).astype(F32)).astype(BF)
        theirs = core_swap(mine)
        first = core == 0
        taps = jnp.concatenate([jnp.where(first, mine, theirs), jnp.where(first, theirs, mine)], axis=0)
        relay = after(far_b, mine)
        parts_b = [far_b] + [seq_swap(relay, b) for b in (1, 2, 3)]
        near_a = [core_swap(p) for p in parts_a]
        near_b = [core_swap(p) for p in parts_b]
        weights_a = [w_out, w_in, near_out, near_in] + parts_a + near_a
        weights_b = [conv_w, w_out, near_conv, near_out] + parts_b + near_b
    else:
        taps = lax.psum(taps.astype(F32), "roll").astype(BF)
        weights_a, weights_b = [out0, in1], [conv1, out1]

    begin = seq_at * rows
    pos = begin - REACH + jnp.arange(rows + 2 * REACH, dtype=jnp.int32)
    near_valid = jnp.where((pos >= 0) & (pos < lengths[0]), near, -1)
    wide_rows = rows + 2 * EDGE
    lanes = jnp.arange(CODES, dtype=jnp.int32)
    tap_codes = jnp.stack([near_valid[k * DIL0 : k * DIL0 + wide_rows] for k in range(KERNEL)], axis=1)
    hot5 = (tap_codes[:, :, None] == lanes).astype(BF).reshape(wide_rows, KERNEL * CODES)
    center = near[HALF * DIL0 : HALF * DIL0 + wide_rows]
    hot1 = (center[:, None] == lanes).astype(BF)

    span = jnp.stack([begin.astype(jnp.int32) - EDGE, lengths[0]])
    ci, hid = pl.pallas_call(
        functools.partial(rows_kernel, split),
        out_shape=(
            jax.ShapeDtypeStruct((wide_rows, H), BF),
            jax.ShapeDtypeStruct((rows, width), BF),
        ),
        in_specs=[SMEM, VMEM, VMEM, ANY, ANY, VMEM, VMEM, VMEM] + [ANY] * len(weights_a),
        out_specs=(VMEM, VMEM),
        scratch_shapes=[
            pltpu.VMEM((KERNEL * CODES, H), BF),
            pltpu.VMEM((H + CODES, width), BF),
            pltpu.VMEM((width, H), BF),
            pltpu.SemaphoreType.DMA((3,)),
        ],
        compiler_params=params(),
    )(span, hot5, hot1, table, taps, gain_out, gain_in, gain_mid, *weights_a)

    out = pl.pallas_call(
        functools.partial(last_kernel, split),
        out_shape=jax.ShapeDtypeStruct((rows, width), BF),
        in_specs=[VMEM] * 3 + [ANY] * len(weights_b),
        out_specs=VMEM,
        scratch_shapes=[
            pltpu.VMEM((KERNEL * H, H), BF),
            pltpu.VMEM((H, width), BF),
            pltpu.SemaphoreType.DMA((2,)),
        ],
        compiler_params=params(),
    )(ci, hid, gain_out, *weights_b)
    return out[None]


def solution(mesh):
    placed = (
        P("roll", "seq"),
        P("roll", "seq"),
        P("roll"),
        P(),
        P(),
        P(),
        P(),
        P(),
        P(None, "roll", None),
        P(None, "roll", None),
        P(None, "roll", None),
    )
    return jax.shard_map(
        per_device, mesh=mesh, in_specs=placed, out_specs=P("roll", "seq", None), check_vma=False
    )
```

```python
import functools

import jax
import jax.numpy as jnp
from jax import lax
from jax.experimental import pallas as pl
from jax.experimental.pallas import tpu as pltpu
from jax.sharding import PartitionSpec as P

H = 640
KERNEL = 5
VOCAB = 30
SLOT = 32
CODES = 2 * SLOT
BASE_DILATION = 64
DIL0 = BASE_DILATION
DIL1 = 2 * BASE_DILATION
HALF = KERNEL // 2
EDGE = HALF * DIL1
REACH = EDGE + HALF * DIL0
BF = jnp.bfloat16
F32 = jnp.float32
VMEM = pl.BlockSpec(memory_space=pltpu.VMEM)
SMEM = pl.BlockSpec(memory_space=pltpu.SMEM)
ANY = pl.BlockSpec(memory_space=pl.ANY)
HBM = pl.BlockSpec(memory_space=pltpu.HBM)
CUT_A = 18 * 128
CUT_B = 17 * 128


def params(mib):
    return pltpu.CompilerParams(vmem_limit_bytes=mib * 1024 * 1024)


def gelu(x):
    return (0.5 * x) * (1.0 + lax.erf(x * 0.5**0.5))


def norm(x, gain):
    center = jnp.mean(x, axis=-1, keepdims=True)
    d = x - center
    spread = jnp.mean(d * d, axis=-1, keepdims=True)
    return d * lax.rsqrt(spread + 1e-5) * gain


def dot(a, b):
    return jnp.dot(a, b, preferred_element_type=F32)


def place():
    roll, seq = lax.axis_index("roll"), lax.axis_index("seq")
    return lax.div(roll, 2), lax.rem(roll, 2), lax.rem(seq, 2), lax.rem(lax.div(seq, 2), 2)


def start(copies):
    for c in copies:
        c.start()


def wait(copies):
    for c in copies:
        c.wait()


def pick(rows, columns, first):
    i = lax.broadcasted_iota(jnp.int32, (rows, columns), 0)
    j = lax.broadcasted_iota(jnp.int32, (rows, columns), 1)
    return jnp.where(i == j + first, 1.0, 0.0).astype(BF)


def part_kernel(w_in, conv_w, w_out, a, b, sem):
    _, _, y, z = place()
    n = a.shape[0]
    r = pl.multiple_of(z * n, 16)
    r2 = pl.multiple_of(z * 2 * n, 16)
    rest = conv_w.shape[2] - CUT_B

    def go(pairs):
        copies = [pltpu.make_async_copy(s, d, sem) for s, d in pairs]
        start(copies)
        wait(copies)

    @pl.when(y == 0)
    def _():
        go([
            (w_out.at[0, pl.ds(r, n)], a),
            (conv_w.at[1, pl.ds(r, n), 0:CUT_A], b),
        ])

    @pl.when(y == 1)
    def _():
        go([
            (w_in.at[1, pl.ds(r2, n)], a.at[:, 0:H]),
            (w_in.at[1, pl.ds(r2 + n, n)], a.at[:, H : 2 * H]),
            (conv_w.at[1, pl.ds(r, n), CUT_B:], b.at[:, 0:rest]),
            (w_out.at[1, pl.ds(r, n)], b.at[:, rest:]),
        ])


def embed_kernel(embed, brk, gain, w_all, table, part, scratch, w, sem):
    copy = pltpu.make_async_copy(w_all.at[0], w, sem)
    copy.start()
    scratch[...] = jnp.zeros_like(scratch)
    scratch[0:VOCAB] = embed[...]
    scratch[SLOT : SLOT + VOCAB] = embed[...] + brk[...]
    hidden = scratch[...].astype(BF)
    table[...] = hidden
    normed = gelu(norm(hidden.astype(F32), gain[0:1])).astype(BF)
    rows = w.shape[0]
    mine = dot(normed, pick(normed.shape[1], rows, lax.axis_index("roll") * rows)).astype(BF)
    copy.wait()
    part[...] = dot(mine, w[...])


def table_kernel(split, own, other, gain, w_all, *rest):
    *outs, w, full, sem = rest
    copy = pltpu.make_async_copy(w_all.at[0], w, sem)
    copy.start()
    wide = own[...] + other[...].astype(F32)
    t = gelu(norm(wide, gain[0:1])).astype(BF)
    rows = w.shape[0]
    mine = dot(t, pick(t.shape[1], rows, lax.axis_index("roll") * rows)).astype(BF)
    copy.wait()
    full[...] = dot(mine, w[...])
    if split:
        core = lax.rem(lax.axis_index("roll"), 2)
        outs[0][...] = full[pl.ds(pl.multiple_of(core * SLOT, SLOT), SLOT)]
        outs[1][...] = full[pl.ds(pl.multiple_of((1 - core) * SLOT, SLOT), SLOT)].astype(BF)
    else:
        outs[0][...] = full[...]


def hot_kernel(span, near, hot5, hot1):
    codes = near[...]
    count = codes.shape[1]
    rows = hot5.shape[0]
    pos = span[0] - HALF * DIL0 + lax.broadcasted_iota(jnp.int32, codes.shape, 1)
    masked = jnp.where((pos >= 0) & (pos < span[1]), codes, -1)
    lanes = lax.broadcasted_iota(jnp.int32, (CODES, count), 0)
    taps = jnp.where(lanes == masked, 1.0, 0.0).T.astype(BF)
    for k in range(KERNEL):
        hot5[:, k * CODES : (k + 1) * CODES] = taps[k * DIL0 : k * DIL0 + rows]
    center = jnp.where(lanes == codes, 1.0, 0.0).T.astype(BF)
    hot1[...] = center[HALF * DIL0 : HALF * DIL0 + rows]


def rows_kernel(split, span, hot5, hot1, table, gain_out, gain_in, gain_mid, *rest):
    *w, ci, hid, tw, wo, wi, sem = rest
    depth = wo.shape[0] - CODES
    if split:
        core = lax.rem(lax.axis_index("roll"), 2)
        taps = ((w[0], core * SLOT, SLOT), (w[1], (1 - core) * SLOT, SLOT))
        w = w[2:]
    else:
        taps = ((w[0], 0, CODES),)
        w = w[1:]
    first = [
        pltpu.make_async_copy(
            t.at[:, k * H : (k + 1) * H], tw.at[pl.ds(pl.multiple_of(k * CODES + at, 16), n)], sem.at[0]
        )
        for t, at, n in taps
        for k in range(KERNEL)
    ]
    first.append(pltpu.make_async_copy(table, wo.at[depth:], sem.at[0]))
    start(first)
    if not split:
        out_copies = [pltpu.make_async_copy(w[0], wo.at[0:depth], sem.at[1])]
        in_copies = [pltpu.make_async_copy(w[1], wi, sem.at[2])]
        start(out_copies + in_copies)
    else:
        w_out, w_in, near_out, near_in = w[:4]
        parts, near_parts = w[4:8], w[8:12]
        x, core, y, z = place()
        n = w_out.shape[1]
        m = w_in.shape[1]
        half = n // 2
        out_copies, in_copies = [], []
        for c, o, i in ((core, w_out, w_in), (1 - core, near_out, near_in)):
            at = 2 * x + c
            out_copies.append(pltpu.make_async_copy(o.at[0], wo.at[pl.ds(pl.multiple_of(at * n, 16), n)], sem.at[1]))
            in_copies.append(pltpu.make_async_copy(i.at[1], wi.at[pl.ds(pl.multiple_of(at * m, 16), m)], sem.at[2]))

        def far(outs, ins):
            out, into = [], []
            for c, of in ((core, parts), (1 - core, near_parts)):
                at = 2 * (1 - x) + c
                for p, zz in zip(outs, (z, 1 - z)):
                    row = pl.multiple_of(at * n + zz * half, 16)
                    out.append(pltpu.make_async_copy(of[p], wo.at[pl.ds(row, half)], sem.at[1]))
                for p, zz in zip(ins, (z, 1 - z)):
                    for j in range(2):
                        row = pl.multiple_of(at * m + zz * n + j * half, 16)
                        into.append(
                            pltpu.make_async_copy(of[p].at[:, j * H : (j + 1) * H], wi.at[pl.ds(row, half)], sem.at[2])
                        )
            return out, into

        start(out_copies + in_copies)
        far0, far1 = far((0, 2), (1, 3)), far((1, 3), (0, 2))

        @pl.when(y == 0)
        def _():
            start(far0[0] + far0[1])

        @pl.when(y == 1)
        def _():
            start(far1[0] + far1[1])

        out_copies += far0[0]
        in_copies += far0[1]

    wait(first)
    mixed = dot(hot5[...], tw[...])
    act = gelu(norm(mixed, gain_out[0:1])).astype(BF)
    wait(out_copies)
    hidden = dot(jnp.concatenate([act, hot1[...]], axis=1), wo[...]).astype(BF)
    rows = hidden.shape[0]
    hid[...] = hidden[EDGE : rows - EDGE]
    normed = gelu(norm(hidden.astype(F32), gain_in[1:2])).astype(BF)
    wait(in_copies)
    wide = dot(normed, wi[...])
    pos = span[0] + lax.broadcasted_iota(jnp.int32, (rows, 1), 0)
    valid = jnp.where((pos >= 0) & (pos < span[1]), 1.0, 0.0)
    ci[...] = (gelu(norm(wide, gain_mid[1:2])) * valid).astype(BF)


def last_kernel(split, ci, hid, gain_out, *rest):
    *w, out, wt, wo, sem = rest

    def conv(src, col, width, row, n):
        copies = []
        done = 0
        while done < width:
            tap, inner = divmod(col + done, H)
            step = min(H - inner, width - done)
            copies.append(
                pltpu.make_async_copy(
                    src.at[:, done : done + step],
                    wt.at[pl.ds(tap * H + row, n), inner : inner + step],
                    sem.at[0],
                )
            )
            done += step
        return copies

    if not split:
        conv_copies = conv(w[0], 0, KERNEL * H, 0, H)
        out_copies = [pltpu.make_async_copy(w[1], wo, sem.at[1])]
        start(conv_copies + out_copies)
    else:
        w_conv, w_out, near_conv, near_out = w[:4]
        parts, near_parts = w[4:8], w[8:12]
        x, core, y, z = place()
        n = w_out.shape[1]
        half = n // 2
        rest_cols = KERNEL * H - CUT_B
        conv_copies, out_copies = [], []
        for c, v, o in ((core, w_conv, w_out), (1 - core, near_conv, near_out)):
            row = pl.multiple_of((2 * x + c) * n, 16)
            conv_copies += conv(v.at[1], 0, KERNEL * H, row, n)
            out_copies.append(pltpu.make_async_copy(o.at[1], wo.at[pl.ds(row, n)], sem.at[1]))

        def far(head, tail):
            cv, out = [], []
            for c, of in ((core, parts), (1 - core, near_parts)):
                for p, zz in zip(head, (z, 1 - z)):
                    row = pl.multiple_of((2 * (1 - x) + c) * n + zz * half, 16)
                    cv += conv(of[p], 0, CUT_A, row, half)
                for p, zz in zip(tail, (z, 1 - z)):
                    row = pl.multiple_of((2 * (1 - x) + c) * n + zz * half, 16)
                    skip = CUT_A - CUT_B
                    cv += conv(of[p].at[:, skip:rest_cols], CUT_A, rest_cols - skip, row, half)
                    out.append(pltpu.make_async_copy(of[p].at[:, rest_cols:], wo.at[pl.ds(row, half)], sem.at[1]))
            return cv, out

        start(conv_copies + out_copies)
        far0, far1 = far((0, 2), (1, 3)), far((1, 3), (0, 2))

        @pl.when(y == 0)
        def _():
            start(far0[0] + far0[1])

        @pl.when(y == 1)
        def _():
            start(far1[0] + far1[1])

        conv_copies += far0[0]
        out_copies += far0[1]

    rows = out.shape[0]
    blocks = [0, 16 * (rows // 32), rows]
    for b in range(2):
        lo, hi = blocks[b], blocks[b + 1]
        lhs = jnp.concatenate([ci[lo + k * DIL1 : hi + k * DIL1] for k in range(KERNEL)], axis=1)
        if b == 0:
            wait(conv_copies)
        mixed = dot(lhs, wt[...])
        act = gelu(norm(mixed, gain_out[1:2])).astype(BF)
        if b == 0:
            wait(out_copies)
        out[lo:hi] = (hid[lo:hi].astype(F32) + dot(act, wo[...])).astype(BF)


def after(x, *deps):
    return lax.optimization_barrier((x, *deps))[0]


def per_device(tokens, breaks, lengths, embed_table, break_vec, gain_in, gain_mid, gain_out, w_in, conv_w, w_out):
    rows = tokens.shape[1]
    width = embed_table.shape[1]
    roll_at = lax.axis_index("roll")
    seq_at = lax.axis_index("seq")
    rolls = lax.axis_size("roll")
    seqs = lax.axis_size("seq")
    split = rolls == 4 and seqs % 4 == 0

    def core_swap(x):
        return lax.ppermute(x, "roll", [(i, i ^ 1) for i in range(rolls)])

    def x_swap(x):
        return lax.ppermute(x, "roll", [(i, i ^ 2) for i in range(rolls)])

    def seq_swap(x, bits):
        return lax.ppermute(x, "seq", [(i, i ^ bits) for i in range(seqs)])

    span = jnp.stack([(seq_at * rows).astype(jnp.int32) - EDGE, lengths[0]])
    wide_rows = rows + 2 * EDGE
    codes = tokens[0] + SLOT * breaks[0]

    if split:
        shard = w_out.shape[1] // 2
        part_a, part_b = pl.pallas_call(
            part_kernel,
            out_shape=(jax.ShapeDtypeStruct((shard, width), BF), jax.ShapeDtypeStruct((shard, CUT_A), BF)),
            in_specs=[HBM] * 3,
            out_specs=(HBM, HBM),
            scratch_shapes=[pltpu.SemaphoreType.DMA],
            compiler_params=params(4),
        )(w_in, conv_w, w_out)
        far_a = x_swap(part_a)
        near_in, near_conv, near_out = core_swap(w_in), core_swap(conv_w), core_swap(w_out)

    table, part = pl.pallas_call(
        embed_kernel,
        out_shape=(
            jax.ShapeDtypeStruct((CODES, width), BF),
            jax.ShapeDtypeStruct((CODES, H), F32),
        ),
        in_specs=[VMEM, VMEM, VMEM, HBM],
        out_specs=(VMEM, VMEM),
        scratch_shapes=[
            pltpu.VMEM((CODES, width), F32),
            pltpu.VMEM(w_in.shape[1:], BF),
            pltpu.SemaphoreType.DMA,
        ],
        compiler_params=params(12),
    )(embed_table, break_vec[None], gain_in, w_in)

    if split:
        own = part + core_swap(part)
        other = x_swap(own.astype(BF))
        codes = after(codes, own)
        low = seq_at % 2 == 0
        ends = codes[rows - REACH :], codes[:REACH]
        even = seq_swap(jnp.where(low, *ends), 1)
        pairs = [(i, i + 1) for i in range(1, seqs - 1, 2)]
        odd = lax.ppermute(jnp.where(low, *ends[::-1]), "seq", pairs + [(j, i) for i, j in pairs])
        before, behind = jnp.where(low, odd, even), jnp.where(low, even, odd)
        far_b = x_swap(after(part_b, own))
        other = after(other, near_in, near_conv, near_out)
    else:
        own = lax.psum(part, "roll")
        other = jnp.zeros((CODES, H), BF)
        pairs = [(i, i + 1) for i in range(seqs - 1)]
        before = lax.ppermute(codes[rows - REACH :], "seq", pairs)
        behind = lax.ppermute(codes[:REACH], "seq", [(j, i) for i, j in pairs])
    count = rows + 2 * REACH
    spare = jnp.zeros((-count % 128,), jnp.int32)
    near = jnp.concatenate([before, codes, behind, spare])[None]

    wide = KERNEL * H
    shapes = [(SLOT, F32), (SLOT, BF)] if split else [(CODES, F32)]
    taps = pl.pallas_call(
        functools.partial(table_kernel, split),
        out_shape=[jax.ShapeDtypeStruct((n, wide), t) for n, t in shapes],
        in_specs=[VMEM, VMEM, VMEM, HBM],
        out_specs=[VMEM] * len(shapes),
        scratch_shapes=[
            pltpu.VMEM(conv_w.shape[1:], BF),
            pltpu.VMEM((CODES, wide), F32),
            pltpu.SemaphoreType.DMA,
        ],
        compiler_params=params(12),
    )(own, other, gain_mid, conv_w)
    if split:
        mine = taps[0] + core_swap(taps[1]).astype(F32)
        sent = mine.astype(BF)
        relay = after(far_a, sent)
        parts_a = [far_a] + [seq_swap(relay, b) for b in (1, 2, 3)]
        near = after(near, sent)
        other = x_swap(sent)

    hot5, hot1 = pl.pallas_call(
        hot_kernel,
        out_shape=(
            jax.ShapeDtypeStruct((wide_rows, KERNEL * CODES), BF),
            jax.ShapeDtypeStruct((wide_rows, CODES), BF),
        ),
        in_specs=[SMEM, VMEM],
        out_specs=(VMEM, VMEM),
        compiler_params=params(12),
    )(span, near)

    if split:
        mine = (mine + after(other, hot1).astype(F32)).astype(BF)
        theirs = core_swap(mine)
        near_a = [core_swap(relay)] + [core_swap(after(p, theirs)) for p in parts_a[1:]]
        relay = after(far_b, mine)
        parts_b = [far_b] + [seq_swap(relay, b) for b in (1, 2, 3)]
        weights_a = [mine, theirs, w_out, w_in, near_out, near_in] + parts_a + near_a
    else:
        taps = lax.psum(taps[0], "roll").astype(BF)
        gather = lambda w: lax.all_gather(w, "roll", axis=0, tiled=True)
        weights_a, weights_b = [taps, gather(w_out[0]), gather(w_in[1])], [gather(conv_w[1]), gather(w_out[1])]

    ci, hid = pl.pallas_call(
        functools.partial(rows_kernel, split),
        out_shape=(
            jax.ShapeDtypeStruct((wide_rows, H), BF),
            jax.ShapeDtypeStruct((rows, width), BF),
        ),
        in_specs=[SMEM, VMEM, VMEM, ANY, VMEM, VMEM, VMEM] + [HBM if w is w_out or w is w_in else ANY for w in weights_a],
        out_specs=(VMEM, VMEM),
        scratch_shapes=[
            pltpu.VMEM((KERNEL * CODES, H), BF),
            pltpu.VMEM((H + CODES, width), BF),
            pltpu.VMEM((width, H), BF),
            pltpu.SemaphoreType.DMA((3,)),
        ],
        compiler_params=params(36),
    )(span, hot5, hot1, table, gain_out, gain_in, gain_mid, *weights_a)

    if split:
        near_b = [core_swap(after(p, ci)) for p in parts_b]
        weights_b = [conv_w, w_out, near_conv, near_out] + parts_b + near_b
    out = pl.pallas_call(
        functools.partial(last_kernel, split),
        out_shape=jax.ShapeDtypeStruct((rows, width), BF),
        in_specs=[VMEM] * 3 + [HBM if w is w_out or w is conv_w else ANY for w in weights_b],
        out_specs=VMEM,
        scratch_shapes=[
            pltpu.VMEM((KERNEL * H, H), BF),
            pltpu.VMEM((H, width), BF),
            pltpu.SemaphoreType.DMA((2,)),
        ],
        compiler_params=params(24),
    )(ci, hid, gain_out, *weights_b)
    return out[None]


def solution(mesh):
    placed = (
        P("roll", "seq"),
        P("roll", "seq"),
        P("roll"),
        P(),
        P(),
        P(),
        P(),
        P(),
        P(None, "roll", None),
        P(None, "roll", None),
        P(None, "roll", None),
    )
    return jax.shard_map(
        per_device, mesh=mesh, in_specs=placed, out_specs=P("roll", "seq", None), check_vma=False
    )
```

```python
import functools

import jax
import jax.numpy as jnp
from jax import lax
from jax.experimental import pallas as pl
from jax.experimental.pallas import tpu as pltpu
from jax.sharding import PartitionSpec as P

H = 640
KERNEL = 5
VOCAB = 30
SLOT = 32
CODES = 2 * SLOT
BASE_DILATION = 64
DIL0 = BASE_DILATION
DIL1 = 2 * BASE_DILATION
HALF = KERNEL // 2
EDGE = HALF * DIL1
REACH = EDGE + HALF * DIL0
BF = jnp.bfloat16
F32 = jnp.float32
VMEM = pl.BlockSpec(memory_space=pltpu.VMEM)
SMEM = pl.BlockSpec(memory_space=pltpu.SMEM)
ANY = pl.BlockSpec(memory_space=pl.ANY)
HBM = pl.BlockSpec(memory_space=pltpu.HBM)
CUT_A = 18 * 128
CUT_B = 17 * 128


def params(mib):
    return pltpu.CompilerParams(vmem_limit_bytes=mib * 1024 * 1024)


def gelu(x):
    return (0.5 * x) * (1.0 + lax.erf(x * 0.5**0.5))


def norm(x, gain):
    center = jnp.mean(x, axis=-1, keepdims=True)
    d = x - center
    spread = jnp.mean(d * d, axis=-1, keepdims=True)
    return d * lax.rsqrt(spread + 1e-5) * gain


def dot(a, b):
    return jnp.dot(a, b, preferred_element_type=F32)


def place():
    roll, seq = lax.axis_index("roll"), lax.axis_index("seq")
    return lax.div(roll, 2), lax.rem(roll, 2), lax.rem(seq, 2), lax.rem(lax.div(seq, 2), 2)


def start(copies):
    for c in copies:
        c.start()


def wait(copies):
    for c in copies:
        c.wait()


def pick(rows, columns, first):
    i = lax.broadcasted_iota(jnp.int32, (rows, columns), 0)
    j = lax.broadcasted_iota(jnp.int32, (rows, columns), 1)
    return jnp.where(i == j + first, 1.0, 0.0).astype(BF)


def part_copies(y_is_one, row_bit, w_in, conv_w, w_out, a, b, sem):
    n = b.shape[0]
    r = pl.multiple_of(row_bit * n, 16)
    r2 = pl.multiple_of(row_bit * 2 * n, 16)
    rest = conv_w.shape[2] - CUT_B
    if y_is_one:
        pairs = [
            (conv_w.at[1, pl.ds(r, n), CUT_B:], b.at[:, 0:rest]),
            (w_out.at[1, pl.ds(r, n)], b.at[:, rest:]),
        ]
        if a is not None:
            pairs += [
                (w_in.at[1, pl.ds(r2, n)], a.at[:, 0:H]),
                (w_in.at[1, pl.ds(r2 + n, n)], a.at[:, H : 2 * H]),
            ]
    else:
        pairs = [(conv_w.at[1, pl.ds(r, n), 0:CUT_A], b)]
        if a is not None:
            pairs.append((w_out.at[0, pl.ds(r, n)], a))
    return [pltpu.make_async_copy(s, d, sem) for s, d in pairs]


def first_kernel(split, embed, brk, gain, w_in, conv_w, w_out, table, part, *rest):
    *parts, emb, bv, g, w, full, sem = rest
    copies = [
        pltpu.make_async_copy(s, d, sem.at[0])
        for s, d in ((embed, emb), (brk, bv), (gain, g), (w_in.at[0], w))
    ]
    start(copies)
    if split:
        _, _, y, z = place()
        kinds = []
        for kind in range(2):
            kinds.append(
                part_copies(kind == 1, z, w_in, conv_w, w_out, parts[0], parts[1], sem.at[1])
                + part_copies(kind == 0, 1 - z, w_in, conv_w, w_out, None, parts[2], sem.at[1])
            )

            @pl.when(y == kind)
            def _():
                start(kinds[kind])

    wait(copies)
    full[...] = jnp.zeros_like(full)
    full[0:VOCAB] = emb[...]
    full[SLOT : SLOT + VOCAB] = emb[...] + bv[...]
    hidden = full[...].astype(BF)
    table[...] = hidden
    normed = gelu(norm(hidden.astype(F32), g[0:1])).astype(BF)
    rows = w.shape[0]
    mine = dot(normed, pick(normed.shape[1], rows, lax.axis_index("roll") * rows)).astype(BF)
    part[...] = dot(mine, w[...])
    if split:
        for kind in range(2):

            @pl.when(y == kind)
            def _():
                wait(kinds[kind])


def table_kernel(split, own, other, gain, w_all, *rest):
    *outs, w, full, sem = rest
    copy = pltpu.make_async_copy(w_all.at[0], w, sem)
    copy.start()
    wide = own[...] + other[...].astype(F32)
    t = gelu(norm(wide, gain[0:1])).astype(BF)
    rows = w.shape[0]
    mine = dot(t, pick(t.shape[1], rows, lax.axis_index("roll") * rows)).astype(BF)
    copy.wait()
    full[...] = dot(mine, w[...])
    if split:
        core = lax.rem(lax.axis_index("roll"), 2)
        outs[0][...] = full[pl.ds(pl.multiple_of(core * SLOT, SLOT), SLOT)]
        outs[1][...] = full[pl.ds(pl.multiple_of((1 - core) * SLOT, SLOT), SLOT)].astype(BF)
    else:
        outs[0][...] = full[...]


def hot_kernel(span, near, hot5, hot1):
    codes = near[...]
    count = codes.shape[1]
    rows = hot5.shape[0]
    pos = span[0] - HALF * DIL0 + lax.broadcasted_iota(jnp.int32, codes.shape, 1)
    masked = jnp.where((pos >= 0) & (pos < span[1]), codes, -1)
    lanes = lax.broadcasted_iota(jnp.int32, (CODES, count), 0)
    taps = jnp.where(lanes == masked, 1.0, 0.0).T.astype(BF)
    for k in range(KERNEL):
        hot5[:, k * CODES : (k + 1) * CODES] = taps[k * DIL0 : k * DIL0 + rows]
    center = jnp.where(lanes == codes, 1.0, 0.0).T.astype(BF)
    hot1[...] = center[HALF * DIL0 : HALF * DIL0 + rows]


def rows_kernel(split, span, hot5, hot1, table, gain_out, gain_in, gain_mid, *rest):
    *w, ci, hid, tw, wo, wi, sem = rest
    depth = wo.shape[0] - CODES
    if split:
        core = lax.rem(lax.axis_index("roll"), 2)
        taps = ((w[0], core * SLOT, SLOT), (w[1], (1 - core) * SLOT, SLOT))
        w = w[2:]
    else:
        taps = ((w[0], 0, CODES),)
        w = w[1:]
    first = [
        pltpu.make_async_copy(
            t.at[:, k * H : (k + 1) * H], tw.at[pl.ds(pl.multiple_of(k * CODES + at, 16), n)], sem.at[0]
        )
        for t, at, n in taps
        for k in range(KERNEL)
    ]
    first.append(pltpu.make_async_copy(table, wo.at[depth:], sem.at[0]))
    start(first)
    if not split:
        out_copies = [pltpu.make_async_copy(w[0], wo.at[0:depth], sem.at[1])]
        in_copies = [pltpu.make_async_copy(w[1], wi, sem.at[2])]
        start(out_copies + in_copies)
    else:
        w_out, w_in, near_out, near_in = w[:4]
        parts, near_parts = w[4:8], w[8:12]
        x, core, y, z = place()
        n = w_out.shape[1]
        m = w_in.shape[1]
        half = n // 2
        out_copies, in_copies = [], []
        for c, o, i in ((core, w_out, w_in), (1 - core, near_out, near_in)):
            at = 2 * x + c
            out_copies.append(pltpu.make_async_copy(o.at[0], wo.at[pl.ds(pl.multiple_of(at * n, 16), n)], sem.at[1]))
            in_copies.append(pltpu.make_async_copy(i.at[1], wi.at[pl.ds(pl.multiple_of(at * m, 16), m)], sem.at[2]))

        def far(outs, ins):
            out, into = [], []
            for c, of in ((core, parts), (1 - core, near_parts)):
                at = 2 * (1 - x) + c
                for p, zz in zip(outs, (z, 1 - z)):
                    row = pl.multiple_of(at * n + zz * half, 16)
                    out.append(pltpu.make_async_copy(of[p], wo.at[pl.ds(row, half)], sem.at[1]))
                for p, zz in zip(ins, (z, 1 - z)):
                    for j in range(2):
                        row = pl.multiple_of(at * m + zz * n + j * half, 16)
                        into.append(
                            pltpu.make_async_copy(of[p].at[:, j * H : (j + 1) * H], wi.at[pl.ds(row, half)], sem.at[2])
                        )
            return out, into

        start(out_copies + in_copies)
        far0, far1 = far((0, 2), (1, 3)), far((1, 3), (0, 2))

        @pl.when(y == 0)
        def _():
            start(far0[0] + far0[1])

        @pl.when(y == 1)
        def _():
            start(far1[0] + far1[1])

        out_copies += far0[0]
        in_copies += far0[1]

    wait(first)
    mixed = dot(hot5[...], tw[...])
    act = gelu(norm(mixed, gain_out[0:1])).astype(BF)
    wait(out_copies)
    hidden = dot(jnp.concatenate([act, hot1[...]], axis=1), wo[...]).astype(BF)
    rows = hidden.shape[0]
    hid[...] = hidden[EDGE : rows - EDGE]
    normed = gelu(norm(hidden.astype(F32), gain_in[1:2])).astype(BF)
    wait(in_copies)
    wide = dot(normed, wi[...])
    pos = span[0] + lax.broadcasted_iota(jnp.int32, (rows, 1), 0)
    valid = jnp.where((pos >= 0) & (pos < span[1]), 1.0, 0.0)
    ci[...] = (gelu(norm(wide, gain_mid[1:2])) * valid).astype(BF)


def last_kernel(split, ci, hid, gain_out, *rest):
    *w, out, wt, wo, sem = rest

    def conv(src, col, width, row, n):
        copies = []
        done = 0
        while done < width:
            tap, inner = divmod(col + done, H)
            step = min(H - inner, width - done)
            copies.append(
                pltpu.make_async_copy(
                    src.at[:, done : done + step],
                    wt.at[pl.ds(tap * H + row, n), inner : inner + step],
                    sem.at[0],
                )
            )
            done += step
        return copies

    if not split:
        conv_copies = conv(w[0], 0, KERNEL * H, 0, H)
        out_copies = [pltpu.make_async_copy(w[1], wo, sem.at[1])]
        start(conv_copies + out_copies)
    else:
        w_conv, w_out, near_conv, near_out = w[:4]
        parts, near_parts = w[4:8], w[8:12]
        x, core, y, z = place()
        n = w_out.shape[1]
        half = n // 2
        rest_cols = KERNEL * H - CUT_B
        conv_copies, out_copies = [], []
        for c, v, o in ((core, w_conv, w_out), (1 - core, near_conv, near_out)):
            row = pl.multiple_of((2 * x + c) * n, 16)
            conv_copies += conv(v.at[1], 0, KERNEL * H, row, n)
            out_copies.append(pltpu.make_async_copy(o.at[1], wo.at[pl.ds(row, n)], sem.at[1]))

        def far(head, tail):
            cv, out = [], []
            for c, of in ((core, parts), (1 - core, near_parts)):
                for p, zz in zip(head, (z, 1 - z)):
                    row = pl.multiple_of((2 * (1 - x) + c) * n + zz * half, 16)
                    cv += conv(of[p], 0, CUT_A, row, half)
                for p, zz in zip(tail, (z, 1 - z)):
                    row = pl.multiple_of((2 * (1 - x) + c) * n + zz * half, 16)
                    skip = CUT_A - CUT_B
                    cv += conv(of[p].at[:, skip:rest_cols], CUT_A, rest_cols - skip, row, half)
                    out.append(pltpu.make_async_copy(of[p].at[:, rest_cols:], wo.at[pl.ds(row, half)], sem.at[1]))
            return cv, out

        start(conv_copies + out_copies)
        far0, far1 = far((0, 2), (1, 3)), far((1, 3), (0, 2))

        @pl.when(y == 0)
        def _():
            start(far0[0] + far0[1])

        @pl.when(y == 1)
        def _():
            start(far1[0] + far1[1])

        conv_copies += far0[0]
        out_copies += far0[1]

    rows = out.shape[0]
    blocks = [0, 16 * (rows // 32), rows]
    for b in range(2):
        lo, hi = blocks[b], blocks[b + 1]
        lhs = jnp.concatenate([ci[lo + k * DIL1 : hi + k * DIL1] for k in range(KERNEL)], axis=1)
        if b == 0:
            wait(conv_copies)
        mixed = dot(lhs, wt[...])
        act = gelu(norm(mixed, gain_out[1:2])).astype(BF)
        if b == 0:
            wait(out_copies)
        out[lo:hi] = (hid[lo:hi].astype(F32) + dot(act, wo[...])).astype(BF)


def after(x, *deps):
    return lax.optimization_barrier((x, *deps))[0]


def per_device(tokens, breaks, lengths, embed_table, break_vec, gain_in, gain_mid, gain_out, w_in, conv_w, w_out):
    rows = tokens.shape[1]
    width = embed_table.shape[1]
    roll_at = lax.axis_index("roll")
    seq_at = lax.axis_index("seq")
    rolls = lax.axis_size("roll")
    seqs = lax.axis_size("seq")
    split = rolls == 4 and seqs % 4 == 0

    def core_swap(x):
        return lax.ppermute(x, "roll", [(i, i ^ 1) for i in range(rolls)])

    def x_swap(x):
        return lax.ppermute(x, "roll", [(i, i ^ 2) for i in range(rolls)])

    def seq_swap(x, bits):
        return lax.ppermute(x, "seq", [(i, i ^ bits) for i in range(seqs)])

    span = jnp.stack([(seq_at * rows).astype(jnp.int32) - EDGE, lengths[0]])
    wide_rows = rows + 2 * EDGE
    codes = tokens[0] + SLOT * breaks[0]

    shard = w_out.shape[1] // 2
    shapes = [((CODES, width), BF), ((CODES, H), F32)]
    if split:
        near_in, near_conv, near_out = core_swap(w_in), core_swap(conv_w), core_swap(w_out)
        shapes += [((shard, width), BF), ((shard, CUT_A), BF), ((shard, CUT_A), BF)]
    table, part, *parts = pl.pallas_call(
        functools.partial(first_kernel, split),
        out_shape=[jax.ShapeDtypeStruct(n, t) for n, t in shapes],
        in_specs=[HBM] * 6,
        out_specs=[VMEM] * 2 + [HBM] * (len(shapes) - 2),
        scratch_shapes=[
            pltpu.VMEM(embed_table.shape, F32),
            pltpu.VMEM((1, width), F32),
            pltpu.VMEM(gain_in.shape, F32),
            pltpu.VMEM(w_in.shape[1:], BF),
            pltpu.VMEM((CODES, width), F32),
            pltpu.SemaphoreType.DMA((2,)),
        ],
        compiler_params=params(56),
    )(embed_table, break_vec[None], gain_in, w_in, conv_w, w_out)

    if split:
        own = part + core_swap(part)
        far_a = x_swap(parts[0])
        other = x_swap(own.astype(BF))
        codes = after(codes, own)
        low = seq_at % 2 == 0
        ends = codes[rows - REACH :], codes[:REACH]
        even = seq_swap(jnp.where(low, *ends), 1)
        pairs = [(i, i + 1) for i in range(1, seqs - 1, 2)]
        odd = lax.ppermute(jnp.where(low, *ends[::-1]), "seq", pairs + [(j, i) for i, j in pairs])
        before, behind = jnp.where(low, odd, even), jnp.where(low, even, odd)
        far_b = x_swap(after(parts[1], own))
        other = after(other, near_in, near_conv, near_out)
    else:
        own = lax.psum(part, "roll")
        other = jnp.zeros((CODES, H), BF)
        pairs = [(i, i + 1) for i in range(seqs - 1)]
        before = lax.ppermute(codes[rows - REACH :], "seq", pairs)
        behind = lax.ppermute(codes[:REACH], "seq", [(j, i) for i, j in pairs])
    count = rows + 2 * REACH
    spare = jnp.zeros((-count % 128,), jnp.int32)
    near = jnp.concatenate([before, codes, behind, spare])[None]

    wide = KERNEL * H
    shapes = [(SLOT, F32), (SLOT, BF)] if split else [(CODES, F32)]
    taps = pl.pallas_call(
        functools.partial(table_kernel, split),
        out_shape=[jax.ShapeDtypeStruct((n, wide), t) for n, t in shapes],
        in_specs=[VMEM, VMEM, VMEM, HBM],
        out_specs=[VMEM] * len(shapes),
        scratch_shapes=[
            pltpu.VMEM(conv_w.shape[1:], BF),
            pltpu.VMEM((CODES, wide), F32),
            pltpu.SemaphoreType.DMA,
        ],
        compiler_params=params(12),
    )(own, other, gain_mid, conv_w)
    if split:
        mine = taps[0] + core_swap(taps[1]).astype(F32)
        sent = mine.astype(BF)
        relay = after(far_a, taps[1])
        parts_a = [far_a] + [seq_swap(relay, b) for b in (1, 2, 3)]
        near = after(near, sent)
        other = x_swap(sent)

    hot5, hot1 = pl.pallas_call(
        hot_kernel,
        out_shape=(
            jax.ShapeDtypeStruct((wide_rows, KERNEL * CODES), BF),
            jax.ShapeDtypeStruct((wide_rows, CODES), BF),
        ),
        in_specs=[SMEM, VMEM],
        out_specs=(VMEM, VMEM),
        compiler_params=params(12),
    )(span, near)

    if split:
        mine = (mine + after(other, hot1, *parts_a).astype(F32)).astype(BF)
        theirs = core_swap(mine)
        near_a = [core_swap(relay)] + [core_swap(after(p, mine)) for p in parts_a[1:]]
        relay = after(far_b, mine)
        parts_b = [far_b, seq_swap(relay, 1), seq_swap(relay, 2), x_swap(after(parts[2], mine))]
        weights_a = [mine, theirs, w_out, w_in, near_out, near_in] + parts_a + near_a
    else:
        taps = lax.psum(taps[0], "roll").astype(BF)
        gather = lambda w: lax.all_gather(w, "roll", axis=0, tiled=True)
        weights_a, weights_b = [taps, gather(w_out[0]), gather(w_in[1])], [gather(conv_w[1]), gather(w_out[1])]

    ci, hid = pl.pallas_call(
        functools.partial(rows_kernel, split),
        out_shape=(
            jax.ShapeDtypeStruct((wide_rows, H), BF),
            jax.ShapeDtypeStruct((rows, width), BF),
        ),
        in_specs=[SMEM, VMEM, VMEM, ANY, VMEM, VMEM, VMEM] + [HBM if w is w_out or w is w_in else ANY for w in weights_a],
        out_specs=(VMEM, VMEM),
        scratch_shapes=[
            pltpu.VMEM((KERNEL * CODES, H), BF),
            pltpu.VMEM((H + CODES, width), BF),
            pltpu.VMEM((width, H), BF),
            pltpu.SemaphoreType.DMA((3,)),
        ],
        compiler_params=params(30),
    )(span, hot5, hot1, table, gain_out, gain_in, gain_mid, *weights_a)

    if split:
        near_b = [core_swap(after(p, ci)) for p in parts_b]
        weights_b = [conv_w, w_out, near_conv, near_out] + parts_b + near_b
    out = pl.pallas_call(
        functools.partial(last_kernel, split),
        out_shape=jax.ShapeDtypeStruct((rows, width), BF),
        in_specs=[VMEM] * 3 + [HBM if w is w_out or w is conv_w else ANY for w in weights_b],
        out_specs=VMEM,
        scratch_shapes=[
            pltpu.VMEM((KERNEL * H, H), BF),
            pltpu.VMEM((H, width), BF),
            pltpu.SemaphoreType.DMA((2,)),
        ],
        compiler_params=params(24),
    )(ci, hid, gain_out, *weights_b)
    return out[None]


def solution(mesh):
    placed = (
        P("roll", "seq"),
        P("roll", "seq"),
        P("roll"),
        P(),
        P(),
        P(),
        P(),
        P(),
        P(None, "roll", None),
        P(None, "roll", None),
        P(None, "roll", None),
    )
    return jax.shard_map(
        per_device, mesh=mesh, in_specs=placed, out_specs=P("roll", "seq", None), check_vma=False
    )
```

```python
import functools

import jax
import jax.numpy as jnp
from jax import lax
from jax.experimental import pallas as pl
from jax.experimental.pallas import tpu as pltpu
from jax.sharding import PartitionSpec as P

H = 640
KERNEL = 5
VOCAB = 30
SLOT = 32
CODES = 2 * SLOT
BASE_DILATION = 64
DIL0 = BASE_DILATION
DIL1 = 2 * BASE_DILATION
HALF = KERNEL // 2
EDGE = HALF * DIL1
REACH = EDGE + HALF * DIL0
BF = jnp.bfloat16
F32 = jnp.float32
VMEM = pl.BlockSpec(memory_space=pltpu.VMEM)
SMEM = pl.BlockSpec(memory_space=pltpu.SMEM)
ANY = pl.BlockSpec(memory_space=pl.ANY)
HBM = pl.BlockSpec(memory_space=pltpu.HBM)
CUT_A = 18 * 128
CUT_B = 17 * 128


def params(mib):
    return pltpu.CompilerParams(vmem_limit_bytes=mib * 1024 * 1024)


def gelu(x):
    return (0.5 * x) * (1.0 + lax.erf(x * 0.5**0.5))


def norm(x, gain):
    center = jnp.mean(x, axis=-1, keepdims=True)
    d = x - center
    spread = jnp.mean(d * d, axis=-1, keepdims=True)
    return d * lax.rsqrt(spread + 1e-5) * gain


def dot(a, b):
    return jnp.dot(a, b, preferred_element_type=F32)


def place():
    roll, seq = lax.axis_index("roll"), lax.axis_index("seq")
    return lax.div(roll, 2), lax.rem(roll, 2), lax.rem(seq, 2), lax.rem(lax.div(seq, 2), 2)


def start(copies):
    for c in copies:
        c.start()


def wait(copies):
    for c in copies:
        c.wait()


def stagger(stages):
    for t in range(len(stages) + 1):
        for b in range(2):
            if 0 <= t - b < len(stages):
                stages[t - b](b)


def pick(rows, columns, first):
    i = lax.broadcasted_iota(jnp.int32, (rows, columns), 0)
    j = lax.broadcasted_iota(jnp.int32, (rows, columns), 1)
    return jnp.where(i == j + first, 1.0, 0.0).astype(BF)


def part_copies(y_is_one, row_bit, w_in, conv_w, w_out, a, b, sem):
    n = b.shape[0]
    r = pl.multiple_of(row_bit * n, 16)
    r2 = pl.multiple_of(row_bit * 2 * n, 16)
    rest = conv_w.shape[2] - CUT_B
    if y_is_one:
        pairs = [
            (conv_w.at[1, pl.ds(r, n), CUT_B:], b.at[:, 0:rest]),
            (w_out.at[1, pl.ds(r, n)], b.at[:, rest:]),
        ]
        if a is not None:
            pairs += [
                (w_in.at[1, pl.ds(r2, n)], a.at[:, 0:H]),
                (w_in.at[1, pl.ds(r2 + n, n)], a.at[:, H : 2 * H]),
            ]
    else:
        pairs = [(conv_w.at[1, pl.ds(r, n), 0:CUT_A], b)]
        if a is not None:
            pairs.append((w_out.at[0, pl.ds(r, n)], a))
    return [pltpu.make_async_copy(s, d, sem) for s, d in pairs]


def first_kernel(split, embed, brk, gain, w_in, conv_w, w_out, table, part, *rest):
    *parts, emb, bv, g, w, full, sem = rest
    copies = [
        pltpu.make_async_copy(s, d, sem.at[0])
        for s, d in ((embed, emb), (brk, bv), (gain, g), (w_in.at[0], w))
    ]
    start(copies)
    if split:
        _, _, y, z = place()
        kinds = []
        for kind in range(2):
            kinds.append(
                part_copies(kind == 1, z, w_in, conv_w, w_out, parts[0], parts[1], sem.at[1])
                + part_copies(kind == 0, 1 - z, w_in, conv_w, w_out, None, parts[2], sem.at[1])
            )

            @pl.when(y == kind)
            def _():
                start(kinds[kind])

    wait(copies)
    full[...] = jnp.zeros_like(full)
    full[0:VOCAB] = emb[...]
    full[SLOT : SLOT + VOCAB] = emb[...] + bv[...][None, :]
    hidden = full[...].astype(BF)
    table[...] = hidden
    normed = gelu(norm(hidden.astype(F32), g[0:1])).astype(BF)
    rows = w.shape[0]
    mine = dot(normed, pick(normed.shape[1], rows, lax.axis_index("roll") * rows)).astype(BF)
    part[...] = dot(mine, w[...])
    if split:
        for kind in range(2):

            @pl.when(y == kind)
            def _():
                wait(kinds[kind])


def table_kernel(split, own, other, gain, w_all, *rest):
    *outs, w, full, sem = rest
    copy = pltpu.make_async_copy(w_all.at[0], w, sem)
    copy.start()
    wide = own[...] + other[...].astype(F32)
    t = gelu(norm(wide, gain[0:1])).astype(BF)
    rows = w.shape[0]
    mine = dot(t, pick(t.shape[1], rows, lax.axis_index("roll") * rows)).astype(BF)
    copy.wait()
    full[...] = dot(mine, w[...])
    if split:
        core = lax.rem(lax.axis_index("roll"), 2)
        outs[0][...] = full[pl.ds(pl.multiple_of(core * SLOT, SLOT), SLOT)]
        outs[1][...] = full[pl.ds(pl.multiple_of((1 - core) * SLOT, SLOT), SLOT)].astype(BF)
    else:
        outs[0][...] = full[...]


def hot_kernel(span, near, hot5, hot1):
    codes = near[...]
    count = codes.shape[1]
    rows = hot5.shape[0]
    pos = span[0] - HALF * DIL0 + lax.broadcasted_iota(jnp.int32, codes.shape, 1)
    masked = jnp.where((pos >= 0) & (pos < span[1]), codes, -1)
    lanes = lax.broadcasted_iota(jnp.int32, (CODES, count), 0)
    taps = jnp.where(lanes == masked, 1.0, 0.0).T.astype(BF)
    for k in range(KERNEL):
        hot5[:, k * CODES : (k + 1) * CODES] = taps[k * DIL0 : k * DIL0 + rows]
    center = jnp.where(lanes == codes, 1.0, 0.0).T.astype(BF)
    hot1[...] = center[HALF * DIL0 : HALF * DIL0 + rows]


def rows_kernel(split, span, hot5, hot1, table, gain_out, gain_in, gain_mid, *rest):
    *w, ci, hid, tw, wo, wi, sem = rest
    depth = wo.shape[0] - CODES
    if split:
        core = lax.rem(lax.axis_index("roll"), 2)
        taps = ((w[0], core * SLOT, SLOT), (w[1], (1 - core) * SLOT, SLOT))
        w = w[2:]
    else:
        taps = ((w[0], 0, CODES),)
        w = w[1:]
    first = [
        pltpu.make_async_copy(
            t.at[:, k * H : (k + 1) * H], tw.at[pl.ds(pl.multiple_of(k * CODES + at, 16), n)], sem.at[0]
        )
        for t, at, n in taps
        for k in range(KERNEL)
    ]
    first.append(pltpu.make_async_copy(table, wo.at[depth:], sem.at[0]))
    start(first)
    if not split:
        out_copies = [pltpu.make_async_copy(w[0], wo.at[0:depth], sem.at[1])]
        in_copies = [pltpu.make_async_copy(w[1], wi, sem.at[2])]
        start(out_copies + in_copies)
    else:
        w_out, w_in, near_out, near_in = w[:4]
        parts, near_parts = w[4:8], w[8:12]
        x, core, y, z = place()
        n = w_out.shape[1]
        m = w_in.shape[1]
        half = n // 2
        out_copies, in_copies = [], []
        for c, o, i in ((core, w_out, w_in), (1 - core, near_out, near_in)):
            at = 2 * x + c
            out_copies.append(pltpu.make_async_copy(o.at[0], wo.at[pl.ds(pl.multiple_of(at * n, 16), n)], sem.at[1]))
            in_copies.append(pltpu.make_async_copy(i.at[1], wi.at[pl.ds(pl.multiple_of(at * m, 16), m)], sem.at[2]))

        def far(outs, ins):
            out, into = [], []
            for c, of in ((core, parts), (1 - core, near_parts)):
                at = 2 * (1 - x) + c
                for p, zz in zip(outs, (z, 1 - z)):
                    row = pl.multiple_of(at * n + zz * half, 16)
                    out.append(pltpu.make_async_copy(of[p], wo.at[pl.ds(row, half)], sem.at[1]))
                for p, zz in zip(ins, (z, 1 - z)):
                    for j in range(2):
                        row = pl.multiple_of(at * m + zz * n + j * half, 16)
                        into.append(
                            pltpu.make_async_copy(of[p].at[:, j * H : (j + 1) * H], wi.at[pl.ds(row, half)], sem.at[2])
                        )
            return out, into

        start(out_copies + in_copies)
        far0, far1 = far((0, 2), (1, 3)), far((1, 3), (0, 2))

        @pl.when(y == 0)
        def _():
            start(far0[0] + far0[1])

        @pl.when(y == 1)
        def _():
            start(far1[0] + far1[1])

        out_copies += far0[0]
        in_copies += far0[1]

    rows = hid.shape[0] + 2 * EDGE
    cuts = [0, 512, rows]
    state = [None, None]

    def once(b, copies):
        if b == 0:
            wait(copies)

    def mix(b):
        once(b, first)
        state[b] = dot(hot5[cuts[b] : cuts[b + 1]], tw[...])

    def act(b):
        state[b] = gelu(norm(state[b], gain_out[0:1])).astype(BF)

    def update(b):
        once(b, out_copies)
        lhs = jnp.concatenate([state[b], hot1[cuts[b] : cuts[b + 1]]], axis=1)
        state[b] = dot(lhs, wo[...]).astype(BF)

    def enter(b):
        hidden = state[b]
        lo, hi = max(cuts[b], EDGE), min(cuts[b + 1], rows - EDGE)
        hid[lo - EDGE : hi - EDGE] = hidden[lo - cuts[b] : hi - cuts[b]]
        state[b] = gelu(norm(hidden.astype(F32), gain_in[1:2])).astype(BF)

    def widen(b):
        once(b, in_copies)
        state[b] = dot(state[b], wi[...])

    def leave(b):
        n = cuts[b + 1] - cuts[b]
        pos = span[0] + cuts[b] + lax.broadcasted_iota(jnp.int32, (n, 1), 0)
        valid = jnp.where((pos >= 0) & (pos < span[1]), 1.0, 0.0)
        ci[cuts[b] : cuts[b + 1]] = (gelu(norm(state[b], gain_mid[1:2])) * valid).astype(BF)

    stagger((mix, act, update, enter, widen, leave))


def last_kernel(split, ci, hid, gain_out, *rest):
    *w, out, wt, wo, sem = rest

    def conv(src, col, width, row, n):
        copies = []
        done = 0
        while done < width:
            tap, inner = divmod(col + done, H)
            step = min(H - inner, width - done)
            copies.append(
                pltpu.make_async_copy(
                    src.at[:, done : done + step],
                    wt.at[pl.ds(tap * H + row, n), inner : inner + step],
                    sem.at[0],
                )
            )
            done += step
        return copies

    if not split:
        conv_copies = conv(w[0], 0, KERNEL * H, 0, H)
        out_copies = [pltpu.make_async_copy(w[1], wo, sem.at[1])]
        start(conv_copies + out_copies)
    else:
        w_conv, w_out, near_conv, near_out = w[:4]
        parts, near_parts = w[4:8], w[8:12]
        x, core, y, z = place()
        n = w_out.shape[1]
        half = n // 2
        rest_cols = KERNEL * H - CUT_B
        conv_copies, out_copies = [], []
        for c, v, o in ((core, w_conv, w_out), (1 - core, near_conv, near_out)):
            row = pl.multiple_of((2 * x + c) * n, 16)
            conv_copies += conv(v.at[1], 0, KERNEL * H, row, n)
            out_copies.append(pltpu.make_async_copy(o.at[1], wo.at[pl.ds(row, n)], sem.at[1]))

        def far(head, tail):
            cv, out = [], []
            for c, of in ((core, parts), (1 - core, near_parts)):
                for p, zz in zip(head, (z, 1 - z)):
                    row = pl.multiple_of((2 * (1 - x) + c) * n + zz * half, 16)
                    cv += conv(of[p], 0, CUT_A, row, half)
                for p, zz in zip(tail, (z, 1 - z)):
                    row = pl.multiple_of((2 * (1 - x) + c) * n + zz * half, 16)
                    skip = CUT_A - CUT_B
                    cv += conv(of[p].at[:, skip:rest_cols], CUT_A, rest_cols - skip, row, half)
                    out.append(pltpu.make_async_copy(of[p].at[:, rest_cols:], wo.at[pl.ds(row, half)], sem.at[1]))
            return cv, out

        start(conv_copies + out_copies)
        far0, far1 = far((0, 2), (1, 3)), far((1, 3), (0, 2))

        @pl.when(y == 0)
        def _():
            start(far0[0] + far0[1])

        @pl.when(y == 1)
        def _():
            start(far1[0] + far1[1])

        conv_copies += far0[0]
        out_copies += far0[1]

    rows = out.shape[0]
    cuts = [0, 16 * ((rows + 31) // 32), rows]
    state = [None, None]

    def mix(b):
        lhs = jnp.concatenate([ci[cuts[b] + k * DIL1 : cuts[b + 1] + k * DIL1] for k in range(KERNEL)], axis=1)
        if b == 0:
            wait(conv_copies)
        state[b] = dot(lhs, wt[...])

    def act(b):
        state[b] = gelu(norm(state[b], gain_out[1:2])).astype(BF)

    def update(b):
        if b == 0:
            wait(out_copies)
        hidden = hid[cuts[b] : cuts[b + 1]].astype(F32)
        out[cuts[b] : cuts[b + 1]] = (hidden + dot(state[b], wo[...])).astype(BF)

    stagger((mix, act, update))


def after(x, *deps):
    return lax.optimization_barrier((x, *deps))[0]


def per_device(tokens, breaks, lengths, embed_table, break_vec, gain_in, gain_mid, gain_out, w_in, conv_w, w_out):
    rows = tokens.shape[1]
    width = embed_table.shape[1]
    roll_at = lax.axis_index("roll")
    seq_at = lax.axis_index("seq")
    rolls = lax.axis_size("roll")
    seqs = lax.axis_size("seq")
    split = rolls == 4 and seqs % 4 == 0

    def core_swap(x):
        return lax.ppermute(x, "roll", [(i, i ^ 1) for i in range(rolls)])

    def x_swap(x):
        return lax.ppermute(x, "roll", [(i, i ^ 2) for i in range(rolls)])

    def seq_swap(x, bits):
        return lax.ppermute(x, "seq", [(i, i ^ bits) for i in range(seqs)])

    span = jnp.stack([(seq_at * rows).astype(jnp.int32) - EDGE, lengths[0]])
    wide_rows = rows + 2 * EDGE
    codes = tokens[0] + SLOT * breaks[0]

    shard = w_out.shape[1] // 2
    shapes = [((CODES, width), BF), ((CODES, H), F32)]
    if split:
        shapes += [((shard, width), BF), ((shard, CUT_A), BF), ((shard, CUT_A), BF)]
    table, part, *parts = pl.pallas_call(
        functools.partial(first_kernel, split),
        out_shape=[jax.ShapeDtypeStruct(n, t) for n, t in shapes],
        in_specs=[HBM] * 6,
        out_specs=[VMEM] * len(shapes),
        scratch_shapes=[
            pltpu.VMEM(embed_table.shape, F32),
            pltpu.VMEM((width,), F32),
            pltpu.VMEM(gain_in.shape, F32),
            pltpu.VMEM(w_in.shape[1:], BF),
            pltpu.VMEM((CODES, width), F32),
            pltpu.SemaphoreType.DMA((2,)),
        ],
        compiler_params=params(48),
    )(embed_table, break_vec, gain_in, w_in, conv_w, w_out)

    if split:
        own = part + core_swap(part)
        near_in, near_conv, near_out = [core_swap(after(w, own)) for w in (w_in, conv_w, w_out)]
        far_a = x_swap(parts[0])
        other = x_swap(own.astype(BF))
        codes = after(codes, own)
        low = seq_at % 2 == 0
        ends = codes[rows - REACH :], codes[:REACH]
        even = seq_swap(jnp.where(low, *ends), 1)
        pairs = [(i, i + 1) for i in range(1, seqs - 1, 2)]
        pairs.append((seqs - 1, 0))
        odd = lax.ppermute(jnp.where(low, *ends[::-1]), "seq", pairs + [(j, i) for i, j in pairs])
        before, behind = jnp.where(low, odd, even), jnp.where(low, even, odd)
        far_b = x_swap(after(parts[1], own))
        other = after(other, before, behind)
    else:
        own = lax.psum(part, "roll")
        other = jnp.zeros((CODES, H), BF)
        pairs = [(i, i + 1) for i in range(seqs - 1)]
        before = lax.ppermute(codes[rows - REACH :], "seq", pairs)
        behind = lax.ppermute(codes[:REACH], "seq", [(j, i) for i, j in pairs])
    count = rows + 2 * REACH
    spare = jnp.zeros((-count % 128,), jnp.int32)
    near = jnp.concatenate([before, codes, behind, spare])[None]

    wide = KERNEL * H
    shapes = [(SLOT, F32), (SLOT, BF)] if split else [(CODES, F32)]
    taps = pl.pallas_call(
        functools.partial(table_kernel, split),
        out_shape=[jax.ShapeDtypeStruct((n, wide), t) for n, t in shapes],
        in_specs=[VMEM, VMEM, VMEM, HBM],
        out_specs=[VMEM] * len(shapes),
        scratch_shapes=[
            pltpu.VMEM(conv_w.shape[1:], BF),
            pltpu.VMEM((CODES, wide), F32),
            pltpu.SemaphoreType.DMA,
        ],
        compiler_params=params(12),
    )(own, other, gain_mid, conv_w)
    if split:
        mine = taps[0] + core_swap(taps[1]).astype(F32)
        sent = mine.astype(BF)
        relay = after(far_a, sent)
        parts_a = [far_a] + [seq_swap(relay, b) for b in (1, 2, 3)]
        near = after(near, sent)
        other = x_swap(sent)

    hot5, hot1 = pl.pallas_call(
        hot_kernel,
        out_shape=(
            jax.ShapeDtypeStruct((wide_rows, KERNEL * CODES), BF),
            jax.ShapeDtypeStruct((wide_rows, CODES), BF),
        ),
        in_specs=[SMEM, VMEM],
        out_specs=(VMEM, VMEM),
        compiler_params=params(12),
    )(span, near)

    if split:
        mine = (mine + after(other, hot1, *parts_a).astype(F32)).astype(BF)
        theirs = core_swap(mine)
        near_a = [core_swap(relay)] + [core_swap(after(p, mine)) for p in parts_a[1:]]
        relay = after(far_b, mine)
        parts_b = [far_b, seq_swap(relay, 1), seq_swap(relay, 2), x_swap(after(parts[2], mine))]
        weights_a = [mine, theirs, w_out, w_in, near_out, near_in] + parts_a + near_a
    else:
        taps = lax.psum(taps[0], "roll").astype(BF)
        gather = lambda w: lax.all_gather(w, "roll", axis=0, tiled=True)
        weights_a, weights_b = [taps, gather(w_out[0]), gather(w_in[1])], [gather(conv_w[1]), gather(w_out[1])]

    ci, hid = pl.pallas_call(
        functools.partial(rows_kernel, split),
        out_shape=(
            jax.ShapeDtypeStruct((wide_rows, H), BF),
            jax.ShapeDtypeStruct((rows, width), BF),
        ),
        in_specs=[SMEM, VMEM, VMEM, ANY, VMEM, VMEM, VMEM] + [HBM if w is w_out or w is w_in else ANY for w in weights_a],
        out_specs=(VMEM, VMEM),
        scratch_shapes=[
            pltpu.VMEM((KERNEL * CODES, H), BF),
            pltpu.VMEM((H + CODES, width), BF),
            pltpu.VMEM((width, H), BF),
            pltpu.SemaphoreType.DMA((3,)),
        ],
        compiler_params=params(30),
    )(span, hot5, hot1, table, gain_out, gain_in, gain_mid, *weights_a)

    if split:
        near_b = [core_swap(after(p, ci)) for p in parts_b]
        weights_b = [conv_w, w_out, near_conv, near_out] + parts_b + near_b
    out = pl.pallas_call(
        functools.partial(last_kernel, split),
        out_shape=jax.ShapeDtypeStruct((rows, width), BF),
        in_specs=[VMEM] * 3 + [HBM if w is w_out or w is conv_w else ANY for w in weights_b],
        out_specs=VMEM,
        scratch_shapes=[
            pltpu.VMEM((KERNEL * H, H), BF),
            pltpu.VMEM((H, width), BF),
            pltpu.SemaphoreType.DMA((2,)),
        ],
        compiler_params=params(24),
    )(ci, hid, gain_out, *weights_b)
    return out[None]


def solution(mesh):
    placed = (
        P("roll", "seq"),
        P("roll", "seq"),
        P("roll"),
        P(),
        P(),
        P(),
        P(),
        P(),
        P(None, "roll", None),
        P(None, "roll", None),
        P(None, "roll", None),
    )
    return jax.shard_map(
        per_device, mesh=mesh, in_specs=placed, out_specs=P("roll", "seq", None), check_vma=False
    )
```

```python
import functools

import jax
import jax.numpy as jnp
from jax import lax
from jax.experimental import pallas as pl
from jax.experimental.pallas import tpu as pltpu
from jax.sharding import PartitionSpec as P

H = 640
KERNEL = 5
VOCAB = 30
SLOT = 32
CODES = 2 * SLOT
BASE_DILATION = 64
DIL0 = BASE_DILATION
DIL1 = 2 * BASE_DILATION
HALF = KERNEL // 2
EDGE = HALF * DIL1
REACH = EDGE + HALF * DIL0
BF = jnp.bfloat16
F32 = jnp.float32
VMEM = pl.BlockSpec(memory_space=pltpu.VMEM)
SMEM = pl.BlockSpec(memory_space=pltpu.SMEM)
ANY = pl.BlockSpec(memory_space=pl.ANY)
HBM = pl.BlockSpec(memory_space=pltpu.HBM)
FREE = pl.CostEstimate(flops=0, bytes_accessed=0, transcendentals=0)
CUT_A = 18 * 128
CUT_B = 17 * 128


def params(mib):
    return pltpu.CompilerParams(vmem_limit_bytes=mib * 1024 * 1024)


def gelu(x):
    return (0.5 * x) * (1.0 + lax.erf(x * 0.5**0.5))


def norm(x, gain):
    center = jnp.mean(x, axis=-1, keepdims=True)
    d = x - center
    spread = jnp.mean(d * d, axis=-1, keepdims=True)
    return d * lax.rsqrt(spread + 1e-5) * gain


def dot(a, b):
    return jnp.dot(a, b, preferred_element_type=F32)


def place():
    roll, seq = lax.axis_index("roll"), lax.axis_index("seq")
    return lax.div(roll, 2), lax.rem(roll, 2), lax.rem(seq, 2), lax.rem(lax.div(seq, 2), 2)


def start(copies):
    for c in copies:
        c.start()


def wait(copies):
    for c in copies:
        c.wait()


def stagger(stages):
    for t in range(len(stages) + 1):
        for b in range(2):
            if 0 <= t - b < len(stages):
                stages[t - b](b)


def pick(rows, columns, first):
    i = lax.broadcasted_iota(jnp.int32, (rows, columns), 0)
    j = lax.broadcasted_iota(jnp.int32, (rows, columns), 1)
    return jnp.where(i == j + first, 1.0, 0.0).astype(BF)


def part_copies(y_is_one, row_bit, w_in, conv_w, w_out, a, b, sem):
    n = b.shape[0]
    r = pl.multiple_of(row_bit * n, 16)
    r2 = pl.multiple_of(row_bit * 2 * n, 16)
    rest = conv_w.shape[2] - CUT_B
    if y_is_one:
        pairs = [
            (conv_w.at[1, pl.ds(r, n), CUT_B:], b.at[:, 0:rest]),
            (w_out.at[1, pl.ds(r, n)], b.at[:, rest:]),
        ]
        if a is not None:
            pairs += [
                (w_in.at[1, pl.ds(r2, n)], a.at[:, 0:H]),
                (w_in.at[1, pl.ds(r2 + n, n)], a.at[:, H : 2 * H]),
            ]
    else:
        pairs = [(conv_w.at[1, pl.ds(r, n), 0:CUT_A], b)]
        if a is not None:
            pairs.append((w_out.at[0, pl.ds(r, n)], a))
    return [pltpu.make_async_copy(s, d, sem) for s, d in pairs]


def first_kernel(split, embed, brk, gain, w_in, conv_w, w_out, table, part, *rest):
    *parts, emb, bv, g, w, full, sem = rest
    copies = [
        pltpu.make_async_copy(s, d, sem.at[0])
        for s, d in ((embed, emb), (brk, bv), (gain, g), (w_in.at[0], w))
    ]
    start(copies)
    if split:
        _, _, y, z = place()
        kinds = []
        for kind in range(2):
            kinds.append(
                part_copies(kind == 1, z, w_in, conv_w, w_out, parts[0], parts[1], sem.at[1])
                + part_copies(kind == 0, 1 - z, w_in, conv_w, w_out, None, parts[2], sem.at[1])
            )

            @pl.when(y == kind)
            def _():
                start(kinds[kind])

    wait(copies)
    full[...] = jnp.zeros_like(full)
    full[0:VOCAB] = emb[...]
    full[SLOT : SLOT + VOCAB] = emb[...] + bv[...][None, :]
    hidden = full[...].astype(BF)
    table[...] = hidden
    normed = gelu(norm(hidden.astype(F32), g[0:1])).astype(BF)
    rows = w.shape[0]
    mine = dot(normed, pick(normed.shape[1], rows, lax.axis_index("roll") * rows)).astype(BF)
    part[...] = dot(mine, w[...])
    if split:
        for kind in range(2):

            @pl.when(y == kind)
            def _():
                wait(kinds[kind])


def table_kernel(split, own, other, gain, w_all, *rest):
    *outs, w, full, sem = rest
    copy = pltpu.make_async_copy(w_all.at[0], w, sem)
    copy.start()
    wide = own[...] + other[...].astype(F32)
    t = gelu(norm(wide, gain[0:1])).astype(BF)
    rows = w.shape[0]
    mine = dot(t, pick(t.shape[1], rows, lax.axis_index("roll") * rows)).astype(BF)
    copy.wait()
    full[...] = dot(mine, w[...])
    if split:
        core = lax.rem(lax.axis_index("roll"), 2)
        outs[0][...] = full[pl.ds(pl.multiple_of(core * SLOT, SLOT), SLOT)]
        outs[1][...] = full[pl.ds(pl.multiple_of((1 - core) * SLOT, SLOT), SLOT)].astype(BF)
    else:
        outs[0][...] = full[...]


def hot_kernel(span, near, hot5, hot1):
    codes = near[...]
    count = codes.shape[1]
    rows = hot5.shape[0]
    pos = span[0] - HALF * DIL0 + lax.broadcasted_iota(jnp.int32, codes.shape, 1)
    masked = jnp.where((pos >= 0) & (pos < span[1]), codes, -1)
    lanes = lax.broadcasted_iota(jnp.int32, (CODES, count), 0)
    taps = jnp.where(lanes == masked, 1.0, 0.0).T.astype(BF)
    for k in range(KERNEL):
        hot5[:, k * CODES : (k + 1) * CODES] = taps[k * DIL0 : k * DIL0 + rows]
    center = jnp.where(lanes == codes, 1.0, 0.0).T.astype(BF)
    hot1[...] = center[HALF * DIL0 : HALF * DIL0 + rows]


def rows_kernel(split, span, hot5, hot1, table, gain_out, gain_in, gain_mid, *rest):
    *w, ci, hid, tw, wo, wi, sem = rest
    depth = wo.shape[0] - CODES
    if split:
        core = lax.rem(lax.axis_index("roll"), 2)
        taps = [(t, core * SLOT, SLOT, 0) for t in w[:2]] + [(t, (1 - core) * SLOT, SLOT, 0) for t in w[2:4]]
        taps = [(t, at, n, i % 2) for i, (t, at, n, _) in enumerate(taps)]
        w = w[4:]
    else:
        taps = [(w[0], 0, CODES, 0)]
        w = w[1:]
    first = [
        pltpu.make_async_copy(
            t.at[:, k * H : (k + 1) * H], tw.at[i, pl.ds(pl.multiple_of(k * CODES + at, 16), n)], sem.at[0]
        )
        for t, at, n, i in taps
        for k in range(KERNEL)
    ]
    first.append(pltpu.make_async_copy(table, wo.at[depth:], sem.at[0]))
    start(first)
    if not split:
        out_copies = [pltpu.make_async_copy(w[0], wo.at[0:depth], sem.at[1])]
        in_copies = [pltpu.make_async_copy(w[1], wi, sem.at[2])]
        start(out_copies + in_copies)
    else:
        w_out, w_in, near_out, near_in = w[:4]
        parts, near_parts = w[4:8], w[8:12]
        x, core, y, z = place()
        n = w_out.shape[1]
        m = w_in.shape[1]
        half = n // 2
        out_copies, in_copies = [], []
        for c, o, i in ((core, w_out, w_in), (1 - core, near_out, near_in)):
            at = 2 * x + c
            out_copies.append(pltpu.make_async_copy(o.at[0], wo.at[pl.ds(pl.multiple_of(at * n, 16), n)], sem.at[1]))
            in_copies.append(pltpu.make_async_copy(i.at[1], wi.at[pl.ds(pl.multiple_of(at * m, 16), m)], sem.at[2]))

        def far(outs, ins):
            out, into = [], []
            for c, of in ((core, parts), (1 - core, near_parts)):
                at = 2 * (1 - x) + c
                for p, zz in zip(outs, (z, 1 - z)):
                    row = pl.multiple_of(at * n + zz * half, 16)
                    out.append(pltpu.make_async_copy(of[p], wo.at[pl.ds(row, half)], sem.at[1]))
                for p, zz in zip(ins, (z, 1 - z)):
                    for j in range(2):
                        row = pl.multiple_of(at * m + zz * n + j * half, 16)
                        into.append(
                            pltpu.make_async_copy(of[p].at[:, j * H : (j + 1) * H], wi.at[pl.ds(row, half)], sem.at[2])
                        )
            return out, into

        start(out_copies + in_copies)
        far0, far1 = far((0, 2), (1, 3)), far((1, 3), (0, 2))

        @pl.when(y == 0)
        def _():
            start(far0[0] + far0[1])

        @pl.when(y == 1)
        def _():
            start(far1[0] + far1[1])

        out_copies += far0[0]
        in_copies += far0[1]

    rows = hid.shape[0] + 2 * EDGE
    cuts = [0, 512, rows]
    state = [None, None]

    def once(b, copies):
        if b == 0:
            wait(copies)

    def mix(b):
        if b == 0:
            wait(first)
            if split:
                tw[0] = (tw[0].astype(F32) + tw[1].astype(F32)).astype(BF)
        state[b] = dot(hot5[cuts[b] : cuts[b + 1]], tw[0])

    def act(b):
        state[b] = gelu(norm(state[b], gain_out[0:1])).astype(BF)

    def update(b):
        once(b, out_copies)
        lhs = jnp.concatenate([state[b], hot1[cuts[b] : cuts[b + 1]]], axis=1)
        state[b] = dot(lhs, wo[...]).astype(BF)

    def enter(b):
        hidden = state[b]
        lo, hi = max(cuts[b], EDGE), min(cuts[b + 1], rows - EDGE)
        hid[lo - EDGE : hi - EDGE] = hidden[lo - cuts[b] : hi - cuts[b]]
        state[b] = gelu(norm(hidden.astype(F32), gain_in[1:2])).astype(BF)

    def widen(b):
        once(b, in_copies)
        state[b] = dot(state[b], wi[...])

    def leave(b):
        n = cuts[b + 1] - cuts[b]
        pos = span[0] + cuts[b] + lax.broadcasted_iota(jnp.int32, (n, 1), 0)
        valid = jnp.where((pos >= 0) & (pos < span[1]), 1.0, 0.0)
        ci[cuts[b] : cuts[b + 1]] = (gelu(norm(state[b], gain_mid[1:2])) * valid).astype(BF)

    stagger((mix, act, update, enter, widen, leave))


def conv_copies(src, col, width, wt, per_tap, row, n, sem):
    copies = []
    done = 0
    while done < width:
        tap, inner = divmod(col + done, H)
        step = min(H - inner, width - done)
        copies.append(
            pltpu.make_async_copy(
                src.at[:, done : done + step],
                wt.at[pl.ds(pl.multiple_of(tap * per_tap + row, 16), n), inner : inner + step],
                sem,
            )
        )
        done += step
    return copies


HEAD = 256
TAIL = H - HEAD


def windows(ci, lo, hi, first, width):
    first = pl.multiple_of(first, 128)
    return jnp.concatenate(
        [ci[lo + k * DIL1 : hi + k * DIL1, pl.ds(first, width)] for k in range(KERNEL)], axis=1
    )


def head_kernel(ci, w_conv, near_conv, out, wt, sem):
    x, core, _, _ = place()
    n = w_conv.shape[1]
    short = HEAD - n
    done = None
    for xx in range(2):
        for cc in range(2):
            copies = []
            for c, w in ((cc, w_conv), (1 - cc, near_conv)):
                if c == xx:
                    copies += conv_copies(w.at[1], 0, KERNEL * H, wt, HEAD, short * xx, n, sem)
                else:
                    part = w.at[1, (n - short) * xx : (n - short) * xx + short]
                    copies += conv_copies(part, 0, KERNEL * H, wt, HEAD, n * (1 - xx), short, sem)
            done = copies

            @pl.when((x == xx) & (core == cc))
            def _():
                start(copies)

    rows = out.shape[0]
    half = 16 * ((rows + 31) // 32)
    for b, (lo, hi) in enumerate(((0, half), (half, rows))):
        lhs = windows(ci, lo, hi, x * TAIL, HEAD)
        if b == 0:
            wait(done)
        out[lo:hi] = dot(lhs, wt[...])


def last_kernel(split, ci, hid, gain_out, *rest):
    *w, out, wt, wo, sem = rest
    if not split:
        conv_in = conv_copies(w[0], 0, KERNEL * H, wt, H, 0, H, sem.at[0])
        out_in = [pltpu.make_async_copy(w[1], wo, sem.at[1])]
        start(conv_in + out_in)
        first, width = 0, H
    else:
        head, w_conv, w_out, near_conv, near_out = w[:5]
        parts, near_parts = w[5:9], w[9:13]
        x, core, y, z = place()
        n = w_out.shape[1]
        half = n // 2
        left = 2 * n - HEAD
        rest_cols = KERNEL * H - CUT_B
        first, width = (1 - x) * HEAD, TAIL
        out_in = []
        for c, o in ((core, w_out), (1 - core, near_out)):
            row = pl.multiple_of((2 * x + c) * n, 16)
            out_in.append(pltpu.make_async_copy(o.at[1], wo.at[pl.ds(row, n)], sem.at[1]))
        from_row = pl.multiple_of((n - left) * (1 - x), 16)
        own_in, near_in = [
            conv_copies(v.at[1, pl.ds(from_row, left)], 0, KERNEL * H, wt, TAIL, 2 * n * x, left, sem.at[0])
            for v in (w_conv, near_conv)
        ]

        @pl.when(core + x == 1)
        def _():
            start(own_in)

        @pl.when(core + x != 1)
        def _():
            start(near_in)

        def far(head, tail):
            cv, out = [], []
            for c, of in ((core, parts), (1 - core, near_parts)):
                at = c * n + left * (1 - x)
                for p, zz in zip(head, (z, 1 - z)):
                    cv += conv_copies(of[p], 0, CUT_A, wt, TAIL, at + zz * half, half, sem.at[0])
                for p, zz in zip(tail, (z, 1 - z)):
                    skip = CUT_A - CUT_B
                    cv += conv_copies(
                        of[p].at[:, skip:rest_cols], CUT_A, rest_cols - skip, wt, TAIL, at + zz * half, half, sem.at[0]
                    )
                    row = pl.multiple_of((2 * (1 - x) + c) * n + zz * half, 16)
                    out.append(pltpu.make_async_copy(of[p].at[:, rest_cols:], wo.at[pl.ds(row, half)], sem.at[1]))
            return cv, out

        start(out_in)
        far0, far1 = far((0, 2), (1, 3)), far((1, 3), (0, 2))

        @pl.when(y == 0)
        def _():
            start(far0[0] + far0[1])

        @pl.when(y == 1)
        def _():
            start(far1[0] + far1[1])

        conv_in = own_in + far0[0]
        out_in += far0[1]

    rows = out.shape[0]
    cuts = [0, 16 * ((rows + 31) // 32), rows]
    state = [None, None]

    def mix(b):
        lhs = windows(ci, cuts[b], cuts[b + 1], first, width)
        if b == 0:
            wait(conv_in)
        state[b] = dot(lhs, wt[...])
        if split:
            state[b] += head[cuts[b] : cuts[b + 1]]

    def act(b):
        state[b] = gelu(norm(state[b], gain_out[1:2])).astype(BF)

    def update(b):
        if b == 0:
            wait(out_in)
        hidden = hid[cuts[b] : cuts[b + 1]].astype(F32)
        out[cuts[b] : cuts[b + 1]] = (hidden + dot(state[b], wo[...])).astype(BF)

    stagger((mix, act, update))


def after(x, *deps):
    return lax.optimization_barrier((x, *deps))[0]


def per_device(tokens, breaks, lengths, embed_table, break_vec, gain_in, gain_mid, gain_out, w_in, conv_w, w_out):
    rows = tokens.shape[1]
    width = embed_table.shape[1]
    roll_at = lax.axis_index("roll")
    seq_at = lax.axis_index("seq")
    rolls = lax.axis_size("roll")
    seqs = lax.axis_size("seq")
    split = rolls == 4 and seqs % 4 == 0

    def core_swap(x):
        return lax.ppermute(x, "roll", [(i, i ^ 1) for i in range(rolls)])

    def x_swap(x):
        return lax.ppermute(x, "roll", [(i, i ^ 2) for i in range(rolls)])

    def seq_swap(x, bits):
        return lax.ppermute(x, "seq", [(i, i ^ bits) for i in range(seqs)])

    span = jnp.stack([(seq_at * rows).astype(jnp.int32) - EDGE, lengths[0]])
    wide_rows = rows + 2 * EDGE
    codes = tokens[0] + SLOT * breaks[0]

    shard = w_out.shape[1] // 2
    shapes = [((CODES, width), BF), ((CODES, H), F32)]
    if split:
        shapes += [((shard, width), BF), ((shard, CUT_A), BF), ((shard, CUT_A), BF)]
    table, part, *parts = pl.pallas_call(
        functools.partial(first_kernel, split),
        out_shape=[jax.ShapeDtypeStruct(n, t) for n, t in shapes],
        in_specs=[HBM] * 6,
        out_specs=[VMEM] * len(shapes),
        scratch_shapes=[
            pltpu.VMEM(embed_table.shape, F32),
            pltpu.VMEM((width,), F32),
            pltpu.VMEM(gain_in.shape, F32),
            pltpu.VMEM(w_in.shape[1:], BF),
            pltpu.VMEM((CODES, width), F32),
            pltpu.SemaphoreType.DMA((2,)),
        ],
        cost_estimate=FREE,
        compiler_params=params(60),
    )(embed_table, break_vec, gain_in, w_in, conv_w, w_out)

    if split:
        own = part + core_swap(part)
        near_in, near_conv, near_out = [core_swap(after(w, own)) for w in (w_in, conv_w, w_out)]
        far_a = x_swap(parts[0])
        other = x_swap(own.astype(BF))
        far_b = x_swap(after(parts[1], own))
        other = after(other, far_a)
    else:
        own = lax.psum(part, "roll")
        other = jnp.zeros((CODES, H), BF)
        pairs = [(i, i + 1) for i in range(seqs - 1)]
        before = lax.ppermute(codes[rows - REACH :], "seq", pairs)
        behind = lax.ppermute(codes[:REACH], "seq", [(j, i) for i, j in pairs])
    wide = KERNEL * H
    shapes = [(SLOT, F32), (SLOT, BF)] if split else [(CODES, F32)]
    taps = pl.pallas_call(
        functools.partial(table_kernel, split),
        out_shape=[jax.ShapeDtypeStruct((n, wide), t) for n, t in shapes],
        in_specs=[VMEM, VMEM, VMEM, HBM],
        out_specs=[VMEM] * len(shapes),
        scratch_shapes=[
            pltpu.VMEM(conv_w.shape[1:], BF),
            pltpu.VMEM((CODES, wide), F32),
            pltpu.SemaphoreType.DMA,
        ],
        cost_estimate=FREE,
        compiler_params=params(12),
    )(own, other, gain_mid, conv_w)
    if split:
        sent = (taps[0] + core_swap(taps[1]).astype(F32)).astype(BF)
        received = x_swap(sent)
        near_sent = core_swap(sent)
        relay = after(far_a, sent)
        parts_a = [far_a] + [seq_swap(relay, b) for b in (1, 2, 3)]
        codes = after(codes, sent)
        ends = codes[rows - REACH :], codes[:REACH]
        low = seq_at % 2 == 0
        even = seq_swap(jnp.where(low, *ends), 1)
        pairs = [(i, i + 1) for i in range(1, seqs - 1, 2)]
        pairs.append((seqs - 1, 0))
        odd = lax.ppermute(jnp.where(low, *ends[::-1]), "seq", pairs + [(j, i) for i, j in pairs])
        before, behind = jnp.where(low, odd, even), jnp.where(low, even, odd)
    spare = jnp.zeros((-(rows + 2 * REACH) % 128,), jnp.int32)
    near = jnp.concatenate([before, codes, behind, spare])[None]

    hot5, hot1 = pl.pallas_call(
        hot_kernel,
        out_shape=(
            jax.ShapeDtypeStruct((wide_rows, KERNEL * CODES), BF),
            jax.ShapeDtypeStruct((wide_rows, CODES), BF),
        ),
        in_specs=[SMEM, VMEM],
        out_specs=(VMEM, VMEM),
        cost_estimate=FREE,
        compiler_params=params(12),
    )(span, near)

    if split:
        received = after(received, hot1, *parts_a)
        near_received = core_swap(received)
        near_a = [core_swap(relay)] + [core_swap(after(p, received)) for p in parts_a[1:]]
        relay = after(far_b, received)
        parts_b = [far_b, seq_swap(relay, 1), seq_swap(relay, 2), x_swap(after(parts[2], received))]
        near_b = [core_swap(relay)]
        weights_a = [sent, received, near_sent, near_received, w_out, w_in, near_out, near_in] + parts_a + near_a
    else:
        taps = lax.psum(taps[0], "roll").astype(BF)
        gather = lambda w: lax.all_gather(w, "roll", axis=0, tiled=True)
        weights_a, weights_b = [taps, gather(w_out[0]), gather(w_in[1])], [gather(conv_w[1]), gather(w_out[1])]

    ci, hid = pl.pallas_call(
        functools.partial(rows_kernel, split),
        out_shape=(
            jax.ShapeDtypeStruct((wide_rows, H), BF),
            jax.ShapeDtypeStruct((rows, width), BF),
        ),
        in_specs=[SMEM, VMEM, VMEM, ANY, VMEM, VMEM, VMEM] + [HBM if w is w_out or w is w_in else ANY for w in weights_a],
        out_specs=(VMEM, VMEM),
        scratch_shapes=[
            pltpu.VMEM((2, KERNEL * CODES, H), BF),
            pltpu.VMEM((H + CODES, width), BF),
            pltpu.VMEM((width, H), BF),
            pltpu.SemaphoreType.DMA((3,)),
        ],
        cost_estimate=FREE,
        compiler_params=params(30),
    )(span, hot5, hot1, table, gain_out, gain_in, gain_mid, *weights_a)

    if split:
        near_b += [core_swap(after(p, ci)) for p in parts_b[1:]]
        head = pl.pallas_call(
            head_kernel,
            out_shape=jax.ShapeDtypeStruct((rows, H), F32),
            in_specs=[VMEM, HBM, ANY],
            out_specs=VMEM,
            scratch_shapes=[pltpu.VMEM((KERNEL * HEAD, H), BF), pltpu.SemaphoreType.DMA],
            cost_estimate=FREE,
            compiler_params=params(16),
        )(ci, conv_w, near_conv)
        weights_b = [head, conv_w, w_out, near_conv, near_out] + parts_b + near_b
    out = pl.pallas_call(
        functools.partial(last_kernel, split),
        out_shape=jax.ShapeDtypeStruct((rows, width), BF),
        in_specs=[VMEM] * 3
        + [HBM if w is w_out or w is conv_w else VMEM if split and w is head else ANY for w in weights_b],
        out_specs=VMEM,
        scratch_shapes=[
            pltpu.VMEM((KERNEL * (TAIL if split else H), H), BF),
            pltpu.VMEM((H, width), BF),
            pltpu.SemaphoreType.DMA((2,)),
        ],
        cost_estimate=FREE,
        compiler_params=params(24),
    )(ci, hid, gain_out, *weights_b)
    return out[None]


def solution(mesh):
    placed = (
        P("roll", "seq"),
        P("roll", "seq"),
        P("roll"),
        P(),
        P(),
        P(),
        P(),
        P(),
        P(None, "roll", None),
        P(None, "roll", None),
        P(None, "roll", None),
    )
    return jax.shard_map(
        per_device, mesh=mesh, in_specs=placed, out_specs=P("roll", "seq", None), check_vma=False
    )
```

```python
import functools

import jax
import jax.numpy as jnp
from jax import lax
from jax.experimental import pallas as pl
from jax.experimental.pallas import tpu as pltpu
from jax.sharding import PartitionSpec as P

H = 640
KERNEL = 5
VOCAB = 30
SLOT = 32
CODES = 2 * SLOT
BASE_DILATION = 64
DIL0 = BASE_DILATION
DIL1 = 2 * BASE_DILATION
HALF = KERNEL // 2
EDGE = HALF * DIL1
REACH = EDGE + HALF * DIL0
BF = jnp.bfloat16
F32 = jnp.float32
VMEM = pl.BlockSpec(memory_space=pltpu.VMEM)
SMEM = pl.BlockSpec(memory_space=pltpu.SMEM)
ANY = pl.BlockSpec(memory_space=pl.ANY)
HBM = pl.BlockSpec(memory_space=pltpu.HBM)
FREE = pl.CostEstimate(flops=0, bytes_accessed=0, transcendentals=0)
CUT_A = 18 * 128
CUT_B = 17 * 128


def params(mib):
    return pltpu.CompilerParams(vmem_limit_bytes=mib * 1024 * 1024)


def gelu(x):
    return (0.5 * x) * (1.0 + lax.erf(x * 0.5**0.5))


def norm(x, gain):
    center = jnp.mean(x, axis=-1, keepdims=True)
    d = x - center
    spread = jnp.mean(d * d, axis=-1, keepdims=True)
    return d * lax.rsqrt(spread + 1e-5) * gain


def dot(a, b):
    return jnp.dot(a, b, preferred_element_type=F32)


def place():
    roll, seq = lax.axis_index("roll"), lax.axis_index("seq")
    return lax.div(roll, 2), lax.rem(roll, 2), lax.rem(seq, 2), lax.rem(lax.div(seq, 2), 2)


def start(copies):
    for c in copies:
        c.start()


def wait(copies):
    for c in copies:
        c.wait()


def stagger(stages):
    for t in range(len(stages) + 1):
        for b in range(2):
            if 0 <= t - b < len(stages):
                stages[t - b](b)


def pick(rows, columns, first):
    i = lax.broadcasted_iota(jnp.int32, (rows, columns), 0)
    j = lax.broadcasted_iota(jnp.int32, (rows, columns), 1)
    return jnp.where(i == j + first, 1.0, 0.0).astype(BF)


def part_copies(y_is_one, row_bit, w_in, conv_w, w_out, a, b, sem):
    n = b.shape[0]
    r = pl.multiple_of(row_bit * n, 16)
    r2 = pl.multiple_of(row_bit * 2 * n, 16)
    rest = conv_w.shape[2] - CUT_B
    if y_is_one:
        pairs = [
            (conv_w.at[1, pl.ds(r, n), CUT_B:], b.at[:, 0:rest]),
            (w_out.at[1, pl.ds(r, n)], b.at[:, rest:]),
        ]
        if a is not None:
            pairs += [
                (w_in.at[1, pl.ds(r2, n)], a.at[:, 0:H]),
                (w_in.at[1, pl.ds(r2 + n, n)], a.at[:, H : 2 * H]),
            ]
    else:
        pairs = [(conv_w.at[1, pl.ds(r, n), 0:CUT_A], b)]
        if a is not None:
            pairs.append((w_out.at[0, pl.ds(r, n)], a))
    return [pltpu.make_async_copy(s, d, sem) for s, d in pairs]


def first_kernel(split, embed, brk, gain, w_in, conv_w, w_out, table, part, *rest):
    count = 3 if split else 0
    parts, rest = rest[:count], rest[count:]
    emb, bv, g, w, full, sem, *held = rest
    copies = [
        pltpu.make_async_copy(s, d, sem.at[0])
        for s, d in ((embed, emb), (brk, bv), (gain, g), (w_in.at[0], w))
    ]
    start(copies)
    leaving = []
    if split:
        _, _, y, z = place()
        kinds = []
        for kind in range(2):
            kinds.append(
                part_copies(kind == 1, z, w_in, conv_w, w_out, held[0], held[1], sem.at[1])
                + part_copies(kind == 0, 1 - z, w_in, conv_w, w_out, None, held[2], sem.at[1])
            )

            @pl.when(y == kind)
            def _():
                start(kinds[kind])

        leaving = [pltpu.make_async_copy(s, d, sem.at[2]) for s, d in zip(held, parts)]

    wait(copies)
    if split:
        for kind in range(2):

            @pl.when(y == kind)
            def _():
                wait(kinds[kind])

        start(leaving)
    full[...] = jnp.zeros_like(full)
    full[0:VOCAB] = emb[...]
    full[SLOT : SLOT + VOCAB] = emb[...] + bv[...][None, :]
    hidden = full[...].astype(BF)
    table[...] = hidden
    normed = gelu(norm(hidden.astype(F32), g[0:1])).astype(BF)
    rows = w.shape[0]
    mine = dot(normed, pick(normed.shape[1], rows, lax.axis_index("roll") * rows)).astype(BF)
    part[...] = dot(mine, w[...])
    wait(leaving)


def table_kernel(split, own, other, gain, w_all, *rest):
    *outs, w, full, sem = rest
    copy = pltpu.make_async_copy(w_all.at[0], w, sem)
    copy.start()
    wide = own[...] + other[...].astype(F32)
    t = gelu(norm(wide, gain[0:1])).astype(BF)
    rows = w.shape[0]
    mine = dot(t, pick(t.shape[1], rows, lax.axis_index("roll") * rows)).astype(BF)
    copy.wait()
    full[...] = dot(mine, w[...])
    if split:
        core = lax.rem(lax.axis_index("roll"), 2)
        outs[0][...] = full[pl.ds(pl.multiple_of(core * SLOT, SLOT), SLOT)]
        outs[1][...] = full[pl.ds(pl.multiple_of((1 - core) * SLOT, SLOT), SLOT)].astype(BF)
    else:
        outs[0][...] = full[...]


def hot_kernel(split, span, near, *rest):
    copies = []
    if split:
        *w, hot5, hot1, near_out, near_in, near_conv, sem = rest
        copies = chip_copies(*w, near_out, near_in, near_conv, sem)
    else:
        hot5, hot1 = rest
    codes = near[...]
    count = codes.shape[1]
    rows = hot5.shape[0]
    pos = span[0] - HALF * DIL0 + lax.broadcasted_iota(jnp.int32, codes.shape, 1)
    masked = jnp.where((pos >= 0) & (pos < span[1]), codes, -1)
    lanes = lax.broadcasted_iota(jnp.int32, (CODES, count), 0)
    taps = jnp.where(lanes == masked, 1.0, 0.0).T.astype(BF)
    for k in range(KERNEL):
        hot5[:, k * CODES : (k + 1) * CODES] = taps[k * DIL0 : k * DIL0 + rows]
    center = jnp.where(lanes == codes, 1.0, 0.0).T.astype(BF)
    hot1[...] = center[HALF * DIL0 : HALF * DIL0 + rows]
    wait(copies)


def rows_kernel(split, span, hot5, hot1, gain_out, gain_in, gain_mid, *rest):
    *w, ci, hid, tw, wo, wi, sem = rest
    depth = wo.shape[0] - CODES
    if split:
        core = lax.rem(lax.axis_index("roll"), 2)
        taps = [(t, core * SLOT, SLOT, 0) for t in w[:2]] + [(t, (1 - core) * SLOT, SLOT, 0) for t in w[2:4]]
        taps = [(t, at, n, i % 2) for i, (t, at, n, _) in enumerate(taps)]
        w = w[4:]
    else:
        taps = [(w[0], 0, CODES, 0)]
        table, *w = w[1:]
    first = [
        pltpu.make_async_copy(
            t.at[:, k * H : (k + 1) * H], tw.at[i, pl.ds(pl.multiple_of(k * CODES + at, 16), n)], sem.at[0]
        )
        for t, at, n, i in taps
        for k in range(KERNEL)
    ]
    start(first)
    if not split:
        first.append(pltpu.make_async_copy(table, wo.at[depth:], sem.at[0]))
        first[-1].start()
        out_copies = [pltpu.make_async_copy(w[0], wo.at[0:depth], sem.at[1])]
        in_copies = [pltpu.make_async_copy(w[1], wi, sem.at[2])]
        start(out_copies + in_copies)
    else:
        chip_out, chip_in = w[:2]
        parts, near_parts = w[2:6], w[6:10]
        x, core, y, z = place()
        n = depth // 4
        m = 2 * n
        half = n // 2
        row = pl.multiple_of(x * 2 * n, 16)
        out_copies = [
            pltpu.make_async_copy(chip_out.at[0 : 2 * n], wo.at[pl.ds(row, 2 * n)], sem.at[1]),
            pltpu.make_async_copy(chip_out.at[2 * n :], wo.at[depth:], sem.at[1]),
        ]
        row = pl.multiple_of(x * 2 * m, 16)
        in_copies = [pltpu.make_async_copy(chip_in, wi.at[pl.ds(row, 2 * m)], sem.at[2])]

        def far(outs, ins):
            out, into = [], []
            for c, of in ((core, parts), (1 - core, near_parts)):
                at = 2 * (1 - x) + c
                for p, zz in zip(outs, (z, 1 - z)):
                    row = pl.multiple_of(at * n + zz * half, 16)
                    out.append(pltpu.make_async_copy(of[p], wo.at[pl.ds(row, half)], sem.at[1]))
                for p, zz in zip(ins, (z, 1 - z)):
                    for j in range(2):
                        row = pl.multiple_of(at * m + zz * n + j * half, 16)
                        into.append(
                            pltpu.make_async_copy(of[p].at[:, j * H : (j + 1) * H], wi.at[pl.ds(row, half)], sem.at[2])
                        )
            return out, into

        start(out_copies + in_copies)
        far0, far1 = far((0, 2), (1, 3)), far((1, 3), (0, 2))

        @pl.when(y == 0)
        def _():
            start(far0[0] + far0[1])

        @pl.when(y == 1)
        def _():
            start(far1[0] + far1[1])

        out_copies += far0[0]
        in_copies += far0[1]

    rows = hid.shape[0] + 2 * EDGE
    cuts = [0, 512, rows]
    state = [None, None]

    def once(b, copies):
        if b == 0:
            wait(copies)

    def mix(b):
        if b == 0:
            wait(first)
            if split:
                tw[0] = (tw[0].astype(F32) + tw[1].astype(F32)).astype(BF)
        state[b] = dot(hot5[cuts[b] : cuts[b + 1]], tw[0])

    def act(b):
        state[b] = gelu(norm(state[b], gain_out[0:1])).astype(BF)

    def update(b):
        once(b, out_copies)
        lhs = jnp.concatenate([state[b], hot1[cuts[b] : cuts[b + 1]]], axis=1)
        state[b] = dot(lhs, wo[...]).astype(BF)

    def enter(b):
        hidden = state[b]
        lo, hi = max(cuts[b], EDGE), min(cuts[b + 1], rows - EDGE)
        hid[lo - EDGE : hi - EDGE] = hidden[lo - cuts[b] : hi - cuts[b]]
        state[b] = gelu(norm(hidden.astype(F32), gain_in[1:2])).astype(BF)

    def widen(b):
        once(b, in_copies)
        state[b] = dot(state[b], wi[...])

    def leave(b):
        n = cuts[b + 1] - cuts[b]
        pos = span[0] + cuts[b] + lax.broadcasted_iota(jnp.int32, (n, 1), 0)
        valid = jnp.where((pos >= 0) & (pos < span[1]), 1.0, 0.0)
        ci[cuts[b] : cuts[b + 1]] = (gelu(norm(state[b], gain_mid[1:2])) * valid).astype(BF)

    stagger((mix, act, update, enter, widen, leave))


def conv_copies(src, col, width, wt, per_tap, row, n, sem):
    copies = []
    done = 0
    while done < width:
        tap, inner = divmod(col + done, H)
        step = min(H - inner, width - done)
        copies.append(
            pltpu.make_async_copy(
                src.at[:, done : done + step],
                wt.at[pl.ds(pl.multiple_of(tap * per_tap + row, 16), n), inner : inner + step],
                sem,
            )
        )
        done += step
    return copies


HEAD = 256
TAIL = H - HEAD


def windows(ci, lo, hi, first, width):
    first = pl.multiple_of(first, 128)
    return jnp.concatenate(
        [ci[lo + k * DIL1 : hi + k * DIL1, pl.ds(first, width)] for k in range(KERNEL)], axis=1
    )


def chip_copies(table, w_out, w_in, w_conv, near_out, near_in, near_conv, chip_out, chip_in, chip_conv, sem):
    x, core, _, _ = place()
    n = w_out.shape[1]
    m = w_in.shape[1]
    short = HEAD - n
    done = None
    for xx in range(2):
        for cc in range(2):
            copies = [pltpu.make_async_copy(table, chip_out.at[2 * n :], sem)]
            for c, o, i, w in ((cc, w_out, w_in, w_conv), (1 - cc, near_out, near_in, near_conv)):
                copies.append(pltpu.make_async_copy(o.at[0], chip_out.at[c * n : (c + 1) * n], sem))
                copies.append(pltpu.make_async_copy(i.at[1], chip_in.at[c * m : (c + 1) * m], sem))
                if c == xx:
                    copies += conv_copies(w.at[1], 0, KERNEL * H, chip_conv, HEAD, short * xx, n, sem)
                else:
                    part = w.at[1, (n - short) * xx : (n - short) * xx + short]
                    copies += conv_copies(part, 0, KERNEL * H, chip_conv, HEAD, n * (1 - xx), short, sem)
            done = copies

            @pl.when((x == xx) & (core == cc))
            def _():
                start(copies)

    return done


def head_kernel(ci, w_conv, out):
    x, _, _, _ = place()
    rows = out.shape[0]
    half = 16 * ((rows + 31) // 32)
    for lo, hi in ((0, half), (half, rows)):
        out[lo:hi] = dot(windows(ci, lo, hi, x * TAIL, HEAD), w_conv[...])


def last_kernel(split, ci, hid, gain_out, *rest):
    *w, out, wt, wo, sem = rest
    if not split:
        conv_in = conv_copies(w[0], 0, KERNEL * H, wt, H, 0, H, sem.at[0])
        out_in = [pltpu.make_async_copy(w[1], wo, sem.at[1])]
        start(conv_in + out_in)
        first, width = 0, H
    else:
        head, w_conv, w_out, near_conv, near_out = w[:5]
        parts, near_parts = w[5:9], w[9:13]
        x, core, y, z = place()
        n = w_out.shape[1]
        half = n // 2
        left = 2 * n - HEAD
        rest_cols = KERNEL * H - CUT_B
        first, width = (1 - x) * HEAD, TAIL
        out_in = []
        for c, o in ((core, w_out), (1 - core, near_out)):
            row = pl.multiple_of((2 * x + c) * n, 16)
            out_in.append(pltpu.make_async_copy(o.at[1], wo.at[pl.ds(row, n)], sem.at[1]))
        from_row = pl.multiple_of((n - left) * (1 - x), 16)
        own_in, near_in = [
            conv_copies(v.at[1, pl.ds(from_row, left)], 0, KERNEL * H, wt, TAIL, 2 * n * x, left, sem.at[0])
            for v in (w_conv, near_conv)
        ]

        @pl.when(core + x == 1)
        def _():
            start(own_in)

        @pl.when(core + x != 1)
        def _():
            start(near_in)

        def far(head, tail):
            cv, out = [], []
            for c, of in ((core, parts), (1 - core, near_parts)):
                at = c * n + left * (1 - x)
                for p, zz in zip(head, (z, 1 - z)):
                    cv += conv_copies(of[p], 0, CUT_A, wt, TAIL, at + zz * half, half, sem.at[0])
                for p, zz in zip(tail, (z, 1 - z)):
                    skip = CUT_A - CUT_B
                    cv += conv_copies(
                        of[p].at[:, skip:rest_cols], CUT_A, rest_cols - skip, wt, TAIL, at + zz * half, half, sem.at[0]
                    )
                    row = pl.multiple_of((2 * (1 - x) + c) * n + zz * half, 16)
                    out.append(pltpu.make_async_copy(of[p].at[:, rest_cols:], wo.at[pl.ds(row, half)], sem.at[1]))
            return cv, out

        start(out_in)
        far0, far1 = far((0, 2), (1, 3)), far((1, 3), (0, 2))

        @pl.when(y == 0)
        def _():
            start(far0[0] + far0[1])

        @pl.when(y == 1)
        def _():
            start(far1[0] + far1[1])

        conv_in = own_in + far0[0]
        out_in += far0[1]

    rows = out.shape[0]
    cuts = [0, 16 * ((rows + 31) // 32), rows]
    state = [None, None]

    def mix(b):
        lhs = windows(ci, cuts[b], cuts[b + 1], first, width)
        if b == 0:
            wait(conv_in)
        state[b] = dot(lhs, wt[...])
        if split:
            state[b] += head[cuts[b] : cuts[b + 1]]

    def act(b):
        state[b] = gelu(norm(state[b], gain_out[1:2])).astype(BF)

    def update(b):
        if b == 0:
            wait(out_in)
        hidden = hid[cuts[b] : cuts[b + 1]].astype(F32)
        out[cuts[b] : cuts[b + 1]] = (hidden + dot(state[b], wo[...])).astype(BF)

    stagger((mix, act, update))


def after(x, *deps):
    return lax.optimization_barrier((x, *deps))[0]


def per_device(tokens, breaks, lengths, embed_table, break_vec, gain_in, gain_mid, gain_out, w_in, conv_w, w_out):
    rows = tokens.shape[1]
    width = embed_table.shape[1]
    roll_at = lax.axis_index("roll")
    seq_at = lax.axis_index("seq")
    rolls = lax.axis_size("roll")
    seqs = lax.axis_size("seq")
    split = rolls == 4 and seqs % 4 == 0

    def core_swap(x):
        return lax.ppermute(x, "roll", [(i, i ^ 1) for i in range(rolls)])

    def x_swap(x):
        return lax.ppermute(x, "roll", [(i, i ^ 2) for i in range(rolls)])

    def seq_swap(x, bits):
        return lax.ppermute(x, "seq", [(i, i ^ bits) for i in range(seqs)])

    span = jnp.stack([(seq_at * rows).astype(jnp.int32) - EDGE, lengths[0]])
    wide_rows = rows + 2 * EDGE
    codes = tokens[0] + SLOT * breaks[0]

    shard = w_out.shape[1] // 2
    shapes = [((CODES, width), BF), ((CODES, H), F32)]
    if split:
        shapes += [((shard, width), BF), ((shard, CUT_A), BF), ((shard, CUT_A), BF)]
    table, part, *parts = pl.pallas_call(
        functools.partial(first_kernel, split),
        out_shape=[jax.ShapeDtypeStruct(n, t) for n, t in shapes],
        in_specs=[HBM] * 6,
        out_specs=[VMEM] * 2 + [HBM] * (len(shapes) - 2),
        scratch_shapes=[
            pltpu.VMEM(embed_table.shape, F32),
            pltpu.VMEM((width,), F32),
            pltpu.VMEM(gain_in.shape, F32),
            pltpu.VMEM(w_in.shape[1:], BF),
            pltpu.VMEM((CODES, width), F32),
            pltpu.SemaphoreType.DMA((3,)),
        ]
        + [pltpu.VMEM(n, t) for n, t in shapes[2:]],
        cost_estimate=FREE,
        compiler_params=params(60),
    )(embed_table, break_vec, gain_in, w_in, conv_w, w_out)

    if split:
        own = part + core_swap(part)
        sent = own.astype(BF)
        other = x_swap(sent)
        pace = core_swap(sent[:16, :128])
        far_a = x_swap(after(parts[0], pace))
        near_out, near_in, near_conv = [core_swap(after(w, pace)) for w in (w_out, w_in, conv_w)]
    else:
        own = lax.psum(part, "roll")
        other = jnp.zeros((CODES, H), BF)
        pairs = [(i, i + 1) for i in range(seqs - 1)]
        before = lax.ppermute(codes[rows - REACH :], "seq", pairs)
        behind = lax.ppermute(codes[:REACH], "seq", [(j, i) for i, j in pairs])
    wide = KERNEL * H
    shapes = [(SLOT, F32), (SLOT, BF)] if split else [(CODES, F32)]
    taps = pl.pallas_call(
        functools.partial(table_kernel, split),
        out_shape=[jax.ShapeDtypeStruct((n, wide), t) for n, t in shapes],
        in_specs=[VMEM, VMEM, VMEM, HBM],
        out_specs=[VMEM] * len(shapes),
        scratch_shapes=[
            pltpu.VMEM(conv_w.shape[1:], BF),
            pltpu.VMEM((CODES, wide), F32),
            pltpu.SemaphoreType.DMA,
        ],
        cost_estimate=FREE,
        compiler_params=params(12),
    )(own, other, gain_mid, conv_w)
    if split:
        sent = (taps[0] + core_swap(taps[1]).astype(F32)).astype(BF)
        received = x_swap(sent)
        near_sent = core_swap(sent)
        relay = after(far_a, near_sent)
        parts_a = [far_a] + [seq_swap(relay, b) for b in (1, 2, 3)]
        far_b = x_swap(after(parts[1], near_sent))
        near_received = core_swap(received)
        codes = after(codes, received)
        ends = codes[rows - REACH :], codes[:REACH]
        low = seq_at % 2 == 0
        even = seq_swap(jnp.where(low, *ends), 1)
        pairs = [(i, i + 1) for i in range(1, seqs - 1, 2)]
        pairs.append((seqs - 1, 0))
        odd = lax.ppermute(jnp.where(low, *ends[::-1]), "seq", pairs + [(j, i) for i, j in pairs])
        before, behind = jnp.where(low, odd, even), jnp.where(low, even, odd)
    spare = jnp.zeros((-(rows + 2 * REACH) % 128,), jnp.int32)
    near = jnp.concatenate([before, codes, behind, spare])[None]

    shapes = [(wide_rows, KERNEL * CODES), (wide_rows, CODES)]
    operands, scratch = [], []
    if split:
        operands = [table, w_out, w_in, conv_w, near_out, near_in, near_conv]
        shapes += [(4 * shard + CODES, width), (8 * shard, H), (KERNEL * HEAD, H)]
        scratch = [pltpu.SemaphoreType.DMA]
    hot5, hot1, *chip = pl.pallas_call(
        functools.partial(hot_kernel, split),
        out_shape=[jax.ShapeDtypeStruct(n, BF) for n in shapes],
        in_specs=[SMEM, VMEM] + [ANY] * len(operands),
        out_specs=[VMEM] * len(shapes),
        scratch_shapes=scratch,
        cost_estimate=FREE,
        compiler_params=params(16),
    )(span, near, *operands)

    if split:
        near_a = [core_swap(relay)] + [core_swap(after(p, hot1)) for p in parts_a[1:]]
        relay = after(far_b, hot1)
        parts_b = [far_b, seq_swap(relay, 1), seq_swap(relay, 2), x_swap(after(parts[2], hot1))]
        near_b = [core_swap(relay)]
        weights_a = [sent, received, near_sent, near_received] + chip[:2] + parts_a + near_a
    else:
        taps = lax.psum(taps[0], "roll").astype(BF)
        gather = lambda w: lax.all_gather(w, "roll", axis=0, tiled=True)
        weights_a, weights_b = [taps, table, gather(w_out[0]), gather(w_in[1])], [gather(conv_w[1]), gather(w_out[1])]

    ci, hid = pl.pallas_call(
        functools.partial(rows_kernel, split),
        out_shape=(
            jax.ShapeDtypeStruct((wide_rows, H), BF),
            jax.ShapeDtypeStruct((rows, width), BF),
        ),
        in_specs=[SMEM] + [VMEM] * 5 + [ANY] * len(weights_a),
        out_specs=(VMEM, VMEM),
        scratch_shapes=[
            pltpu.VMEM((2, KERNEL * CODES, H), BF),
            pltpu.VMEM((H + CODES, width), BF),
            pltpu.VMEM((width, H), BF),
            pltpu.SemaphoreType.DMA((3,)),
        ],
        cost_estimate=FREE,
        compiler_params=params(30),
    )(span, hot5, hot1, gain_out, gain_in, gain_mid, *weights_a)

    if split:
        near_b += [core_swap(after(p, ci)) for p in parts_b[1:]]
        head = pl.pallas_call(
            head_kernel,
            out_shape=jax.ShapeDtypeStruct((rows, H), F32),
            in_specs=[VMEM] * 2,
            out_specs=VMEM,
            cost_estimate=FREE,
            compiler_params=params(16),
        )(ci, chip[2])
        weights_b = [head, conv_w, w_out, near_conv, near_out] + parts_b + near_b
    out = pl.pallas_call(
        functools.partial(last_kernel, split),
        out_shape=jax.ShapeDtypeStruct((rows, width), BF),
        in_specs=[VMEM] * 3
        + [HBM if w is w_out or w is conv_w else VMEM if split and w is head else ANY for w in weights_b],
        out_specs=VMEM,
        scratch_shapes=[
            pltpu.VMEM((KERNEL * (TAIL if split else H), H), BF),
            pltpu.VMEM((H, width), BF),
            pltpu.SemaphoreType.DMA((2,)),
        ],
        cost_estimate=FREE,
        compiler_params=params(24),
    )(ci, hid, gain_out, *weights_b)
    return out[None]


def solution(mesh):
    placed = (
        P("roll", "seq"),
        P("roll", "seq"),
        P("roll"),
        P(),
        P(),
        P(),
        P(),
        P(),
        P(None, "roll", None),
        P(None, "roll", None),
        P(None, "roll", None),
    )
    return jax.shard_map(
        per_device, mesh=mesh, in_specs=placed, out_specs=P("roll", "seq", None), check_vma=False
    )
```

```python
import functools

import jax
import jax.numpy as jnp
from jax import lax
from jax.experimental import pallas as pl
from jax.experimental.pallas import tpu as pltpu
from jax.sharding import PartitionSpec as P

H = 640
KERNEL = 5
VOCAB = 30
SLOT = 32
CODES = 2 * SLOT
BASE_DILATION = 64
DIL0 = BASE_DILATION
DIL1 = 2 * BASE_DILATION
HALF = KERNEL // 2
EDGE = HALF * DIL1
REACH = EDGE + HALF * DIL0
BF = jnp.bfloat16
F32 = jnp.float32
VMEM = pl.BlockSpec(memory_space=pltpu.VMEM)
SMEM = pl.BlockSpec(memory_space=pltpu.SMEM)
ANY = pl.BlockSpec(memory_space=pl.ANY)
HBM = pl.BlockSpec(memory_space=pltpu.HBM)
FREE = pl.CostEstimate(flops=0, bytes_accessed=0, transcendentals=0)
LONG = pl.CostEstimate(flops=2 * 10**10, bytes_accessed=0, transcendentals=0)
CUT_A = 18 * 128
CUT_B = 17 * 128


def params(mib):
    return pltpu.CompilerParams(vmem_limit_bytes=mib * 1024 * 1024)


def gelu(x):
    return (0.5 * x) * (1.0 + lax.erf(x * 0.5**0.5))


def norm(x, gain):
    center = jnp.mean(x, axis=-1, keepdims=True)
    d = x - center
    spread = jnp.mean(d * d, axis=-1, keepdims=True)
    return d * lax.rsqrt(spread + 1e-5) * gain


def dot(a, b):
    return jnp.dot(a, b, preferred_element_type=F32)


def place():
    roll, seq = lax.axis_index("roll"), lax.axis_index("seq")
    return lax.div(roll, 2), lax.rem(roll, 2), lax.rem(seq, 2), lax.rem(lax.div(seq, 2), 2)


def start(copies):
    for c in copies:
        c.start()


def wait(copies):
    for c in copies:
        c.wait()


def stagger(stages):
    for t in range(len(stages) + 1):
        for b in range(2):
            if 0 <= t - b < len(stages):
                stages[t - b](b)


def pick(rows, columns, first):
    i = lax.broadcasted_iota(jnp.int32, (rows, columns), 0)
    j = lax.broadcasted_iota(jnp.int32, (rows, columns), 1)
    return jnp.where(i == j + first, 1.0, 0.0).astype(BF)


def part_copies(y_is_one, row_bit, w_in, conv_w, w_out, a, b, sem):
    n = b.shape[0]
    r = pl.multiple_of(row_bit * n, 16)
    r2 = pl.multiple_of(row_bit * 2 * n, 16)
    rest = conv_w.shape[2] - CUT_B
    if y_is_one:
        pairs = [
            (conv_w.at[1, pl.ds(r, n), CUT_B:], b.at[:, 0:rest]),
            (w_out.at[1, pl.ds(r, n)], b.at[:, rest:]),
        ]
        if a is not None:
            pairs += [
                (w_in.at[1, pl.ds(r2, n)], a.at[:, 0:H]),
                (w_in.at[1, pl.ds(r2 + n, n)], a.at[:, H : 2 * H]),
            ]
    else:
        pairs = [(conv_w.at[1, pl.ds(r, n), 0:CUT_A], b)]
        if a is not None:
            pairs.append((w_out.at[0, pl.ds(r, n)], a))
    return [pltpu.make_async_copy(s, d, sem) for s, d in pairs]


def first_kernel(split, embed, brk, gain, w_in, conv_w, w_out, table, part, *rest):
    count = 3 if split else 0
    parts, rest = rest[:count], rest[count:]
    emb, bv, g, w, full, sem, *held = rest
    copies = [
        pltpu.make_async_copy(s, d, sem.at[0])
        for s, d in ((embed, emb), (brk, bv), (gain, g), (w_in.at[0], w))
    ]
    start(copies)
    leaving = []
    if split:
        _, _, y, z = place()
        kinds = []
        for kind in range(2):
            kinds.append(
                part_copies(kind == 1, z, w_in, conv_w, w_out, held[0], held[1], sem.at[1])
                + part_copies(kind == 0, 1 - z, w_in, conv_w, w_out, None, held[2], sem.at[1])
            )

            @pl.when(y == kind)
            def _():
                start(kinds[kind])

        leaving = [pltpu.make_async_copy(s, d, sem.at[2]) for s, d in zip(held, parts)]

    wait(copies)
    if split:
        for kind in range(2):

            @pl.when(y == kind)
            def _():
                wait(kinds[kind])

        start(leaving)
    full[...] = jnp.zeros_like(full)
    full[0:VOCAB] = emb[...]
    full[SLOT : SLOT + VOCAB] = emb[...] + bv[...][None, :]
    hidden = full[...].astype(BF)
    table[...] = hidden
    normed = gelu(norm(hidden.astype(F32), g[0:1])).astype(BF)
    rows = w.shape[0]
    mine = dot(normed, pick(normed.shape[1], rows, lax.axis_index("roll") * rows)).astype(BF)
    part[...] = dot(mine, w[...])
    wait(leaving)


def table_kernel(split, own, other, gain, w_all, *rest):
    *outs, w, full, sem = rest
    copy = pltpu.make_async_copy(w_all.at[0], w, sem)
    copy.start()
    wide = own[...] + other[...].astype(F32)
    t = gelu(norm(wide, gain[0:1])).astype(BF)
    rows = w.shape[0]
    mine = dot(t, pick(t.shape[1], rows, lax.axis_index("roll") * rows)).astype(BF)
    copy.wait()
    full[...] = dot(mine, w[...])
    if split:
        core = lax.rem(lax.axis_index("roll"), 2)
        outs[0][...] = full[pl.ds(pl.multiple_of(core * SLOT, SLOT), SLOT)]
        outs[1][...] = full[pl.ds(pl.multiple_of((1 - core) * SLOT, SLOT), SLOT)].astype(BF)
    else:
        outs[0][...] = full[...]


def stage_kernel(*refs):
    wait(chip_copies(*refs))


def hot_kernel(span, near, hot5, hot1):
    codes = near[...]
    count = codes.shape[1]
    rows = hot5.shape[0]
    pos = span[0] - HALF * DIL0 + lax.broadcasted_iota(jnp.int32, codes.shape, 1)
    masked = jnp.where((pos >= 0) & (pos < span[1]), codes, -1)
    lanes = lax.broadcasted_iota(jnp.int32, (CODES, count), 0)
    taps = jnp.where(lanes == masked, 1.0, 0.0).T.astype(BF)
    for k in range(KERNEL):
        hot5[:, k * CODES : (k + 1) * CODES] = taps[k * DIL0 : k * DIL0 + rows]
    center = jnp.where(lanes == codes, 1.0, 0.0).T.astype(BF)
    hot1[...] = center[HALF * DIL0 : HALF * DIL0 + rows]


def rows_kernel(split, span, hot5, hot1, gain_out, gain_in, gain_mid, *rest):
    *w, ci, hid, tw, wo, wi, sem = rest
    depth = wo.shape[0] - CODES
    if split:
        core = lax.rem(lax.axis_index("roll"), 2)
        taps = [(t, core * SLOT, SLOT, 0) for t in w[:2]] + [(t, (1 - core) * SLOT, SLOT, 0) for t in w[2:4]]
        taps = [(t, at, n, i % 2) for i, (t, at, n, _) in enumerate(taps)]
        w = w[4:]
    else:
        taps = [(w[0], 0, CODES, 0)]
        table, *w = w[1:]
    first = [
        pltpu.make_async_copy(
            t.at[:, k * H : (k + 1) * H], tw.at[i, pl.ds(pl.multiple_of(k * CODES + at, 16), n)], sem.at[0]
        )
        for t, at, n, i in taps
        for k in range(KERNEL)
    ]
    start(first)
    if not split:
        first.append(pltpu.make_async_copy(table, wo.at[depth:], sem.at[0]))
        first[-1].start()
        out_copies = [pltpu.make_async_copy(w[0], wo.at[0:depth], sem.at[1])]
        in_copies = [pltpu.make_async_copy(w[1], wi, sem.at[2])]
        start(out_copies + in_copies)
    else:
        chip_out, chip_in = w[:2]
        parts, near_parts = w[2:6], w[6:10]
        x, core, y, z = place()
        n = depth // 4
        m = 2 * n
        half = n // 2
        row = pl.multiple_of(x * 2 * n, 16)
        out_copies = [
            pltpu.make_async_copy(chip_out.at[0 : 2 * n], wo.at[pl.ds(row, 2 * n)], sem.at[1]),
            pltpu.make_async_copy(chip_out.at[2 * n :], wo.at[depth:], sem.at[1]),
        ]
        row = pl.multiple_of(x * 2 * m, 16)
        in_copies = [pltpu.make_async_copy(chip_in, wi.at[pl.ds(row, 2 * m)], sem.at[2])]

        def far(outs, ins):
            out, into = [], []
            for c, of in ((core, parts), (1 - core, near_parts)):
                at = 2 * (1 - x) + c
                for p, zz in zip(outs, (z, 1 - z)):
                    row = pl.multiple_of(at * n + zz * half, 16)
                    out.append(pltpu.make_async_copy(of[p], wo.at[pl.ds(row, half)], sem.at[1]))
                for p, zz in zip(ins, (z, 1 - z)):
                    for j in range(2):
                        row = pl.multiple_of(at * m + zz * n + j * half, 16)
                        into.append(
                            pltpu.make_async_copy(of[p].at[:, j * H : (j + 1) * H], wi.at[pl.ds(row, half)], sem.at[2])
                        )
            return out, into

        start(out_copies + in_copies)
        far0, far1 = far((0, 2), (1, 3)), far((1, 3), (0, 2))

        @pl.when(y == 0)
        def _():
            start(far0[0] + far0[1])

        @pl.when(y == 1)
        def _():
            start(far1[0] + far1[1])

        out_copies += far0[0]
        in_copies += far0[1]

    rows = hid.shape[0] + 2 * EDGE
    cuts = [0, 512, rows]
    state = [None, None]

    def once(b, copies):
        if b == 0:
            wait(copies)

    def mix(b):
        if b == 0:
            wait(first)
            if split:
                tw[0] = (tw[0].astype(F32) + tw[1].astype(F32)).astype(BF)
        state[b] = dot(hot5[cuts[b] : cuts[b + 1]], tw[0])

    def act(b):
        state[b] = gelu(norm(state[b], gain_out[0:1])).astype(BF)

    def update(b):
        once(b, out_copies)
        lhs = jnp.concatenate([state[b], hot1[cuts[b] : cuts[b + 1]]], axis=1)
        state[b] = dot(lhs, wo[...]).astype(BF)

    def enter(b):
        hidden = state[b]
        lo, hi = max(cuts[b], EDGE), min(cuts[b + 1], rows - EDGE)
        hid[lo - EDGE : hi - EDGE] = hidden[lo - cuts[b] : hi - cuts[b]]
        state[b] = gelu(norm(hidden.astype(F32), gain_in[1:2])).astype(BF)

    def widen(b):
        once(b, in_copies)
        state[b] = dot(state[b], wi[...])

    def leave(b):
        n = cuts[b + 1] - cuts[b]
        pos = span[0] + cuts[b] + lax.broadcasted_iota(jnp.int32, (n, 1), 0)
        valid = jnp.where((pos >= 0) & (pos < span[1]), 1.0, 0.0)
        ci[cuts[b] : cuts[b + 1]] = (gelu(norm(state[b], gain_mid[1:2])) * valid).astype(BF)

    stagger((mix, act, update, enter, widen, leave))


def conv_copies(src, col, width, wt, per_tap, row, n, sem):
    copies = []
    done = 0
    while done < width:
        tap, inner = divmod(col + done, H)
        step = min(H - inner, width - done)
        copies.append(
            pltpu.make_async_copy(
                src.at[:, done : done + step],
                wt.at[pl.ds(pl.multiple_of(tap * per_tap + row, 16), n), inner : inner + step],
                sem,
            )
        )
        done += step
    return copies


HEAD = 256
TAIL = H - HEAD


def windows(ci, lo, hi, first, width):
    first = pl.multiple_of(first, 128)
    return jnp.concatenate(
        [ci[lo + k * DIL1 : hi + k * DIL1, pl.ds(first, width)] for k in range(KERNEL)], axis=1
    )


def chip_copies(table, w_out, w_in, w_conv, near_out, near_in, near_conv, chip_out, chip_in, chip_conv, sem):
    x, core, _, _ = place()
    n = w_out.shape[1]
    m = w_in.shape[1]
    short = HEAD - n
    done = None
    for xx in range(2):
        for cc in range(2):
            copies = [pltpu.make_async_copy(table, chip_out.at[2 * n :], sem)]
            for c, o, i, w in ((cc, w_out, w_in, w_conv), (1 - cc, near_out, near_in, near_conv)):
                copies.append(pltpu.make_async_copy(o.at[0], chip_out.at[c * n : (c + 1) * n], sem))
                copies.append(pltpu.make_async_copy(i.at[1], chip_in.at[c * m : (c + 1) * m], sem))
                if c == xx:
                    copies += conv_copies(w.at[1], 0, KERNEL * H, chip_conv, HEAD, short * xx, n, sem)
                else:
                    part = w.at[1, (n - short) * xx : (n - short) * xx + short]
                    copies += conv_copies(part, 0, KERNEL * H, chip_conv, HEAD, n * (1 - xx), short, sem)
            done = copies

            @pl.when((x == xx) & (core == cc))
            def _():
                start(copies)

    return done


def head_kernel(ci, w_conv, out):
    x, _, _, _ = place()
    rows = out.shape[0]
    half = 16 * ((rows + 31) // 32)
    for lo, hi in ((0, half), (half, rows)):
        out[lo:hi] = dot(windows(ci, lo, hi, x * TAIL, HEAD), w_conv[...])


def last_kernel(split, ci, hid, gain_out, *rest):
    *w, out, wt, wo, sem = rest
    if not split:
        conv_in = conv_copies(w[0], 0, KERNEL * H, wt, H, 0, H, sem.at[0])
        out_in = [pltpu.make_async_copy(w[1], wo, sem.at[1])]
        start(conv_in + out_in)
        first, width = 0, H
    else:
        head, w_conv, w_out, near_conv, near_out = w[:5]
        parts, near_parts = w[5:9], w[9:13]
        x, core, y, z = place()
        n = w_out.shape[1]
        half = n // 2
        left = 2 * n - HEAD
        rest_cols = KERNEL * H - CUT_B
        first, width = (1 - x) * HEAD, TAIL
        out_in = []
        for c, o in ((core, w_out), (1 - core, near_out)):
            row = pl.multiple_of((2 * x + c) * n, 16)
            out_in.append(pltpu.make_async_copy(o.at[1], wo.at[pl.ds(row, n)], sem.at[1]))
        from_row = pl.multiple_of((n - left) * (1 - x), 16)
        own_in, near_in = [
            conv_copies(v.at[1, pl.ds(from_row, left)], 0, KERNEL * H, wt, TAIL, 2 * n * x, left, sem.at[0])
            for v in (w_conv, near_conv)
        ]

        @pl.when(core + x == 1)
        def _():
            start(own_in)

        @pl.when(core + x != 1)
        def _():
            start(near_in)

        def far(head, tail):
            cv, out = [], []
            for c, of in ((core, parts), (1 - core, near_parts)):
                at = c * n + left * (1 - x)
                for p, zz in zip(head, (z, 1 - z)):
                    cv += conv_copies(of[p], 0, CUT_A, wt, TAIL, at + zz * half, half, sem.at[0])
                for p, zz in zip(tail, (z, 1 - z)):
                    skip = CUT_A - CUT_B
                    cv += conv_copies(
                        of[p].at[:, skip:rest_cols], CUT_A, rest_cols - skip, wt, TAIL, at + zz * half, half, sem.at[0]
                    )
                    row = pl.multiple_of((2 * (1 - x) + c) * n + zz * half, 16)
                    out.append(pltpu.make_async_copy(of[p].at[:, rest_cols:], wo.at[pl.ds(row, half)], sem.at[1]))
            return cv, out

        start(out_in)
        far0, far1 = far((0, 2), (1, 3)), far((1, 3), (0, 2))

        @pl.when(y == 0)
        def _():
            start(far0[0] + far0[1])

        @pl.when(y == 1)
        def _():
            start(far1[0] + far1[1])

        conv_in = own_in + far0[0]
        out_in += far0[1]

    rows = out.shape[0]
    cuts = [0, 16 * ((rows + 31) // 32), rows]
    state = [None, None]

    def mix(b):
        lhs = windows(ci, cuts[b], cuts[b + 1], first, width)
        if b == 0:
            wait(conv_in)
        state[b] = dot(lhs, wt[...])
        if split:
            state[b] += head[cuts[b] : cuts[b + 1]]

    def act(b):
        state[b] = gelu(norm(state[b], gain_out[1:2])).astype(BF)

    def update(b):
        if b == 0:
            wait(out_in)
        hidden = hid[cuts[b] : cuts[b + 1]].astype(F32)
        out[cuts[b] : cuts[b + 1]] = (hidden + dot(state[b], wo[...])).astype(BF)

    stagger((mix, act, update))


def after(x, *deps):
    return lax.optimization_barrier((x, *deps))[0]


def per_device(tokens, breaks, lengths, embed_table, break_vec, gain_in, gain_mid, gain_out, w_in, conv_w, w_out):
    rows = tokens.shape[1]
    width = embed_table.shape[1]
    roll_at = lax.axis_index("roll")
    seq_at = lax.axis_index("seq")
    rolls = lax.axis_size("roll")
    seqs = lax.axis_size("seq")
    split = rolls == 4 and seqs % 4 == 0

    def core_swap(x):
        return lax.ppermute(x, "roll", [(i, i ^ 1) for i in range(rolls)])

    def x_swap(x):
        return lax.ppermute(x, "roll", [(i, i ^ 2) for i in range(rolls)])

    def seq_swap(x, bits):
        return lax.ppermute(x, "seq", [(i, i ^ bits) for i in range(seqs)])

    span = jnp.stack([(seq_at * rows).astype(jnp.int32) - EDGE, lengths[0]])
    wide_rows = rows + 2 * EDGE
    codes = tokens[0] + SLOT * breaks[0]

    shard = w_out.shape[1] // 2
    shapes = [((CODES, width), BF), ((CODES, H), F32)]
    if split:
        shapes += [((shard, width), BF), ((shard, CUT_A), BF), ((shard, CUT_A), BF)]
    table, part, *parts = pl.pallas_call(
        functools.partial(first_kernel, split),
        out_shape=[jax.ShapeDtypeStruct(n, t) for n, t in shapes],
        in_specs=[HBM] * 6,
        out_specs=[VMEM] * 2 + [HBM] * (len(shapes) - 2),
        scratch_shapes=[
            pltpu.VMEM(embed_table.shape, F32),
            pltpu.VMEM((width,), F32),
            pltpu.VMEM(gain_in.shape, F32),
            pltpu.VMEM(w_in.shape[1:], BF),
            pltpu.VMEM((CODES, width), F32),
            pltpu.SemaphoreType.DMA((3,)),
        ]
        + [pltpu.VMEM(n, t) for n, t in shapes[2:]],
        cost_estimate=FREE,
        compiler_params=params(60),
    )(embed_table, break_vec, gain_in, w_in, conv_w, w_out)

    if split:
        far_a = x_swap(parts[0])
        own = part + core_swap(part)
        other = x_swap(own.astype(BF))
        near_out, near_in = core_swap(w_out), core_swap(w_in)
        ends = codes[rows - REACH :], codes[:REACH]
        low = seq_at % 2 == 0
        even = seq_swap(jnp.where(low, *ends), 1)
        pairs = [(i, i + 1) for i in range(1, seqs - 1, 2)]
        pairs.append((seqs - 1, 0))
        odd = lax.ppermute(jnp.where(low, *ends[::-1]), "seq", pairs + [(j, i) for i, j in pairs])
        before, behind = jnp.where(low, odd, even), jnp.where(low, even, odd)
        other = after(other, far_a, near_out, near_in, before, behind)
    else:
        own = lax.psum(part, "roll")
        other = jnp.zeros((CODES, H), BF)
        pairs = [(i, i + 1) for i in range(seqs - 1)]
        before = lax.ppermute(codes[rows - REACH :], "seq", pairs)
        behind = lax.ppermute(codes[:REACH], "seq", [(j, i) for i, j in pairs])
    wide = KERNEL * H
    shapes = [(SLOT, F32), (SLOT, BF)] if split else [(CODES, F32)]
    taps = pl.pallas_call(
        functools.partial(table_kernel, split),
        out_shape=[jax.ShapeDtypeStruct((n, wide), t) for n, t in shapes],
        in_specs=[VMEM, VMEM, VMEM, HBM],
        out_specs=[VMEM] * len(shapes),
        scratch_shapes=[
            pltpu.VMEM(conv_w.shape[1:], BF),
            pltpu.VMEM((CODES, wide), F32),
            pltpu.SemaphoreType.DMA,
        ],
        cost_estimate=FREE,
        compiler_params=params(12),
    )(own, other, gain_mid, conv_w)
    if split:
        near_conv = core_swap(after(conv_w, taps[1]))
        relay = after(far_a, taps[1])
        parts_a = [far_a] + [seq_swap(relay, b) for b in (1, 2, 3)]
        sent = (taps[0] + core_swap(taps[1]).astype(F32)).astype(BF)
        received = x_swap(sent)
        far_b = x_swap(after(parts[1], near_conv))
        chip = pl.pallas_call(
            stage_kernel,
            out_shape=[
                jax.ShapeDtypeStruct(n, BF)
                for n in ((4 * shard + CODES, width), (8 * shard, H), (KERNEL * HEAD, H))
            ],
            in_specs=[ANY] * 7,
            out_specs=[VMEM] * 3,
            scratch_shapes=[pltpu.SemaphoreType.DMA],
            cost_estimate=LONG,
            compiler_params=params(16),
        )(after(table, sent), w_out, w_in, conv_w, near_out, near_in, near_conv)
    spare = jnp.zeros((-(rows + 2 * REACH) % 128,), jnp.int32)
    near = jnp.concatenate([before, codes, behind, spare])[None]
    if split:
        near = after(near, chip[0])

    hot5, hot1 = pl.pallas_call(
        hot_kernel,
        out_shape=[jax.ShapeDtypeStruct((wide_rows, n), BF) for n in (KERNEL * CODES, CODES)],
        in_specs=[SMEM, VMEM],
        out_specs=[VMEM] * 2,
        cost_estimate=FREE,
        compiler_params=params(12),
    )(span, near)

    if split:
        received = after(received, hot1, *parts_a)
        near_received = core_swap(received)
        near_sent = core_swap(after(sent, received))
        near_a = [core_swap(after(p, received)) for p in parts_a]
        relay = after(far_b, received)
        parts_b = [far_b, seq_swap(relay, 1), seq_swap(relay, 2), x_swap(after(parts[2], received))]
        weights_a = [sent, received, near_sent, near_received] + list(chip[:2]) + parts_a + near_a
    else:
        taps = lax.psum(taps[0], "roll").astype(BF)
        gather = lambda w: lax.all_gather(w, "roll", axis=0, tiled=True)
        weights_a, weights_b = [taps, table, gather(w_out[0]), gather(w_in[1])], [gather(conv_w[1]), gather(w_out[1])]

    ci, hid = pl.pallas_call(
        functools.partial(rows_kernel, split),
        out_shape=(
            jax.ShapeDtypeStruct((wide_rows, H), BF),
            jax.ShapeDtypeStruct((rows, width), BF),
        ),
        in_specs=[SMEM] + [VMEM] * 5 + [ANY] * len(weights_a),
        out_specs=(VMEM, VMEM),
        scratch_shapes=[
            pltpu.VMEM((2, KERNEL * CODES, H), BF),
            pltpu.VMEM((H + CODES, width), BF),
            pltpu.VMEM((width, H), BF),
            pltpu.SemaphoreType.DMA((3,)),
        ],
        cost_estimate=LONG,
        compiler_params=params(30),
    )(span, hot5, hot1, gain_out, gain_in, gain_mid, *weights_a)

    if split:
        near_b = [core_swap(after(p, ci)) for p in parts_b]
        head = pl.pallas_call(
            head_kernel,
            out_shape=jax.ShapeDtypeStruct((rows, H), F32),
            in_specs=[VMEM] * 2,
            out_specs=VMEM,
            cost_estimate=LONG,
            compiler_params=params(16),
        )(ci, chip[2])
        weights_b = [head, conv_w, w_out, near_conv, near_out] + parts_b + near_b
    out = pl.pallas_call(
        functools.partial(last_kernel, split),
        out_shape=jax.ShapeDtypeStruct((rows, width), BF),
        in_specs=[VMEM] * 3
        + [HBM if w is w_out or w is conv_w else VMEM if split and w is head else ANY for w in weights_b],
        out_specs=VMEM,
        scratch_shapes=[
            pltpu.VMEM((KERNEL * (TAIL if split else H), H), BF),
            pltpu.VMEM((H, width), BF),
            pltpu.SemaphoreType.DMA((2,)),
        ],
        cost_estimate=FREE,
        compiler_params=params(24),
    )(ci, hid, gain_out, *weights_b)
    return out[None]


def solution(mesh):
    placed = (
        P("roll", "seq"),
        P("roll", "seq"),
        P("roll"),
        P(),
        P(),
        P(),
        P(),
        P(),
        P(None, "roll", None),
        P(None, "roll", None),
        P(None, "roll", None),
    )
    return jax.shard_map(
        per_device, mesh=mesh, in_specs=placed, out_specs=P("roll", "seq", None), check_vma=False
    )
```

```python
import functools

import jax
import jax.numpy as jnp
from jax import lax
from jax.experimental import pallas as pl
from jax.experimental.pallas import tpu as pltpu
from jax.sharding import PartitionSpec as P

H = 640
KERNEL = 5
VOCAB = 30
SLOT = 32
CODES = 2 * SLOT
BASE_DILATION = 64
DIL0 = BASE_DILATION
DIL1 = 2 * BASE_DILATION
HALF = KERNEL // 2
EDGE = HALF * DIL1
REACH = EDGE + HALF * DIL0
BF = jnp.bfloat16
F32 = jnp.float32
VMEM = pl.BlockSpec(memory_space=pltpu.VMEM)
SMEM = pl.BlockSpec(memory_space=pltpu.SMEM)
ANY = pl.BlockSpec(memory_space=pl.ANY)
HBM = pl.BlockSpec(memory_space=pltpu.HBM)
FREE = pl.CostEstimate(flops=0, bytes_accessed=0, transcendentals=0)
CUT_A = 18 * 128
CUT_B = 17 * 128


def params(mib):
    return pltpu.CompilerParams(vmem_limit_bytes=mib * 1024 * 1024)


def gelu(x):
    return (0.5 * x) * (1.0 + lax.erf(x * 0.5**0.5))


def norm(x, gain):
    center = jnp.mean(x, axis=-1, keepdims=True)
    d = x - center
    spread = jnp.mean(d * d, axis=-1, keepdims=True)
    return d * lax.rsqrt(spread + 1e-5) * gain


def dot(a, b):
    return jnp.dot(a, b, preferred_element_type=F32)


def place():
    roll, seq = lax.axis_index("roll"), lax.axis_index("seq")
    return lax.div(roll, 2), lax.rem(roll, 2), lax.rem(seq, 2), lax.rem(lax.div(seq, 2), 2)


def start(copies):
    for c in copies:
        c.start()


def wait(copies):
    for c in copies:
        c.wait()


def stagger(stages):
    for t in range(len(stages) + 1):
        for b in range(2):
            if 0 <= t - b < len(stages):
                stages[t - b](b)


def pick(rows, columns, first):
    i = lax.broadcasted_iota(jnp.int32, (rows, columns), 0)
    j = lax.broadcasted_iota(jnp.int32, (rows, columns), 1)
    return jnp.where(i == j + first, 1.0, 0.0).astype(BF)


def part_copies(y_is_one, row_bit, w_in, conv_w, w_out, a, b, sem):
    n = b.shape[0]
    r = pl.multiple_of(row_bit * n, 16)
    r2 = pl.multiple_of(row_bit * 2 * n, 16)
    rest = conv_w.shape[2] - CUT_B
    if y_is_one:
        pairs = [
            (conv_w.at[1, pl.ds(r, n), CUT_B:], b.at[:, 0:rest]),
            (w_out.at[1, pl.ds(r, n)], b.at[:, rest:]),
        ]
        if a is not None:
            pairs += [
                (w_in.at[1, pl.ds(r2, n)], a.at[:, 0:H]),
                (w_in.at[1, pl.ds(r2 + n, n)], a.at[:, H : 2 * H]),
            ]
    else:
        pairs = [(conv_w.at[1, pl.ds(r, n), 0:CUT_A], b)]
        if a is not None:
            pairs.append((w_out.at[0, pl.ds(r, n)], a))
    return [pltpu.make_async_copy(s, d, sem) for s, d in pairs]


def first_kernel(split, embed, brk, gain, w_in, conv_w, w_out, table, part, *rest):
    count = 3 if split else 0
    parts, rest = rest[:count], rest[count:]
    emb, bv, g, w, full, sem, *held = rest
    copies = [
        pltpu.make_async_copy(s, d, sem.at[0])
        for s, d in ((embed, emb), (brk, bv), (gain, g), (w_in.at[0], w))
    ]
    start(copies)
    leaving = []
    if split:
        _, _, y, z = place()
        kinds = []
        for kind in range(2):
            kinds.append(
                part_copies(kind == 1, z, w_in, conv_w, w_out, held[0], held[1], sem.at[1])
                + part_copies(kind == 0, 1 - z, w_in, conv_w, w_out, None, held[2], sem.at[1])
            )

            @pl.when(y == kind)
            def _():
                start(kinds[kind])

        leaving = [pltpu.make_async_copy(s, d, sem.at[2]) for s, d in zip(held, parts)]

    wait(copies)
    if split:
        for kind in range(2):

            @pl.when(y == kind)
            def _():
                wait(kinds[kind])

        start(leaving)
    full[...] = jnp.zeros_like(full)
    full[0:VOCAB] = emb[...]
    full[SLOT : SLOT + VOCAB] = emb[...] + bv[...][None, :]
    hidden = full[...].astype(BF)
    table[...] = hidden
    normed = gelu(norm(hidden.astype(F32), g[0:1])).astype(BF)
    rows = w.shape[0]
    mine = dot(normed, pick(normed.shape[1], rows, lax.axis_index("roll") * rows)).astype(BF)
    part[...] = dot(mine, w[...])
    wait(leaving)


def table_kernel(split, own, other, gain, w_all, table, *rest):
    *outs, table_out, w, full, sem = rest
    copies = [pltpu.make_async_copy(table, table_out, sem.at[1])]
    start(copies)
    copy = pltpu.make_async_copy(w_all.at[0], w, sem.at[0])
    copy.start()
    wide = own[...] + other[...].astype(F32)
    t = gelu(norm(wide, gain[0:1])).astype(BF)
    rows = w.shape[0]
    mine = dot(t, pick(t.shape[1], rows, lax.axis_index("roll") * rows)).astype(BF)
    copy.wait()
    full[...] = dot(mine, w[...])
    if split:
        core = lax.rem(lax.axis_index("roll"), 2)
        outs[0][...] = full[pl.ds(pl.multiple_of(core * SLOT, SLOT), SLOT)]
        outs[1][...] = full[pl.ds(pl.multiple_of((1 - core) * SLOT, SLOT), SLOT)].astype(BF)
    else:
        outs[0][...] = full[...]
    wait(copies)


def hot_kernel(span, near, hot5, hot1):
    codes = near[...]
    count = codes.shape[1]
    rows = hot5.shape[0]
    pos = span[0] - HALF * DIL0 + lax.broadcasted_iota(jnp.int32, codes.shape, 1)
    masked = jnp.where((pos >= 0) & (pos < span[1]), codes, -1)
    lanes = lax.broadcasted_iota(jnp.int32, (CODES, count), 0)
    taps = jnp.where(lanes == masked, 1.0, 0.0).T.astype(BF)
    for k in range(KERNEL):
        hot5[:, k * CODES : (k + 1) * CODES] = taps[k * DIL0 : k * DIL0 + rows]
    center = jnp.where(lanes == codes, 1.0, 0.0).T.astype(BF)
    hot1[...] = center[HALF * DIL0 : HALF * DIL0 + rows]


def rows_kernel(split, span, hot5, hot1, gain_out, gain_in, gain_mid, *rest):
    *w, ci, hid, tw, wo, wi, sem = rest
    depth = wo.shape[0] - CODES
    if split:
        core = lax.rem(lax.axis_index("roll"), 2)
        taps = [(t, core * SLOT, SLOT, 0) for t in w[:2]] + [(t, (1 - core) * SLOT, SLOT, 0) for t in w[2:4]]
        taps = [(t, at, n, i % 2) for i, (t, at, n, _) in enumerate(taps)]
        w = w[4:]
    else:
        taps = [(w[0], 0, CODES, 0)]
        table, *w = w[1:]
    first = [
        pltpu.make_async_copy(
            t.at[:, k * H : (k + 1) * H], tw.at[i, pl.ds(pl.multiple_of(k * CODES + at, 16), n)], sem.at[0]
        )
        for t, at, n, i in taps
        for k in range(KERNEL)
    ]
    start(first)
    if not split:
        first.append(pltpu.make_async_copy(table, wo.at[depth:], sem.at[0]))
        first[-1].start()
        out_copies = [pltpu.make_async_copy(w[0], wo.at[0:depth], sem.at[1])]
        in_copies = [pltpu.make_async_copy(w[1], wi, sem.at[2])]
        start(out_copies + in_copies)
    else:
        w_out, w_in, near_out, near_in, table = w[:5]
        parts, near_parts = w[5:9], w[9:13]
        x, core, y, z = place()
        n = w_out.shape[1]
        m = w_in.shape[1]
        half = n // 2
        out_copies, in_copies = [pltpu.make_async_copy(table, wo.at[depth:], sem.at[1])], []
        for c, o, i in ((core, w_out, w_in), (1 - core, near_out, near_in)):
            at = 2 * x + c
            out_copies.append(pltpu.make_async_copy(o.at[0], wo.at[pl.ds(pl.multiple_of(at * n, 16), n)], sem.at[1]))
            in_copies.append(pltpu.make_async_copy(i.at[1], wi.at[pl.ds(pl.multiple_of(at * m, 16), m)], sem.at[2]))

        def far(outs, ins):
            out, into = [], []
            for c, of in ((core, parts), (1 - core, near_parts)):
                at = 2 * (1 - x) + c
                for p, zz in zip(outs, (z, 1 - z)):
                    row = pl.multiple_of(at * n + zz * half, 16)
                    out.append(pltpu.make_async_copy(of[p], wo.at[pl.ds(row, half)], sem.at[1]))
                for p, zz in zip(ins, (z, 1 - z)):
                    for j in range(2):
                        row = pl.multiple_of(at * m + zz * n + j * half, 16)
                        into.append(
                            pltpu.make_async_copy(of[p].at[:, j * H : (j + 1) * H], wi.at[pl.ds(row, half)], sem.at[2])
                        )
            return out, into

        start(out_copies + in_copies)
        far0, far1 = far((0, 2), (1, 3)), far((1, 3), (0, 2))

        @pl.when(y == 0)
        def _():
            start(far0[0] + far0[1])

        @pl.when(y == 1)
        def _():
            start(far1[0] + far1[1])

        out_copies += far0[0]
        in_copies += far0[1]

    rows = hid.shape[0] + 2 * EDGE
    cuts = [0, 512, rows]
    state = [None, None]

    def once(b, copies):
        if b == 0:
            wait(copies)

    def mix(b):
        if b == 0:
            wait(first)
            if split:
                tw[0] = (tw[0].astype(F32) + tw[1].astype(F32)).astype(BF)
        state[b] = dot(hot5[cuts[b] : cuts[b + 1]], tw[0])

    def act(b):
        state[b] = gelu(norm(state[b], gain_out[0:1])).astype(BF)

    def update(b):
        once(b, out_copies)
        lhs = jnp.concatenate([state[b], hot1[cuts[b] : cuts[b + 1]]], axis=1)
        state[b] = dot(lhs, wo[...]).astype(BF)

    def enter(b):
        hidden = state[b]
        lo, hi = max(cuts[b], EDGE), min(cuts[b + 1], rows - EDGE)
        hid[lo - EDGE : hi - EDGE] = hidden[lo - cuts[b] : hi - cuts[b]]
        state[b] = gelu(norm(hidden.astype(F32), gain_in[1:2])).astype(BF)

    def widen(b):
        once(b, in_copies)
        state[b] = dot(state[b], wi[...])

    def leave(b):
        n = cuts[b + 1] - cuts[b]
        pos = span[0] + cuts[b] + lax.broadcasted_iota(jnp.int32, (n, 1), 0)
        valid = jnp.where((pos >= 0) & (pos < span[1]), 1.0, 0.0)
        ci[cuts[b] : cuts[b + 1]] = (gelu(norm(state[b], gain_mid[1:2])) * valid).astype(BF)

    stagger((mix, act, update, enter, widen, leave))


def conv_copies(src, col, width, wt, per_tap, row, n, sem):
    copies = []
    done = 0
    while done < width:
        tap, inner = divmod(col + done, H)
        step = min(H - inner, width - done)
        copies.append(
            pltpu.make_async_copy(
                src.at[:, done : done + step],
                wt.at[pl.ds(pl.multiple_of(tap * per_tap + row, 16), n), inner : inner + step],
                sem,
            )
        )
        done += step
    return copies


HEAD = 256
TAIL = H - HEAD


def windows(ci, lo, hi, first, width):
    first = pl.multiple_of(first, 128)
    return jnp.concatenate(
        [ci[lo + k * DIL1 : hi + k * DIL1, pl.ds(first, width)] for k in range(KERNEL)], axis=1
    )


def head_kernel(ci, w_conv, near_conv, out, wt, sem):
    x, core, _, _ = place()
    n = w_conv.shape[1]
    short = HEAD - n
    done = None
    for xx in range(2):
        for cc in range(2):
            copies = []
            for c, w in ((cc, w_conv), (1 - cc, near_conv)):
                if c == xx:
                    copies += conv_copies(w.at[1], 0, KERNEL * H, wt, HEAD, short * xx, n, sem)
                else:
                    part = w.at[1, (n - short) * xx : (n - short) * xx + short]
                    copies += conv_copies(part, 0, KERNEL * H, wt, HEAD, n * (1 - xx), short, sem)
            done = copies

            @pl.when((x == xx) & (core == cc))
            def _():
                start(copies)

    rows = out.shape[0]
    half = 16 * ((rows + 31) // 32)
    for b, (lo, hi) in enumerate(((0, half), (half, rows))):
        lhs = windows(ci, lo, hi, x * TAIL, HEAD)
        if b == 0:
            wait(done)
        out[lo:hi] = dot(lhs, wt[...])


def last_kernel(split, ci, hid, gain_out, *rest):
    *w, out, wt, wo, sem = rest
    if not split:
        conv_in = conv_copies(w[0], 0, KERNEL * H, wt, H, 0, H, sem.at[0])
        out_in = [pltpu.make_async_copy(w[1], wo, sem.at[1])]
        start(conv_in + out_in)
        first, width = 0, H
    else:
        head, w_conv, w_out, near_conv, near_out = w[:5]
        parts, near_parts = w[5:9], w[9:13]
        x, core, y, z = place()
        n = w_out.shape[1]
        half = n // 2
        left = 2 * n - HEAD
        rest_cols = KERNEL * H - CUT_B
        first, width = (1 - x) * HEAD, TAIL
        out_in = []
        for c, o in ((core, w_out), (1 - core, near_out)):
            row = pl.multiple_of((2 * x + c) * n, 16)
            out_in.append(pltpu.make_async_copy(o.at[1], wo.at[pl.ds(row, n)], sem.at[1]))
        from_row = pl.multiple_of((n - left) * (1 - x), 16)
        own_in, near_in = [
            conv_copies(v.at[1, pl.ds(from_row, left)], 0, KERNEL * H, wt, TAIL, 2 * n * x, left, sem.at[0])
            for v in (w_conv, near_conv)
        ]

        @pl.when(core + x == 1)
        def _():
            start(own_in)

        @pl.when(core + x != 1)
        def _():
            start(near_in)

        def far(head, tail):
            cv, out = [], []
            for c, of in ((core, parts), (1 - core, near_parts)):
                at = c * n + left * (1 - x)
                for p, zz in zip(head, (z, 1 - z)):
                    cv += conv_copies(of[p], 0, CUT_A, wt, TAIL, at + zz * half, half, sem.at[0])
                for p, zz in zip(tail, (z, 1 - z)):
                    skip = CUT_A - CUT_B
                    cv += conv_copies(
                        of[p].at[:, skip:rest_cols], CUT_A, rest_cols - skip, wt, TAIL, at + zz * half, half, sem.at[0]
                    )
                    row = pl.multiple_of((2 * (1 - x) + c) * n + zz * half, 16)
                    out.append(pltpu.make_async_copy(of[p].at[:, rest_cols:], wo.at[pl.ds(row, half)], sem.at[1]))
            return cv, out

        start(out_in)
        far0, far1 = far((0, 2), (1, 3)), far((1, 3), (0, 2))

        @pl.when(y == 0)
        def _():
            start(far0[0] + far0[1])

        @pl.when(y == 1)
        def _():
            start(far1[0] + far1[1])

        conv_in = own_in + far0[0]
        out_in += far0[1]

    rows = out.shape[0]
    cuts = [0, 16 * ((rows + 31) // 32), rows]
    state = [None, None]

    def mix(b):
        lhs = windows(ci, cuts[b], cuts[b + 1], first, width)
        if b == 0:
            wait(conv_in)
        state[b] = dot(lhs, wt[...])
        if split:
            state[b] += head[cuts[b] : cuts[b + 1]]

    def act(b):
        state[b] = gelu(norm(state[b], gain_out[1:2])).astype(BF)

    def update(b):
        if b == 0:
            wait(out_in)
        hidden = hid[cuts[b] : cuts[b + 1]].astype(F32)
        out[cuts[b] : cuts[b + 1]] = (hidden + dot(state[b], wo[...])).astype(BF)

    stagger((mix, act, update))


def after(x, *deps):
    return lax.optimization_barrier((x, *deps))[0]


def per_device(tokens, breaks, lengths, embed_table, break_vec, gain_in, gain_mid, gain_out, w_in, conv_w, w_out):
    rows = tokens.shape[1]
    width = embed_table.shape[1]
    roll_at = lax.axis_index("roll")
    seq_at = lax.axis_index("seq")
    rolls = lax.axis_size("roll")
    seqs = lax.axis_size("seq")
    split = rolls == 4 and seqs % 4 == 0

    def core_swap(x):
        return lax.ppermute(x, "roll", [(i, i ^ 1) for i in range(rolls)])

    def x_swap(x):
        return lax.ppermute(x, "roll", [(i, i ^ 2) for i in range(rolls)])

    def seq_swap(x, bits):
        return lax.ppermute(x, "seq", [(i, i ^ bits) for i in range(seqs)])

    span = jnp.stack([(seq_at * rows).astype(jnp.int32) - EDGE, lengths[0]])
    wide_rows = rows + 2 * EDGE
    codes = tokens[0] + SLOT * breaks[0]

    shard = w_out.shape[1] // 2
    shapes = [((CODES, width), BF), ((CODES, H), F32)]
    if split:
        shapes += [((shard, width), BF), ((shard, CUT_A), BF), ((shard, CUT_A), BF)]
    table, part, *parts = pl.pallas_call(
        functools.partial(first_kernel, split),
        out_shape=[jax.ShapeDtypeStruct(n, t) for n, t in shapes],
        in_specs=[HBM] * 6,
        out_specs=[VMEM] * 2 + [HBM] * (len(shapes) - 2),
        scratch_shapes=[
            pltpu.VMEM(embed_table.shape, F32),
            pltpu.VMEM((width,), F32),
            pltpu.VMEM(gain_in.shape, F32),
            pltpu.VMEM(w_in.shape[1:], BF),
            pltpu.VMEM((CODES, width), F32),
            pltpu.SemaphoreType.DMA((3,)),
        ]
        + [pltpu.VMEM(n, t) for n, t in shapes[2:]],
        cost_estimate=FREE,
        compiler_params=params(60),
    )(embed_table, break_vec, gain_in, w_in, conv_w, w_out)

    if split:
        far_a = x_swap(parts[0])
        near_out, near_in = core_swap(w_out), core_swap(w_in)
        own = part + after(core_swap(part), near_out, near_in)
        other = x_swap(own.astype(BF))
        ends = codes[rows - REACH :], codes[:REACH]
        low = seq_at % 2 == 0
        even = seq_swap(jnp.where(low, *ends), 1)
        pairs = [(i, i + 1) for i in range(1, seqs - 1, 2)]
        pairs.append((seqs - 1, 0))
        odd = lax.ppermute(jnp.where(low, *ends[::-1]), "seq", pairs + [(j, i) for i, j in pairs])
        before, behind = jnp.where(low, odd, even), jnp.where(low, even, odd)
        other = after(other, far_a)
    else:
        own = lax.psum(part, "roll")
        other = jnp.zeros((CODES, H), BF)
        pairs = [(i, i + 1) for i in range(seqs - 1)]
        before = lax.ppermute(codes[rows - REACH :], "seq", pairs)
        behind = lax.ppermute(codes[:REACH], "seq", [(j, i) for i, j in pairs])
    wide = KERNEL * H
    shapes = [(SLOT, F32), (SLOT, BF)] if split else [(CODES, F32)]
    *taps, table = pl.pallas_call(
        functools.partial(table_kernel, split),
        out_shape=[jax.ShapeDtypeStruct((n, wide), t) for n, t in shapes]
        + [jax.ShapeDtypeStruct(table.shape, BF)],
        in_specs=[VMEM, VMEM, VMEM, HBM, HBM],
        out_specs=[VMEM] * (len(shapes) + 1),
        scratch_shapes=[
            pltpu.VMEM(conv_w.shape[1:], BF),
            pltpu.VMEM((CODES, wide), F32),
            pltpu.SemaphoreType.DMA((2,)),
        ],
        cost_estimate=FREE,
        compiler_params=params(12),
    )(own, other, gain_mid, conv_w, table)
    if split:
        relay = after(far_a, taps[1])
        parts_a = [far_a] + [seq_swap(relay, b) for b in (1, 2, 3)]
        sent = (taps[0] + after(core_swap(taps[1]), before, behind).astype(F32)).astype(BF)
        received = x_swap(sent)
        far_b = x_swap(after(parts[1], taps[1]))
    spare = jnp.zeros((-(rows + 2 * REACH) % 128,), jnp.int32)
    near = jnp.concatenate([before, codes, behind, spare])[None]
    if split:
        near = after(near, sent)

    hot5, hot1 = pl.pallas_call(
        hot_kernel,
        out_shape=[jax.ShapeDtypeStruct((wide_rows, n), BF) for n in (KERNEL * CODES, CODES)],
        in_specs=[SMEM, VMEM],
        out_specs=[VMEM] * 2,
        cost_estimate=FREE,
        compiler_params=params(12),
    )(span, near)

    if split:
        received = after(received, hot1, far_b, *parts_a)
        near_received = core_swap(received)
        near_sent = core_swap(after(sent, received))
        near_a = [core_swap(after(p, received)) for p in parts_a]
        relay = after(far_b, received)
        parts_b = [far_b, seq_swap(relay, 1), seq_swap(relay, 2), x_swap(after(parts[2], received))]
        weights_a = [sent, received, near_sent, near_received, w_out, w_in, near_out, near_in, table] + parts_a + near_a
        near_conv = core_swap(after(conv_w, near_received))
    else:
        taps = lax.psum(taps[0], "roll").astype(BF)
        gather = lambda w: lax.all_gather(w, "roll", axis=0, tiled=True)
        weights_a, weights_b = [taps, table, gather(w_out[0]), gather(w_in[1])], [gather(conv_w[1]), gather(w_out[1])]

    ci, hid = pl.pallas_call(
        functools.partial(rows_kernel, split),
        out_shape=(
            jax.ShapeDtypeStruct((wide_rows, H), BF),
            jax.ShapeDtypeStruct((rows, width), BF),
        ),
        in_specs=[SMEM] + [VMEM] * 5 + [ANY] * len(weights_a),
        out_specs=(VMEM, VMEM),
        scratch_shapes=[
            pltpu.VMEM((2, KERNEL * CODES, H), BF),
            pltpu.VMEM((H + CODES, width), BF),
            pltpu.VMEM((width, H), BF),
            pltpu.SemaphoreType.DMA((3,)),
        ],
        cost_estimate=FREE,
        compiler_params=params(30),
    )(span, hot5, hot1, gain_out, gain_in, gain_mid, *weights_a)

    if split:
        near_b = [core_swap(after(p, ci)) for p in parts_b]
        head = pl.pallas_call(
            head_kernel,
            out_shape=jax.ShapeDtypeStruct((rows, H), F32),
            in_specs=[VMEM, HBM, ANY],
            out_specs=VMEM,
            scratch_shapes=[pltpu.VMEM((KERNEL * HEAD, H), BF), pltpu.SemaphoreType.DMA],
            cost_estimate=FREE,
            compiler_params=params(16),
        )(ci, conv_w, near_conv)
        weights_b = [head, conv_w, w_out, near_conv, near_out] + parts_b + near_b
    out = pl.pallas_call(
        functools.partial(last_kernel, split),
        out_shape=jax.ShapeDtypeStruct((rows, width), BF),
        in_specs=[VMEM] * 3
        + [HBM if w is w_out or w is conv_w else VMEM if split and w is head else ANY for w in weights_b],
        out_specs=VMEM,
        scratch_shapes=[
            pltpu.VMEM((KERNEL * (TAIL if split else H), H), BF),
            pltpu.VMEM((H, width), BF),
            pltpu.SemaphoreType.DMA((2,)),
        ],
        cost_estimate=FREE,
        compiler_params=params(24),
    )(ci, hid, gain_out, *weights_b)
    return out[None]


def solution(mesh):
    placed = (
        P("roll", "seq"),
        P("roll", "seq"),
        P("roll"),
        P(),
        P(),
        P(),
        P(),
        P(),
        P(None, "roll", None),
        P(None, "roll", None),
        P(None, "roll", None),
    )
    return jax.shard_map(
        per_device, mesh=mesh, in_specs=placed, out_specs=P("roll", "seq", None), check_vma=False
    )
```

```python
import functools

import jax
import jax.numpy as jnp
from jax import lax
from jax.experimental import pallas as pl
from jax.experimental.pallas import tpu as pltpu
from jax.sharding import PartitionSpec as P

H = 640
KERNEL = 5
VOCAB = 30
SLOT = 32
CODES = 2 * SLOT
BASE_DILATION = 64
DIL0 = BASE_DILATION
DIL1 = 2 * BASE_DILATION
HALF = KERNEL // 2
EDGE = HALF * DIL1
REACH = EDGE + HALF * DIL0
BF = jnp.bfloat16
F32 = jnp.float32
VMEM = pl.BlockSpec(memory_space=pltpu.VMEM)
SMEM = pl.BlockSpec(memory_space=pltpu.SMEM)
ANY = pl.BlockSpec(memory_space=pl.ANY)
HBM = pl.BlockSpec(memory_space=pltpu.HBM)
FREE = pl.CostEstimate(flops=0, bytes_accessed=0, transcendentals=0)
CUT_A = 18 * 128
CUT_B = 17 * 128


def params(mib):
    return pltpu.CompilerParams(vmem_limit_bytes=mib * 1024 * 1024)


def gelu(x):
    return (0.5 * x) * (1.0 + lax.erf(x * 0.5**0.5))


def norm(x, gain):
    center = jnp.mean(x, axis=-1, keepdims=True)
    d = x - center
    spread = jnp.mean(d * d, axis=-1, keepdims=True)
    return d * lax.rsqrt(spread + 1e-5) * gain


def dot(a, b):
    return jnp.dot(a, b, preferred_element_type=F32)


def place():
    roll, seq = lax.axis_index("roll"), lax.axis_index("seq")
    return lax.div(roll, 2), lax.rem(roll, 2), lax.rem(seq, 2), lax.rem(lax.div(seq, 2), 2)


def start(copies):
    for c in copies:
        c.start()


def wait(copies):
    for c in copies:
        c.wait()


def stagger(stages):
    for t in range(len(stages) + 1):
        for b in range(2):
            if 0 <= t - b < len(stages):
                stages[t - b](b)


def pick(rows, columns, first):
    i = lax.broadcasted_iota(jnp.int32, (rows, columns), 0)
    j = lax.broadcasted_iota(jnp.int32, (rows, columns), 1)
    return jnp.where(i == j + first, 1.0, 0.0).astype(BF)


def part_copies(y_is_one, row_bit, w_in, conv_w, w_out, a, b, sem):
    n = b.shape[0]
    r = pl.multiple_of(row_bit * n, 16)
    r2 = pl.multiple_of(row_bit * 2 * n, 16)
    rest = conv_w.shape[2] - CUT_B
    if y_is_one:
        pairs = [
            (conv_w.at[1, pl.ds(r, n), CUT_B:], b.at[:, 0:rest]),
            (w_out.at[1, pl.ds(r, n)], b.at[:, rest:]),
        ]
        if a is not None:
            pairs += [
                (w_in.at[1, pl.ds(r2, n)], a.at[:, 0:H]),
                (w_in.at[1, pl.ds(r2 + n, n)], a.at[:, H : 2 * H]),
            ]
    else:
        pairs = [(conv_w.at[1, pl.ds(r, n), 0:CUT_A], b)]
        if a is not None:
            pairs.append((w_out.at[0, pl.ds(r, n)], a))
    return [pltpu.make_async_copy(s, d, sem) for s, d in pairs]


def first_kernel(split, embed, brk, gain, w_in, conv_w, w_out, table, part, *rest):
    count = 3 if split else 0
    parts, rest = rest[:count], rest[count:]
    emb, bv, g, w, full, sem, *held = rest
    copies = [
        pltpu.make_async_copy(s, d, sem.at[0])
        for s, d in ((embed, emb), (brk, bv), (gain, g), (w_in.at[0], w))
    ]
    start(copies)
    leaving = []
    if split:
        _, _, y, z = place()
        kinds = []
        for kind in range(2):
            kinds.append(
                part_copies(kind == 1, z, w_in, conv_w, w_out, held[0], held[1], sem.at[1])
                + part_copies(kind == 0, 1 - z, w_in, conv_w, w_out, None, held[2], sem.at[1])
            )

            @pl.when(y == kind)
            def _():
                start(kinds[kind])

        leaving = [pltpu.make_async_copy(s, d, sem.at[2]) for s, d in zip(held, parts)]

    wait(copies)
    if split:
        for kind in range(2):

            @pl.when(y == kind)
            def _():
                wait(kinds[kind])

        start(leaving)
    full[...] = jnp.zeros_like(full)
    full[0:VOCAB] = emb[...]
    full[SLOT : SLOT + VOCAB] = emb[...] + bv[...][None, :]
    hidden = full[...].astype(BF)
    table[...] = hidden
    normed = gelu(norm(hidden.astype(F32), g[0:1])).astype(BF)
    rows = w.shape[0]
    mine = dot(normed, pick(normed.shape[1], rows, lax.axis_index("roll") * rows)).astype(BF)
    part[...] = dot(mine, w[...])
    wait(leaving)


def table_kernel(split, own, other, gain, w_all, *rest):
    *outs, w, full, sem = rest
    copy = pltpu.make_async_copy(w_all.at[0], w, sem)
    copy.start()
    wide = own[...] + other[...].astype(F32)
    t = gelu(norm(wide, gain[0:1])).astype(BF)
    rows = w.shape[0]
    mine = dot(t, pick(t.shape[1], rows, lax.axis_index("roll") * rows)).astype(BF)
    copy.wait()
    full[...] = dot(mine, w[...])
    if split:
        core = lax.rem(lax.axis_index("roll"), 2)
        outs[0][...] = full[pl.ds(pl.multiple_of(core * SLOT, SLOT), SLOT)]
        outs[1][...] = full[pl.ds(pl.multiple_of((1 - core) * SLOT, SLOT), SLOT)].astype(BF)
    else:
        outs[0][...] = full[...]


def stage_kernel(table, w_out, w_in, near_out, near_in, chip_out, chip_in, sem):
    _, core, _, _ = place()
    n, m = w_out.shape[1], w_in.shape[1]
    copies = [pltpu.make_async_copy(table, chip_out.at[2 * n :], sem)]
    for c, o, i in ((core, w_out, w_in), (1 - core, near_out, near_in)):
        copies.append(pltpu.make_async_copy(o.at[0], chip_out.at[pl.ds(pl.multiple_of(c * n, 16), n)], sem))
        copies.append(pltpu.make_async_copy(i.at[1], chip_in.at[pl.ds(pl.multiple_of(c * m, 16), m)], sem))
    start(copies)
    wait(copies)


def hot_kernel(span, near, hot5, hot1):
    codes = near[...]
    count = codes.shape[1]
    rows = hot5.shape[0]
    pos = span[0] - HALF * DIL0 + lax.broadcasted_iota(jnp.int32, codes.shape, 1)
    masked = jnp.where((pos >= 0) & (pos < span[1]), codes, -1)
    lanes = lax.broadcasted_iota(jnp.int32, (CODES, count), 0)
    taps = jnp.where(lanes == masked, 1.0, 0.0).T.astype(BF)
    for k in range(KERNEL):
        hot5[:, k * CODES : (k + 1) * CODES] = taps[k * DIL0 : k * DIL0 + rows]
    center = jnp.where(lanes == codes, 1.0, 0.0).T.astype(BF)
    hot1[...] = center[HALF * DIL0 : HALF * DIL0 + rows]


def rows_kernel(split, span, hot5, hot1, gain_out, gain_in, gain_mid, *rest):
    *w, ci, hid, tw, wo, wi, sem = rest
    depth = wo.shape[0] - CODES
    if split:
        core = lax.rem(lax.axis_index("roll"), 2)
        taps = [(t, core * SLOT, SLOT, 0) for t in w[:2]] + [(t, (1 - core) * SLOT, SLOT, 0) for t in w[2:4]]
        taps = [(t, at, n, i % 2) for i, (t, at, n, _) in enumerate(taps)]
        w = w[4:]
    else:
        taps = [(w[0], 0, CODES, 0)]
        table, *w = w[1:]
    first = [
        pltpu.make_async_copy(
            t.at[:, k * H : (k + 1) * H], tw.at[i, pl.ds(pl.multiple_of(k * CODES + at, 16), n)], sem.at[0]
        )
        for t, at, n, i in taps
        for k in range(KERNEL)
    ]
    start(first)
    if not split:
        first.append(pltpu.make_async_copy(table, wo.at[depth:], sem.at[0]))
        first[-1].start()
        out_copies = [pltpu.make_async_copy(w[0], wo.at[0:depth], sem.at[1])]
        in_copies = [pltpu.make_async_copy(w[1], wi, sem.at[2])]
        start(out_copies + in_copies)
    else:
        chip_out, chip_in = w[:2]
        parts, near_parts = w[2:6], w[6:10]
        x, core, y, z = place()
        n = depth // 4
        m = 2 * n
        half = n // 2
        row = pl.multiple_of(x * 2 * n, 16)
        out_copies = [
            pltpu.make_async_copy(chip_out.at[0 : 2 * n], wo.at[pl.ds(row, 2 * n)], sem.at[1]),
            pltpu.make_async_copy(chip_out.at[2 * n :], wo.at[depth:], sem.at[1]),
        ]
        row = pl.multiple_of(x * 2 * m, 16)
        in_copies = [pltpu.make_async_copy(chip_in, wi.at[pl.ds(row, 2 * m)], sem.at[2])]

        def far(outs, ins):
            out, into = [], []
            for c, of in ((core, parts), (1 - core, near_parts)):
                at = 2 * (1 - x) + c
                for p, zz in zip(outs, (z, 1 - z)):
                    row = pl.multiple_of(at * n + zz * half, 16)
                    out.append(pltpu.make_async_copy(of[p], wo.at[pl.ds(row, half)], sem.at[1]))
                for p, zz in zip(ins, (z, 1 - z)):
                    for j in range(2):
                        row = pl.multiple_of(at * m + zz * n + j * half, 16)
                        into.append(
                            pltpu.make_async_copy(of[p].at[:, j * H : (j + 1) * H], wi.at[pl.ds(row, half)], sem.at[2])
                        )
            return out, into

        start(out_copies + in_copies)
        far0, far1 = far((0, 2), (1, 3)), far((1, 3), (0, 2))

        @pl.when(y == 0)
        def _():
            start(far0[0] + far0[1])

        @pl.when(y == 1)
        def _():
            start(far1[0] + far1[1])

        out_copies += far0[0]
        in_copies += far0[1]

    rows = hid.shape[0] + 2 * EDGE
    cuts = [0, 512, rows]
    state = [None, None]

    def once(b, copies):
        if b == 0:
            wait(copies)

    def mix(b):
        if b == 0:
            wait(first)
            if split:
                tw[0] = (tw[0].astype(F32) + tw[1].astype(F32)).astype(BF)
        state[b] = dot(hot5[cuts[b] : cuts[b + 1]], tw[0])

    def act(b):
        state[b] = gelu(norm(state[b], gain_out[0:1])).astype(BF)

    def update(b):
        once(b, out_copies)
        lhs = jnp.concatenate([state[b], hot1[cuts[b] : cuts[b + 1]]], axis=1)
        state[b] = dot(lhs, wo[...]).astype(BF)

    def enter(b):
        hidden = state[b]
        lo, hi = max(cuts[b], EDGE), min(cuts[b + 1], rows - EDGE)
        hid[lo - EDGE : hi - EDGE] = hidden[lo - cuts[b] : hi - cuts[b]]
        state[b] = gelu(norm(hidden.astype(F32), gain_in[1:2])).astype(BF)

    def widen(b):
        once(b, in_copies)
        state[b] = dot(state[b], wi[...])

    def leave(b):
        n = cuts[b + 1] - cuts[b]
        pos = span[0] + cuts[b] + lax.broadcasted_iota(jnp.int32, (n, 1), 0)
        valid = jnp.where((pos >= 0) & (pos < span[1]), 1.0, 0.0)
        ci[cuts[b] : cuts[b + 1]] = (gelu(norm(state[b], gain_mid[1:2])) * valid).astype(BF)

    stagger((mix, act, update, enter, widen, leave))


def conv_copies(src, col, width, wt, per_tap, row, n, sem):
    copies = []
    done = 0
    while done < width:
        tap, inner = divmod(col + done, H)
        step = min(H - inner, width - done)
        copies.append(
            pltpu.make_async_copy(
                src.at[:, done : done + step],
                wt.at[pl.ds(pl.multiple_of(tap * per_tap + row, 16), n), inner : inner + step],
                sem,
            )
        )
        done += step
    return copies


HEAD = 256
TAIL = H - HEAD


def windows(ci, lo, hi, first, width):
    first = pl.multiple_of(first, 128)
    return jnp.concatenate(
        [ci[lo + k * DIL1 : hi + k * DIL1, pl.ds(first, width)] for k in range(KERNEL)], axis=1
    )


def head_kernel(ci, w_conv, near_conv, out, wt, sem):
    x, core, _, _ = place()
    n = w_conv.shape[1]
    short = HEAD - n
    done = None
    for xx in range(2):
        for cc in range(2):
            copies = []
            for c, w in ((cc, w_conv), (1 - cc, near_conv)):
                if c == xx:
                    copies += conv_copies(w.at[1], 0, KERNEL * H, wt, HEAD, short * xx, n, sem)
                else:
                    part = w.at[1, (n - short) * xx : (n - short) * xx + short]
                    copies += conv_copies(part, 0, KERNEL * H, wt, HEAD, n * (1 - xx), short, sem)
            done = copies

            @pl.when((x == xx) & (core == cc))
            def _():
                start(copies)

    rows = out.shape[0]
    half = 16 * ((rows + 31) // 32)
    for b, (lo, hi) in enumerate(((0, half), (half, rows))):
        lhs = windows(ci, lo, hi, x * TAIL, HEAD)
        if b == 0:
            wait(done)
        out[lo:hi] = dot(lhs, wt[...])


def last_kernel(split, ci, hid, gain_out, *rest):
    *w, out, wt, wo, sem = rest
    if not split:
        conv_in = conv_copies(w[0], 0, KERNEL * H, wt, H, 0, H, sem.at[0])
        out_in = [pltpu.make_async_copy(w[1], wo, sem.at[1])]
        start(conv_in + out_in)
        first, width = 0, H
    else:
        head, w_conv, w_out, near_conv, near_out = w[:5]
        parts, near_parts = w[5:9], w[9:13]
        x, core, y, z = place()
        n = w_out.shape[1]
        half = n // 2
        left = 2 * n - HEAD
        rest_cols = KERNEL * H - CUT_B
        first, width = (1 - x) * HEAD, TAIL
        out_in = []
        for c, o in ((core, w_out), (1 - core, near_out)):
            row = pl.multiple_of((2 * x + c) * n, 16)
            out_in.append(pltpu.make_async_copy(o.at[1], wo.at[pl.ds(row, n)], sem.at[1]))
        from_row = pl.multiple_of((n - left) * (1 - x), 16)
        own_in, near_in = [
            conv_copies(v.at[1, pl.ds(from_row, left)], 0, KERNEL * H, wt, TAIL, 2 * n * x, left, sem.at[0])
            for v in (w_conv, near_conv)
        ]

        @pl.when(core + x == 1)
        def _():
            start(own_in)

        @pl.when(core + x != 1)
        def _():
            start(near_in)

        def far(head, tail):
            cv, out = [], []
            for c, of in ((core, parts), (1 - core, near_parts)):
                at = c * n + left * (1 - x)
                for p, zz in zip(head, (z, 1 - z)):
                    cv += conv_copies(of[p], 0, CUT_A, wt, TAIL, at + zz * half, half, sem.at[0])
                for p, zz in zip(tail, (z, 1 - z)):
                    skip = CUT_A - CUT_B
                    cv += conv_copies(
                        of[p].at[:, skip:rest_cols], CUT_A, rest_cols - skip, wt, TAIL, at + zz * half, half, sem.at[0]
                    )
                    row = pl.multiple_of((2 * (1 - x) + c) * n + zz * half, 16)
                    out.append(pltpu.make_async_copy(of[p].at[:, rest_cols:], wo.at[pl.ds(row, half)], sem.at[1]))
            return cv, out

        start(out_in)
        far0, far1 = far((0, 2), (1, 3)), far((1, 3), (0, 2))

        @pl.when(y == 0)
        def _():
            start(far0[0] + far0[1])

        @pl.when(y == 1)
        def _():
            start(far1[0] + far1[1])

        conv_in = own_in + far0[0]
        out_in += far0[1]

    rows = out.shape[0]
    cuts = [0, 16 * ((rows + 31) // 32), rows]
    state = [None, None]

    def mix(b):
        lhs = windows(ci, cuts[b], cuts[b + 1], first, width)
        if b == 0:
            wait(conv_in)
        state[b] = dot(lhs, wt[...])
        if split:
            state[b] += head[cuts[b] : cuts[b + 1]]

    def act(b):
        state[b] = gelu(norm(state[b], gain_out[1:2])).astype(BF)

    def update(b):
        if b == 0:
            wait(out_in)
        hidden = hid[cuts[b] : cuts[b + 1]].astype(F32)
        out[cuts[b] : cuts[b + 1]] = (hidden + dot(state[b], wo[...])).astype(BF)

    stagger((mix, act, update))


def after(x, *deps):
    return lax.optimization_barrier((x, *deps))[0]


def per_device(tokens, breaks, lengths, embed_table, break_vec, gain_in, gain_mid, gain_out, w_in, conv_w, w_out):
    rows = tokens.shape[1]
    width = embed_table.shape[1]
    roll_at = lax.axis_index("roll")
    seq_at = lax.axis_index("seq")
    rolls = lax.axis_size("roll")
    seqs = lax.axis_size("seq")
    split = rolls == 4 and seqs % 4 == 0

    def core_swap(x):
        return lax.ppermute(x, "roll", [(i, i ^ 1) for i in range(rolls)])

    def x_swap(x):
        return lax.ppermute(x, "roll", [(i, i ^ 2) for i in range(rolls)])

    def seq_swap(x, bits):
        return lax.ppermute(x, "seq", [(i, i ^ bits) for i in range(seqs)])

    span = jnp.stack([(seq_at * rows).astype(jnp.int32) - EDGE, lengths[0]])
    wide_rows = rows + 2 * EDGE
    codes = tokens[0] + SLOT * breaks[0]

    shard = w_out.shape[1] // 2
    shapes = [((CODES, width), BF), ((CODES, H), F32)]
    if split:
        shapes += [((shard, width), BF), ((shard, CUT_A), BF), ((shard, CUT_A), BF)]
    table, part, *parts = pl.pallas_call(
        functools.partial(first_kernel, split),
        out_shape=[jax.ShapeDtypeStruct(n, t) for n, t in shapes],
        in_specs=[HBM] * 6,
        out_specs=[VMEM] * 2 + [HBM] * (len(shapes) - 2),
        scratch_shapes=[
            pltpu.VMEM(embed_table.shape, F32),
            pltpu.VMEM((width,), F32),
            pltpu.VMEM(gain_in.shape, F32),
            pltpu.VMEM(w_in.shape[1:], BF),
            pltpu.VMEM((CODES, width), F32),
            pltpu.SemaphoreType.DMA((3,)),
        ]
        + [pltpu.VMEM(n, t) for n, t in shapes[2:]],
        cost_estimate=FREE,
        compiler_params=params(60),
    )(embed_table, break_vec, gain_in, w_in, conv_w, w_out)

    if split:
        far_a = x_swap(parts[0])
        own = part + core_swap(part)
        other = x_swap(own.astype(BF))
        ends = codes[rows - REACH :], codes[:REACH]
        low = seq_at % 2 == 0
        even = seq_swap(jnp.where(low, *ends), 1)
        pairs = [(i, i + 1) for i in range(1, seqs - 1, 2)]
        pairs.append((seqs - 1, 0))
        odd = lax.ppermute(jnp.where(low, *ends[::-1]), "seq", pairs + [(j, i) for i, j in pairs])
        before, behind = jnp.where(low, odd, even), jnp.where(low, even, odd)
        far_b = x_swap(after(parts[1], other))
        other = after(other, far_a)
    else:
        own = lax.psum(part, "roll")
        other = jnp.zeros((CODES, H), BF)
        pairs = [(i, i + 1) for i in range(seqs - 1)]
        before = lax.ppermute(codes[rows - REACH :], "seq", pairs)
        behind = lax.ppermute(codes[:REACH], "seq", [(j, i) for i, j in pairs])
    wide = KERNEL * H
    shapes = [(SLOT, F32), (SLOT, BF)] if split else [(CODES, F32)]
    taps = pl.pallas_call(
        functools.partial(table_kernel, split),
        out_shape=[jax.ShapeDtypeStruct((n, wide), t) for n, t in shapes],
        in_specs=[VMEM, VMEM, VMEM, HBM],
        out_specs=[VMEM] * len(shapes),
        scratch_shapes=[
            pltpu.VMEM(conv_w.shape[1:], BF),
            pltpu.VMEM((CODES, wide), F32),
            pltpu.SemaphoreType.DMA,
        ],
        cost_estimate=FREE,
        compiler_params=params(12),
    )(own, other, gain_mid, conv_w)
    if split:
        relay = after(far_a, taps[1])
        parts_a = [far_a] + [seq_swap(relay, b) for b in (1, 2, 3)]
        sent = (taps[0] + after(core_swap(taps[1]), before, behind, far_b).astype(F32)).astype(BF)
        received = x_swap(sent)
        near_sent = core_swap(sent)
        near_out, near_in = core_swap(after(w_out, sent)), core_swap(after(w_in, sent))
        chip = pl.pallas_call(
            stage_kernel,
            out_shape=[jax.ShapeDtypeStruct(n, BF) for n in ((4 * shard + CODES, width), (8 * shard, H))],
            in_specs=[ANY] * 5,
            out_specs=[VMEM] * 2,
            scratch_shapes=[pltpu.SemaphoreType.DMA],
            cost_estimate=FREE,
            compiler_params=params(16),
        )(after(table, sent), w_out, w_in, near_out, near_in)
    spare = jnp.zeros((-(rows + 2 * REACH) % 128,), jnp.int32)
    near = jnp.concatenate([before, codes, behind, spare])[None]
    if split:
        near = after(near, sent, chip[0])

    hot5, hot1 = pl.pallas_call(
        hot_kernel,
        out_shape=[jax.ShapeDtypeStruct((wide_rows, n), BF) for n in (KERNEL * CODES, CODES)],
        in_specs=[SMEM, VMEM],
        out_specs=[VMEM] * 2,
        cost_estimate=FREE,
        compiler_params=params(12),
    )(span, near)

    if split:
        received = after(received, hot1, near_sent)
        near_received = core_swap(received)
        near_a = [core_swap(after(p, hot1)) for p in parts_a]
        relay = after(far_b, received)
        parts_b = [far_b, seq_swap(relay, 1), seq_swap(relay, 2), x_swap(after(parts[2], received))]
        weights_a = [sent, received, near_sent, near_received] + list(chip) + parts_a + near_a
        near_conv = core_swap(after(conv_w, near_received, *near_a))
    else:
        taps = lax.psum(taps[0], "roll").astype(BF)
        gather = lambda w: lax.all_gather(w, "roll", axis=0, tiled=True)
        weights_a, weights_b = [taps, table, gather(w_out[0]), gather(w_in[1])], [gather(conv_w[1]), gather(w_out[1])]

    ci, hid = pl.pallas_call(
        functools.partial(rows_kernel, split),
        out_shape=(
            jax.ShapeDtypeStruct((wide_rows, H), BF),
            jax.ShapeDtypeStruct((rows, width), BF),
        ),
        in_specs=[SMEM] + [VMEM] * 5 + [ANY] * len(weights_a),
        out_specs=(VMEM, VMEM),
        scratch_shapes=[
            pltpu.VMEM((2, KERNEL * CODES, H), BF),
            pltpu.VMEM((H + CODES, width), BF),
            pltpu.VMEM((width, H), BF),
            pltpu.SemaphoreType.DMA((3,)),
        ],
        cost_estimate=FREE,
        compiler_params=params(30),
    )(span, hot5, hot1, gain_out, gain_in, gain_mid, *weights_a)

    if split:
        near_b = [core_swap(after(p, ci)) for p in parts_b]
        head = pl.pallas_call(
            head_kernel,
            out_shape=jax.ShapeDtypeStruct((rows, H), F32),
            in_specs=[VMEM, HBM, ANY],
            out_specs=VMEM,
            scratch_shapes=[pltpu.VMEM((KERNEL * HEAD, H), BF), pltpu.SemaphoreType.DMA],
            cost_estimate=FREE,
            compiler_params=params(16),
        )(ci, conv_w, near_conv)
        weights_b = [head, conv_w, w_out, near_conv, near_out] + parts_b + near_b
    out = pl.pallas_call(
        functools.partial(last_kernel, split),
        out_shape=jax.ShapeDtypeStruct((rows, width), BF),
        in_specs=[VMEM] * 3
        + [HBM if w is w_out or w is conv_w else VMEM if split and w is head else ANY for w in weights_b],
        out_specs=VMEM,
        scratch_shapes=[
            pltpu.VMEM((KERNEL * (TAIL if split else H), H), BF),
            pltpu.VMEM((H, width), BF),
            pltpu.SemaphoreType.DMA((2,)),
        ],
        cost_estimate=FREE,
        compiler_params=params(24),
    )(ci, hid, gain_out, *weights_b)
    return out[None]


def solution(mesh):
    placed = (
        P("roll", "seq"),
        P("roll", "seq"),
        P("roll"),
        P(),
        P(),
        P(),
        P(),
        P(),
        P(None, "roll", None),
        P(None, "roll", None),
        P(None, "roll", None),
    )
    return jax.shard_map(
        per_device, mesh=mesh, in_specs=placed, out_specs=P("roll", "seq", None), check_vma=False
    )
```

```python
import functools

import jax
import jax.numpy as jnp
from jax import lax
from jax.experimental import pallas as pl
from jax.experimental.pallas import tpu as pltpu
from jax.sharding import PartitionSpec as P

H = 640
KERNEL = 5
VOCAB = 30
SLOT = 32
CODES = 2 * SLOT
BASE_DILATION = 64
DIL0 = BASE_DILATION
DIL1 = 2 * BASE_DILATION
HALF = KERNEL // 2
EDGE = HALF * DIL1
REACH = EDGE + HALF * DIL0
BF = jnp.bfloat16
F32 = jnp.float32
VMEM = pl.BlockSpec(memory_space=pltpu.VMEM)
SMEM = pl.BlockSpec(memory_space=pltpu.SMEM)
ANY = pl.BlockSpec(memory_space=pl.ANY)
HBM = pl.BlockSpec(memory_space=pltpu.HBM)
FREE = pl.CostEstimate(flops=0, bytes_accessed=0, transcendentals=0)
CUT_A = 18 * 128
CUT_B = 17 * 128


def params(mib):
    return pltpu.CompilerParams(vmem_limit_bytes=mib * 1024 * 1024)


def gelu(x):
    return (0.5 * x) * (1.0 + lax.erf(x * 0.5**0.5))


def norm(x, gain):
    center = jnp.mean(x, axis=-1, keepdims=True)
    d = x - center
    spread = jnp.mean(d * d, axis=-1, keepdims=True)
    return d * lax.rsqrt(spread + 1e-5) * gain


def dot(a, b):
    return jnp.dot(a, b, preferred_element_type=F32)


def place():
    roll, seq = lax.axis_index("roll"), lax.axis_index("seq")
    return lax.div(roll, 2), lax.rem(roll, 2), lax.rem(seq, 2), lax.rem(lax.div(seq, 2), 2)


def start(copies):
    for c in copies:
        c.start()


def wait(copies):
    for c in copies:
        c.wait()


def stagger(stages):
    for t in range(len(stages) + 1):
        for b in range(2):
            if 0 <= t - b < len(stages):
                stages[t - b](b)


def pick(rows, columns, first):
    i = lax.broadcasted_iota(jnp.int32, (rows, columns), 0)
    j = lax.broadcasted_iota(jnp.int32, (rows, columns), 1)
    return jnp.where(i == j + first, 1.0, 0.0).astype(BF)


def part_copies(y_is_one, row_bit, w_in, conv_w, w_out, a, b, sem):
    n = b.shape[0]
    r = pl.multiple_of(row_bit * n, 16)
    r2 = pl.multiple_of(row_bit * 2 * n, 16)
    rest = conv_w.shape[2] - CUT_B
    if y_is_one:
        pairs = [
            (conv_w.at[1, pl.ds(r, n), CUT_B:], b.at[:, 0:rest]),
            (w_out.at[1, pl.ds(r, n)], b.at[:, rest:]),
        ]
        if a is not None:
            pairs += [
                (w_in.at[1, pl.ds(r2, n)], a.at[:, 0:H]),
                (w_in.at[1, pl.ds(r2 + n, n)], a.at[:, H : 2 * H]),
            ]
    else:
        pairs = [(conv_w.at[1, pl.ds(r, n), 0:CUT_A], b)]
        if a is not None:
            pairs.append((w_out.at[0, pl.ds(r, n)], a))
    return [pltpu.make_async_copy(s, d, sem) for s, d in pairs]


def first_kernel(split, embed, brk, gain, w_in, conv_w, w_out, table, part, *rest):
    count = 3 if split else 0
    parts, rest = rest[:count], rest[count:]
    emb, bv, g, w, full, sem, *held = rest
    copies = [
        pltpu.make_async_copy(s, d, sem.at[0])
        for s, d in ((embed, emb), (brk, bv), (gain, g), (w_in.at[0], w))
    ]
    start(copies)
    leaving = []
    if split:
        _, _, y, z = place()
        kinds = []
        for kind in range(2):
            kinds.append(
                part_copies(kind == 1, z, w_in, conv_w, w_out, held[0], held[1], sem.at[1])
                + part_copies(kind == 0, 1 - z, w_in, conv_w, w_out, None, held[2], sem.at[1])
            )

            @pl.when(y == kind)
            def _():
                start(kinds[kind])

        leaving = [pltpu.make_async_copy(s, d, sem.at[2]) for s, d in zip(held, parts)]

    wait(copies)
    if split:
        for kind in range(2):

            @pl.when(y == kind)
            def _():
                wait(kinds[kind])

        start(leaving)
    full[...] = jnp.zeros_like(full)
    full[0:VOCAB] = emb[...]
    full[SLOT : SLOT + VOCAB] = emb[...] + bv[...][None, :]
    hidden = full[...].astype(BF)
    table[...] = hidden
    normed = gelu(norm(hidden.astype(F32), g[0:1])).astype(BF)
    rows = w.shape[0]
    mine = dot(normed, pick(normed.shape[1], rows, lax.axis_index("roll") * rows)).astype(BF)
    part[...] = dot(mine, w[...])
    wait(leaving)


def table_kernel(split, own, other, gain, w_all, *rest):
    *outs, w, full, sem = rest
    copy = pltpu.make_async_copy(w_all.at[0], w, sem)
    copy.start()
    wide = own[...] + other[...].astype(F32)
    t = gelu(norm(wide, gain[0:1])).astype(BF)
    rows = w.shape[0]
    mine = dot(t, pick(t.shape[1], rows, lax.axis_index("roll") * rows)).astype(BF)
    copy.wait()
    full[...] = dot(mine, w[...])
    if split:
        core = lax.rem(lax.axis_index("roll"), 2)
        outs[0][...] = full[pl.ds(pl.multiple_of(core * SLOT, SLOT), SLOT)]
        outs[1][...] = full[pl.ds(pl.multiple_of((1 - core) * SLOT, SLOT), SLOT)].astype(BF)
    else:
        outs[0][...] = full[...]


def chip_copies(table, w_out, w_in, near_out, near_in, chip_out, chip_in, sem):
    _, core, _, _ = place()
    n, m = w_out.shape[1], w_in.shape[1]
    copies = [pltpu.make_async_copy(table, chip_out.at[2 * n :], sem)]
    for c, o, i in ((core, w_out, w_in), (1 - core, near_out, near_in)):
        copies.append(pltpu.make_async_copy(o.at[0], chip_out.at[pl.ds(pl.multiple_of(c * n, 16), n)], sem))
        copies.append(pltpu.make_async_copy(i.at[1], chip_in.at[pl.ds(pl.multiple_of(c * m, 16), m)], sem))
    return copies


def hot_kernel(split, span, near, *rest):
    copies = []
    if split:
        *w, hot5, hot1, chip_out, chip_in, sem = rest
        copies = chip_copies(*w, chip_out, chip_in, sem)
    else:
        hot5, hot1 = rest
    start(copies)
    codes = near[...]
    count = codes.shape[1]
    rows = hot5.shape[0]
    pos = span[0] - HALF * DIL0 + lax.broadcasted_iota(jnp.int32, codes.shape, 1)
    masked = jnp.where((pos >= 0) & (pos < span[1]), codes, -1)
    lanes = lax.broadcasted_iota(jnp.int32, (CODES, count), 0)
    taps = jnp.where(lanes == masked, 1.0, 0.0).T.astype(BF)
    for k in range(KERNEL):
        hot5[:, k * CODES : (k + 1) * CODES] = taps[k * DIL0 : k * DIL0 + rows]
    center = jnp.where(lanes == codes, 1.0, 0.0).T.astype(BF)
    hot1[...] = center[HALF * DIL0 : HALF * DIL0 + rows]
    wait(copies)


def rows_kernel(split, span, hot5, hot1, gain_out, gain_in, gain_mid, *rest):
    *w, ci, hid, tw, wo, wi, sem = rest
    depth = wo.shape[0] - CODES
    if split:
        core = lax.rem(lax.axis_index("roll"), 2)
        taps = [(t, core * SLOT, SLOT, 0) for t in w[:2]] + [(t, (1 - core) * SLOT, SLOT, 0) for t in w[2:4]]
        taps = [(t, at, n, i % 2) for i, (t, at, n, _) in enumerate(taps)]
        w = w[4:]
    else:
        taps = [(w[0], 0, CODES, 0)]
        table, *w = w[1:]
    first = [
        pltpu.make_async_copy(
            t.at[:, k * H : (k + 1) * H], tw.at[i, pl.ds(pl.multiple_of(k * CODES + at, 16), n)], sem.at[0]
        )
        for t, at, n, i in taps
        for k in range(KERNEL)
    ]
    start(first)
    if not split:
        first.append(pltpu.make_async_copy(table, wo.at[depth:], sem.at[0]))
        first[-1].start()
        out_copies = [pltpu.make_async_copy(w[0], wo.at[0:depth], sem.at[1])]
        in_copies = [pltpu.make_async_copy(w[1], wi, sem.at[2])]
        start(out_copies + in_copies)
    else:
        chip_out, chip_in = w[:2]
        parts, near_parts = w[2:6], w[6:10]
        x, core, y, z = place()
        n = depth // 4
        m = 2 * n
        half = n // 2
        row = pl.multiple_of(x * 2 * n, 16)
        out_copies = [
            pltpu.make_async_copy(chip_out.at[0 : 2 * n], wo.at[pl.ds(row, 2 * n)], sem.at[1]),
            pltpu.make_async_copy(chip_out.at[2 * n :], wo.at[depth:], sem.at[1]),
        ]
        row = pl.multiple_of(x * 2 * m, 16)
        in_copies = [pltpu.make_async_copy(chip_in, wi.at[pl.ds(row, 2 * m)], sem.at[2])]

        def far(outs, ins):
            out, into = [], []
            for c, of in ((core, parts), (1 - core, near_parts)):
                at = 2 * (1 - x) + c
                for p, zz in zip(outs, (z, 1 - z)):
                    row = pl.multiple_of(at * n + zz * half, 16)
                    out.append(pltpu.make_async_copy(of[p], wo.at[pl.ds(row, half)], sem.at[1]))
                for p, zz in zip(ins, (z, 1 - z)):
                    for j in range(2):
                        row = pl.multiple_of(at * m + zz * n + j * half, 16)
                        into.append(
                            pltpu.make_async_copy(of[p].at[:, j * H : (j + 1) * H], wi.at[pl.ds(row, half)], sem.at[2])
                        )
            return out, into

        start(out_copies + in_copies)
        far0, far1 = far((0, 2), (1, 3)), far((1, 3), (0, 2))

        @pl.when(y == 0)
        def _():
            start(far0[0] + far0[1])

        @pl.when(y == 1)
        def _():
            start(far1[0] + far1[1])

        out_copies += far0[0]
        in_copies += far0[1]

    rows = hid.shape[0] + 2 * EDGE
    cuts = [0, 512, rows]
    state = [None, None]

    def once(b, copies):
        if b == 0:
            wait(copies)

    def mix(b):
        if b == 0:
            wait(first)
            if split:
                tw[0] = (tw[0].astype(F32) + tw[1].astype(F32)).astype(BF)
        state[b] = dot(hot5[cuts[b] : cuts[b + 1]], tw[0])

    def act(b):
        state[b] = gelu(norm(state[b], gain_out[0:1])).astype(BF)

    def update(b):
        once(b, out_copies)
        lhs = jnp.concatenate([state[b], hot1[cuts[b] : cuts[b + 1]]], axis=1)
        state[b] = dot(lhs, wo[...]).astype(BF)

    def enter(b):
        hidden = state[b]
        lo, hi = max(cuts[b], EDGE), min(cuts[b + 1], rows - EDGE)
        hid[lo - EDGE : hi - EDGE] = hidden[lo - cuts[b] : hi - cuts[b]]
        state[b] = gelu(norm(hidden.astype(F32), gain_in[1:2])).astype(BF)

    def widen(b):
        once(b, in_copies)
        state[b] = dot(state[b], wi[...])

    def leave(b):
        n = cuts[b + 1] - cuts[b]
        pos = span[0] + cuts[b] + lax.broadcasted_iota(jnp.int32, (n, 1), 0)
        valid = jnp.where((pos >= 0) & (pos < span[1]), 1.0, 0.0)
        ci[cuts[b] : cuts[b + 1]] = (gelu(norm(state[b], gain_mid[1:2])) * valid).astype(BF)

    stagger((mix, act, update, enter, widen, leave))


def conv_copies(src, col, width, wt, per_tap, row, n, sem):
    copies = []
    done = 0
    while done < width:
        tap, inner = divmod(col + done, H)
        step = min(H - inner, width - done)
        copies.append(
            pltpu.make_async_copy(
                src.at[:, done : done + step],
                wt.at[pl.ds(pl.multiple_of(tap * per_tap + row, 16), n), inner : inner + step],
                sem,
            )
        )
        done += step
    return copies


HEAD = 256
TAIL = H - HEAD


def windows(ci, lo, hi, first, width):
    first = pl.multiple_of(first, 128)
    return jnp.concatenate(
        [ci[lo + k * DIL1 : hi + k * DIL1, pl.ds(first, width)] for k in range(KERNEL)], axis=1
    )


def head_kernel(ci, w_conv, near_conv, out, wt, sem):
    x, core, _, _ = place()
    n = w_conv.shape[1]
    short = HEAD - n
    done = None
    for xx in range(2):
        for cc in range(2):
            copies = []
            for c, w in ((cc, w_conv), (1 - cc, near_conv)):
                if c == xx:
                    copies += conv_copies(w.at[1], 0, KERNEL * H, wt, HEAD, short * xx, n, sem)
                else:
                    part = w.at[1, (n - short) * xx : (n - short) * xx + short]
                    copies += conv_copies(part, 0, KERNEL * H, wt, HEAD, n * (1 - xx), short, sem)
            done = copies

            @pl.when((x == xx) & (core == cc))
            def _():
                start(copies)

    rows = out.shape[0]
    half = 16 * ((rows + 31) // 32)
    for b, (lo, hi) in enumerate(((0, half), (half, rows))):
        lhs = windows(ci, lo, hi, x * TAIL, HEAD)
        if b == 0:
            wait(done)
        out[lo:hi] = dot(lhs, wt[...])


def last_kernel(split, ci, hid, gain_out, *rest):
    *w, out, wt, wo, sem = rest
    if not split:
        conv_in = conv_copies(w[0], 0, KERNEL * H, wt, H, 0, H, sem.at[0])
        out_in = [pltpu.make_async_copy(w[1], wo, sem.at[1])]
        start(conv_in + out_in)
        first, width = 0, H
    else:
        head, w_conv, w_out, near_conv, near_out = w[:5]
        parts, near_parts = w[5:9], w[9:13]
        x, core, y, z = place()
        n = w_out.shape[1]
        half = n // 2
        left = 2 * n - HEAD
        rest_cols = KERNEL * H - CUT_B
        first, width = (1 - x) * HEAD, TAIL
        out_in = []
        for c, o in ((core, w_out), (1 - core, near_out)):
            row = pl.multiple_of((2 * x + c) * n, 16)
            out_in.append(pltpu.make_async_copy(o.at[1], wo.at[pl.ds(row, n)], sem.at[1]))
        from_row = pl.multiple_of((n - left) * (1 - x), 16)
        own_in, near_in = [
            conv_copies(v.at[1, pl.ds(from_row, left)], 0, KERNEL * H, wt, TAIL, 2 * n * x, left, sem.at[0])
            for v in (w_conv, near_conv)
        ]

        @pl.when(core + x == 1)
        def _():
            start(own_in)

        @pl.when(core + x != 1)
        def _():
            start(near_in)

        def far(head, tail):
            cv, out = [], []
            for c, of in ((core, parts), (1 - core, near_parts)):
                at = c * n + left * (1 - x)
                for p, zz in zip(head, (z, 1 - z)):
                    cv += conv_copies(of[p], 0, CUT_A, wt, TAIL, at + zz * half, half, sem.at[0])
                for p, zz in zip(tail, (z, 1 - z)):
                    skip = CUT_A - CUT_B
                    cv += conv_copies(
                        of[p].at[:, skip:rest_cols], CUT_A, rest_cols - skip, wt, TAIL, at + zz * half, half, sem.at[0]
                    )
                    row = pl.multiple_of((2 * (1 - x) + c) * n + zz * half, 16)
                    out.append(pltpu.make_async_copy(of[p].at[:, rest_cols:], wo.at[pl.ds(row, half)], sem.at[1]))
            return cv, out

        start(out_in)
        far0, far1 = far((0, 2), (1, 3)), far((1, 3), (0, 2))

        @pl.when(y == 0)
        def _():
            start(far0[0] + far0[1])

        @pl.when(y == 1)
        def _():
            start(far1[0] + far1[1])

        conv_in = own_in + far0[0]
        out_in += far0[1]

    rows = out.shape[0]
    cuts = [0, 16 * ((rows + 31) // 32), rows]
    state = [None, None]

    def mix(b):
        lhs = windows(ci, cuts[b], cuts[b + 1], first, width)
        if b == 0:
            wait(conv_in)
        state[b] = dot(lhs, wt[...])
        if split:
            state[b] += head[cuts[b] : cuts[b + 1]]

    def act(b):
        state[b] = gelu(norm(state[b], gain_out[1:2])).astype(BF)

    def update(b):
        if b == 0:
            wait(out_in)
        hidden = hid[cuts[b] : cuts[b + 1]].astype(F32)
        out[cuts[b] : cuts[b + 1]] = (hidden + dot(state[b], wo[...])).astype(BF)

    stagger((mix, act, update))


def after(x, *deps):
    return lax.optimization_barrier((x, *deps))[0]


def per_device(tokens, breaks, lengths, embed_table, break_vec, gain_in, gain_mid, gain_out, w_in, conv_w, w_out):
    rows = tokens.shape[1]
    width = embed_table.shape[1]
    roll_at = lax.axis_index("roll")
    seq_at = lax.axis_index("seq")
    rolls = lax.axis_size("roll")
    seqs = lax.axis_size("seq")
    split = rolls == 4 and seqs % 4 == 0

    def core_swap(x):
        return lax.ppermute(x, "roll", [(i, i ^ 1) for i in range(rolls)])

    def x_swap(x):
        return lax.ppermute(x, "roll", [(i, i ^ 2) for i in range(rolls)])

    def seq_swap(x, bits):
        return lax.ppermute(x, "seq", [(i, i ^ bits) for i in range(seqs)])

    span = jnp.stack([(seq_at * rows).astype(jnp.int32) - EDGE, lengths[0]])
    wide_rows = rows + 2 * EDGE
    codes = tokens[0] + SLOT * breaks[0]

    shard = w_out.shape[1] // 2
    shapes = [((CODES, width), BF), ((CODES, H), F32)]
    if split:
        shapes += [((shard, width), BF), ((shard, CUT_A), BF), ((shard, CUT_A), BF)]
    table, part, *parts = pl.pallas_call(
        functools.partial(first_kernel, split),
        out_shape=[jax.ShapeDtypeStruct(n, t) for n, t in shapes],
        in_specs=[HBM] * 6,
        out_specs=[VMEM] * 2 + [HBM] * (len(shapes) - 2),
        scratch_shapes=[
            pltpu.VMEM(embed_table.shape, F32),
            pltpu.VMEM((width,), F32),
            pltpu.VMEM(gain_in.shape, F32),
            pltpu.VMEM(w_in.shape[1:], BF),
            pltpu.VMEM((CODES, width), F32),
            pltpu.SemaphoreType.DMA((3,)),
        ]
        + [pltpu.VMEM(n, t) for n, t in shapes[2:]],
        cost_estimate=FREE,
        compiler_params=params(60),
    )(embed_table, break_vec, gain_in, w_in, conv_w, w_out)

    if split:
        near_out, near_in = core_swap(w_out), core_swap(w_in)
        low = roll_at % 2 == 0
        ends = codes[rows - REACH :], codes[:REACH]
        theirs = core_swap(jnp.where(low, *ends[::-1]))
        own = part + after(core_swap(part), theirs)
        other = x_swap(own.astype(BF))
        far_a = x_swap(after(parts[0], own))
        pack = jnp.stack([jnp.where(low, *ends), theirs])
        places = [(s, r) for s in range(seqs) for r in range(rolls)]
        moves = [(s * rolls + r, (s + (1, -1)[r % 2]) % seqs * rolls + r) for s, r in places]
        moved = lax.ppermute(after(pack, own), ("seq", "roll"), moves)
        other = after(other, moved, near_out, near_in)
        far_b = x_swap(after(parts[1], other))
        came = core_swap(moved[1])
        before, behind = jnp.where(low, moved[0], came), jnp.where(low, came, moved[0])
    else:
        own = lax.psum(part, "roll")
        other = jnp.zeros((CODES, H), BF)
        pairs = [(i, i + 1) for i in range(seqs - 1)]
        before = lax.ppermute(codes[rows - REACH :], "seq", pairs)
        behind = lax.ppermute(codes[:REACH], "seq", [(j, i) for i, j in pairs])
    wide = KERNEL * H
    shapes = [(SLOT, F32), (SLOT, BF)] if split else [(CODES, F32)]
    taps = pl.pallas_call(
        functools.partial(table_kernel, split),
        out_shape=[jax.ShapeDtypeStruct((n, wide), t) for n, t in shapes],
        in_specs=[VMEM, VMEM, VMEM, HBM],
        out_specs=[VMEM] * len(shapes),
        scratch_shapes=[
            pltpu.VMEM(conv_w.shape[1:], BF),
            pltpu.VMEM((CODES, wide), F32),
            pltpu.SemaphoreType.DMA,
        ],
        cost_estimate=FREE,
        compiler_params=params(12),
    )(own, other, gain_mid, conv_w)
    if split:
        relay = after(far_a, taps[1])
        parts_a = [far_a] + [seq_swap(relay, b) for b in (1, 2, 3)]
        sent = (taps[0] + core_swap(taps[1]).astype(F32)).astype(BF)
        received = x_swap(sent)
    spare = jnp.zeros((-(rows + 2 * REACH) % 128,), jnp.int32)
    near = jnp.concatenate([before, codes, behind, spare])[None]
    if split:
        near = after(near, sent)

    shapes = [(wide_rows, KERNEL * CODES), (wide_rows, CODES)]
    operands, scratch = [], []
    if split:
        operands = [table, w_out, w_in, near_out, near_in]
        shapes += [(4 * shard + CODES, width), (8 * shard, H)]
        scratch = [pltpu.SemaphoreType.DMA]
    hot5, hot1, *chip = pl.pallas_call(
        functools.partial(hot_kernel, split),
        out_shape=[jax.ShapeDtypeStruct(n, BF) for n in shapes],
        in_specs=[SMEM, VMEM] + [ANY] * len(operands),
        out_specs=[VMEM] * len(shapes),
        scratch_shapes=scratch,
        cost_estimate=FREE,
        compiler_params=params(16),
    )(span, near, *operands)

    if split:
        near_sent = core_swap(after(sent, hot1))
        received = after(received, hot1)
        near_received = core_swap(received)
        near_a = [core_swap(after(p, hot1, far_b)) for p in parts_a]
        relay = after(far_b, received, near_sent)
        parts_b = [far_b, seq_swap(relay, 1), seq_swap(relay, 2), x_swap(after(parts[2], received))]
        weights_a = [sent, received, near_sent, near_received] + chip + parts_a + near_a
        near_conv = core_swap(after(conv_w, near_received, *near_a))
    else:
        taps = lax.psum(taps[0], "roll").astype(BF)
        gather = lambda w: lax.all_gather(w, "roll", axis=0, tiled=True)
        weights_a, weights_b = [taps, table, gather(w_out[0]), gather(w_in[1])], [gather(conv_w[1]), gather(w_out[1])]

    ci, hid = pl.pallas_call(
        functools.partial(rows_kernel, split),
        out_shape=(
            jax.ShapeDtypeStruct((wide_rows, H), BF),
            jax.ShapeDtypeStruct((rows, width), BF),
        ),
        in_specs=[SMEM] + [VMEM] * 5 + [ANY] * len(weights_a),
        out_specs=(VMEM, VMEM),
        scratch_shapes=[
            pltpu.VMEM((2, KERNEL * CODES, H), BF),
            pltpu.VMEM((H + CODES, width), BF),
            pltpu.VMEM((width, H), BF),
            pltpu.SemaphoreType.DMA((3,)),
        ],
        cost_estimate=FREE,
        compiler_params=params(30),
    )(span, hot5, hot1, gain_out, gain_in, gain_mid, *weights_a)

    if split:
        near_b = [core_swap(after(p, ci)) for p in parts_b]
        head = pl.pallas_call(
            head_kernel,
            out_shape=jax.ShapeDtypeStruct((rows, H), F32),
            in_specs=[VMEM, HBM, ANY],
            out_specs=VMEM,
            scratch_shapes=[pltpu.VMEM((KERNEL * HEAD, H), BF), pltpu.SemaphoreType.DMA],
            cost_estimate=FREE,
            compiler_params=params(16),
        )(ci, conv_w, near_conv)
        weights_b = [head, conv_w, w_out, near_conv, near_out] + parts_b + near_b
    out = pl.pallas_call(
        functools.partial(last_kernel, split),
        out_shape=jax.ShapeDtypeStruct((rows, width), BF),
        in_specs=[VMEM] * 3
        + [HBM if w is w_out or w is conv_w else VMEM if split and w is head else ANY for w in weights_b],
        out_specs=VMEM,
        scratch_shapes=[
            pltpu.VMEM((KERNEL * (TAIL if split else H), H), BF),
            pltpu.VMEM((H, width), BF),
            pltpu.SemaphoreType.DMA((2,)),
        ],
        cost_estimate=FREE,
        compiler_params=params(24),
    )(ci, hid, gain_out, *weights_b)
    return out[None]


def solution(mesh):
    placed = (
        P("roll", "seq"),
        P("roll", "seq"),
        P("roll"),
        P(),
        P(),
        P(),
        P(),
        P(),
        P(None, "roll", None),
        P(None, "roll", None),
        P(None, "roll", None),
    )
    return jax.shard_map(
        per_device, mesh=mesh, in_specs=placed, out_specs=P("roll", "seq", None), check_vma=False
    )
```

```python
import functools

import jax
import jax.numpy as jnp
from jax import lax
from jax.experimental import pallas as pl
from jax.experimental.pallas import tpu as pltpu
from jax.sharding import PartitionSpec as P

H = 640
KERNEL = 5
VOCAB = 30
SLOT = 32
CODES = 2 * SLOT
BASE_DILATION = 64
DIL0 = BASE_DILATION
DIL1 = 2 * BASE_DILATION
HALF = KERNEL // 2
EDGE = HALF * DIL1
REACH = EDGE + HALF * DIL0
BF = jnp.bfloat16
F32 = jnp.float32
VMEM = pl.BlockSpec(memory_space=pltpu.VMEM)
SMEM = pl.BlockSpec(memory_space=pltpu.SMEM)
ANY = pl.BlockSpec(memory_space=pl.ANY)
HBM = pl.BlockSpec(memory_space=pltpu.HBM)
FREE = pl.CostEstimate(flops=0, bytes_accessed=0, transcendentals=0)
CUT_A = 18 * 128
CUT_B = 17 * 128


def params(mib):
    return pltpu.CompilerParams(vmem_limit_bytes=mib * 1024 * 1024)


def gelu(x):
    return (0.5 * x) * (1.0 + lax.erf(x * 0.5**0.5))


def norm(x, gain):
    center = jnp.mean(x, axis=-1, keepdims=True)
    d = x - center
    spread = jnp.mean(d * d, axis=-1, keepdims=True)
    return d * lax.rsqrt(spread + 1e-5) * gain


def dot(a, b):
    return jnp.dot(a, b, preferred_element_type=F32)


def place():
    roll, seq = lax.axis_index("roll"), lax.axis_index("seq")
    return lax.div(roll, 2), lax.rem(roll, 2), lax.rem(seq, 2), lax.rem(lax.div(seq, 2), 2)


def start(copies):
    for c in copies:
        c.start()


def wait(copies):
    for c in copies:
        c.wait()


def stagger(stages):
    for t in range(len(stages) + 1):
        for b in range(2):
            if 0 <= t - b < len(stages):
                stages[t - b](b)


def pick(rows, columns, first):
    i = lax.broadcasted_iota(jnp.int32, (rows, columns), 0)
    j = lax.broadcasted_iota(jnp.int32, (rows, columns), 1)
    return jnp.where(i == j + first, 1.0, 0.0).astype(BF)


def part_copies(y_is_one, row_bit, w_in, conv_w, w_out, a, b, sem):
    n = b.shape[0]
    r = pl.multiple_of(row_bit * n, 16)
    r2 = pl.multiple_of(row_bit * 2 * n, 16)
    rest = conv_w.shape[2] - CUT_B
    if y_is_one:
        pairs = [
            (conv_w.at[1, pl.ds(r, n), CUT_B:], b.at[:, 0:rest]),
            (w_out.at[1, pl.ds(r, n)], b.at[:, rest:]),
        ]
        if a is not None:
            pairs += [
                (w_in.at[1, pl.ds(r2, n)], a.at[:, 0:H]),
                (w_in.at[1, pl.ds(r2 + n, n)], a.at[:, H : 2 * H]),
            ]
    else:
        pairs = [(conv_w.at[1, pl.ds(r, n), 0:CUT_A], b)]
        if a is not None:
            pairs.append((w_out.at[0, pl.ds(r, n)], a))
    return [pltpu.make_async_copy(s, d, sem) for s, d in pairs]


def first_kernel(split, embed, brk, gain, w_in, conv_w, w_out, table, part, *rest):
    count = 3 if split else 0
    parts, rest = rest[:count], rest[count:]
    emb, bv, g, w, full, sem, *held = rest
    copies = [
        pltpu.make_async_copy(s, d, sem.at[0])
        for s, d in ((embed, emb), (brk, bv), (gain, g), (w_in.at[0], w))
    ]
    start(copies)
    leaving = []
    if split:
        _, _, y, z = place()
        kinds = []
        for kind in range(2):
            kinds.append(
                part_copies(kind == 1, z, w_in, conv_w, w_out, held[0], held[1], sem.at[1])
                + part_copies(kind == 0, 1 - z, w_in, conv_w, w_out, None, held[2], sem.at[1])
            )

            @pl.when(y == kind)
            def _():
                start(kinds[kind])

        leaving = [pltpu.make_async_copy(s, d, sem.at[2]) for s, d in zip(held, parts)]

    wait(copies)
    if split:
        for kind in range(2):

            @pl.when(y == kind)
            def _():
                wait(kinds[kind])

        start(leaving)
    full[...] = jnp.zeros_like(full)
    full[0:VOCAB] = emb[...]
    full[SLOT : SLOT + VOCAB] = emb[...] + bv[...][None, :]
    hidden = full[...].astype(BF)
    table[...] = hidden
    normed = gelu(norm(hidden.astype(F32), g[0:1])).astype(BF)
    rows = w.shape[0]
    mine = dot(normed, pick(normed.shape[1], rows, lax.axis_index("roll") * rows)).astype(BF)
    part[...] = dot(mine, w[...])
    wait(leaving)


def table_kernel(split, own, other, gain, w_all, *rest):
    *outs, w, full, sem = rest
    copy = pltpu.make_async_copy(w_all.at[0], w, sem)
    copy.start()
    wide = own[...] + other[...].astype(F32)
    t = gelu(norm(wide, gain[0:1])).astype(BF)
    rows = w.shape[0]
    mine = dot(t, pick(t.shape[1], rows, lax.axis_index("roll") * rows)).astype(BF)
    copy.wait()
    full[...] = dot(mine, w[...])
    if split:
        core = lax.rem(lax.axis_index("roll"), 2)
        outs[0][...] = full[pl.ds(pl.multiple_of(core * SLOT, SLOT), SLOT)]
        outs[1][...] = full[pl.ds(pl.multiple_of((1 - core) * SLOT, SLOT), SLOT)].astype(BF)
    else:
        outs[0][...] = full[...]


def chip_copies(table, w_out, w_in, near_out, near_in, chip_out, chip_in, sem):
    _, core, _, _ = place()
    n, m = w_out.shape[1], w_in.shape[1]
    copies = [pltpu.make_async_copy(table, chip_out.at[2 * n :], sem)]
    for c, o, i in ((core, w_out, w_in), (1 - core, near_out, near_in)):
        copies.append(pltpu.make_async_copy(o.at[0], chip_out.at[pl.ds(pl.multiple_of(c * n, 16), n)], sem))
        copies.append(pltpu.make_async_copy(i.at[1], chip_in.at[pl.ds(pl.multiple_of(c * m, 16), m)], sem))
    return copies


def hot_kernel(split, span, near, *rest):
    copies = []
    if split:
        *w, hot5, hot1, chip_out, chip_in, sem = rest
        copies = chip_copies(*w, chip_out, chip_in, sem)
    else:
        hot5, hot1 = rest
    start(copies)
    codes = near[...]
    count = codes.shape[1]
    rows = hot5.shape[0]
    pos = span[0] - HALF * DIL0 + lax.broadcasted_iota(jnp.int32, codes.shape, 1)
    masked = jnp.where((pos >= 0) & (pos < span[1]), codes, -1)
    lanes = lax.broadcasted_iota(jnp.int32, (CODES, count), 0)
    taps = jnp.where(lanes == masked, 1.0, 0.0).T.astype(BF)
    for k in range(KERNEL):
        hot5[:, k * CODES : (k + 1) * CODES] = taps[k * DIL0 : k * DIL0 + rows]
    center = jnp.where(lanes == codes, 1.0, 0.0).T.astype(BF)
    hot1[...] = center[HALF * DIL0 : HALF * DIL0 + rows]
    wait(copies)


def rows_kernel(split, span, hot5, hot1, gain_out, gain_in, gain_mid, *rest):
    *w, ci, hid, tw, wo, wi, sem = rest
    depth = wo.shape[0] - CODES
    if split:
        core = lax.rem(lax.axis_index("roll"), 2)
        taps = [(t, core * SLOT, SLOT, 0) for t in w[:2]] + [(t, (1 - core) * SLOT, SLOT, 0) for t in w[2:4]]
        taps = [(t, at, n, i % 2) for i, (t, at, n, _) in enumerate(taps)]
        w = w[4:]
    else:
        taps = [(w[0], 0, CODES, 0)]
        table, *w = w[1:]
    first = [
        pltpu.make_async_copy(
            t.at[:, k * H : (k + 1) * H], tw.at[i, pl.ds(pl.multiple_of(k * CODES + at, 16), n)], sem.at[0]
        )
        for t, at, n, i in taps
        for k in range(KERNEL)
    ]
    start(first)
    if not split:
        first.append(pltpu.make_async_copy(table, wo.at[depth:], sem.at[0]))
        first[-1].start()
        out_copies = [pltpu.make_async_copy(w[0], wo.at[0:depth], sem.at[1])]
        in_copies = [pltpu.make_async_copy(w[1], wi, sem.at[2])]
        start(out_copies + in_copies)
    else:
        chip_out, chip_in = w[:2]
        parts, near_parts = w[2:6], w[6:10]
        x, core, y, z = place()
        n = depth // 4
        m = 2 * n
        half = n // 2
        row = pl.multiple_of(x * 2 * n, 16)
        out_copies = [
            pltpu.make_async_copy(chip_out.at[0 : 2 * n], wo.at[pl.ds(row, 2 * n)], sem.at[1]),
            pltpu.make_async_copy(chip_out.at[2 * n :], wo.at[depth:], sem.at[1]),
        ]
        row = pl.multiple_of(x * 2 * m, 16)
        in_copies = [pltpu.make_async_copy(chip_in, wi.at[pl.ds(row, 2 * m)], sem.at[2])]

        def far(outs, ins):
            out, into = [], []
            for c, of in ((core, parts), (1 - core, near_parts)):
                at = 2 * (1 - x) + c
                for p, zz in zip(outs, (z, 1 - z)):
                    row = pl.multiple_of(at * n + zz * half, 16)
                    out.append(pltpu.make_async_copy(of[p], wo.at[pl.ds(row, half)], sem.at[1]))
                for p, zz in zip(ins, (z, 1 - z)):
                    for j in range(2):
                        row = pl.multiple_of(at * m + zz * n + j * half, 16)
                        into.append(
                            pltpu.make_async_copy(of[p].at[:, j * H : (j + 1) * H], wi.at[pl.ds(row, half)], sem.at[2])
                        )
            return out, into

        start(out_copies + in_copies)
        far0, far1 = far((0, 2), (1, 3)), far((1, 3), (0, 2))

        @pl.when(y == 0)
        def _():
            start(far0[0] + far0[1])

        @pl.when(y == 1)
        def _():
            start(far1[0] + far1[1])

        out_copies += far0[0]
        in_copies += far0[1]

    rows = hid.shape[0] + 2 * EDGE
    cuts = [0, 512, rows]
    state = [None, None]

    def once(b, copies):
        if b == 0:
            wait(copies)

    def mix(b):
        if b == 0:
            wait(first)
            if split:
                tw[0] = (tw[0].astype(F32) + tw[1].astype(F32)).astype(BF)
        state[b] = dot(hot5[cuts[b] : cuts[b + 1]], tw[0])

    def act(b):
        state[b] = gelu(norm(state[b], gain_out[0:1])).astype(BF)

    def update(b):
        once(b, out_copies)
        lhs = jnp.concatenate([state[b], hot1[cuts[b] : cuts[b + 1]]], axis=1)
        state[b] = dot(lhs, wo[...]).astype(BF)

    def enter(b):
        hidden = state[b]
        lo, hi = max(cuts[b], EDGE), min(cuts[b + 1], rows - EDGE)
        hid[lo - EDGE : hi - EDGE] = hidden[lo - cuts[b] : hi - cuts[b]]
        state[b] = gelu(norm(hidden.astype(F32), gain_in[1:2])).astype(BF)

    def widen(b):
        once(b, in_copies)
        state[b] = dot(state[b], wi[...])

    def leave(b):
        n = cuts[b + 1] - cuts[b]
        pos = span[0] + cuts[b] + lax.broadcasted_iota(jnp.int32, (n, 1), 0)
        valid = jnp.where((pos >= 0) & (pos < span[1]), 1.0, 0.0)
        ci[cuts[b] : cuts[b + 1]] = (gelu(norm(state[b], gain_mid[1:2])) * valid).astype(BF)

    stagger((mix, act, update, enter, widen, leave))


def conv_copies(src, col, width, wt, per_tap, row, n, sem):
    copies = []
    done = 0
    while done < width:
        tap, inner = divmod(col + done, H)
        step = min(H - inner, width - done)
        copies.append(
            pltpu.make_async_copy(
                src.at[:, done : done + step],
                wt.at[pl.ds(pl.multiple_of(tap * per_tap + row, 16), n), inner : inner + step],
                sem,
            )
        )
        done += step
    return copies


HEAD = 256
TAIL = H - HEAD


def windows(ci, lo, hi, first, width):
    first = pl.multiple_of(first, 128)
    return jnp.concatenate(
        [ci[lo + k * DIL1 : hi + k * DIL1, pl.ds(first, width)] for k in range(KERNEL)], axis=1
    )


def head_kernel(ci, w_conv, near_conv, out, wt, sem):
    x, core, _, _ = place()
    n = w_conv.shape[1]
    short = HEAD - n
    done = None
    for xx in range(2):
        for cc in range(2):
            copies = []
            for c, w in ((cc, w_conv), (1 - cc, near_conv)):
                if c == xx:
                    copies += conv_copies(w.at[1], 0, KERNEL * H, wt, HEAD, short * xx, n, sem)
                else:
                    part = w.at[1, (n - short) * xx : (n - short) * xx + short]
                    copies += conv_copies(part, 0, KERNEL * H, wt, HEAD, n * (1 - xx), short, sem)
            done = copies

            @pl.when((x == xx) & (core == cc))
            def _():
                start(copies)

    rows = out.shape[0]
    half = 16 * ((rows + 31) // 32)
    for b, (lo, hi) in enumerate(((0, half), (half, rows))):
        lhs = windows(ci, lo, hi, x * TAIL, HEAD)
        if b == 0:
            wait(done)
        out[lo:hi] = dot(lhs, wt[...])


def last_kernel(split, ci, hid, gain_out, *rest):
    *w, out, wt, wo, sem = rest
    if not split:
        conv_in = conv_copies(w[0], 0, KERNEL * H, wt, H, 0, H, sem.at[0])
        out_in = [pltpu.make_async_copy(w[1], wo, sem.at[1])]
        start(conv_in + out_in)
        first, width = 0, H
    else:
        head, w_conv, w_out, near_conv, near_out = w[:5]
        parts, near_parts = w[5:9], w[9:13]
        x, core, y, z = place()
        n = w_out.shape[1]
        half = n // 2
        left = 2 * n - HEAD
        rest_cols = KERNEL * H - CUT_B
        first, width = (1 - x) * HEAD, TAIL
        out_in = []
        for c, o in ((core, w_out), (1 - core, near_out)):
            row = pl.multiple_of((2 * x + c) * n, 16)
            out_in.append(pltpu.make_async_copy(o.at[1], wo.at[pl.ds(row, n)], sem.at[1]))
        from_row = pl.multiple_of((n - left) * (1 - x), 16)
        own_in, near_in = [
            conv_copies(v.at[1, pl.ds(from_row, left)], 0, KERNEL * H, wt, TAIL, 2 * n * x, left, sem.at[0])
            for v in (w_conv, near_conv)
        ]

        @pl.when(core + x == 1)
        def _():
            start(own_in)

        @pl.when(core + x != 1)
        def _():
            start(near_in)

        def far(head, tail):
            cv, out = [], []
            for c, of in ((core, parts), (1 - core, near_parts)):
                at = c * n + left * (1 - x)
                for p, zz in zip(head, (z, 1 - z)):
                    cv += conv_copies(of[p], 0, CUT_A, wt, TAIL, at + zz * half, half, sem.at[0])
                for p, zz in zip(tail, (z, 1 - z)):
                    skip = CUT_A - CUT_B
                    cv += conv_copies(
                        of[p].at[:, skip:rest_cols], CUT_A, rest_cols - skip, wt, TAIL, at + zz * half, half, sem.at[0]
                    )
                    row = pl.multiple_of((2 * (1 - x) + c) * n + zz * half, 16)
                    out.append(pltpu.make_async_copy(of[p].at[:, rest_cols:], wo.at[pl.ds(row, half)], sem.at[1]))
            return cv, out

        start(out_in)
        far0, far1 = far((0, 2), (1, 3)), far((1, 3), (0, 2))

        @pl.when(y == 0)
        def _():
            start(far0[0] + far0[1])

        @pl.when(y == 1)
        def _():
            start(far1[0] + far1[1])

        conv_in = own_in + far0[0]
        out_in += far0[1]

    rows = out.shape[0]
    cuts = [0, 16 * ((rows + 31) // 32), rows]
    state = [None, None]

    def mix(b):
        lhs = windows(ci, cuts[b], cuts[b + 1], first, width)
        if b == 0:
            wait(conv_in)
        state[b] = dot(lhs, wt[...])
        if split:
            state[b] += head[cuts[b] : cuts[b + 1]]

    def act(b):
        state[b] = gelu(norm(state[b], gain_out[1:2])).astype(BF)

    def update(b):
        if b == 0:
            wait(out_in)
        hidden = hid[cuts[b] : cuts[b + 1]].astype(F32)
        out[cuts[b] : cuts[b + 1]] = (hidden + dot(state[b], wo[...])).astype(BF)

    stagger((mix, act, update))


def after(x, *deps):
    return lax.optimization_barrier((x, *deps))[0]


def per_device(tokens, breaks, lengths, embed_table, break_vec, gain_in, gain_mid, gain_out, w_in, conv_w, w_out):
    rows = tokens.shape[1]
    width = embed_table.shape[1]
    roll_at = lax.axis_index("roll")
    seq_at = lax.axis_index("seq")
    rolls = lax.axis_size("roll")
    seqs = lax.axis_size("seq")
    split = rolls == 4 and seqs % 4 == 0

    def core_swap(x):
        return lax.ppermute(x, "roll", [(i, i ^ 1) for i in range(rolls)])

    def x_swap(x):
        return lax.ppermute(x, "roll", [(i, i ^ 2) for i in range(rolls)])

    def seq_swap(x, bits):
        return lax.ppermute(x, "seq", [(i, i ^ bits) for i in range(seqs)])

    span = jnp.stack([(seq_at * rows).astype(jnp.int32) - EDGE, lengths[0]])
    wide_rows = rows + 2 * EDGE
    codes = tokens[0] + SLOT * breaks[0]

    shard = w_out.shape[1] // 2
    shapes = [((CODES, width), BF), ((CODES, H), F32)]
    if split:
        shapes += [((shard, width), BF), ((shard, CUT_A), BF), ((shard, CUT_A), BF)]
    table, part, *parts = pl.pallas_call(
        functools.partial(first_kernel, split),
        out_shape=[jax.ShapeDtypeStruct(n, t) for n, t in shapes],
        in_specs=[HBM] * 6,
        out_specs=[VMEM] * 2 + [HBM] * (len(shapes) - 2),
        scratch_shapes=[
            pltpu.VMEM(embed_table.shape, F32),
            pltpu.VMEM((width,), F32),
            pltpu.VMEM(gain_in.shape, F32),
            pltpu.VMEM(w_in.shape[1:], BF),
            pltpu.VMEM((CODES, width), F32),
            pltpu.SemaphoreType.DMA((3,)),
        ]
        + [pltpu.VMEM(n, t) for n, t in shapes[2:]],
        cost_estimate=FREE,
        compiler_params=params(60),
    )(embed_table, break_vec, gain_in, w_in, conv_w, w_out)

    if split:
        near_out, near_in = core_swap(w_out), core_swap(w_in)
        low = roll_at % 2 == 0
        ends = codes[rows - REACH :], codes[:REACH]
        theirs = core_swap(jnp.where(low, *ends[::-1]))
        own = part + after(core_swap(part), theirs)
        other = x_swap(own.astype(BF))
        far_a = x_swap(after(parts[0], own))
        far_b = x_swap(after(parts[1], own))
        pack = jnp.stack([jnp.where(low, *ends), theirs])
        places = [(s, r) for s in range(seqs) for r in range(rolls)]
        moves = [(s * rolls + r, (s + (1, -1)[r % 2]) % seqs * rolls + r) for s, r in places]
        moved = lax.ppermute(after(pack, own), ("seq", "roll"), moves)
        other = after(other, moved, near_out, near_in)
        came = core_swap(moved[1])
        before, behind = jnp.where(low, moved[0], came), jnp.where(low, came, moved[0])
    else:
        own = lax.psum(part, "roll")
        other = jnp.zeros((CODES, H), BF)
        pairs = [(i, i + 1) for i in range(seqs - 1)]
        before = lax.ppermute(codes[rows - REACH :], "seq", pairs)
        behind = lax.ppermute(codes[:REACH], "seq", [(j, i) for i, j in pairs])
    wide = KERNEL * H
    shapes = [(SLOT, F32), (SLOT, BF)] if split else [(CODES, F32)]
    taps = pl.pallas_call(
        functools.partial(table_kernel, split),
        out_shape=[jax.ShapeDtypeStruct((n, wide), t) for n, t in shapes],
        in_specs=[VMEM, VMEM, VMEM, HBM],
        out_specs=[VMEM] * len(shapes),
        scratch_shapes=[
            pltpu.VMEM(conv_w.shape[1:], BF),
            pltpu.VMEM((CODES, wide), F32),
            pltpu.SemaphoreType.DMA,
        ],
        cost_estimate=FREE,
        compiler_params=params(12),
    )(own, other, gain_mid, conv_w)
    if split:
        relay = after(far_a, taps[1])
        parts_a = [far_a] + [seq_swap(relay, b) for b in (1, 2, 3)]
        sent = (taps[0] + core_swap(taps[1]).astype(F32)).astype(BF)
        received = x_swap(sent)
    spare = jnp.zeros((-(rows + 2 * REACH) % 128,), jnp.int32)
    near = jnp.concatenate([before, codes, behind, spare])[None]
    if split:
        near = after(near, sent)

    shapes = [(wide_rows, KERNEL * CODES), (wide_rows, CODES)]
    operands, scratch = [], []
    if split:
        operands = [table, w_out, w_in, near_out, near_in]
        shapes += [(4 * shard + CODES, width), (8 * shard, H)]
        scratch = [pltpu.SemaphoreType.DMA]
    hot5, hot1, *chip = pl.pallas_call(
        functools.partial(hot_kernel, split),
        out_shape=[jax.ShapeDtypeStruct(n, BF) for n in shapes],
        in_specs=[SMEM, VMEM] + [ANY] * len(operands),
        out_specs=[VMEM] * len(shapes),
        scratch_shapes=scratch,
        cost_estimate=FREE,
        compiler_params=params(16),
    )(span, near, *operands)

    if split:
        near_sent = core_swap(after(sent, hot1))
        received = after(received, hot1)
        near_received = core_swap(received)
        near_a = [core_swap(after(p, hot1, far_b)) for p in parts_a]
        relay = after(far_b, received)
        parts_b = [far_b, seq_swap(relay, 1), seq_swap(relay, 2), x_swap(after(parts[2], received))]
        weights_a = [sent, received, near_sent, near_received] + chip + parts_a + near_a
        near_conv = core_swap(after(conv_w, near_received, near_sent, *near_a))
    else:
        taps = lax.psum(taps[0], "roll").astype(BF)
        gather = lambda w: lax.all_gather(w, "roll", axis=0, tiled=True)
        weights_a, weights_b = [taps, table, gather(w_out[0]), gather(w_in[1])], [gather(conv_w[1]), gather(w_out[1])]

    ci, hid = pl.pallas_call(
        functools.partial(rows_kernel, split),
        out_shape=(
            jax.ShapeDtypeStruct((wide_rows, H), BF),
            jax.ShapeDtypeStruct((rows, width), BF),
        ),
        in_specs=[SMEM] + [VMEM] * 5 + [ANY] * len(weights_a),
        out_specs=(VMEM, VMEM),
        scratch_shapes=[
            pltpu.VMEM((2, KERNEL * CODES, H), BF),
            pltpu.VMEM((H + CODES, width), BF),
            pltpu.VMEM((width, H), BF),
            pltpu.SemaphoreType.DMA((3,)),
        ],
        cost_estimate=FREE,
        compiler_params=params(30),
    )(span, hot5, hot1, gain_out, gain_in, gain_mid, *weights_a)

    if split:
        near_b = [core_swap(after(p, ci)) for p in parts_b]
        head = pl.pallas_call(
            head_kernel,
            out_shape=jax.ShapeDtypeStruct((rows, H), F32),
            in_specs=[VMEM, HBM, ANY],
            out_specs=VMEM,
            scratch_shapes=[pltpu.VMEM((KERNEL * HEAD, H), BF), pltpu.SemaphoreType.DMA],
            cost_estimate=FREE,
            compiler_params=params(16),
        )(ci, conv_w, near_conv)
        weights_b = [head, conv_w, w_out, near_conv, near_out] + parts_b + near_b
    out = pl.pallas_call(
        functools.partial(last_kernel, split),
        out_shape=jax.ShapeDtypeStruct((rows, width), BF),
        in_specs=[VMEM] * 3
        + [HBM if w is w_out or w is conv_w else VMEM if split and w is head else ANY for w in weights_b],
        out_specs=VMEM,
        scratch_shapes=[
            pltpu.VMEM((KERNEL * (TAIL if split else H), H), BF),
            pltpu.VMEM((H, width), BF),
            pltpu.SemaphoreType.DMA((2,)),
        ],
        cost_estimate=FREE,
        compiler_params=params(24),
    )(ci, hid, gain_out, *weights_b)
    return out[None]


def solution(mesh):
    placed = (
        P("roll", "seq"),
        P("roll", "seq"),
        P("roll"),
        P(),
        P(),
        P(),
        P(),
        P(),
        P(None, "roll", None),
        P(None, "roll", None),
        P(None, "roll", None),
    )
    return jax.shard_map(
        per_device, mesh=mesh, in_specs=placed, out_specs=P("roll", "seq", None), check_vma=False
    )
```

```python
import functools

import jax
import jax.numpy as jnp
from jax import lax
from jax.experimental import pallas as pl
from jax.experimental.pallas import tpu as pltpu
from jax.sharding import PartitionSpec as P

H = 640
KERNEL = 5
VOCAB = 30
SLOT = 32
CODES = 2 * SLOT
BASE_DILATION = 64
DIL0 = BASE_DILATION
DIL1 = 2 * BASE_DILATION
HALF = KERNEL // 2
EDGE = HALF * DIL1
REACH = EDGE + HALF * DIL0
BF = jnp.bfloat16
F32 = jnp.float32
VMEM = pl.BlockSpec(memory_space=pltpu.VMEM)
SMEM = pl.BlockSpec(memory_space=pltpu.SMEM)
ANY = pl.BlockSpec(memory_space=pl.ANY)
HBM = pl.BlockSpec(memory_space=pltpu.HBM)
FREE = pl.CostEstimate(flops=0, bytes_accessed=0, transcendentals=0)
CUT_A = 18 * 128
CUT_B = 17 * 128


def params(mib):
    return pltpu.CompilerParams(vmem_limit_bytes=mib * 1024 * 1024)


def gelu(x):
    return (0.5 * x) * (1.0 + lax.erf(x * 0.5**0.5))


def norm(x, gain):
    center = jnp.mean(x, axis=-1, keepdims=True)
    d = x - center
    spread = jnp.mean(d * d, axis=-1, keepdims=True)
    return d * lax.rsqrt(spread + 1e-5) * gain


def dot(a, b):
    return jnp.dot(a, b, preferred_element_type=F32)


def place():
    roll, seq = lax.axis_index("roll"), lax.axis_index("seq")
    return lax.div(roll, 2), lax.rem(roll, 2), lax.rem(seq, 2), lax.rem(lax.div(seq, 2), 2)


def start(copies):
    for c in copies:
        c.start()


def wait(copies):
    for c in copies:
        c.wait()


def stagger(stages):
    for t in range(len(stages) + 1):
        for b in range(2):
            if 0 <= t - b < len(stages):
                stages[t - b](b)


def pick(rows, columns, first):
    i = lax.broadcasted_iota(jnp.int32, (rows, columns), 0)
    j = lax.broadcasted_iota(jnp.int32, (rows, columns), 1)
    return jnp.where(i == j + first, 1.0, 0.0).astype(BF)


def part_copies(y_is_one, row_bit, w_in, conv_w, w_out, a, b, sem):
    n = b.shape[0]
    r = pl.multiple_of(row_bit * n, 16)
    r2 = pl.multiple_of(row_bit * 2 * n, 16)
    rest = conv_w.shape[2] - CUT_B
    if y_is_one:
        pairs = [
            (conv_w.at[1, pl.ds(r, n), CUT_B:], b.at[:, 0:rest]),
            (w_out.at[1, pl.ds(r, n)], b.at[:, rest:]),
        ]
        if a is not None:
            pairs += [
                (w_in.at[1, pl.ds(r2, n)], a.at[:, 0:H]),
                (w_in.at[1, pl.ds(r2 + n, n)], a.at[:, H : 2 * H]),
            ]
    else:
        pairs = [(conv_w.at[1, pl.ds(r, n), 0:CUT_A], b)]
        if a is not None:
            pairs.append((w_out.at[0, pl.ds(r, n)], a))
    return [pltpu.make_async_copy(s, d, sem) for s, d in pairs]


def first_kernel(split, embed, brk, gain, w_in, conv_w, w_out, table, part, *rest):
    count = 3 if split else 0
    parts, rest = rest[:count], rest[count:]
    emb, bv, g, w, full, sem, *held = rest
    copies = [
        pltpu.make_async_copy(s, d, sem.at[0])
        for s, d in ((embed, emb), (brk, bv), (gain, g), (w_in.at[0], w))
    ]
    start(copies)
    leaving = []
    if split:
        _, _, y, z = place()
        kinds = []
        for kind in range(2):
            kinds.append(
                part_copies(kind == 1, z, w_in, conv_w, w_out, held[0], held[1], sem.at[1])
                + part_copies(kind == 0, 1 - z, w_in, conv_w, w_out, None, held[2], sem.at[1])
            )

            @pl.when(y == kind)
            def _():
                start(kinds[kind])

        leaving = [pltpu.make_async_copy(s, d, sem.at[2]) for s, d in zip(held, parts)]

    wait(copies)
    full[...] = jnp.zeros_like(full)
    full[0:VOCAB] = emb[...]
    full[SLOT : SLOT + VOCAB] = emb[...] + bv[...][None, :]
    hidden = full[...].astype(BF)
    table[...] = hidden
    normed = gelu(norm(hidden.astype(F32), g[0:1])).astype(BF)
    if split:
        for kind in range(2):

            @pl.when(y == kind)
            def _():
                wait(kinds[kind])

        start(leaving)
    rows = w.shape[0]
    mine = dot(normed, pick(normed.shape[1], rows, lax.axis_index("roll") * rows)).astype(BF)
    part[...] = dot(mine, w[...])
    wait(leaving)


def table_kernel(split, own, other, gain, w_all, *rest):
    *outs, w, full, sem = rest
    copy = pltpu.make_async_copy(w_all.at[0], w, sem)
    copy.start()
    wide = own[...] + other[...].astype(F32)
    t = gelu(norm(wide, gain[0:1])).astype(BF)
    rows = w.shape[0]
    mine = dot(t, pick(t.shape[1], rows, lax.axis_index("roll") * rows)).astype(BF)
    copy.wait()
    full[...] = dot(mine, w[...])
    if split:
        core = lax.rem(lax.axis_index("roll"), 2)
        outs[0][...] = full[pl.ds(pl.multiple_of(core * SLOT, SLOT), SLOT)]
        outs[1][...] = full[pl.ds(pl.multiple_of((1 - core) * SLOT, SLOT), SLOT)].astype(BF)
    else:
        outs[0][...] = full[...]


def chip_copies(table, w_out, w_in, near_out, near_in, chip_out, chip_in, sem):
    _, core, _, _ = place()
    n, m = w_out.shape[1], w_in.shape[1]
    copies = [pltpu.make_async_copy(table, chip_out.at[2 * n :], sem)]
    for c, o, i in ((core, w_out, w_in), (1 - core, near_out, near_in)):
        copies.append(pltpu.make_async_copy(o.at[0], chip_out.at[pl.ds(pl.multiple_of(c * n, 16), n)], sem))
        copies.append(pltpu.make_async_copy(i.at[1], chip_in.at[pl.ds(pl.multiple_of(c * m, 16), m)], sem))
    return copies


def hot_kernel(split, span, near, *rest):
    copies = []
    if split:
        *w, hot5, hot1, chip_out, chip_in, sem = rest
        copies = chip_copies(*w, chip_out, chip_in, sem)
    else:
        hot5, hot1 = rest
    start(copies)
    codes = near[...]
    count = codes.shape[1]
    rows = hot5.shape[0]
    pos = span[0] - HALF * DIL0 + lax.broadcasted_iota(jnp.int32, codes.shape, 1)
    masked = jnp.where((pos >= 0) & (pos < span[1]), codes, -1)
    lanes = lax.broadcasted_iota(jnp.int32, (CODES, count), 0)
    taps = jnp.where(lanes == masked, 1.0, 0.0).T.astype(BF)
    for k in range(KERNEL):
        hot5[:, k * CODES : (k + 1) * CODES] = taps[k * DIL0 : k * DIL0 + rows]
    center = jnp.where(lanes == codes, 1.0, 0.0).T.astype(BF)
    hot1[...] = center[HALF * DIL0 : HALF * DIL0 + rows]
    wait(copies)


def rows_kernel(split, span, hot5, hot1, gain_out, gain_in, gain_mid, *rest):
    *w, ci, hid, tw, wo, wi, sem = rest
    depth = wo.shape[0] - CODES
    if split:
        core = lax.rem(lax.axis_index("roll"), 2)
        taps = [(t, core * SLOT, SLOT, 0) for t in w[:2]] + [(t, (1 - core) * SLOT, SLOT, 0) for t in w[2:4]]
        taps = [(t, at, n, i % 2) for i, (t, at, n, _) in enumerate(taps)]
        w = w[4:]
    else:
        taps = [(w[0], 0, CODES, 0)]
        table, *w = w[1:]
    first = [
        pltpu.make_async_copy(
            t.at[:, k * H : (k + 1) * H], tw.at[i, pl.ds(pl.multiple_of(k * CODES + at, 16), n)], sem.at[0]
        )
        for t, at, n, i in taps
        for k in range(KERNEL)
    ]
    start(first)
    if not split:
        first.append(pltpu.make_async_copy(table, wo.at[depth:], sem.at[0]))
        first[-1].start()
        out_copies = [pltpu.make_async_copy(w[0], wo.at[0:depth], sem.at[1])]
        in_copies = [pltpu.make_async_copy(w[1], wi, sem.at[2])]
        start(out_copies + in_copies)
    else:
        chip_out, chip_in = w[:2]
        parts, near_parts = w[2:6], w[6:10]
        x, core, y, z = place()
        n = depth // 4
        m = 2 * n
        half = n // 2
        row = pl.multiple_of(x * 2 * n, 16)
        out_copies = [
            pltpu.make_async_copy(chip_out.at[0 : 2 * n], wo.at[pl.ds(row, 2 * n)], sem.at[1]),
            pltpu.make_async_copy(chip_out.at[2 * n :], wo.at[depth:], sem.at[1]),
        ]
        row = pl.multiple_of(x * 2 * m, 16)
        in_copies = [pltpu.make_async_copy(chip_in, wi.at[pl.ds(row, 2 * m)], sem.at[2])]

        def far(outs, ins):
            out, into = [], []
            for c, of in ((core, parts), (1 - core, near_parts)):
                at = 2 * (1 - x) + c
                for p, zz in zip(outs, (z, 1 - z)):
                    row = pl.multiple_of(at * n + zz * half, 16)
                    out.append(pltpu.make_async_copy(of[p], wo.at[pl.ds(row, half)], sem.at[1]))
                for p, zz in zip(ins, (z, 1 - z)):
                    for j in range(2):
                        row = pl.multiple_of(at * m + zz * n + j * half, 16)
                        into.append(
                            pltpu.make_async_copy(of[p].at[:, j * H : (j + 1) * H], wi.at[pl.ds(row, half)], sem.at[2])
                        )
            return out, into

        start(out_copies + in_copies)
        far0, far1 = far((0, 2), (1, 3)), far((1, 3), (0, 2))

        @pl.when(y == 0)
        def _():
            start(far0[0] + far0[1])

        @pl.when(y == 1)
        def _():
            start(far1[0] + far1[1])

        out_copies += far0[0]
        in_copies += far0[1]

    rows = hid.shape[0] + 2 * EDGE
    cuts = [0, 512, rows]
    state = [None, None]

    def once(b, copies):
        if b == 0:
            wait(copies)

    def mix(b):
        if b == 0:
            wait(first)
            if split:
                tw[0] = (tw[0].astype(F32) + tw[1].astype(F32)).astype(BF)
        state[b] = dot(hot5[cuts[b] : cuts[b + 1]], tw[0])

    def act(b):
        state[b] = gelu(norm(state[b], gain_out[0:1])).astype(BF)

    def update(b):
        once(b, out_copies)
        lhs = jnp.concatenate([state[b], hot1[cuts[b] : cuts[b + 1]]], axis=1)
        state[b] = dot(lhs, wo[...]).astype(BF)

    def enter(b):
        hidden = state[b]
        lo, hi = max(cuts[b], EDGE), min(cuts[b + 1], rows - EDGE)
        hid[lo - EDGE : hi - EDGE] = hidden[lo - cuts[b] : hi - cuts[b]]
        state[b] = gelu(norm(hidden.astype(F32), gain_in[1:2])).astype(BF)

    def widen(b):
        once(b, in_copies)
        state[b] = dot(state[b], wi[...])

    def leave(b):
        n = cuts[b + 1] - cuts[b]
        pos = span[0] + cuts[b] + lax.broadcasted_iota(jnp.int32, (n, 1), 0)
        valid = jnp.where((pos >= 0) & (pos < span[1]), 1.0, 0.0)
        ci[cuts[b] : cuts[b + 1]] = (gelu(norm(state[b], gain_mid[1:2])) * valid).astype(BF)

    stagger((mix, act, update, enter, widen, leave))


def conv_copies(src, col, width, wt, per_tap, row, n, sem):
    copies = []
    done = 0
    while done < width:
        tap, inner = divmod(col + done, H)
        step = min(H - inner, width - done)
        copies.append(
            pltpu.make_async_copy(
                src.at[:, done : done + step],
                wt.at[pl.ds(pl.multiple_of(tap * per_tap + row, 16), n), inner : inner + step],
                sem,
            )
        )
        done += step
    return copies


HEAD = 256
TAIL = H - HEAD


def windows(ci, lo, hi, first, width):
    first = pl.multiple_of(first, 128)
    return jnp.concatenate(
        [ci[lo + k * DIL1 : hi + k * DIL1, pl.ds(first, width)] for k in range(KERNEL)], axis=1
    )


def head_kernel(ci, w_conv, near_conv, out, wt, sem):
    x, core, _, _ = place()
    n = w_conv.shape[1]
    short = HEAD - n
    done = None
    for xx in range(2):
        for cc in range(2):
            copies = []
            for c, w in ((cc, w_conv), (1 - cc, near_conv)):
                if c == xx:
                    copies += conv_copies(w.at[1], 0, KERNEL * H, wt, HEAD, short * xx, n, sem)
                else:
                    part = w.at[1, (n - short) * xx : (n - short) * xx + short]
                    copies += conv_copies(part, 0, KERNEL * H, wt, HEAD, n * (1 - xx), short, sem)
            done = copies

            @pl.when((x == xx) & (core == cc))
            def _():
                start(copies)

    rows = out.shape[0]
    half = 16 * ((rows + 31) // 32)
    for b, (lo, hi) in enumerate(((0, half), (half, rows))):
        lhs = windows(ci, lo, hi, x * TAIL, HEAD)
        if b == 0:
            wait(done)
        out[lo:hi] = dot(lhs, wt[...])


def last_kernel(split, ci, hid, gain_out, *rest):
    *w, out, wt, wo, sem = rest
    if not split:
        conv_in = conv_copies(w[0], 0, KERNEL * H, wt, H, 0, H, sem.at[0])
        out_in = [pltpu.make_async_copy(w[1], wo, sem.at[1])]
        start(conv_in + out_in)
        first, width = 0, H
    else:
        head, w_conv, w_out, near_conv, near_out = w[:5]
        parts, near_parts = w[5:9], w[9:13]
        x, core, y, z = place()
        n = w_out.shape[1]
        half = n // 2
        left = 2 * n - HEAD
        rest_cols = KERNEL * H - CUT_B
        first, width = (1 - x) * HEAD, TAIL
        out_in = []
        for c, o in ((core, w_out), (1 - core, near_out)):
            row = pl.multiple_of((2 * x + c) * n, 16)
            out_in.append(pltpu.make_async_copy(o.at[1], wo.at[pl.ds(row, n)], sem.at[1]))
        from_row = pl.multiple_of((n - left) * (1 - x), 16)
        own_in, near_in = [
            conv_copies(v.at[1, pl.ds(from_row, left)], 0, KERNEL * H, wt, TAIL, 2 * n * x, left, sem.at[0])
            for v in (w_conv, near_conv)
        ]

        @pl.when(core + x == 1)
        def _():
            start(own_in)

        @pl.when(core + x != 1)
        def _():
            start(near_in)

        def far(head, tail):
            cv, out = [], []
            for c, of in ((core, parts), (1 - core, near_parts)):
                at = c * n + left * (1 - x)
                for p, zz in zip(head, (z, 1 - z)):
                    cv += conv_copies(of[p], 0, CUT_A, wt, TAIL, at + zz * half, half, sem.at[0])
                for p, zz in zip(tail, (z, 1 - z)):
                    skip = CUT_A - CUT_B
                    cv += conv_copies(
                        of[p].at[:, skip:rest_cols], CUT_A, rest_cols - skip, wt, TAIL, at + zz * half, half, sem.at[0]
                    )
                    row = pl.multiple_of((2 * (1 - x) + c) * n + zz * half, 16)
                    out.append(pltpu.make_async_copy(of[p].at[:, rest_cols:], wo.at[pl.ds(row, half)], sem.at[1]))
            return cv, out

        start(out_in)
        far0, far1 = far((0, 2), (1, 3)), far((1, 3), (0, 2))

        @pl.when(y == 0)
        def _():
            start(far0[0] + far0[1])

        @pl.when(y == 1)
        def _():
            start(far1[0] + far1[1])

        conv_in = own_in + far0[0]
        out_in += far0[1]

    rows = out.shape[0]
    cuts = [0, 16 * ((rows + 31) // 32), rows]
    state = [None, None]

    def mix(b):
        lhs = windows(ci, cuts[b], cuts[b + 1], first, width)
        if b == 0:
            wait(conv_in)
        state[b] = dot(lhs, wt[...])
        if split:
            state[b] += head[cuts[b] : cuts[b + 1]]

    def act(b):
        state[b] = gelu(norm(state[b], gain_out[1:2])).astype(BF)

    def update(b):
        if b == 0:
            wait(out_in)
        hidden = hid[cuts[b] : cuts[b + 1]].astype(F32)
        out[cuts[b] : cuts[b + 1]] = (hidden + dot(state[b], wo[...])).astype(BF)

    stagger((mix, act, update))


def after(x, *deps):
    return lax.optimization_barrier((x, *deps))[0]


def per_device(tokens, breaks, lengths, embed_table, break_vec, gain_in, gain_mid, gain_out, w_in, conv_w, w_out):
    rows = tokens.shape[1]
    width = embed_table.shape[1]
    roll_at = lax.axis_index("roll")
    seq_at = lax.axis_index("seq")
    rolls = lax.axis_size("roll")
    seqs = lax.axis_size("seq")
    split = rolls == 4 and seqs % 4 == 0

    def core_swap(x):
        return lax.ppermute(x, "roll", [(i, i ^ 1) for i in range(rolls)])

    def x_swap(x):
        return lax.ppermute(x, "roll", [(i, i ^ 2) for i in range(rolls)])

    def seq_swap(x, bits):
        return lax.ppermute(x, "seq", [(i, i ^ bits) for i in range(seqs)])

    span = jnp.stack([(seq_at * rows).astype(jnp.int32) - EDGE, lengths[0]])
    wide_rows = rows + 2 * EDGE
    codes = tokens[0] + SLOT * breaks[0]

    shard = w_out.shape[1] // 2
    shapes = [((CODES, width), BF), ((CODES, H), F32)]
    if split:
        shapes += [((shard, width), BF), ((shard, CUT_A), BF), ((shard, CUT_A), BF)]
    table, part, *parts = pl.pallas_call(
        functools.partial(first_kernel, split),
        out_shape=[jax.ShapeDtypeStruct(n, t) for n, t in shapes],
        in_specs=[HBM] * 6,
        out_specs=[VMEM] * 2 + [HBM] * (len(shapes) - 2),
        scratch_shapes=[
            pltpu.VMEM(embed_table.shape, F32),
            pltpu.VMEM((width,), F32),
            pltpu.VMEM(gain_in.shape, F32),
            pltpu.VMEM(w_in.shape[1:], BF),
            pltpu.VMEM((CODES, width), F32),
            pltpu.SemaphoreType.DMA((3,)),
        ]
        + [pltpu.VMEM(n, t) for n, t in shapes[2:]],
        cost_estimate=FREE,
        compiler_params=params(60),
    )(embed_table, break_vec, gain_in, w_in, conv_w, w_out)

    if split:
        far_a = x_swap(parts[0])
        near_out, near_in = core_swap(w_out), core_swap(w_in)
        low = roll_at % 2 == 0
        ends = codes[rows - REACH :], codes[:REACH]
        theirs = core_swap(jnp.where(low, *ends[::-1]))
        own = part + after(core_swap(part), theirs)
        other = x_swap(own.astype(BF))
        far_b = x_swap(after(parts[1], own))
        pack = jnp.stack([jnp.where(low, *ends), theirs])
        places = [(s, r) for s in range(seqs) for r in range(rolls)]
        moves = [(s * rolls + r, (s + (1, -1)[r % 2]) % seqs * rolls + r) for s, r in places]
        moved = lax.ppermute(after(pack, own), ("seq", "roll"), moves)
        other = after(other, near_out, near_in)
        came = core_swap(moved[1])
        before, behind = jnp.where(low, moved[0], came), jnp.where(low, came, moved[0])
    else:
        own = lax.psum(part, "roll")
        other = jnp.zeros((CODES, H), BF)
        pairs = [(i, i + 1) for i in range(seqs - 1)]
        before = lax.ppermute(codes[rows - REACH :], "seq", pairs)
        behind = lax.ppermute(codes[:REACH], "seq", [(j, i) for i, j in pairs])
    wide = KERNEL * H
    shapes = [(SLOT, F32), (SLOT, BF)] if split else [(CODES, F32)]
    taps = pl.pallas_call(
        functools.partial(table_kernel, split),
        out_shape=[jax.ShapeDtypeStruct((n, wide), t) for n, t in shapes],
        in_specs=[VMEM, VMEM, VMEM, HBM],
        out_specs=[VMEM] * len(shapes),
        scratch_shapes=[
            pltpu.VMEM(conv_w.shape[1:], BF),
            pltpu.VMEM((CODES, wide), F32),
            pltpu.SemaphoreType.DMA,
        ],
        cost_estimate=FREE,
        compiler_params=params(12),
    )(own, other, gain_mid, conv_w)
    if split:
        relay = after(far_a, taps[1])
        parts_a = [far_a] + [seq_swap(relay, b) for b in (1, 2, 3)]
        sent = (taps[0] + after(core_swap(taps[1]), before, behind).astype(F32)).astype(BF)
        received = x_swap(sent)
    spare = jnp.zeros((-(rows + 2 * REACH) % 128,), jnp.int32)
    near = jnp.concatenate([before, codes, behind, spare])[None]
    if split:
        near = after(near, sent)

    shapes = [(wide_rows, KERNEL * CODES), (wide_rows, CODES)]
    operands, scratch = [], []
    if split:
        operands = [table, w_out, w_in, near_out, near_in]
        shapes += [(4 * shard + CODES, width), (8 * shard, H)]
        scratch = [pltpu.SemaphoreType.DMA]
    hot5, hot1, *chip = pl.pallas_call(
        functools.partial(hot_kernel, split),
        out_shape=[jax.ShapeDtypeStruct(n, BF) for n in shapes],
        in_specs=[SMEM, VMEM] + [ANY] * len(operands),
        out_specs=[VMEM] * len(shapes),
        scratch_shapes=scratch,
        cost_estimate=FREE,
        compiler_params=params(16),
    )(span, near, *operands)

    if split:
        near_sent = core_swap(after(sent, hot1))
        received = after(received, hot1)
        near_received = core_swap(received)
        near_a = [core_swap(after(p, hot1, far_b)) for p in parts_a]
        relay = after(far_b, received)
        parts_b = [far_b, seq_swap(relay, 1), seq_swap(relay, 2), x_swap(after(parts[2], received))]
        weights_a = [sent, received, near_sent, near_received] + chip + parts_a + near_a
        near_conv = core_swap(after(conv_w, near_received, near_sent, *near_a))
    else:
        taps = lax.psum(taps[0], "roll").astype(BF)
        gather = lambda w: lax.all_gather(w, "roll", axis=0, tiled=True)
        weights_a, weights_b = [taps, table, gather(w_out[0]), gather(w_in[1])], [gather(conv_w[1]), gather(w_out[1])]

    ci, hid = pl.pallas_call(
        functools.partial(rows_kernel, split),
        out_shape=(
            jax.ShapeDtypeStruct((wide_rows, H), BF),
            jax.ShapeDtypeStruct((rows, width), BF),
        ),
        in_specs=[SMEM] + [VMEM] * 5 + [ANY] * len(weights_a),
        out_specs=(VMEM, VMEM),
        scratch_shapes=[
            pltpu.VMEM((2, KERNEL * CODES, H), BF),
            pltpu.VMEM((H + CODES, width), BF),
            pltpu.VMEM((width, H), BF),
            pltpu.SemaphoreType.DMA((3,)),
        ],
        cost_estimate=FREE,
        compiler_params=params(30),
    )(span, hot5, hot1, gain_out, gain_in, gain_mid, *weights_a)

    if split:
        near_b = [core_swap(after(p, ci)) for p in parts_b]
        head = pl.pallas_call(
            head_kernel,
            out_shape=jax.ShapeDtypeStruct((rows, H), F32),
            in_specs=[VMEM, HBM, ANY],
            out_specs=VMEM,
            scratch_shapes=[pltpu.VMEM((KERNEL * HEAD, H), BF), pltpu.SemaphoreType.DMA],
            cost_estimate=FREE,
            compiler_params=params(16),
        )(ci, conv_w, near_conv)
        weights_b = [head, conv_w, w_out, near_conv, near_out] + parts_b + near_b
    out = pl.pallas_call(
        functools.partial(last_kernel, split),
        out_shape=jax.ShapeDtypeStruct((rows, width), BF),
        in_specs=[VMEM] * 3
        + [HBM if w is w_out or w is conv_w else VMEM if split and w is head else ANY for w in weights_b],
        out_specs=VMEM,
        scratch_shapes=[
            pltpu.VMEM((KERNEL * (TAIL if split else H), H), BF),
            pltpu.VMEM((H, width), BF),
            pltpu.SemaphoreType.DMA((2,)),
        ],
        cost_estimate=FREE,
        compiler_params=params(24),
    )(ci, hid, gain_out, *weights_b)
    return out[None]


def solution(mesh):
    placed = (
        P("roll", "seq"),
        P("roll", "seq"),
        P("roll"),
        P(),
        P(),
        P(),
        P(),
        P(),
        P(None, "roll", None),
        P(None, "roll", None),
        P(None, "roll", None),
    )
    return jax.shard_map(
        per_device, mesh=mesh, in_specs=placed, out_specs=P("roll", "seq", None), check_vma=False
    )
```

```python
import functools

import jax
import jax.numpy as jnp
from jax import lax
from jax.experimental import pallas as pl
from jax.experimental.pallas import tpu as pltpu
from jax.sharding import PartitionSpec as P

H = 640
KERNEL = 5
VOCAB = 30
SLOT = 32
CODES = 2 * SLOT
BASE_DILATION = 64
DIL0 = BASE_DILATION
DIL1 = 2 * BASE_DILATION
HALF = KERNEL // 2
EDGE = HALF * DIL1
REACH = EDGE + HALF * DIL0
BF = jnp.bfloat16
F32 = jnp.float32
VMEM = pl.BlockSpec(memory_space=pltpu.VMEM)
SMEM = pl.BlockSpec(memory_space=pltpu.SMEM)
ANY = pl.BlockSpec(memory_space=pl.ANY)
HBM = pl.BlockSpec(memory_space=pltpu.HBM)
FREE = pl.CostEstimate(flops=0, bytes_accessed=0, transcendentals=0)
CUT_A = 18 * 128
CUT_B = 17 * 128


def params(mib):
    return pltpu.CompilerParams(vmem_limit_bytes=mib * 1024 * 1024)


def gelu(x):
    return (0.5 * x) * (1.0 + lax.erf(x * 0.5**0.5))


def norm(x, gain):
    center = jnp.mean(x, axis=-1, keepdims=True)
    d = x - center
    spread = jnp.mean(d * d, axis=-1, keepdims=True)
    return d * lax.rsqrt(spread + 1e-5) * gain


def dot(a, b):
    return jnp.dot(a, b, preferred_element_type=F32)


def place():
    roll, seq = lax.axis_index("roll"), lax.axis_index("seq")
    return lax.div(roll, 2), lax.rem(roll, 2), lax.rem(seq, 2), lax.rem(lax.div(seq, 2), 2)


def start(copies):
    for c in copies:
        c.start()


def wait(copies):
    for c in copies:
        c.wait()


def stagger(stages):
    for t in range(len(stages) + 1):
        for b in range(2):
            if 0 <= t - b < len(stages):
                stages[t - b](b)


def pick(rows, columns, first):
    i = lax.broadcasted_iota(jnp.int32, (rows, columns), 0)
    j = lax.broadcasted_iota(jnp.int32, (rows, columns), 1)
    return jnp.where(i == j + first, 1.0, 0.0).astype(BF)


def part_copies(y_is_one, row_bit, w_in, conv_w, w_out, a, b, sem):
    n = b.shape[0]
    r = pl.multiple_of(row_bit * n, 16)
    r2 = pl.multiple_of(row_bit * 2 * n, 16)
    rest = conv_w.shape[2] - CUT_B
    if y_is_one:
        pairs = [
            (conv_w.at[1, pl.ds(r, n), CUT_B:], b.at[:, 0:rest]),
            (w_out.at[1, pl.ds(r, n)], b.at[:, rest:]),
        ]
        if a is not None:
            pairs += [
                (w_in.at[1, pl.ds(r2, n)], a.at[:, 0:H]),
                (w_in.at[1, pl.ds(r2 + n, n)], a.at[:, H : 2 * H]),
            ]
    else:
        pairs = [(conv_w.at[1, pl.ds(r, n), 0:CUT_A], b)]
        if a is not None:
            pairs.append((w_out.at[0, pl.ds(r, n)], a))
    return [pltpu.make_async_copy(s, d, sem) for s, d in pairs]


def first_kernel(split, embed, brk, gain, w_in, conv_w, w_out, table, part, *rest):
    count = 3 if split else 0
    parts, rest = rest[:count], rest[count:]
    emb, bv, g, w, full, sem, *held = rest
    copies = [
        pltpu.make_async_copy(s, d, sem.at[0])
        for s, d in ((embed, emb), (brk, bv), (gain, g), (w_in.at[0], w))
    ]
    start(copies)
    leaving = []
    if split:
        _, _, y, z = place()
        kinds = []
        for kind in range(2):
            kinds.append(
                part_copies(kind == 1, z, w_in, conv_w, w_out, held[0], held[1], sem.at[1])
                + part_copies(kind == 0, 1 - z, w_in, conv_w, w_out, None, held[2], sem.at[1])
            )

            @pl.when(y == kind)
            def _():
                start(kinds[kind])

        leaving = [pltpu.make_async_copy(s, d, sem.at[2]) for s, d in zip(held, parts)]

    wait(copies)
    full[...] = jnp.zeros_like(full)
    full[0:VOCAB] = emb[...]
    full[SLOT : SLOT + VOCAB] = emb[...] + bv[...][None, :]
    hidden = full[...].astype(BF)
    table[...] = hidden
    normed = gelu(norm(hidden.astype(F32), g[0:1])).astype(BF)
    if split:
        for kind in range(2):

            @pl.when(y == kind)
            def _():
                wait(kinds[kind])

        start(leaving)
    rows = w.shape[0]
    mine = dot(normed, pick(normed.shape[1], rows, lax.axis_index("roll") * rows)).astype(BF)
    part[...] = dot(mine, w[...])
    wait(leaving)


def table_kernel(split, own, other, gain, w_all, *rest):
    *outs, w, full, sem = rest
    copy = pltpu.make_async_copy(w_all.at[0], w, sem)
    copy.start()
    wide = own[...] + other[...].astype(F32)
    t = gelu(norm(wide, gain[0:1])).astype(BF)
    rows = w.shape[0]
    mine = dot(t, pick(t.shape[1], rows, lax.axis_index("roll") * rows)).astype(BF)
    copy.wait()
    full[...] = dot(mine, w[...])
    if split:
        core = lax.rem(lax.axis_index("roll"), 2)
        outs[0][...] = full[pl.ds(pl.multiple_of(core * SLOT, SLOT), SLOT)]
        outs[1][...] = full[pl.ds(pl.multiple_of((1 - core) * SLOT, SLOT), SLOT)].astype(BF)
    else:
        outs[0][...] = full[...]


def chip_copies(table, w_out, w_in, near_out, near_in, chip_out, chip_in, sem):
    _, core, _, _ = place()
    n, m = w_out.shape[1], w_in.shape[1]
    copies = [pltpu.make_async_copy(table, chip_out.at[2 * n :], sem)]
    for c, o, i in ((core, w_out, w_in), (1 - core, near_out, near_in)):
        copies.append(pltpu.make_async_copy(o.at[0], chip_out.at[pl.ds(pl.multiple_of(c * n, 16), n)], sem))
        copies.append(pltpu.make_async_copy(i.at[1], chip_in.at[pl.ds(pl.multiple_of(c * m, 16), m)], sem))
    return copies


def hot_kernel(split, span, near, *rest):
    copies = []
    if split:
        *w, hot5, hot1, chip_out, chip_in, sem = rest
        copies = chip_copies(*w, chip_out, chip_in, sem)
    else:
        hot5, hot1 = rest
    start(copies)
    codes = near[...]
    count = codes.shape[1]
    rows = hot5.shape[0]
    pos = span[0] - HALF * DIL0 + lax.broadcasted_iota(jnp.int32, codes.shape, 1)
    masked = jnp.where((pos >= 0) & (pos < span[1]), codes, -1)
    lanes = lax.broadcasted_iota(jnp.int32, (CODES, count), 0)
    taps = jnp.where(lanes == masked, 1.0, 0.0).T.astype(BF)
    for k in range(KERNEL):
        hot5[:, k * CODES : (k + 1) * CODES] = taps[k * DIL0 : k * DIL0 + rows]
    center = jnp.where(lanes == codes, 1.0, 0.0).T.astype(BF)
    hot1[...] = center[HALF * DIL0 : HALF * DIL0 + rows]
    wait(copies)


def rows_kernel(split, span, hot5, hot1, gain_out, gain_in, gain_mid, *rest):
    *w, ci, hid, tw, wo, wi, sem = rest
    depth = wo.shape[0] - CODES
    if split:
        core = lax.rem(lax.axis_index("roll"), 2)
        taps = [(t, core * SLOT, SLOT, 0) for t in w[:2]] + [(t, (1 - core) * SLOT, SLOT, 0) for t in w[2:4]]
        taps = [(t, at, n, i % 2) for i, (t, at, n, _) in enumerate(taps)]
        w = w[4:]
    else:
        taps = [(w[0], 0, CODES, 0)]
        table, *w = w[1:]
    first = [
        pltpu.make_async_copy(
            t.at[:, k * H : (k + 1) * H], tw.at[i, pl.ds(pl.multiple_of(k * CODES + at, 16), n)], sem.at[0]
        )
        for t, at, n, i in taps
        for k in range(KERNEL)
    ]
    start(first)
    if not split:
        first.append(pltpu.make_async_copy(table, wo.at[depth:], sem.at[0]))
        first[-1].start()
        out_copies = [pltpu.make_async_copy(w[0], wo.at[0:depth], sem.at[1])]
        in_copies = [pltpu.make_async_copy(w[1], wi, sem.at[2])]
        start(out_copies + in_copies)
    else:
        chip_out, chip_in = w[:2]
        parts, near_parts = w[2:6], w[6:10]
        x, core, y, z = place()
        n = depth // 4
        m = 2 * n
        half = n // 2
        row = pl.multiple_of(x * 2 * n, 16)
        out_copies = [
            pltpu.make_async_copy(chip_out.at[0 : 2 * n], wo.at[pl.ds(row, 2 * n)], sem.at[1]),
            pltpu.make_async_copy(chip_out.at[2 * n :], wo.at[depth:], sem.at[1]),
        ]
        row = pl.multiple_of(x * 2 * m, 16)
        in_copies = [pltpu.make_async_copy(chip_in, wi.at[pl.ds(row, 2 * m)], sem.at[2])]

        def far(outs, ins):
            out, into = [], []
            for c, of in ((core, parts), (1 - core, near_parts)):
                at = 2 * (1 - x) + c
                for p, zz in zip(outs, (z, 1 - z)):
                    row = pl.multiple_of(at * n + zz * half, 16)
                    out.append(pltpu.make_async_copy(of[p], wo.at[pl.ds(row, half)], sem.at[1]))
                for p, zz in zip(ins, (z, 1 - z)):
                    for j in range(2):
                        row = pl.multiple_of(at * m + zz * n + j * half, 16)
                        into.append(
                            pltpu.make_async_copy(of[p].at[:, j * H : (j + 1) * H], wi.at[pl.ds(row, half)], sem.at[2])
                        )
            return out, into

        start(out_copies + in_copies)
        far0, far1 = far((0, 2), (1, 3)), far((1, 3), (0, 2))

        @pl.when(y == 0)
        def _():
            start(far0[0] + far0[1])

        @pl.when(y == 1)
        def _():
            start(far1[0] + far1[1])

        out_copies += far0[0]
        in_copies += far0[1]

    rows = hid.shape[0] + 2 * EDGE
    cuts = [0, 512, rows]
    state = [None, None]

    def once(b, copies):
        if b == 0:
            wait(copies)

    def mix(b):
        if b == 0:
            wait(first)
            if split:
                tw[0] = (tw[0].astype(F32) + tw[1].astype(F32)).astype(BF)
        state[b] = dot(hot5[cuts[b] : cuts[b + 1]], tw[0])

    def act(b):
        state[b] = gelu(norm(state[b], gain_out[0:1])).astype(BF)

    def update(b):
        once(b, out_copies)
        lhs = jnp.concatenate([state[b], hot1[cuts[b] : cuts[b + 1]]], axis=1)
        state[b] = dot(lhs, wo[...]).astype(BF)

    def enter(b):
        hidden = state[b]
        lo, hi = max(cuts[b], EDGE), min(cuts[b + 1], rows - EDGE)
        hid[lo - EDGE : hi - EDGE] = hidden[lo - cuts[b] : hi - cuts[b]]
        state[b] = gelu(norm(hidden.astype(F32), gain_in[1:2])).astype(BF)

    def widen(b):
        once(b, in_copies)
        state[b] = dot(state[b], wi[...])

    def leave(b):
        n = cuts[b + 1] - cuts[b]
        pos = span[0] + cuts[b] + lax.broadcasted_iota(jnp.int32, (n, 1), 0)
        valid = jnp.where((pos >= 0) & (pos < span[1]), 1.0, 0.0)
        ci[cuts[b] : cuts[b + 1]] = (gelu(norm(state[b], gain_mid[1:2])) * valid).astype(BF)

    stagger((mix, act, update, enter, widen, leave))


def conv_copies(src, col, width, wt, per_tap, row, n, sem):
    copies = []
    done = 0
    while done < width:
        tap, inner = divmod(col + done, H)
        step = min(H - inner, width - done)
        copies.append(
            pltpu.make_async_copy(
                src.at[:, done : done + step],
                wt.at[pl.ds(pl.multiple_of(tap * per_tap + row, 16), n), inner : inner + step],
                sem,
            )
        )
        done += step
    return copies


HEAD = 256
TAIL = H - HEAD


def windows(ci, lo, hi, first, width):
    first = pl.multiple_of(first, 128)
    return jnp.concatenate(
        [ci[lo + k * DIL1 : hi + k * DIL1, pl.ds(first, width)] for k in range(KERNEL)], axis=1
    )


def head_kernel(ci, w_conv, near_conv, out, wt, sem):
    x, core, _, _ = place()
    n = w_conv.shape[1]
    short = HEAD - n
    done = None
    for xx in range(2):
        for cc in range(2):
            copies = []
            for c, w in ((cc, w_conv), (1 - cc, near_conv)):
                if c == xx:
                    copies += conv_copies(w.at[1], 0, KERNEL * H, wt, HEAD, short * xx, n, sem)
                else:
                    part = w.at[1, (n - short) * xx : (n - short) * xx + short]
                    copies += conv_copies(part, 0, KERNEL * H, wt, HEAD, n * (1 - xx), short, sem)
            done = copies

            @pl.when((x == xx) & (core == cc))
            def _():
                start(copies)

    rows = out.shape[0]
    half = 16 * ((rows + 31) // 32)
    for b, (lo, hi) in enumerate(((0, half), (half, rows))):
        lhs = windows(ci, lo, hi, x * TAIL, HEAD)
        if b == 0:
            wait(done)
        out[lo:hi] = dot(lhs, wt[...])


def last_kernel(split, ci, hid, gain_out, *rest):
    *w, out, wt, wo, sem = rest
    if not split:
        conv_in = conv_copies(w[0], 0, KERNEL * H, wt, H, 0, H, sem.at[0])
        out_in = [pltpu.make_async_copy(w[1], wo, sem.at[1])]
        start(conv_in + out_in)
        first, width = 0, H
    else:
        head, w_conv, w_out, near_conv, near_out = w[:5]
        parts, near_parts = w[5:9], w[9:13]
        x, core, y, z = place()
        n = w_out.shape[1]
        half = n // 2
        left = 2 * n - HEAD
        rest_cols = KERNEL * H - CUT_B
        first, width = (1 - x) * HEAD, TAIL
        out_in = []
        for c, o in ((core, w_out), (1 - core, near_out)):
            row = pl.multiple_of((2 * x + c) * n, 16)
            out_in.append(pltpu.make_async_copy(o.at[1], wo.at[pl.ds(row, n)], sem.at[1]))
        from_row = pl.multiple_of((n - left) * (1 - x), 16)
        own_in, near_in = [
            conv_copies(v.at[1, pl.ds(from_row, left)], 0, KERNEL * H, wt, TAIL, 2 * n * x, left, sem.at[0])
            for v in (w_conv, near_conv)
        ]

        @pl.when(core + x == 1)
        def _():
            start(own_in)

        @pl.when(core + x != 1)
        def _():
            start(near_in)

        def far(head, tail):
            cv, out = [], []
            for c, of in ((core, parts), (1 - core, near_parts)):
                at = c * n + left * (1 - x)
                for p, zz in zip(head, (z, 1 - z)):
                    cv += conv_copies(of[p], 0, CUT_A, wt, TAIL, at + zz * half, half, sem.at[0])
                for p, zz in zip(tail, (z, 1 - z)):
                    skip = CUT_A - CUT_B
                    cv += conv_copies(
                        of[p].at[:, skip:rest_cols], CUT_A, rest_cols - skip, wt, TAIL, at + zz * half, half, sem.at[0]
                    )
                    row = pl.multiple_of((2 * (1 - x) + c) * n + zz * half, 16)
                    out.append(pltpu.make_async_copy(of[p].at[:, rest_cols:], wo.at[pl.ds(row, half)], sem.at[1]))
            return cv, out

        start(out_in)
        far0, far1 = far((0, 2), (1, 3)), far((1, 3), (0, 2))

        @pl.when(y == 0)
        def _():
            start(far0[0] + far0[1])

        @pl.when(y == 1)
        def _():
            start(far1[0] + far1[1])

        conv_in = own_in + far0[0]
        out_in += far0[1]

    rows = out.shape[0]
    cuts = [0, 16 * ((rows + 31) // 32), rows]
    state = [None, None]

    def mix(b):
        lhs = windows(ci, cuts[b], cuts[b + 1], first, width)
        if b == 0:
            wait(conv_in)
        state[b] = dot(lhs, wt[...])
        if split:
            state[b] += head[cuts[b] : cuts[b + 1]]

    def act(b):
        state[b] = gelu(norm(state[b], gain_out[1:2])).astype(BF)

    def update(b):
        if b == 0:
            wait(out_in)
        hidden = hid[cuts[b] : cuts[b + 1]].astype(F32)
        out[cuts[b] : cuts[b + 1]] = (hidden + dot(state[b], wo[...])).astype(BF)

    stagger((mix, act, update))


def after(x, *deps):
    return lax.optimization_barrier((x, *deps))[0]


def per_device(tokens, breaks, lengths, embed_table, break_vec, gain_in, gain_mid, gain_out, w_in, conv_w, w_out):
    rows = tokens.shape[1]
    width = embed_table.shape[1]
    roll_at = lax.axis_index("roll")
    seq_at = lax.axis_index("seq")
    rolls = lax.axis_size("roll")
    seqs = lax.axis_size("seq")
    split = rolls == 4 and seqs % 4 == 0

    def core_swap(x):
        return lax.ppermute(x, "roll", [(i, i ^ 1) for i in range(rolls)])

    def x_swap(x):
        return lax.ppermute(x, "roll", [(i, i ^ 2) for i in range(rolls)])

    def seq_swap(x, bits):
        return lax.ppermute(x, "seq", [(i, i ^ bits) for i in range(seqs)])

    span = jnp.stack([(seq_at * rows).astype(jnp.int32) - EDGE, lengths[0]])
    wide_rows = rows + 2 * EDGE
    codes = tokens[0] + SLOT * breaks[0]

    shard = w_out.shape[1] // 2
    shapes = [((CODES, width), BF), ((CODES, H), F32)]
    if split:
        shapes += [((shard, width), BF), ((shard, CUT_A), BF), ((shard, CUT_A), BF)]
    table, part, *parts = pl.pallas_call(
        functools.partial(first_kernel, split),
        out_shape=[jax.ShapeDtypeStruct(n, t) for n, t in shapes],
        in_specs=[HBM] * 6,
        out_specs=[VMEM] * 2 + [HBM] * (len(shapes) - 2),
        scratch_shapes=[
            pltpu.VMEM(embed_table.shape, F32),
            pltpu.VMEM((width,), F32),
            pltpu.VMEM(gain_in.shape, F32),
            pltpu.VMEM(w_in.shape[1:], BF),
            pltpu.VMEM((CODES, width), F32),
            pltpu.SemaphoreType.DMA((3,)),
        ]
        + [pltpu.VMEM(n, t) for n, t in shapes[2:]],
        cost_estimate=FREE,
        compiler_params=params(60),
    )(embed_table, break_vec, gain_in, w_in, conv_w, w_out)

    if split:
        far_a = x_swap(parts[0])
        near_out, near_in = core_swap(w_out), core_swap(w_in)
        low = roll_at % 2 == 0
        ends = codes[rows - REACH :], codes[:REACH]
        theirs = core_swap(jnp.where(low, *ends[::-1]))
        own = part + after(core_swap(part), theirs)
        other = x_swap(own.astype(BF))
        far_b = x_swap(after(parts[1], other))
        pack = jnp.stack([jnp.where(low, *ends), theirs])
        places = [(s, r) for s in range(seqs) for r in range(rolls)]
        moves = [(s * rolls + r, (s + (1, -1)[r % 2]) % seqs * rolls + r) for s, r in places]
        moved = lax.ppermute(after(pack, own), ("seq", "roll"), moves)
        other = after(other, near_out, near_in, far_a)
    else:
        own = lax.psum(part, "roll")
        other = jnp.zeros((CODES, H), BF)
        pairs = [(i, i + 1) for i in range(seqs - 1)]
        before = lax.ppermute(codes[rows - REACH :], "seq", pairs)
        behind = lax.ppermute(codes[:REACH], "seq", [(j, i) for i, j in pairs])
    wide = KERNEL * H
    shapes = [(SLOT, F32), (SLOT, BF)] if split else [(CODES, F32)]
    taps = pl.pallas_call(
        functools.partial(table_kernel, split),
        out_shape=[jax.ShapeDtypeStruct((n, wide), t) for n, t in shapes],
        in_specs=[VMEM, VMEM, VMEM, HBM],
        out_specs=[VMEM] * len(shapes),
        scratch_shapes=[
            pltpu.VMEM(conv_w.shape[1:], BF),
            pltpu.VMEM((CODES, wide), F32),
            pltpu.SemaphoreType.DMA,
        ],
        cost_estimate=FREE,
        compiler_params=params(12),
    )(own, other, gain_mid, conv_w)
    if split:
        relay = after(far_a, taps[1])
        parts_a = [far_a] + [seq_swap(relay, b) for b in (1, 2, 3)]
        sent = (taps[0] + core_swap(taps[1]).astype(F32)).astype(BF)
        received = x_swap(sent)
    if split:
        came = core_swap(after(moved[1], sent))
        before, behind = jnp.where(low, moved[0], came), jnp.where(low, came, moved[0])
    spare = jnp.zeros((-(rows + 2 * REACH) % 128,), jnp.int32)
    near = jnp.concatenate([before, codes, behind, spare])[None]
    if split:
        near = after(near, sent)

    shapes = [(wide_rows, KERNEL * CODES), (wide_rows, CODES)]
    operands, scratch = [], []
    if split:
        operands = [table, w_out, w_in, near_out, near_in]
        shapes += [(4 * shard + CODES, width), (8 * shard, H)]
        scratch = [pltpu.SemaphoreType.DMA]
    hot5, hot1, *chip = pl.pallas_call(
        functools.partial(hot_kernel, split),
        out_shape=[jax.ShapeDtypeStruct(n, BF) for n in shapes],
        in_specs=[SMEM, VMEM] + [ANY] * len(operands),
        out_specs=[VMEM] * len(shapes),
        scratch_shapes=scratch,
        cost_estimate=FREE,
        compiler_params=params(16),
    )(span, near, *operands)

    if split:
        near_sent = core_swap(after(sent, hot1))
        received = after(received, hot1)
        near_received = core_swap(received)
        near_a = [core_swap(after(p, hot1, far_b)) for p in parts_a]
        relay = after(far_b, received)
        parts_b = [far_b, seq_swap(relay, 1), seq_swap(relay, 2), x_swap(after(parts[2], received))]
        weights_a = [sent, received, near_sent, near_received] + chip + parts_a + near_a
        near_conv = core_swap(after(conv_w, near_received, near_sent, *near_a))
    else:
        taps = lax.psum(taps[0], "roll").astype(BF)
        gather = lambda w: lax.all_gather(w, "roll", axis=0, tiled=True)
        weights_a, weights_b = [taps, table, gather(w_out[0]), gather(w_in[1])], [gather(conv_w[1]), gather(w_out[1])]

    ci, hid = pl.pallas_call(
        functools.partial(rows_kernel, split),
        out_shape=(
            jax.ShapeDtypeStruct((wide_rows, H), BF),
            jax.ShapeDtypeStruct((rows, width), BF),
        ),
        in_specs=[SMEM] + [VMEM] * 5 + [ANY] * len(weights_a),
        out_specs=(VMEM, VMEM),
        scratch_shapes=[
            pltpu.VMEM((2, KERNEL * CODES, H), BF),
            pltpu.VMEM((H + CODES, width), BF),
            pltpu.VMEM((width, H), BF),
            pltpu.SemaphoreType.DMA((3,)),
        ],
        cost_estimate=FREE,
        compiler_params=params(30),
    )(span, hot5, hot1, gain_out, gain_in, gain_mid, *weights_a)

    if split:
        near_b = [core_swap(after(p, ci)) for p in parts_b]
        head = pl.pallas_call(
            head_kernel,
            out_shape=jax.ShapeDtypeStruct((rows, H), F32),
            in_specs=[VMEM, HBM, ANY],
            out_specs=VMEM,
            scratch_shapes=[pltpu.VMEM((KERNEL * HEAD, H), BF), pltpu.SemaphoreType.DMA],
            cost_estimate=FREE,
            compiler_params=params(16),
        )(ci, conv_w, near_conv)
        weights_b = [head, conv_w, w_out, near_conv, near_out] + parts_b + near_b
    out = pl.pallas_call(
        functools.partial(last_kernel, split),
        out_shape=jax.ShapeDtypeStruct((rows, width), BF),
        in_specs=[VMEM] * 3
        + [HBM if w is w_out or w is conv_w else VMEM if split and w is head else ANY for w in weights_b],
        out_specs=VMEM,
        scratch_shapes=[
            pltpu.VMEM((KERNEL * (TAIL if split else H), H), BF),
            pltpu.VMEM((H, width), BF),
            pltpu.SemaphoreType.DMA((2,)),
        ],
        cost_estimate=FREE,
        compiler_params=params(24),
    )(ci, hid, gain_out, *weights_b)
    return out[None]


def solution(mesh):
    placed = (
        P("roll", "seq"),
        P("roll", "seq"),
        P("roll"),
        P(),
        P(),
        P(),
        P(),
        P(),
        P(None, "roll", None),
        P(None, "roll", None),
        P(None, "roll", None),
    )
    return jax.shard_map(
        per_device, mesh=mesh, in_specs=placed, out_specs=P("roll", "seq", None), check_vma=False
    )
```

```python
import functools

import jax
import jax.numpy as jnp
from jax import lax
from jax.experimental import pallas as pl
from jax.experimental.pallas import tpu as pltpu
from jax.sharding import PartitionSpec as P

H = 640
KERNEL = 5
VOCAB = 30
SLOT = 32
CODES = 2 * SLOT
BASE_DILATION = 64
DIL0 = BASE_DILATION
DIL1 = 2 * BASE_DILATION
HALF = KERNEL // 2
EDGE = HALF * DIL1
REACH = EDGE + HALF * DIL0
BF = jnp.bfloat16
F32 = jnp.float32
VMEM = pl.BlockSpec(memory_space=pltpu.VMEM)
SMEM = pl.BlockSpec(memory_space=pltpu.SMEM)
ANY = pl.BlockSpec(memory_space=pl.ANY)
HBM = pl.BlockSpec(memory_space=pltpu.HBM)
FREE = pl.CostEstimate(flops=0, bytes_accessed=0, transcendentals=0)
CUT_A = 18 * 128
CUT_B = 17 * 128


def params(mib):
    return pltpu.CompilerParams(vmem_limit_bytes=mib * 1024 * 1024)


def gelu(x):
    return (0.5 * x) * (1.0 + lax.erf(x * 0.5**0.5))


def norm(x, gain):
    center = jnp.mean(x, axis=-1, keepdims=True)
    d = x - center
    spread = jnp.mean(d * d, axis=-1, keepdims=True)
    return d * lax.rsqrt(spread + 1e-5) * gain


def dot(a, b):
    return jnp.dot(a, b, preferred_element_type=F32)


def place():
    roll, seq = lax.axis_index("roll"), lax.axis_index("seq")
    return lax.div(roll, 2), lax.rem(roll, 2), lax.rem(seq, 2), lax.rem(lax.div(seq, 2), 2)


def start(copies):
    for c in copies:
        c.start()


def wait(copies):
    for c in copies:
        c.wait()


def stagger(stages):
    for t in range(len(stages) + 1):
        for b in range(2):
            if 0 <= t - b < len(stages):
                stages[t - b](b)


def pick(rows, columns, first):
    i = lax.broadcasted_iota(jnp.int32, (rows, columns), 0)
    j = lax.broadcasted_iota(jnp.int32, (rows, columns), 1)
    return jnp.where(i == j + first, 1.0, 0.0).astype(BF)


def part_copies(y_is_one, row_bit, w_in, conv_w, w_out, a, b, sem):
    n = b.shape[0]
    r = pl.multiple_of(row_bit * n, 16)
    r2 = pl.multiple_of(row_bit * 2 * n, 16)
    rest = conv_w.shape[2] - CUT_B
    if y_is_one:
        pairs = [
            (conv_w.at[1, pl.ds(r, n), CUT_B:], b.at[:, 0:rest]),
            (w_out.at[1, pl.ds(r, n)], b.at[:, rest:]),
        ]
        if a is not None:
            pairs += [
                (w_in.at[1, pl.ds(r2, n)], a.at[:, 0:H]),
                (w_in.at[1, pl.ds(r2 + n, n)], a.at[:, H : 2 * H]),
            ]
    else:
        pairs = [(conv_w.at[1, pl.ds(r, n), 0:CUT_A], b)]
        if a is not None:
            pairs.append((w_out.at[0, pl.ds(r, n)], a))
    return [pltpu.make_async_copy(s, d, sem) for s, d in pairs]


def first_kernel(split, embed, brk, gain, w_in, conv_w, w_out, table, part, *rest):
    count = 3 if split else 0
    parts, rest = rest[:count], rest[count:]
    emb, bv, g, w, full, sem, *held = rest
    copies = [
        pltpu.make_async_copy(s, d, sem.at[0])
        for s, d in ((embed, emb), (brk, bv), (gain, g), (w_in.at[0], w))
    ]
    start(copies)
    leaving = []
    if split:
        _, _, y, z = place()
        kinds = []
        for kind in range(2):
            kinds.append(
                part_copies(kind == 1, z, w_in, conv_w, w_out, held[0], held[1], sem.at[1])
                + part_copies(kind == 0, 1 - z, w_in, conv_w, w_out, None, held[2], sem.at[1])
            )

            @pl.when(y == kind)
            def _():
                start(kinds[kind])

        leaving = [pltpu.make_async_copy(s, d, sem.at[2]) for s, d in zip(held, parts)]

    wait(copies)
    full[...] = jnp.zeros_like(full)
    full[0:VOCAB] = emb[...]
    full[SLOT : SLOT + VOCAB] = emb[...] + bv[...][None, :]
    hidden = full[...].astype(BF)
    table[...] = hidden
    normed = gelu(norm(hidden.astype(F32), g[0:1])).astype(BF)
    if split:
        for kind in range(2):

            @pl.when(y == kind)
            def _():
                wait(kinds[kind])

        start(leaving)
    rows = w.shape[0]
    mine = dot(normed, pick(normed.shape[1], rows, lax.axis_index("roll") * rows)).astype(BF)
    part[...] = dot(mine, w[...])
    wait(leaving)


def table_kernel(split, own, other, gain, w_all, *rest):
    *outs, w, full, sem = rest
    copy = pltpu.make_async_copy(w_all.at[0], w, sem)
    copy.start()
    wide = own[...] + other[...].astype(F32)
    t = gelu(norm(wide, gain[0:1])).astype(BF)
    rows = w.shape[0]
    mine = dot(t, pick(t.shape[1], rows, lax.axis_index("roll") * rows)).astype(BF)
    copy.wait()
    full[...] = dot(mine, w[...])
    if split:
        core = lax.rem(lax.axis_index("roll"), 2)
        outs[0][...] = full[pl.ds(pl.multiple_of(core * SLOT, SLOT), SLOT)]
        outs[1][...] = full[pl.ds(pl.multiple_of((1 - core) * SLOT, SLOT), SLOT)].astype(BF)
    else:
        outs[0][...] = full[...]


def chip_copies(table, w_out, w_in, near_out, near_in, chip_out, chip_in, sem):
    _, core, _, _ = place()
    n, m = w_out.shape[1], w_in.shape[1]
    copies = [pltpu.make_async_copy(table, chip_out.at[2 * n :], sem)]
    for c, o, i in ((core, w_out, w_in), (1 - core, near_out, near_in)):
        copies.append(pltpu.make_async_copy(o.at[0], chip_out.at[pl.ds(pl.multiple_of(c * n, 16), n)], sem))
        copies.append(pltpu.make_async_copy(i.at[1], chip_in.at[pl.ds(pl.multiple_of(c * m, 16), m)], sem))
    return copies


def hot_kernel(split, span, near, *rest):
    copies = []
    if split:
        *w, hot5, hot1, chip_out, chip_in, sem = rest
        copies = chip_copies(*w, chip_out, chip_in, sem)
    else:
        hot5, hot1 = rest
    start(copies)
    codes = near[...]
    count = codes.shape[1]
    rows = hot5.shape[0]
    pos = span[0] - HALF * DIL0 + lax.broadcasted_iota(jnp.int32, codes.shape, 1)
    masked = jnp.where((pos >= 0) & (pos < span[1]), codes, -1)
    lanes = lax.broadcasted_iota(jnp.int32, (CODES, count), 0)
    taps = jnp.where(lanes == masked, 1.0, 0.0).T.astype(BF)
    for k in range(KERNEL):
        hot5[:, k * CODES : (k + 1) * CODES] = taps[k * DIL0 : k * DIL0 + rows]
    center = jnp.where(lanes == codes, 1.0, 0.0).T.astype(BF)
    hot1[...] = center[HALF * DIL0 : HALF * DIL0 + rows]
    wait(copies)


def rows_kernel(split, span, hot5, hot1, gain_out, gain_in, gain_mid, *rest):
    *w, ci, hid, tw, wo, wi, sem = rest
    depth = wo.shape[0] - CODES
    if split:
        core = lax.rem(lax.axis_index("roll"), 2)
        taps = [(t, core * SLOT, SLOT, 0) for t in w[:2]] + [(t, (1 - core) * SLOT, SLOT, 0) for t in w[2:4]]
        taps = [(t, at, n, i % 2) for i, (t, at, n, _) in enumerate(taps)]
        w = w[4:]
    else:
        taps = [(w[0], 0, CODES, 0)]
        table, *w = w[1:]
    first = [
        pltpu.make_async_copy(
            t.at[:, k * H : (k + 1) * H], tw.at[i, pl.ds(pl.multiple_of(k * CODES + at, 16), n)], sem.at[0]
        )
        for t, at, n, i in taps
        for k in range(KERNEL)
    ]
    start(first)
    if not split:
        first.append(pltpu.make_async_copy(table, wo.at[depth:], sem.at[0]))
        first[-1].start()
        out_copies = [pltpu.make_async_copy(w[0], wo.at[0:depth], sem.at[1])]
        in_copies = [pltpu.make_async_copy(w[1], wi, sem.at[2])]
        start(out_copies + in_copies)
    else:
        chip_out, chip_in = w[:2]
        parts, near_parts = w[2:6], w[6:10]
        x, core, y, z = place()
        n = depth // 4
        m = 2 * n
        half = n // 2
        row = pl.multiple_of(x * 2 * n, 16)
        out_copies = [
            pltpu.make_async_copy(chip_out.at[0 : 2 * n], wo.at[pl.ds(row, 2 * n)], sem.at[1]),
            pltpu.make_async_copy(chip_out.at[2 * n :], wo.at[depth:], sem.at[1]),
        ]
        row = pl.multiple_of(x * 2 * m, 16)
        in_copies = [pltpu.make_async_copy(chip_in, wi.at[pl.ds(row, 2 * m)], sem.at[2])]

        def far(outs, ins):
            out, into = [], []
            for c, of in ((core, parts), (1 - core, near_parts)):
                at = 2 * (1 - x) + c
                for p, zz in zip(outs, (z, 1 - z)):
                    row = pl.multiple_of(at * n + zz * half, 16)
                    out.append(pltpu.make_async_copy(of[p], wo.at[pl.ds(row, half)], sem.at[1]))
                for p, zz in zip(ins, (z, 1 - z)):
                    for j in range(2):
                        row = pl.multiple_of(at * m + zz * n + j * half, 16)
                        into.append(
                            pltpu.make_async_copy(of[p].at[:, j * H : (j + 1) * H], wi.at[pl.ds(row, half)], sem.at[2])
                        )
            return out, into

        start(out_copies + in_copies)
        far0, far1 = far((0, 2), (1, 3)), far((1, 3), (0, 2))

        @pl.when(y == 0)
        def _():
            start(far0[0] + far0[1])

        @pl.when(y == 1)
        def _():
            start(far1[0] + far1[1])

        out_copies += far0[0]
        in_copies += far0[1]

    rows = hid.shape[0] + 2 * EDGE
    cuts = [0, 512, rows]
    state = [None, None]

    def once(b, copies):
        if b == 0:
            wait(copies)

    def mix(b):
        if b == 0:
            wait(first)
            if split:
                tw[0] = (tw[0].astype(F32) + tw[1].astype(F32)).astype(BF)
        state[b] = dot(hot5[cuts[b] : cuts[b + 1]], tw[0])

    def act(b):
        state[b] = gelu(norm(state[b], gain_out[0:1])).astype(BF)

    def update(b):
        once(b, out_copies)
        lhs = jnp.concatenate([state[b], hot1[cuts[b] : cuts[b + 1]]], axis=1)
        state[b] = dot(lhs, wo[...]).astype(BF)

    def enter(b):
        hidden = state[b]
        lo, hi = max(cuts[b], EDGE), min(cuts[b + 1], rows - EDGE)
        hid[lo - EDGE : hi - EDGE] = hidden[lo - cuts[b] : hi - cuts[b]]
        state[b] = gelu(norm(hidden.astype(F32), gain_in[1:2])).astype(BF)

    def widen(b):
        once(b, in_copies)
        state[b] = dot(state[b], wi[...])

    def leave(b):
        n = cuts[b + 1] - cuts[b]
        pos = span[0] + cuts[b] + lax.broadcasted_iota(jnp.int32, (n, 1), 0)
        valid = jnp.where((pos >= 0) & (pos < span[1]), 1.0, 0.0)
        ci[cuts[b] : cuts[b + 1]] = (gelu(norm(state[b], gain_mid[1:2])) * valid).astype(BF)

    stagger((mix, act, update, enter, widen, leave))


def conv_copies(src, col, width, wt, per_tap, row, n, sem):
    copies = []
    done = 0
    while done < width:
        tap, inner = divmod(col + done, H)
        step = min(H - inner, width - done)
        copies.append(
            pltpu.make_async_copy(
                src.at[:, done : done + step],
                wt.at[pl.ds(pl.multiple_of(tap * per_tap + row, 16), n), inner : inner + step],
                sem,
            )
        )
        done += step
    return copies


HEAD = 256
TAIL = H - HEAD


def windows(ci, lo, hi, first, width):
    first = pl.multiple_of(first, 128)
    return jnp.concatenate(
        [ci[lo + k * DIL1 : hi + k * DIL1, pl.ds(first, width)] for k in range(KERNEL)], axis=1
    )


def head_kernel(ci, w_conv, near_conv, out, wt, sem):
    x, core, _, _ = place()
    n = w_conv.shape[1]
    short = HEAD - n
    done = None
    for xx in range(2):
        for cc in range(2):
            copies = []
            for c, w in ((cc, w_conv), (1 - cc, near_conv)):
                if c == xx:
                    copies += conv_copies(w.at[1], 0, KERNEL * H, wt, HEAD, short * xx, n, sem)
                else:
                    part = w.at[1, (n - short) * xx : (n - short) * xx + short]
                    copies += conv_copies(part, 0, KERNEL * H, wt, HEAD, n * (1 - xx), short, sem)
            done = copies

            @pl.when((x == xx) & (core == cc))
            def _():
                start(copies)

    rows = out.shape[0]
    half = 16 * ((rows + 31) // 32)
    for b, (lo, hi) in enumerate(((0, half), (half, rows))):
        lhs = windows(ci, lo, hi, x * TAIL, HEAD)
        if b == 0:
            wait(done)
        out[lo:hi] = dot(lhs, wt[...])


def last_kernel(split, ci, hid, gain_out, *rest):
    *w, out, wt, wo, sem = rest
    if not split:
        conv_in = conv_copies(w[0], 0, KERNEL * H, wt, H, 0, H, sem.at[0])
        out_in = [pltpu.make_async_copy(w[1], wo, sem.at[1])]
        start(conv_in + out_in)
        first, width = 0, H
    else:
        head, w_conv, w_out, near_conv, near_out = w[:5]
        parts, near_parts = w[5:9], w[9:13]
        x, core, y, z = place()
        n = w_out.shape[1]
        half = n // 2
        left = 2 * n - HEAD
        rest_cols = KERNEL * H - CUT_B
        first, width = (1 - x) * HEAD, TAIL
        out_in = []
        for c, o in ((core, w_out), (1 - core, near_out)):
            row = pl.multiple_of((2 * x + c) * n, 16)
            out_in.append(pltpu.make_async_copy(o.at[1], wo.at[pl.ds(row, n)], sem.at[1]))
        from_row = pl.multiple_of((n - left) * (1 - x), 16)
        own_in, near_in = [
            conv_copies(v.at[1, pl.ds(from_row, left)], 0, KERNEL * H, wt, TAIL, 2 * n * x, left, sem.at[0])
            for v in (w_conv, near_conv)
        ]

        @pl.when(core + x == 1)
        def _():
            start(own_in)

        @pl.when(core + x != 1)
        def _():
            start(near_in)

        def far(head, tail):
            cv, out = [], []
            for c, of in ((core, parts), (1 - core, near_parts)):
                at = c * n + left * (1 - x)
                for p, zz in zip(head, (z, 1 - z)):
                    cv += conv_copies(of[p], 0, CUT_A, wt, TAIL, at + zz * half, half, sem.at[0])
                for p, zz in zip(tail, (z, 1 - z)):
                    skip = CUT_A - CUT_B
                    cv += conv_copies(
                        of[p].at[:, skip:rest_cols], CUT_A, rest_cols - skip, wt, TAIL, at + zz * half, half, sem.at[0]
                    )
                    row = pl.multiple_of((2 * (1 - x) + c) * n + zz * half, 16)
                    out.append(pltpu.make_async_copy(of[p].at[:, rest_cols:], wo.at[pl.ds(row, half)], sem.at[1]))
            return cv, out

        start(out_in)
        far0, far1 = far((0, 2), (1, 3)), far((1, 3), (0, 2))

        @pl.when(y == 0)
        def _():
            start(far0[0] + far0[1])

        @pl.when(y == 1)
        def _():
            start(far1[0] + far1[1])

        conv_in = own_in + far0[0]
        out_in += far0[1]

    rows = out.shape[0]
    cuts = [0, 16 * ((rows + 31) // 32), rows]
    state = [None, None]

    def mix(b):
        lhs = windows(ci, cuts[b], cuts[b + 1], first, width)
        if b == 0:
            wait(conv_in)
        state[b] = dot(lhs, wt[...])
        if split:
            state[b] += head[cuts[b] : cuts[b + 1]]

    def act(b):
        state[b] = gelu(norm(state[b], gain_out[1:2])).astype(BF)

    def update(b):
        if b == 0:
            wait(out_in)
        hidden = hid[cuts[b] : cuts[b + 1]].astype(F32)
        out[cuts[b] : cuts[b + 1]] = (hidden + dot(state[b], wo[...])).astype(BF)

    stagger((mix, act, update))


def after(x, *deps):
    return lax.optimization_barrier((x, *deps))[0]


def per_device(tokens, breaks, lengths, embed_table, break_vec, gain_in, gain_mid, gain_out, w_in, conv_w, w_out):
    rows = tokens.shape[1]
    width = embed_table.shape[1]
    roll_at = lax.axis_index("roll")
    seq_at = lax.axis_index("seq")
    rolls = lax.axis_size("roll")
    seqs = lax.axis_size("seq")
    split = rolls == 4 and seqs % 4 == 0

    def core_swap(x):
        return lax.ppermute(x, "roll", [(i, i ^ 1) for i in range(rolls)])

    def x_swap(x):
        return lax.ppermute(x, "roll", [(i, i ^ 2) for i in range(rolls)])

    def seq_swap(x, bits):
        return lax.ppermute(x, "seq", [(i, i ^ bits) for i in range(seqs)])

    span = jnp.stack([(seq_at * rows).astype(jnp.int32) - EDGE, lengths[0]])
    wide_rows = rows + 2 * EDGE
    codes = tokens[0] + SLOT * breaks[0]

    shard = w_out.shape[1] // 2
    shapes = [((CODES, width), BF), ((CODES, H), F32)]
    if split:
        shapes += [((shard, width), BF), ((shard, CUT_A), BF), ((shard, CUT_A), BF)]
    table, part, *parts = pl.pallas_call(
        functools.partial(first_kernel, split),
        out_shape=[jax.ShapeDtypeStruct(n, t) for n, t in shapes],
        in_specs=[HBM] * 6,
        out_specs=[VMEM] * 2 + [HBM] * (len(shapes) - 2),
        scratch_shapes=[
            pltpu.VMEM(embed_table.shape, F32),
            pltpu.VMEM((width,), F32),
            pltpu.VMEM(gain_in.shape, F32),
            pltpu.VMEM(w_in.shape[1:], BF),
            pltpu.VMEM((CODES, width), F32),
            pltpu.SemaphoreType.DMA((3,)),
        ]
        + [pltpu.VMEM(n, t) for n, t in shapes[2:]],
        cost_estimate=FREE,
        compiler_params=params(60),
    )(embed_table, break_vec, gain_in, w_in, conv_w, w_out)

    if split:
        far_a = x_swap(parts[0])
        near_out, near_in = core_swap(w_out), core_swap(w_in)
        low = roll_at % 2 == 0
        ends = codes[rows - REACH :], codes[:REACH]
        theirs = core_swap(jnp.where(low, *ends[::-1]))
        own = part + after(core_swap(part), theirs)
        other = x_swap(own.astype(BF))
        far_b = x_swap(after(parts[1], other))
        pack = jnp.stack([jnp.where(low, *ends), theirs])
        places = [(s, r) for s in range(seqs) for r in range(rolls)]
        moves = [(s * rolls + r, (s + (1, -1)[r % 2]) % seqs * rolls + r) for s, r in places]
        moved = lax.ppermute(after(pack, own), ("seq", "roll"), moves)
        other = after(other, near_out, near_in, far_a)
    else:
        own = lax.psum(part, "roll")
        other = jnp.zeros((CODES, H), BF)
        pairs = [(i, i + 1) for i in range(seqs - 1)]
        before = lax.ppermute(codes[rows - REACH :], "seq", pairs)
        behind = lax.ppermute(codes[:REACH], "seq", [(j, i) for i, j in pairs])
    wide = KERNEL * H
    shapes = [(SLOT, F32), (SLOT, BF)] if split else [(CODES, F32)]
    taps = pl.pallas_call(
        functools.partial(table_kernel, split),
        out_shape=[jax.ShapeDtypeStruct((n, wide), t) for n, t in shapes],
        in_specs=[VMEM, VMEM, VMEM, HBM],
        out_specs=[VMEM] * len(shapes),
        scratch_shapes=[
            pltpu.VMEM(conv_w.shape[1:], BF),
            pltpu.VMEM((CODES, wide), F32),
            pltpu.SemaphoreType.DMA,
        ],
        cost_estimate=FREE,
        compiler_params=params(12),
    )(own, other, gain_mid, conv_w)
    if split:
        came = core_swap(after(moved[1], taps[1]))
        before, behind = jnp.where(low, moved[0], came), jnp.where(low, came, moved[0])
        relay = after(far_a, taps[1])
        parts_a = [far_a] + [seq_swap(relay, b) for b in (1, 2, 3)]
        sent = (taps[0] + after(core_swap(taps[1]), before, behind).astype(F32)).astype(BF)
        received = x_swap(sent)
    spare = jnp.zeros((-(rows + 2 * REACH) % 128,), jnp.int32)
    near = jnp.concatenate([before, codes, behind, spare])[None]
    if split:
        near = after(near, sent)

    shapes = [(wide_rows, KERNEL * CODES), (wide_rows, CODES)]
    operands, scratch = [], []
    if split:
        operands = [table, w_out, w_in, near_out, near_in]
        shapes += [(4 * shard + CODES, width), (8 * shard, H)]
        scratch = [pltpu.SemaphoreType.DMA]
    hot5, hot1, *chip = pl.pallas_call(
        functools.partial(hot_kernel, split),
        out_shape=[jax.ShapeDtypeStruct(n, BF) for n in shapes],
        in_specs=[SMEM, VMEM] + [ANY] * len(operands),
        out_specs=[VMEM] * len(shapes),
        scratch_shapes=scratch,
        cost_estimate=FREE,
        compiler_params=params(16),
    )(span, near, *operands)

    if split:
        near_sent = core_swap(after(sent, hot1))
        received = after(received, hot1)
        near_received = core_swap(received)
        near_a = [core_swap(after(p, hot1, far_b)) for p in parts_a]
        relay = after(far_b, received)
        parts_b = [far_b, seq_swap(relay, 1), seq_swap(relay, 2), x_swap(after(parts[2], received))]
        weights_a = [sent, received, near_sent, near_received] + chip + parts_a + near_a
        near_conv = core_swap(after(conv_w, near_received, near_sent, *near_a))
    else:
        taps = lax.psum(taps[0], "roll").astype(BF)
        gather = lambda w: lax.all_gather(w, "roll", axis=0, tiled=True)
        weights_a, weights_b = [taps, table, gather(w_out[0]), gather(w_in[1])], [gather(conv_w[1]), gather(w_out[1])]

    ci, hid = pl.pallas_call(
        functools.partial(rows_kernel, split),
        out_shape=(
            jax.ShapeDtypeStruct((wide_rows, H), BF),
            jax.ShapeDtypeStruct((rows, width), BF),
        ),
        in_specs=[SMEM] + [VMEM] * 5 + [ANY] * len(weights_a),
        out_specs=(VMEM, VMEM),
        scratch_shapes=[
            pltpu.VMEM((2, KERNEL * CODES, H), BF),
            pltpu.VMEM((H + CODES, width), BF),
            pltpu.VMEM((width, H), BF),
            pltpu.SemaphoreType.DMA((3,)),
        ],
        cost_estimate=FREE,
        compiler_params=params(30),
    )(span, hot5, hot1, gain_out, gain_in, gain_mid, *weights_a)

    if split:
        near_b = [core_swap(after(p, ci)) for p in parts_b]
        head = pl.pallas_call(
            head_kernel,
            out_shape=jax.ShapeDtypeStruct((rows, H), F32),
            in_specs=[VMEM, HBM, ANY],
            out_specs=VMEM,
            scratch_shapes=[pltpu.VMEM((KERNEL * HEAD, H), BF), pltpu.SemaphoreType.DMA],
            cost_estimate=FREE,
            compiler_params=params(16),
        )(ci, conv_w, near_conv)
        weights_b = [head, conv_w, w_out, near_conv, near_out] + parts_b + near_b
    out = pl.pallas_call(
        functools.partial(last_kernel, split),
        out_shape=jax.ShapeDtypeStruct((rows, width), BF),
        in_specs=[VMEM] * 3
        + [HBM if w is w_out or w is conv_w else VMEM if split and w is head else ANY for w in weights_b],
        out_specs=VMEM,
        scratch_shapes=[
            pltpu.VMEM((KERNEL * (TAIL if split else H), H), BF),
            pltpu.VMEM((H, width), BF),
            pltpu.SemaphoreType.DMA((2,)),
        ],
        cost_estimate=FREE,
        compiler_params=params(24),
    )(ci, hid, gain_out, *weights_b)
    return out[None]


def solution(mesh):
    placed = (
        P("roll", "seq"),
        P("roll", "seq"),
        P("roll"),
        P(),
        P(),
        P(),
        P(),
        P(),
        P(None, "roll", None),
        P(None, "roll", None),
        P(None, "roll", None),
    )
    return jax.shard_map(
        per_device, mesh=mesh, in_specs=placed, out_specs=P("roll", "seq", None), check_vma=False
    )
```

```python
import functools

import jax
import jax.numpy as jnp
from jax import lax
from jax.experimental import pallas as pl
from jax.experimental.pallas import tpu as pltpu
from jax.sharding import PartitionSpec as P

H = 640
KERNEL = 5
VOCAB = 30
SLOT = 32
CODES = 2 * SLOT
BASE_DILATION = 64
DIL0 = BASE_DILATION
DIL1 = 2 * BASE_DILATION
HALF = KERNEL // 2
EDGE = HALF * DIL1
REACH = EDGE + HALF * DIL0
BF = jnp.bfloat16
F32 = jnp.float32
VMEM = pl.BlockSpec(memory_space=pltpu.VMEM)
SMEM = pl.BlockSpec(memory_space=pltpu.SMEM)
ANY = pl.BlockSpec(memory_space=pl.ANY)
HBM = pl.BlockSpec(memory_space=pltpu.HBM)
FREE = pl.CostEstimate(flops=0, bytes_accessed=0, transcendentals=0)
CUT_A = 18 * 128
CUT_B = 17 * 128


def params(mib):
    return pltpu.CompilerParams(vmem_limit_bytes=mib * 1024 * 1024)


def gelu(x):
    return (0.5 * x) * (1.0 + lax.erf(x * 0.5**0.5))


def norm(x, gain):
    center = jnp.mean(x, axis=-1, keepdims=True)
    d = x - center
    spread = jnp.mean(d * d, axis=-1, keepdims=True)
    return d * lax.rsqrt(spread + 1e-5) * gain


def dot(a, b):
    return jnp.dot(a, b, preferred_element_type=F32)


def place():
    roll, seq = lax.axis_index("roll"), lax.axis_index("seq")
    return lax.div(roll, 2), lax.rem(roll, 2), lax.rem(seq, 2), lax.rem(lax.div(seq, 2), 2)


def start(copies):
    for c in copies:
        c.start()


def wait(copies):
    for c in copies:
        c.wait()


def stagger(stages):
    for t in range(len(stages) + 1):
        for b in range(2):
            if 0 <= t - b < len(stages):
                stages[t - b](b)


def pick(rows, columns, first):
    i = lax.broadcasted_iota(jnp.int32, (rows, columns), 0)
    j = lax.broadcasted_iota(jnp.int32, (rows, columns), 1)
    return jnp.where(i == j + first, 1.0, 0.0).astype(BF)


def part_copies(y_is_one, row_bit, w_in, conv_w, w_out, a, b, sem):
    n = b.shape[0]
    r = pl.multiple_of(row_bit * n, 16)
    r2 = pl.multiple_of(row_bit * 2 * n, 16)
    rest = conv_w.shape[2] - CUT_B
    if y_is_one:
        pairs = [
            (conv_w.at[1, pl.ds(r, n), CUT_B:], b.at[:, 0:rest]),
            (w_out.at[1, pl.ds(r, n)], b.at[:, rest:]),
        ]
        if a is not None:
            pairs += [
                (w_in.at[1, pl.ds(r2, n)], a.at[:, 0:H]),
                (w_in.at[1, pl.ds(r2 + n, n)], a.at[:, H : 2 * H]),
            ]
    else:
        pairs = [(conv_w.at[1, pl.ds(r, n), 0:CUT_A], b)]
        if a is not None:
            pairs.append((w_out.at[0, pl.ds(r, n)], a))
    return [pltpu.make_async_copy(s, d, sem) for s, d in pairs]


def parts_kernel(w_in, conv_w, w_out, *rest):
    parts, held, sem = rest[:3], rest[3:6], rest[6]
    _, _, y, z = place()
    for kind in range(2):
        copies = part_copies(kind == 1, z, w_in, conv_w, w_out, held[0], held[1], sem.at[0])
        copies += part_copies(kind == 0, 1 - z, w_in, conv_w, w_out, None, held[2], sem.at[0])

        @pl.when(y == kind)
        def _():
            start(copies)
            wait(copies)

    leaving = [pltpu.make_async_copy(s, d, sem.at[1]) for s, d in zip(held, parts)]
    start(leaving)
    wait(leaving)


def two_shares(split, w_all, w, sem):
    if not split:
        return [pltpu.make_async_copy(w_all[0].at[0], w, sem)]
    _, core, _, _ = place()
    n = w_all[0].shape[1]
    return [
        pltpu.make_async_copy(v.at[0], w.at[pl.ds(pl.multiple_of(c * n, 16), n)], sem)
        for v, c in zip(w_all, (core, 1 - core))
    ]


def chosen(split, x, rows):
    at = place()[0] if split else lax.axis_index("roll")
    return dot(x, pick(x.shape[1], rows, at * rows)).astype(BF)


def embed_kernel(split, embed, brk, gain, *rest):
    *w_all, table, part, sent, emb, bv, g, w, full, sem = rest
    copies = [pltpu.make_async_copy(s, d, sem.at[0]) for s, d in ((embed, emb), (brk, bv), (gain, g))]
    shares = two_shares(split, w_all, w, sem.at[1])
    start(copies + shares)
    wait(copies)
    full[...] = jnp.zeros_like(full)
    full[0:VOCAB] = emb[...]
    full[SLOT : SLOT + VOCAB] = emb[...] + bv[...][None, :]
    hidden = full[...].astype(BF)
    table[...] = hidden
    normed = gelu(norm(hidden.astype(F32), g[0:1])).astype(BF)
    mine = chosen(split, normed, w.shape[0])
    wait(shares)
    total = dot(mine, w[...])
    part[...] = total
    sent[...] = total.astype(BF)


def table_kernel(split, own, other, gain, *rest):
    *w_all, out, w, rows, sem = rest
    shares = two_shares(split, w_all, w, sem)
    start(shares)
    wide = own[...] + other[...].astype(F32)
    t = gelu(norm(wide, gain[0:1])).astype(BF)
    rows[...] = chosen(split, t, w.shape[0]).astype(F32)
    if split:
        _, core, _, _ = place()
        mine = rows[pl.ds(pl.multiple_of(core * SLOT, SLOT), SLOT)]
    else:
        mine = rows[...]
    wait(shares)
    out[...] = dot(mine.astype(BF), w[...]).astype(out.dtype)


def chip_copies(table, w_out, w_in, near_out, near_in, chip_out, chip_in, sem):
    _, core, _, _ = place()
    n, m = w_out.shape[1], w_in.shape[1]
    copies = [pltpu.make_async_copy(table, chip_out.at[2 * n :], sem)]
    for c, o, i in ((core, w_out, w_in), (1 - core, near_out, near_in)):
        copies.append(pltpu.make_async_copy(o.at[0], chip_out.at[pl.ds(pl.multiple_of(c * n, 16), n)], sem))
        copies.append(pltpu.make_async_copy(i.at[1], chip_in.at[pl.ds(pl.multiple_of(c * m, 16), m)], sem))
    return copies


def hot_kernel(split, span, near, *rest):
    copies = []
    if split:
        *w, hot5, hot1, chip_out, chip_in, sem = rest
        copies = chip_copies(*w, chip_out, chip_in, sem)
    else:
        hot5, hot1 = rest
    start(copies)
    codes = near[...]
    count = codes.shape[1]
    rows = hot5.shape[0]
    pos = span[0] - HALF * DIL0 + lax.broadcasted_iota(jnp.int32, codes.shape, 1)
    masked = jnp.where((pos >= 0) & (pos < span[1]), codes, -1)
    lanes = lax.broadcasted_iota(jnp.int32, (CODES, count), 0)
    taps = jnp.where(lanes == masked, 1.0, 0.0).T.astype(BF)
    for k in range(KERNEL):
        hot5[:, k * CODES : (k + 1) * CODES] = taps[k * DIL0 : k * DIL0 + rows]
    center = jnp.where(lanes == codes, 1.0, 0.0).T.astype(BF)
    hot1[...] = center[HALF * DIL0 : HALF * DIL0 + rows]
    wait(copies)


def rows_kernel(split, span, hot5, hot1, gain_out, gain_in, gain_mid, *rest):
    *w, ci, hid, tw, wo, wi, sem = rest
    depth = wo.shape[0] - CODES
    if split:
        core = lax.rem(lax.axis_index("roll"), 2)
        taps = [(t, core * SLOT, SLOT, 0) for t in w[:2]] + [(t, (1 - core) * SLOT, SLOT, 0) for t in w[2:4]]
        taps = [(t, at, n, i % 2) for i, (t, at, n, _) in enumerate(taps)]
        w = w[4:]
    else:
        taps = [(w[0], 0, CODES, 0)]
        table, *w = w[1:]
    first = [
        pltpu.make_async_copy(
            t.at[:, k * H : (k + 1) * H], tw.at[i, pl.ds(pl.multiple_of(k * CODES + at, 16), n)], sem.at[0]
        )
        for t, at, n, i in taps
        for k in range(KERNEL)
    ]
    start(first)
    if not split:
        first.append(pltpu.make_async_copy(table, wo.at[depth:], sem.at[0]))
        first[-1].start()
        out_copies = [pltpu.make_async_copy(w[0], wo.at[0:depth], sem.at[1])]
        in_copies = [pltpu.make_async_copy(w[1], wi, sem.at[2])]
        start(out_copies + in_copies)
    else:
        chip_out, chip_in = w[:2]
        parts, near_parts = w[2:6], w[6:10]
        x, core, y, z = place()
        n = depth // 4
        m = 2 * n
        half = n // 2
        row = pl.multiple_of(x * 2 * n, 16)
        out_copies = [
            pltpu.make_async_copy(chip_out.at[0 : 2 * n], wo.at[pl.ds(row, 2 * n)], sem.at[1]),
            pltpu.make_async_copy(chip_out.at[2 * n :], wo.at[depth:], sem.at[1]),
        ]
        row = pl.multiple_of(x * 2 * m, 16)
        in_copies = [pltpu.make_async_copy(chip_in, wi.at[pl.ds(row, 2 * m)], sem.at[2])]

        def far(outs, ins):
            out, into = [], []
            for c, of in ((core, parts), (1 - core, near_parts)):
                at = 2 * (1 - x) + c
                for p, zz in zip(outs, (z, 1 - z)):
                    row = pl.multiple_of(at * n + zz * half, 16)
                    out.append(pltpu.make_async_copy(of[p], wo.at[pl.ds(row, half)], sem.at[1]))
                for p, zz in zip(ins, (z, 1 - z)):
                    for j in range(2):
                        row = pl.multiple_of(at * m + zz * n + j * half, 16)
                        into.append(
                            pltpu.make_async_copy(of[p].at[:, j * H : (j + 1) * H], wi.at[pl.ds(row, half)], sem.at[2])
                        )
            return out, into

        start(out_copies + in_copies)
        far0, far1 = far((0, 2), (1, 3)), far((1, 3), (0, 2))

        @pl.when(y == 0)
        def _():
            start(far0[0] + far0[1])

        @pl.when(y == 1)
        def _():
            start(far1[0] + far1[1])

        out_copies += far0[0]
        in_copies += far0[1]

    rows = hid.shape[0] + 2 * EDGE
    cuts = [0, 512, rows]
    state = [None, None]

    def once(b, copies):
        if b == 0:
            wait(copies)

    def mix(b):
        if b == 0:
            wait(first)
            if split:
                tw[0] = (tw[0].astype(F32) + tw[1].astype(F32)).astype(BF)
        state[b] = dot(hot5[cuts[b] : cuts[b + 1]], tw[0])

    def act(b):
        state[b] = gelu(norm(state[b], gain_out[0:1])).astype(BF)

    def update(b):
        once(b, out_copies)
        lhs = jnp.concatenate([state[b], hot1[cuts[b] : cuts[b + 1]]], axis=1)
        state[b] = dot(lhs, wo[...]).astype(BF)

    def enter(b):
        hidden = state[b]
        lo, hi = max(cuts[b], EDGE), min(cuts[b + 1], rows - EDGE)
        hid[lo - EDGE : hi - EDGE] = hidden[lo - cuts[b] : hi - cuts[b]]
        state[b] = gelu(norm(hidden.astype(F32), gain_in[1:2])).astype(BF)

    def widen(b):
        once(b, in_copies)
        state[b] = dot(state[b], wi[...])

    def leave(b):
        n = cuts[b + 1] - cuts[b]
        pos = span[0] + cuts[b] + lax.broadcasted_iota(jnp.int32, (n, 1), 0)
        valid = jnp.where((pos >= 0) & (pos < span[1]), 1.0, 0.0)
        ci[cuts[b] : cuts[b + 1]] = (gelu(norm(state[b], gain_mid[1:2])) * valid).astype(BF)

    stagger((mix, act, update, enter, widen, leave))


def conv_copies(src, col, width, wt, per_tap, row, n, sem):
    copies = []
    done = 0
    while done < width:
        tap, inner = divmod(col + done, H)
        step = min(H - inner, width - done)
        copies.append(
            pltpu.make_async_copy(
                src.at[:, done : done + step],
                wt.at[pl.ds(pl.multiple_of(tap * per_tap + row, 16), n), inner : inner + step],
                sem,
            )
        )
        done += step
    return copies


HEAD = 256
TAIL = H - HEAD


def windows(ci, lo, hi, first, width):
    first = pl.multiple_of(first, 128)
    return jnp.concatenate(
        [ci[lo + k * DIL1 : hi + k * DIL1, pl.ds(first, width)] for k in range(KERNEL)], axis=1
    )


def head_kernel(ci, w_conv, near_conv, out, wt, sem):
    x, core, _, _ = place()
    n = w_conv.shape[1]
    short = HEAD - n
    done = None
    for xx in range(2):
        for cc in range(2):
            copies = []
            for c, w in ((cc, w_conv), (1 - cc, near_conv)):
                if c == xx:
                    copies += conv_copies(w.at[1], 0, KERNEL * H, wt, HEAD, short * xx, n, sem)
                else:
                    part = w.at[1, (n - short) * xx : (n - short) * xx + short]
                    copies += conv_copies(part, 0, KERNEL * H, wt, HEAD, n * (1 - xx), short, sem)
            done = copies

            @pl.when((x == xx) & (core == cc))
            def _():
                start(copies)

    rows = out.shape[0]
    half = 16 * ((rows + 31) // 32)
    for b, (lo, hi) in enumerate(((0, half), (half, rows))):
        lhs = windows(ci, lo, hi, x * TAIL, HEAD)
        if b == 0:
            wait(done)
        out[lo:hi] = dot(lhs, wt[...])


def last_kernel(split, ci, hid, gain_out, *rest):
    *w, out, wt, wo, sem = rest
    if not split:
        conv_in = conv_copies(w[0], 0, KERNEL * H, wt, H, 0, H, sem.at[0])
        out_in = [pltpu.make_async_copy(w[1], wo, sem.at[1])]
        start(conv_in + out_in)
        first, width = 0, H
    else:
        head, w_conv, w_out, near_conv, near_out = w[:5]
        parts, near_parts = w[5:9], w[9:13]
        x, core, y, z = place()
        n = w_out.shape[1]
        half = n // 2
        left = 2 * n - HEAD
        rest_cols = KERNEL * H - CUT_B
        first, width = (1 - x) * HEAD, TAIL
        out_in = []
        for c, o in ((core, w_out), (1 - core, near_out)):
            row = pl.multiple_of((2 * x + c) * n, 16)
            out_in.append(pltpu.make_async_copy(o.at[1], wo.at[pl.ds(row, n)], sem.at[1]))
        from_row = pl.multiple_of((n - left) * (1 - x), 16)
        own_in, near_in = [
            conv_copies(v.at[1, pl.ds(from_row, left)], 0, KERNEL * H, wt, TAIL, 2 * n * x, left, sem.at[0])
            for v in (w_conv, near_conv)
        ]

        @pl.when(core + x == 1)
        def _():
            start(own_in)

        @pl.when(core + x != 1)
        def _():
            start(near_in)

        def far(head, tail):
            cv, out = [], []
            for c, of in ((core, parts), (1 - core, near_parts)):
                at = c * n + left * (1 - x)
                for p, zz in zip(head, (z, 1 - z)):
                    cv += conv_copies(of[p], 0, CUT_A, wt, TAIL, at + zz * half, half, sem.at[0])
                for p, zz in zip(tail, (z, 1 - z)):
                    skip = CUT_A - CUT_B
                    cv += conv_copies(
                        of[p].at[:, skip:rest_cols], CUT_A, rest_cols - skip, wt, TAIL, at + zz * half, half, sem.at[0]
                    )
                    row = pl.multiple_of((2 * (1 - x) + c) * n + zz * half, 16)
                    out.append(pltpu.make_async_copy(of[p].at[:, rest_cols:], wo.at[pl.ds(row, half)], sem.at[1]))
            return cv, out

        start(out_in)
        far0, far1 = far((0, 2), (1, 3)), far((1, 3), (0, 2))

        @pl.when(y == 0)
        def _():
            start(far0[0] + far0[1])

        @pl.when(y == 1)
        def _():
            start(far1[0] + far1[1])

        conv_in = own_in + far0[0]
        out_in += far0[1]

    rows = out.shape[0]
    cuts = [0, 16 * ((rows + 31) // 32), rows]
    state = [None, None]

    def mix(b):
        lhs = windows(ci, cuts[b], cuts[b + 1], first, width)
        if b == 0:
            wait(conv_in)
        state[b] = dot(lhs, wt[...])
        if split:
            state[b] += head[cuts[b] : cuts[b + 1]]

    def act(b):
        state[b] = gelu(norm(state[b], gain_out[1:2])).astype(BF)

    def update(b):
        if b == 0:
            wait(out_in)
        hidden = hid[cuts[b] : cuts[b + 1]].astype(F32)
        out[cuts[b] : cuts[b + 1]] = (hidden + dot(state[b], wo[...])).astype(BF)

    stagger((mix, act, update))


def after(x, *deps):
    return lax.optimization_barrier((x, *deps))[0]


def per_device(tokens, breaks, lengths, embed_table, break_vec, gain_in, gain_mid, gain_out, w_in, conv_w, w_out):
    rows = tokens.shape[1]
    width = embed_table.shape[1]
    roll_at = lax.axis_index("roll")
    seq_at = lax.axis_index("seq")
    rolls = lax.axis_size("roll")
    seqs = lax.axis_size("seq")
    split = rolls == 4 and seqs % 4 == 0

    def core_swap(x):
        return lax.ppermute(x, "roll", [(i, i ^ 1) for i in range(rolls)])

    def x_swap(x):
        return lax.ppermute(x, "roll", [(i, i ^ 2) for i in range(rolls)])

    def seq_swap(x, bits):
        return lax.ppermute(x, "seq", [(i, i ^ bits) for i in range(seqs)])

    span = jnp.stack([(seq_at * rows).astype(jnp.int32) - EDGE, lengths[0]])
    wide_rows = rows + 2 * EDGE
    codes = tokens[0] + SLOT * breaks[0]

    shard = w_out.shape[1] // 2
    ins, convs, shares = [w_in], [conv_w], 1
    if split:
        near_in, near_conv, near_out = core_swap(w_in), core_swap(conv_w), core_swap(w_out)
        ins, convs, shares = [w_in, near_in], [conv_w, near_conv], 2
        shapes = [(shard, width), (shard, CUT_A), (shard, CUT_A)]
        parts = pl.pallas_call(
            parts_kernel,
            out_shape=[jax.ShapeDtypeStruct(n, BF) for n in shapes],
            in_specs=[HBM] * 3,
            out_specs=[HBM] * 3,
            scratch_shapes=[pltpu.VMEM(n, BF) for n in shapes] + [pltpu.SemaphoreType.DMA((2,))],
            cost_estimate=FREE,
            compiler_params=params(60),
        )(w_in, conv_w, w_out)
        far_a = x_swap(parts[0])
    table, part, sent = pl.pallas_call(
        functools.partial(embed_kernel, split),
        out_shape=[
            jax.ShapeDtypeStruct((CODES, width), BF),
            jax.ShapeDtypeStruct((CODES, H), F32),
            jax.ShapeDtypeStruct((CODES, H), BF),
        ],
        in_specs=[HBM] * (3 + shares),
        out_specs=[VMEM] * 3,
        scratch_shapes=[
            pltpu.VMEM(embed_table.shape, F32),
            pltpu.VMEM((width,), F32),
            pltpu.VMEM(gain_in.shape, F32),
            pltpu.VMEM((shares * w_in.shape[1], H), BF),
            pltpu.VMEM((CODES, width), F32),
            pltpu.SemaphoreType.DMA((2,)),
        ],
        cost_estimate=FREE,
        compiler_params=params(60),
    )(embed_table, break_vec, gain_in, *ins)

    if split:
        own, other = part, x_swap(sent)
        far_b = x_swap(after(parts[1], other))
        low = roll_at % 2 == 0
        ends = codes[rows - REACH :], codes[:REACH]
        pack = jnp.stack([jnp.where(low, *ends), core_swap(after(jnp.where(low, *ends[::-1]), parts[0]))])
        places = [(s, r) for s in range(seqs) for r in range(rolls)]
        moves = [(s * rolls + r, (s + (1, -1)[r % 2]) % seqs * rolls + r) for s, r in places]
        moved = lax.ppermute(after(pack, table), ("seq", "roll"), moves)
        other = after(other, moved, near_out, far_a)
    else:
        own = lax.psum(part, "roll")
        other = jnp.zeros((CODES, H), BF)
        pairs = [(i, i + 1) for i in range(seqs - 1)]
        before = lax.ppermute(codes[rows - REACH :], "seq", pairs)
        behind = lax.ppermute(codes[:REACH], "seq", [(j, i) for i, j in pairs])
    wide = KERNEL * H
    taps = pl.pallas_call(
        functools.partial(table_kernel, split),
        out_shape=jax.ShapeDtypeStruct((SLOT, wide) if split else (CODES, wide), BF if split else F32),
        in_specs=[VMEM] * 3 + [HBM] * shares,
        out_specs=VMEM,
        scratch_shapes=[
            pltpu.VMEM((shares * conv_w.shape[1], wide), BF),
            pltpu.VMEM((CODES, shares * conv_w.shape[1]), F32),
            pltpu.SemaphoreType.DMA,
        ],
        cost_estimate=FREE,
        compiler_params=params(16),
    )(own, other, gain_mid, *convs)
    if split:
        sent = taps
        received = x_swap(sent)
        relay = after(far_a, sent)
        parts_a = [far_a] + [seq_swap(relay, b) for b in (1, 2, 3)]
        came = core_swap(after(moved[1], sent))
        before, behind = jnp.where(low, moved[0], came), jnp.where(low, came, moved[0])
    spare = jnp.zeros((-(rows + 2 * REACH) % 128,), jnp.int32)
    near = jnp.concatenate([before, codes, behind, spare])[None]
    if split:
        near = after(near, sent)

    shapes = [(wide_rows, KERNEL * CODES), (wide_rows, CODES)]
    operands, scratch = [], []
    if split:
        operands = [table, w_out, w_in, near_out, near_in]
        shapes += [(4 * shard + CODES, width), (8 * shard, H)]
        scratch = [pltpu.SemaphoreType.DMA]
    hot5, hot1, *chip = pl.pallas_call(
        functools.partial(hot_kernel, split),
        out_shape=[jax.ShapeDtypeStruct(n, BF) for n in shapes],
        in_specs=[SMEM, VMEM] + [ANY] * len(operands),
        out_specs=[VMEM] * len(shapes),
        scratch_shapes=scratch,
        cost_estimate=FREE,
        compiler_params=params(16),
    )(span, near, *operands)

    if split:
        near_sent = core_swap(after(sent, hot1))
        received = after(received, hot1)
        near_received = core_swap(received)
        near_a = [core_swap(after(p, hot1, far_b)) for p in parts_a]
        relay = after(far_b, received)
        parts_b = [far_b, seq_swap(relay, 1), seq_swap(relay, 2), x_swap(after(parts[2], received))]
        weights_a = [sent, received, near_sent, near_received] + chip + parts_a + near_a
    else:
        taps = lax.psum(taps, "roll").astype(BF)
        gather = lambda w: lax.all_gather(w, "roll", axis=0, tiled=True)
        weights_a, weights_b = [taps, table, gather(w_out[0]), gather(w_in[1])], [gather(conv_w[1]), gather(w_out[1])]

    ci, hid = pl.pallas_call(
        functools.partial(rows_kernel, split),
        out_shape=(
            jax.ShapeDtypeStruct((wide_rows, H), BF),
            jax.ShapeDtypeStruct((rows, width), BF),
        ),
        in_specs=[SMEM] + [VMEM] * 5 + [ANY] * len(weights_a),
        out_specs=(VMEM, VMEM),
        scratch_shapes=[
            pltpu.VMEM((2, KERNEL * CODES, H), BF),
            pltpu.VMEM((H + CODES, width), BF),
            pltpu.VMEM((width, H), BF),
            pltpu.SemaphoreType.DMA((3,)),
        ],
        cost_estimate=FREE,
        compiler_params=params(30),
    )(span, hot5, hot1, gain_out, gain_in, gain_mid, *weights_a)

    if split:
        near_b = [core_swap(after(p, ci)) for p in parts_b]
        head = pl.pallas_call(
            head_kernel,
            out_shape=jax.ShapeDtypeStruct((rows, H), F32),
            in_specs=[VMEM, HBM, ANY],
            out_specs=VMEM,
            scratch_shapes=[pltpu.VMEM((KERNEL * HEAD, H), BF), pltpu.SemaphoreType.DMA],
            cost_estimate=FREE,
            compiler_params=params(16),
        )(ci, conv_w, near_conv)
        weights_b = [head, conv_w, w_out, near_conv, near_out] + parts_b + near_b
    out = pl.pallas_call(
        functools.partial(last_kernel, split),
        out_shape=jax.ShapeDtypeStruct((rows, width), BF),
        in_specs=[VMEM] * 3
        + [HBM if w is w_out or w is conv_w else VMEM if split and w is head else ANY for w in weights_b],
        out_specs=VMEM,
        scratch_shapes=[
            pltpu.VMEM((KERNEL * (TAIL if split else H), H), BF),
            pltpu.VMEM((H, width), BF),
            pltpu.SemaphoreType.DMA((2,)),
        ],
        cost_estimate=FREE,
        compiler_params=params(24),
    )(ci, hid, gain_out, *weights_b)
    return out[None]


def solution(mesh):
    placed = (
        P("roll", "seq"),
        P("roll", "seq"),
        P("roll"),
        P(),
        P(),
        P(),
        P(),
        P(),
        P(None, "roll", None),
        P(None, "roll", None),
        P(None, "roll", None),
    )
    return jax.shard_map(
        per_device, mesh=mesh, in_specs=placed, out_specs=P("roll", "seq", None), check_vma=False
    )
```

```python
import functools

import jax
import jax.numpy as jnp
from jax import lax
from jax.experimental import pallas as pl
from jax.experimental.pallas import tpu as pltpu
from jax.sharding import PartitionSpec as P

H = 640
KERNEL = 5
VOCAB = 30
SLOT = 32
CODES = 2 * SLOT
BASE_DILATION = 64
DIL0 = BASE_DILATION
DIL1 = 2 * BASE_DILATION
HALF = KERNEL // 2
EDGE = HALF * DIL1
REACH = EDGE + HALF * DIL0
BF = jnp.bfloat16
F32 = jnp.float32
VMEM = pl.BlockSpec(memory_space=pltpu.VMEM)
SMEM = pl.BlockSpec(memory_space=pltpu.SMEM)
ANY = pl.BlockSpec(memory_space=pl.ANY)
HBM = pl.BlockSpec(memory_space=pltpu.HBM)
FREE = pl.CostEstimate(flops=0, bytes_accessed=0, transcendentals=0)
CUT_A = 18 * 128
CUT_B = 17 * 128


def params(mib):
    return pltpu.CompilerParams(vmem_limit_bytes=mib * 1024 * 1024)


def gelu(x):
    return (0.5 * x) * (1.0 + lax.erf(x * 0.5**0.5))


def norm(x, gain):
    center = jnp.mean(x, axis=-1, keepdims=True)
    d = x - center
    spread = jnp.mean(d * d, axis=-1, keepdims=True)
    return d * lax.rsqrt(spread + 1e-5) * gain


def dot(a, b):
    return jnp.dot(a, b, preferred_element_type=F32)


def place():
    roll, seq = lax.axis_index("roll"), lax.axis_index("seq")
    return lax.div(roll, 2), lax.rem(roll, 2), lax.rem(seq, 2), lax.rem(lax.div(seq, 2), 2)


def start(copies):
    for c in copies:
        c.start()


def wait(copies):
    for c in copies:
        c.wait()


def stagger(stages):
    for t in range(len(stages) + 1):
        for b in range(2):
            if 0 <= t - b < len(stages):
                stages[t - b](b)


def pick(rows, columns, first):
    i = lax.broadcasted_iota(jnp.int32, (rows, columns), 0)
    j = lax.broadcasted_iota(jnp.int32, (rows, columns), 1)
    return jnp.where(i == j + first, 1.0, 0.0).astype(BF)


def part_copies(y_is_one, row_bit, w_in, conv_w, w_out, a, b, sem):
    n = b.shape[0]
    r = pl.multiple_of(row_bit * n, 16)
    r2 = pl.multiple_of(row_bit * 2 * n, 16)
    rest = conv_w.shape[2] - CUT_B
    if y_is_one:
        pairs = [
            (conv_w.at[1, pl.ds(r, n), CUT_B:], b.at[:, 0:rest]),
            (w_out.at[1, pl.ds(r, n)], b.at[:, rest:]),
        ]
        if a is not None:
            pairs += [
                (w_in.at[1, pl.ds(r2, n)], a.at[:, 0:H]),
                (w_in.at[1, pl.ds(r2 + n, n)], a.at[:, H : 2 * H]),
            ]
    else:
        pairs = [(conv_w.at[1, pl.ds(r, n), 0:CUT_A], b)]
        if a is not None:
            pairs.append((w_out.at[0, pl.ds(r, n)], a))
    return [pltpu.make_async_copy(s, d, sem) for s, d in pairs]


def parts_kernel(w_in, conv_w, w_out, *rest):
    parts, held, sem = rest[:3], rest[3:6], rest[6]
    _, _, y, z = place()
    for kind in range(2):
        copies = part_copies(kind == 1, z, w_in, conv_w, w_out, held[0], held[1], sem.at[0])
        copies += part_copies(kind == 0, 1 - z, w_in, conv_w, w_out, None, held[2], sem.at[0])

        @pl.when(y == kind)
        def _():
            start(copies)
            wait(copies)

    leaving = [pltpu.make_async_copy(s, d, sem.at[1]) for s, d in zip(held, parts)]
    start(leaving)
    wait(leaving)


def two_shares(split, w_all, w, sem):
    if not split:
        return [pltpu.make_async_copy(w_all[0].at[0], w, sem)]
    _, core, _, _ = place()
    n = w_all[0].shape[1]
    return [
        pltpu.make_async_copy(v.at[0], w.at[pl.ds(pl.multiple_of(c * n, 16), n)], sem)
        for v, c in zip(w_all, (core, 1 - core))
    ]


def chosen(split, x, rows):
    at = place()[0] if split else lax.axis_index("roll")
    return dot(x, pick(x.shape[1], rows, at * rows)).astype(BF)


def embed_kernel(split, embed, brk, gain, *rest):
    *w_all, table, part, sent, emb, bv, g, w, full, sem = rest
    copies = [pltpu.make_async_copy(s, d, sem.at[0]) for s, d in ((embed, emb), (brk, bv), (gain, g))]
    shares = two_shares(split, w_all, w, sem.at[1])
    start(copies + shares)
    wait(copies)
    full[...] = jnp.zeros_like(full)
    full[0:VOCAB] = emb[...]
    full[SLOT : SLOT + VOCAB] = emb[...] + bv[...][None, :]
    hidden = full[...].astype(BF)
    table[...] = hidden
    normed = gelu(norm(hidden.astype(F32), g[0:1])).astype(BF)
    mine = chosen(split, normed, w.shape[0])
    wait(shares)
    total = dot(mine, w[...])
    part[...] = total
    sent[...] = total.astype(BF)


def table_kernel(split, own, other, gain, *rest):
    *w_all, out, w, rows, sem = rest
    shares = two_shares(split, w_all, w, sem)
    start(shares)
    wide = own[...] + other[...].astype(F32)
    t = gelu(norm(wide, gain[0:1])).astype(BF)
    rows[...] = chosen(split, t, w.shape[0]).astype(F32)
    if split:
        _, core, _, _ = place()
        mine = rows[pl.ds(pl.multiple_of(core * SLOT, SLOT), SLOT)]
    else:
        mine = rows[...]
    wait(shares)
    out[...] = dot(mine.astype(BF), w[...]).astype(out.dtype)


def chip_copies(table, w_out, w_in, near_out, near_in, chip_out, chip_in, sem):
    _, core, _, _ = place()
    n, m = w_out.shape[1], w_in.shape[1]
    copies = [pltpu.make_async_copy(table, chip_out.at[2 * n :], sem)]
    for c, o, i in ((core, w_out, w_in), (1 - core, near_out, near_in)):
        copies.append(pltpu.make_async_copy(o.at[0], chip_out.at[pl.ds(pl.multiple_of(c * n, 16), n)], sem))
        copies.append(pltpu.make_async_copy(i.at[1], chip_in.at[pl.ds(pl.multiple_of(c * m, 16), m)], sem))
    return copies


def hot_kernel(split, span, near, *rest):
    copies = []
    if split:
        *w, hot5, hot1, chip_out, chip_in, sem = rest
        copies = chip_copies(*w, chip_out, chip_in, sem)
    else:
        hot5, hot1 = rest
    start(copies)
    codes = near[...]
    count = codes.shape[1]
    rows = hot5.shape[0]
    pos = span[0] - HALF * DIL0 + lax.broadcasted_iota(jnp.int32, codes.shape, 1)
    masked = jnp.where((pos >= 0) & (pos < span[1]), codes, -1)
    lanes = lax.broadcasted_iota(jnp.int32, (CODES, count), 0)
    taps = jnp.where(lanes == masked, 1.0, 0.0).T.astype(BF)
    for k in range(KERNEL):
        hot5[:, k * CODES : (k + 1) * CODES] = taps[k * DIL0 : k * DIL0 + rows]
    center = jnp.where(lanes == codes, 1.0, 0.0).T.astype(BF)
    hot1[...] = center[HALF * DIL0 : HALF * DIL0 + rows]
    wait(copies)


def rows_kernel(split, span, hot5, hot1, gain_out, gain_in, gain_mid, *rest):
    *w, ci, hid, tw, wo, wi, sem = rest
    depth = wo.shape[0] - CODES
    if split:
        core = lax.rem(lax.axis_index("roll"), 2)
        taps = [(t, core * SLOT, SLOT, 0) for t in w[:2]] + [(t, (1 - core) * SLOT, SLOT, 0) for t in w[2:4]]
        taps = [(t, at, n, i % 2) for i, (t, at, n, _) in enumerate(taps)]
        w = w[4:]
    else:
        taps = [(w[0], 0, CODES, 0)]
        table, *w = w[1:]
    first = [
        pltpu.make_async_copy(
            t.at[:, k * H : (k + 1) * H], tw.at[i, pl.ds(pl.multiple_of(k * CODES + at, 16), n)], sem.at[0]
        )
        for t, at, n, i in taps
        for k in range(KERNEL)
    ]
    start(first)
    if not split:
        first.append(pltpu.make_async_copy(table, wo.at[depth:], sem.at[0]))
        first[-1].start()
        out_copies = [pltpu.make_async_copy(w[0], wo.at[0:depth], sem.at[1])]
        in_copies = [pltpu.make_async_copy(w[1], wi, sem.at[2])]
        start(out_copies + in_copies)
    else:
        chip_out, chip_in = w[:2]
        parts, near_parts = w[2:6], w[6:10]
        x, core, y, z = place()
        n = depth // 4
        m = 2 * n
        half = n // 2
        row = pl.multiple_of(x * 2 * n, 16)
        out_copies = [
            pltpu.make_async_copy(chip_out.at[0 : 2 * n], wo.at[pl.ds(row, 2 * n)], sem.at[1]),
            pltpu.make_async_copy(chip_out.at[2 * n :], wo.at[depth:], sem.at[1]),
        ]
        row = pl.multiple_of(x * 2 * m, 16)
        in_copies = [pltpu.make_async_copy(chip_in, wi.at[pl.ds(row, 2 * m)], sem.at[2])]

        def far(outs, ins):
            out, into = [], []
            for c, of in ((core, parts), (1 - core, near_parts)):
                at = 2 * (1 - x) + c
                for p, zz in zip(outs, (z, 1 - z)):
                    row = pl.multiple_of(at * n + zz * half, 16)
                    out.append(pltpu.make_async_copy(of[p], wo.at[pl.ds(row, half)], sem.at[1]))
                for p, zz in zip(ins, (z, 1 - z)):
                    for j in range(2):
                        row = pl.multiple_of(at * m + zz * n + j * half, 16)
                        into.append(
                            pltpu.make_async_copy(of[p].at[:, j * H : (j + 1) * H], wi.at[pl.ds(row, half)], sem.at[2])
                        )
            return out, into

        start(out_copies + in_copies)
        far0, far1 = far((0, 2), (1, 3)), far((1, 3), (0, 2))

        @pl.when(y == 0)
        def _():
            start(far0[0] + far0[1])

        @pl.when(y == 1)
        def _():
            start(far1[0] + far1[1])

        out_copies += far0[0]
        in_copies += far0[1]

    rows = hid.shape[0] + 2 * EDGE
    cuts = [0, 512, rows]
    state = [None, None]

    def once(b, copies):
        if b == 0:
            wait(copies)

    def mix(b):
        if b == 0:
            wait(first)
            if split:
                tw[0] = (tw[0].astype(F32) + tw[1].astype(F32)).astype(BF)
        state[b] = dot(hot5[cuts[b] : cuts[b + 1]], tw[0])

    def act(b):
        state[b] = gelu(norm(state[b], gain_out[0:1])).astype(BF)

    def update(b):
        once(b, out_copies)
        lhs = jnp.concatenate([state[b], hot1[cuts[b] : cuts[b + 1]]], axis=1)
        state[b] = dot(lhs, wo[...]).astype(BF)

    def enter(b):
        hidden = state[b]
        lo, hi = max(cuts[b], EDGE), min(cuts[b + 1], rows - EDGE)
        hid[lo - EDGE : hi - EDGE] = hidden[lo - cuts[b] : hi - cuts[b]]
        state[b] = gelu(norm(hidden.astype(F32), gain_in[1:2])).astype(BF)

    def widen(b):
        once(b, in_copies)
        state[b] = dot(state[b], wi[...])

    def leave(b):
        n = cuts[b + 1] - cuts[b]
        pos = span[0] + cuts[b] + lax.broadcasted_iota(jnp.int32, (n, 1), 0)
        valid = jnp.where((pos >= 0) & (pos < span[1]), 1.0, 0.0)
        ci[cuts[b] : cuts[b + 1]] = (gelu(norm(state[b], gain_mid[1:2])) * valid).astype(BF)

    stagger((mix, act, update, enter, widen, leave))


def conv_copies(src, col, width, wt, per_tap, row, n, sem):
    copies = []
    done = 0
    while done < width:
        tap, inner = divmod(col + done, H)
        step = min(H - inner, width - done)
        copies.append(
            pltpu.make_async_copy(
                src.at[:, done : done + step],
                wt.at[pl.ds(pl.multiple_of(tap * per_tap + row, 16), n), inner : inner + step],
                sem,
            )
        )
        done += step
    return copies


HEAD = 256
TAIL = H - HEAD


def windows(ci, lo, hi, first, width):
    first = pl.multiple_of(first, 128)
    return jnp.concatenate(
        [ci[lo + k * DIL1 : hi + k * DIL1, pl.ds(first, width)] for k in range(KERNEL)], axis=1
    )


def head_kernel(ci, w_conv, near_conv, out, wt, sem):
    x, core, _, _ = place()
    n = w_conv.shape[1]
    short = HEAD - n
    done = None
    for xx in range(2):
        for cc in range(2):
            copies = []
            for c, w in ((cc, w_conv), (1 - cc, near_conv)):
                if c == xx:
                    copies += conv_copies(w.at[1], 0, KERNEL * H, wt, HEAD, short * xx, n, sem)
                else:
                    part = w.at[1, (n - short) * xx : (n - short) * xx + short]
                    copies += conv_copies(part, 0, KERNEL * H, wt, HEAD, n * (1 - xx), short, sem)
            done = copies

            @pl.when((x == xx) & (core == cc))
            def _():
                start(copies)

    rows = out.shape[0]
    half = 16 * ((rows + 31) // 32)
    for b, (lo, hi) in enumerate(((0, half), (half, rows))):
        lhs = windows(ci, lo, hi, x * TAIL, HEAD)
        if b == 0:
            wait(done)
        out[lo:hi] = dot(lhs, wt[...])


def last_kernel(split, ci, hid, gain_out, *rest):
    *w, out, wt, wo, sem = rest
    if not split:
        conv_in = conv_copies(w[0], 0, KERNEL * H, wt, H, 0, H, sem.at[0])
        out_in = [pltpu.make_async_copy(w[1], wo, sem.at[1])]
        start(conv_in + out_in)
        first, width = 0, H
    else:
        head, w_conv, w_out, near_conv, near_out = w[:5]
        parts, near_parts = w[5:9], w[9:13]
        x, core, y, z = place()
        n = w_out.shape[1]
        half = n // 2
        left = 2 * n - HEAD
        rest_cols = KERNEL * H - CUT_B
        first, width = (1 - x) * HEAD, TAIL
        out_in = []
        for c, o in ((core, w_out), (1 - core, near_out)):
            row = pl.multiple_of((2 * x + c) * n, 16)
            out_in.append(pltpu.make_async_copy(o.at[1], wo.at[pl.ds(row, n)], sem.at[1]))
        from_row = pl.multiple_of((n - left) * (1 - x), 16)
        own_in, near_in = [
            conv_copies(v.at[1, pl.ds(from_row, left)], 0, KERNEL * H, wt, TAIL, 2 * n * x, left, sem.at[0])
            for v in (w_conv, near_conv)
        ]

        @pl.when(core + x == 1)
        def _():
            start(own_in)

        @pl.when(core + x != 1)
        def _():
            start(near_in)

        def far(head, tail):
            cv, out = [], []
            for c, of in ((core, parts), (1 - core, near_parts)):
                at = c * n + left * (1 - x)
                for p, zz in zip(head, (z, 1 - z)):
                    cv += conv_copies(of[p], 0, CUT_A, wt, TAIL, at + zz * half, half, sem.at[0])
                for p, zz in zip(tail, (z, 1 - z)):
                    skip = CUT_A - CUT_B
                    cv += conv_copies(
                        of[p].at[:, skip:rest_cols], CUT_A, rest_cols - skip, wt, TAIL, at + zz * half, half, sem.at[0]
                    )
                    row = pl.multiple_of((2 * (1 - x) + c) * n + zz * half, 16)
                    out.append(pltpu.make_async_copy(of[p].at[:, rest_cols:], wo.at[pl.ds(row, half)], sem.at[1]))
            return cv, out

        start(out_in)
        far0, far1 = far((0, 2), (1, 3)), far((1, 3), (0, 2))

        @pl.when(y == 0)
        def _():
            start(far0[0] + far0[1])

        @pl.when(y == 1)
        def _():
            start(far1[0] + far1[1])

        conv_in = own_in + far0[0]
        out_in += far0[1]

    rows = out.shape[0]
    cuts = [0, 16 * ((rows + 31) // 32), rows]
    state = [None, None]

    def mix(b):
        lhs = windows(ci, cuts[b], cuts[b + 1], first, width)
        if b == 0:
            wait(conv_in)
        state[b] = dot(lhs, wt[...])
        if split:
            state[b] += head[cuts[b] : cuts[b + 1]]

    def act(b):
        state[b] = gelu(norm(state[b], gain_out[1:2])).astype(BF)

    def update(b):
        if b == 0:
            wait(out_in)
        hidden = hid[cuts[b] : cuts[b + 1]].astype(F32)
        out[cuts[b] : cuts[b + 1]] = (hidden + dot(state[b], wo[...])).astype(BF)

    stagger((mix, act, update))


def after(x, *deps):
    return lax.optimization_barrier((x, *deps))[0]


def per_device(tokens, breaks, lengths, embed_table, break_vec, gain_in, gain_mid, gain_out, w_in, conv_w, w_out):
    rows = tokens.shape[1]
    width = embed_table.shape[1]
    roll_at = lax.axis_index("roll")
    seq_at = lax.axis_index("seq")
    rolls = lax.axis_size("roll")
    seqs = lax.axis_size("seq")
    split = rolls == 4 and seqs % 4 == 0

    def core_swap(x):
        return lax.ppermute(x, "roll", [(i, i ^ 1) for i in range(rolls)])

    def x_swap(x):
        return lax.ppermute(x, "roll", [(i, i ^ 2) for i in range(rolls)])

    def seq_swap(x, bits):
        return lax.ppermute(x, "seq", [(i, i ^ bits) for i in range(seqs)])

    span = jnp.stack([(seq_at * rows).astype(jnp.int32) - EDGE, lengths[0]])
    wide_rows = rows + 2 * EDGE
    codes = tokens[0] + SLOT * breaks[0]

    shard = w_out.shape[1] // 2
    ins, convs, shares = [w_in], [conv_w], 1
    if split:
        near_in, near_conv, near_out = core_swap(w_in), core_swap(conv_w), core_swap(w_out)
        ins, convs, shares = [w_in, near_in], [conv_w, near_conv], 2
        shapes = [(shard, width), (shard, CUT_A), (shard, CUT_A)]
        parts = pl.pallas_call(
            parts_kernel,
            out_shape=[jax.ShapeDtypeStruct(n, BF) for n in shapes],
            in_specs=[HBM] * 3,
            out_specs=[HBM] * 3,
            scratch_shapes=[pltpu.VMEM(n, BF) for n in shapes] + [pltpu.SemaphoreType.DMA((2,))],
            cost_estimate=FREE,
            compiler_params=params(60),
        )(w_in, conv_w, w_out)
        far_a = x_swap(parts[0])
    table, part, sent = pl.pallas_call(
        functools.partial(embed_kernel, split),
        out_shape=[
            jax.ShapeDtypeStruct((CODES, width), BF),
            jax.ShapeDtypeStruct((CODES, H), F32),
            jax.ShapeDtypeStruct((CODES, H), BF),
        ],
        in_specs=[HBM] * (3 + shares),
        out_specs=[VMEM] * 3,
        scratch_shapes=[
            pltpu.VMEM(embed_table.shape, F32),
            pltpu.VMEM((width,), F32),
            pltpu.VMEM(gain_in.shape, F32),
            pltpu.VMEM((shares * w_in.shape[1], H), BF),
            pltpu.VMEM((CODES, width), F32),
            pltpu.SemaphoreType.DMA((2,)),
        ],
        cost_estimate=FREE,
        compiler_params=params(60),
    )(embed_table, break_vec, gain_in, *ins)

    if split:
        own, other = part, x_swap(sent)
        far_b = x_swap(after(parts[1], other))
        low = roll_at % 2 == 0
        ends = codes[rows - REACH :], codes[:REACH]
        pack = jnp.stack([jnp.where(low, *ends), core_swap(after(jnp.where(low, *ends[::-1]), parts[0]))])
        places = [(s, r) for s in range(seqs) for r in range(rolls)]
        moves = [(s * rolls + r, (s + (1, -1)[r % 2]) % seqs * rolls + r) for s, r in places]
        moved = lax.ppermute(after(pack, table, near_out), ("seq", "roll"), moves)
        other = after(other, far_a)
    else:
        own = lax.psum(part, "roll")
        other = jnp.zeros((CODES, H), BF)
        pairs = [(i, i + 1) for i in range(seqs - 1)]
        before = lax.ppermute(codes[rows - REACH :], "seq", pairs)
        behind = lax.ppermute(codes[:REACH], "seq", [(j, i) for i, j in pairs])
    wide = KERNEL * H
    taps = pl.pallas_call(
        functools.partial(table_kernel, split),
        out_shape=jax.ShapeDtypeStruct((SLOT, wide) if split else (CODES, wide), BF if split else F32),
        in_specs=[VMEM] * 3 + [HBM] * shares,
        out_specs=VMEM,
        scratch_shapes=[
            pltpu.VMEM((shares * conv_w.shape[1], wide), BF),
            pltpu.VMEM((CODES, shares * conv_w.shape[1]), F32),
            pltpu.SemaphoreType.DMA,
        ],
        cost_estimate=FREE,
        compiler_params=params(16),
    )(own, other, gain_mid, *convs)
    if split:
        sent = taps
        received = x_swap(sent)
        relay = after(far_a, sent)
        parts_a = [far_a] + [seq_swap(relay, b) for b in (1, 2, 3)]
        came = core_swap(after(moved[1], sent))
        before, behind = jnp.where(low, moved[0], came), jnp.where(low, came, moved[0])
    spare = jnp.zeros((-(rows + 2 * REACH) % 128,), jnp.int32)
    near = jnp.concatenate([before, codes, behind, spare])[None]
    if split:
        near = after(near, sent)

    shapes = [(wide_rows, KERNEL * CODES), (wide_rows, CODES)]
    operands, scratch = [], []
    if split:
        operands = [table, w_out, w_in, near_out, near_in]
        shapes += [(4 * shard + CODES, width), (8 * shard, H)]
        scratch = [pltpu.SemaphoreType.DMA]
    hot5, hot1, *chip = pl.pallas_call(
        functools.partial(hot_kernel, split),
        out_shape=[jax.ShapeDtypeStruct(n, BF) for n in shapes],
        in_specs=[SMEM, VMEM] + [ANY] * len(operands),
        out_specs=[VMEM] * len(shapes),
        scratch_shapes=scratch,
        cost_estimate=FREE,
        compiler_params=params(16),
    )(span, near, *operands)

    if split:
        near_sent = core_swap(after(sent, hot1))
        received = after(received, hot1)
        near_received = core_swap(received)
        near_a = [core_swap(after(p, hot1, far_b)) for p in parts_a]
        relay = after(far_b, received)
        parts_b = [far_b, seq_swap(relay, 1), seq_swap(relay, 2), x_swap(after(parts[2], received))]
        weights_a = [sent, received, near_sent, near_received] + chip + parts_a + near_a
    else:
        taps = lax.psum(taps, "roll").astype(BF)
        gather = lambda w: lax.all_gather(w, "roll", axis=0, tiled=True)
        weights_a, weights_b = [taps, table, gather(w_out[0]), gather(w_in[1])], [gather(conv_w[1]), gather(w_out[1])]

    ci, hid = pl.pallas_call(
        functools.partial(rows_kernel, split),
        out_shape=(
            jax.ShapeDtypeStruct((wide_rows, H), BF),
            jax.ShapeDtypeStruct((rows, width), BF),
        ),
        in_specs=[SMEM] + [VMEM] * 5 + [ANY] * len(weights_a),
        out_specs=(VMEM, VMEM),
        scratch_shapes=[
            pltpu.VMEM((2, KERNEL * CODES, H), BF),
            pltpu.VMEM((H + CODES, width), BF),
            pltpu.VMEM((width, H), BF),
            pltpu.SemaphoreType.DMA((3,)),
        ],
        cost_estimate=FREE,
        compiler_params=params(30),
    )(span, hot5, hot1, gain_out, gain_in, gain_mid, *weights_a)

    if split:
        near_b = [core_swap(after(p, ci)) for p in parts_b]
        head = pl.pallas_call(
            head_kernel,
            out_shape=jax.ShapeDtypeStruct((rows, H), F32),
            in_specs=[VMEM, HBM, ANY],
            out_specs=VMEM,
            scratch_shapes=[pltpu.VMEM((KERNEL * HEAD, H), BF), pltpu.SemaphoreType.DMA],
            cost_estimate=FREE,
            compiler_params=params(16),
        )(ci, conv_w, near_conv)
        weights_b = [head, conv_w, w_out, near_conv, near_out] + parts_b + near_b
    out = pl.pallas_call(
        functools.partial(last_kernel, split),
        out_shape=jax.ShapeDtypeStruct((rows, width), BF),
        in_specs=[VMEM] * 3
        + [HBM if w is w_out or w is conv_w else VMEM if split and w is head else ANY for w in weights_b],
        out_specs=VMEM,
        scratch_shapes=[
            pltpu.VMEM((KERNEL * (TAIL if split else H), H), BF),
            pltpu.VMEM((H, width), BF),
            pltpu.SemaphoreType.DMA((2,)),
        ],
        cost_estimate=FREE,
        compiler_params=params(24),
    )(ci, hid, gain_out, *weights_b)
    return out[None]


def solution(mesh):
    placed = (
        P("roll", "seq"),
        P("roll", "seq"),
        P("roll"),
        P(),
        P(),
        P(),
        P(),
        P(),
        P(None, "roll", None),
        P(None, "roll", None),
        P(None, "roll", None),
    )
    return jax.shard_map(
        per_device, mesh=mesh, in_specs=placed, out_specs=P("roll", "seq", None), check_vma=False
    )
```

```python
import functools

import jax
import jax.numpy as jnp
from jax import lax
from jax.experimental import pallas as pl
from jax.experimental.pallas import tpu as pltpu
from jax.sharding import PartitionSpec as P

H = 640
KERNEL = 5
VOCAB = 30
SLOT = 32
CODES = 2 * SLOT
BASE_DILATION = 64
DIL0 = BASE_DILATION
DIL1 = 2 * BASE_DILATION
HALF = KERNEL // 2
EDGE = HALF * DIL1
REACH = EDGE + HALF * DIL0
BF = jnp.bfloat16
F32 = jnp.float32
VMEM = pl.BlockSpec(memory_space=pltpu.VMEM)
SMEM = pl.BlockSpec(memory_space=pltpu.SMEM)
ANY = pl.BlockSpec(memory_space=pl.ANY)
HBM = pl.BlockSpec(memory_space=pltpu.HBM)
FREE = pl.CostEstimate(flops=0, bytes_accessed=0, transcendentals=0)
CUT_A = 18 * 128
CUT_B = 17 * 128


def params(mib):
    return pltpu.CompilerParams(vmem_limit_bytes=mib * 1024 * 1024)


def gelu(x):
    return (0.5 * x) * (1.0 + lax.erf(x * 0.5**0.5))


def norm(x, gain):
    center = jnp.mean(x, axis=-1, keepdims=True)
    d = x - center
    spread = jnp.mean(d * d, axis=-1, keepdims=True)
    return d * lax.rsqrt(spread + 1e-5) * gain


def dot(a, b):
    return jnp.dot(a, b, preferred_element_type=F32)


def place():
    roll, seq = lax.axis_index("roll"), lax.axis_index("seq")
    return lax.div(roll, 2), lax.rem(roll, 2), lax.rem(seq, 2), lax.rem(lax.div(seq, 2), 2)


def start(copies):
    for c in copies:
        c.start()


def wait(copies):
    for c in copies:
        c.wait()


def stagger(stages):
    for t in range(len(stages) + 1):
        for b in range(2):
            if 0 <= t - b < len(stages):
                stages[t - b](b)


def pick(rows, columns, first):
    i = lax.broadcasted_iota(jnp.int32, (rows, columns), 0)
    j = lax.broadcasted_iota(jnp.int32, (rows, columns), 1)
    return jnp.where(i == j + first, 1.0, 0.0).astype(BF)


def part_copies(y_is_one, row_bit, w_in, conv_w, w_out, a, b, sem):
    n = b.shape[0]
    r = pl.multiple_of(row_bit * n, 16)
    r2 = pl.multiple_of(row_bit * 2 * n, 16)
    rest = conv_w.shape[2] - CUT_B
    if y_is_one:
        pairs = [
            (conv_w.at[1, pl.ds(r, n), CUT_B:], b.at[:, 0:rest]),
            (w_out.at[1, pl.ds(r, n)], b.at[:, rest:]),
        ]
        if a is not None:
            pairs += [
                (w_in.at[1, pl.ds(r2, n)], a.at[:, 0:H]),
                (w_in.at[1, pl.ds(r2 + n, n)], a.at[:, H : 2 * H]),
            ]
    else:
        pairs = [(conv_w.at[1, pl.ds(r, n), 0:CUT_A], b)]
        if a is not None:
            pairs.append((w_out.at[0, pl.ds(r, n)], a))
    return [pltpu.make_async_copy(s, d, sem) for s, d in pairs]


def first_kernel(split, embed, brk, gain, w_in, conv_w, w_out, table, part, *rest):
    count = 3 if split else 0
    parts, rest = rest[:count], rest[count:]
    emb, bv, g, w, full, sem, *held = rest
    copies = [
        pltpu.make_async_copy(s, d, sem.at[0])
        for s, d in ((embed, emb), (brk, bv), (gain, g), (w_in.at[0], w))
    ]
    start(copies)
    leaving = []
    if split:
        _, _, y, z = place()
        kinds = []
        for kind in range(2):
            kinds.append(
                part_copies(kind == 1, z, w_in, conv_w, w_out, held[0], held[1], sem.at[1])
                + part_copies(kind == 0, 1 - z, w_in, conv_w, w_out, None, held[2], sem.at[1])
            )

            @pl.when(y == kind)
            def _():
                start(kinds[kind])

        leaving = [pltpu.make_async_copy(s, d, sem.at[2]) for s, d in zip(held, parts)]

    wait(copies)
    full[...] = jnp.zeros_like(full)
    full[0:VOCAB] = emb[...]
    full[SLOT : SLOT + VOCAB] = emb[...] + bv[...][None, :]
    hidden = full[...].astype(BF)
    table[...] = hidden
    normed = gelu(norm(hidden.astype(F32), g[0:1])).astype(BF)
    if split:
        for kind in range(2):

            @pl.when(y == kind)
            def _():
                wait(kinds[kind])

        start(leaving)
    rows = w.shape[0]
    mine = dot(normed, pick(normed.shape[1], rows, lax.axis_index("roll") * rows)).astype(BF)
    part[...] = dot(mine, w[...])
    wait(leaving)


def table_kernel(split, own, other, gain, w_all, *rest):
    *outs, w, full, sem = rest
    if split:
        outs[2][...] = gain[0:1, 0:128]
    copy = pltpu.make_async_copy(w_all.at[0], w, sem)
    copy.start()
    wide = own[...] + other[...].astype(F32)
    t = gelu(norm(wide, gain[0:1])).astype(BF)
    rows = w.shape[0]
    mine = dot(t, pick(t.shape[1], rows, lax.axis_index("roll") * rows)).astype(BF)
    copy.wait()
    full[...] = dot(mine, w[...])
    if split:
        core = lax.rem(lax.axis_index("roll"), 2)
        outs[0][...] = full[pl.ds(pl.multiple_of(core * SLOT, SLOT), SLOT)]
        outs[1][...] = full[pl.ds(pl.multiple_of((1 - core) * SLOT, SLOT), SLOT)].astype(BF)
    else:
        outs[0][...] = full[...]


def chip_copies(table, w_out, w_in, near_out, near_in, chip_out, chip_in, sem):
    _, core, _, _ = place()
    n, m = w_out.shape[1], w_in.shape[1]
    copies = [pltpu.make_async_copy(table, chip_out.at[2 * n :], sem)]
    for c, o, i in ((core, w_out, w_in), (1 - core, near_out, near_in)):
        copies.append(pltpu.make_async_copy(o.at[0], chip_out.at[pl.ds(pl.multiple_of(c * n, 16), n)], sem))
        copies.append(pltpu.make_async_copy(i.at[1], chip_in.at[pl.ds(pl.multiple_of(c * m, 16), m)], sem))
    return copies


def hot_kernel(split, span, near, *rest):
    copies = []
    if split:
        *w, hot5, hot1, chip_out, chip_in, sem = rest
        copies = chip_copies(*w, chip_out, chip_in, sem)
    else:
        hot5, hot1 = rest
    start(copies)
    codes = near[...]
    count = codes.shape[1]
    rows = hot5.shape[0]
    pos = span[0] - HALF * DIL0 + lax.broadcasted_iota(jnp.int32, codes.shape, 1)
    masked = jnp.where((pos >= 0) & (pos < span[1]), codes, -1)
    lanes = lax.broadcasted_iota(jnp.int32, (CODES, count), 0)
    taps = jnp.where(lanes == masked, 1.0, 0.0).T.astype(BF)
    for k in range(KERNEL):
        hot5[:, k * CODES : (k + 1) * CODES] = taps[k * DIL0 : k * DIL0 + rows]
    center = jnp.where(lanes == codes, 1.0, 0.0).T.astype(BF)
    hot1[...] = center[HALF * DIL0 : HALF * DIL0 + rows]
    wait(copies)


def rows_kernel(split, span, hot5, hot1, gain_out, gain_in, gain_mid, *rest):
    *w, ci, hid, tw, wo, wi, sem = rest
    depth = wo.shape[0] - CODES
    if split:
        core = lax.rem(lax.axis_index("roll"), 2)
        taps = [(t, core * SLOT, SLOT, 0) for t in w[:2]] + [(t, (1 - core) * SLOT, SLOT, 0) for t in w[2:4]]
        taps = [(t, at, n, i % 2) for i, (t, at, n, _) in enumerate(taps)]
        w = w[4:]
    else:
        taps = [(w[0], 0, CODES, 0)]
        table, *w = w[1:]
    first = [
        pltpu.make_async_copy(
            t.at[:, k * H : (k + 1) * H], tw.at[i, pl.ds(pl.multiple_of(k * CODES + at, 16), n)], sem.at[0]
        )
        for t, at, n, i in taps
        for k in range(KERNEL)
    ]
    start(first)
    if not split:
        first.append(pltpu.make_async_copy(table, wo.at[depth:], sem.at[0]))
        first[-1].start()
        out_copies = [pltpu.make_async_copy(w[0], wo.at[0:depth], sem.at[1])]
        in_copies = [pltpu.make_async_copy(w[1], wi, sem.at[2])]
        start(out_copies + in_copies)
    else:
        chip_out, chip_in = w[:2]
        parts, near_parts = w[2:6], w[6:10]
        x, core, y, z = place()
        n = depth // 4
        m = 2 * n
        half = n // 2
        row = pl.multiple_of(x * 2 * n, 16)
        out_copies = [
            pltpu.make_async_copy(chip_out.at[0 : 2 * n], wo.at[pl.ds(row, 2 * n)], sem.at[1]),
            pltpu.make_async_copy(chip_out.at[2 * n :], wo.at[depth:], sem.at[1]),
        ]
        row = pl.multiple_of(x * 2 * m, 16)
        in_copies = [pltpu.make_async_copy(chip_in, wi.at[pl.ds(row, 2 * m)], sem.at[2])]

        def far(outs, ins):
            out, into = [], []
            for c, of in ((core, parts), (1 - core, near_parts)):
                at = 2 * (1 - x) + c
                for p, zz in zip(outs, (z, 1 - z)):
                    row = pl.multiple_of(at * n + zz * half, 16)
                    out.append(pltpu.make_async_copy(of[p], wo.at[pl.ds(row, half)], sem.at[1]))
                for p, zz in zip(ins, (z, 1 - z)):
                    for j in range(2):
                        row = pl.multiple_of(at * m + zz * n + j * half, 16)
                        into.append(
                            pltpu.make_async_copy(of[p].at[:, j * H : (j + 1) * H], wi.at[pl.ds(row, half)], sem.at[2])
                        )
            return out, into

        start(out_copies + in_copies)
        far0, far1 = far((0, 2), (1, 3)), far((1, 3), (0, 2))

        @pl.when(y == 0)
        def _():
            start(far0[0] + far0[1])

        @pl.when(y == 1)
        def _():
            start(far1[0] + far1[1])

        out_copies += far0[0]
        in_copies += far0[1]

    rows = hid.shape[0] + 2 * EDGE
    cuts = [0, 512, rows]
    state = [None, None]

    def once(b, copies):
        if b == 0:
            wait(copies)

    def mix(b):
        if b == 0:
            wait(first)
            if split:
                tw[0] = (tw[0].astype(F32) + tw[1].astype(F32)).astype(BF)
        state[b] = dot(hot5[cuts[b] : cuts[b + 1]], tw[0])

    def act(b):
        state[b] = gelu(norm(state[b], gain_out[0:1])).astype(BF)

    def update(b):
        once(b, out_copies)
        lhs = jnp.concatenate([state[b], hot1[cuts[b] : cuts[b + 1]]], axis=1)
        state[b] = dot(lhs, wo[...]).astype(BF)

    def enter(b):
        hidden = state[b]
        lo, hi = max(cuts[b], EDGE), min(cuts[b + 1], rows - EDGE)
        hid[lo - EDGE : hi - EDGE] = hidden[lo - cuts[b] : hi - cuts[b]]
        state[b] = gelu(norm(hidden.astype(F32), gain_in[1:2])).astype(BF)

    def widen(b):
        once(b, in_copies)
        state[b] = dot(state[b], wi[...])

    def leave(b):
        n = cuts[b + 1] - cuts[b]
        pos = span[0] + cuts[b] + lax.broadcasted_iota(jnp.int32, (n, 1), 0)
        valid = jnp.where((pos >= 0) & (pos < span[1]), 1.0, 0.0)
        ci[cuts[b] : cuts[b + 1]] = (gelu(norm(state[b], gain_mid[1:2])) * valid).astype(BF)

    stagger((mix, act, update, enter, widen, leave))


def conv_copies(src, col, width, wt, per_tap, row, n, sem):
    copies = []
    done = 0
    while done < width:
        tap, inner = divmod(col + done, H)
        step = min(H - inner, width - done)
        copies.append(
            pltpu.make_async_copy(
                src.at[:, done : done + step],
                wt.at[pl.ds(pl.multiple_of(tap * per_tap + row, 16), n), inner : inner + step],
                sem,
            )
        )
        done += step
    return copies


HEAD = 256
TAIL = H - HEAD


def windows(ci, lo, hi, first, width):
    first = pl.multiple_of(first, 128)
    return jnp.concatenate(
        [ci[lo + k * DIL1 : hi + k * DIL1, pl.ds(first, width)] for k in range(KERNEL)], axis=1
    )


def head_kernel(ci, w_conv, near_conv, out, wt, sem):
    x, core, _, _ = place()
    n = w_conv.shape[1]
    short = HEAD - n
    done = None
    for xx in range(2):
        for cc in range(2):
            copies = []
            for c, w in ((cc, w_conv), (1 - cc, near_conv)):
                if c == xx:
                    copies += conv_copies(w.at[1], 0, KERNEL * H, wt, HEAD, short * xx, n, sem)
                else:
                    part = w.at[1, (n - short) * xx : (n - short) * xx + short]
                    copies += conv_copies(part, 0, KERNEL * H, wt, HEAD, n * (1 - xx), short, sem)
            done = copies

            @pl.when((x == xx) & (core == cc))
            def _():
                start(copies)

    rows = out.shape[0]
    half = 16 * ((rows + 31) // 32)
    for b, (lo, hi) in enumerate(((0, half), (half, rows))):
        lhs = windows(ci, lo, hi, x * TAIL, HEAD)
        if b == 0:
            wait(done)
        out[lo:hi] = dot(lhs, wt[...])


def last_kernel(split, ci, hid, gain_out, *rest):
    *w, out, wt, wo, sem = rest
    if not split:
        conv_in = conv_copies(w[0], 0, KERNEL * H, wt, H, 0, H, sem.at[0])
        out_in = [pltpu.make_async_copy(w[1], wo, sem.at[1])]
        start(conv_in + out_in)
        first, width = 0, H
    else:
        head, w_conv, w_out, near_conv, near_out = w[:5]
        parts, near_parts = w[5:9], w[9:13]
        x, core, y, z = place()
        n = w_out.shape[1]
        half = n // 2
        left = 2 * n - HEAD
        rest_cols = KERNEL * H - CUT_B
        first, width = (1 - x) * HEAD, TAIL
        out_in = []
        for c, o in ((core, w_out), (1 - core, near_out)):
            row = pl.multiple_of((2 * x + c) * n, 16)
            out_in.append(pltpu.make_async_copy(o.at[1], wo.at[pl.ds(row, n)], sem.at[1]))
        from_row = pl.multiple_of((n - left) * (1 - x), 16)
        own_in, near_in = [
            conv_copies(v.at[1, pl.ds(from_row, left)], 0, KERNEL * H, wt, TAIL, 2 * n * x, left, sem.at[0])
            for v in (w_conv, near_conv)
        ]

        @pl.when(core + x == 1)
        def _():
            start(own_in)

        @pl.when(core + x != 1)
        def _():
            start(near_in)

        def far(head, tail):
            cv, out = [], []
            for c, of in ((core, parts), (1 - core, near_parts)):
                at = c * n + left * (1 - x)
                for p, zz in zip(head, (z, 1 - z)):
                    cv += conv_copies(of[p], 0, CUT_A, wt, TAIL, at + zz * half, half, sem.at[0])
                for p, zz in zip(tail, (z, 1 - z)):
                    skip = CUT_A - CUT_B
                    cv += conv_copies(
                        of[p].at[:, skip:rest_cols], CUT_A, rest_cols - skip, wt, TAIL, at + zz * half, half, sem.at[0]
                    )
                    row = pl.multiple_of((2 * (1 - x) + c) * n + zz * half, 16)
                    out.append(pltpu.make_async_copy(of[p].at[:, rest_cols:], wo.at[pl.ds(row, half)], sem.at[1]))
            return cv, out

        start(out_in)
        far0, far1 = far((0, 2), (1, 3)), far((1, 3), (0, 2))

        @pl.when(y == 0)
        def _():
            start(far0[0] + far0[1])

        @pl.when(y == 1)
        def _():
            start(far1[0] + far1[1])

        conv_in = own_in + far0[0]
        out_in += far0[1]

    rows = out.shape[0]
    cuts = [0, 16 * ((rows + 31) // 32), rows]
    state = [None, None]

    def mix(b):
        lhs = windows(ci, cuts[b], cuts[b + 1], first, width)
        if b == 0:
            wait(conv_in)
        state[b] = dot(lhs, wt[...])
        if split:
            state[b] += head[cuts[b] : cuts[b + 1]]

    def act(b):
        state[b] = gelu(norm(state[b], gain_out[1:2])).astype(BF)

    def update(b):
        if b == 0:
            wait(out_in)
        hidden = hid[cuts[b] : cuts[b + 1]].astype(F32)
        out[cuts[b] : cuts[b + 1]] = (hidden + dot(state[b], wo[...])).astype(BF)

    stagger((mix, act, update))


def after(x, *deps):
    return lax.optimization_barrier((x, *deps))[0]


def per_device(tokens, breaks, lengths, embed_table, break_vec, gain_in, gain_mid, gain_out, w_in, conv_w, w_out):
    rows = tokens.shape[1]
    width = embed_table.shape[1]
    roll_at = lax.axis_index("roll")
    seq_at = lax.axis_index("seq")
    rolls = lax.axis_size("roll")
    seqs = lax.axis_size("seq")
    split = rolls == 4 and seqs % 4 == 0

    def core_swap(x):
        return lax.ppermute(x, "roll", [(i, i ^ 1) for i in range(rolls)])

    def x_swap(x):
        return lax.ppermute(x, "roll", [(i, i ^ 2) for i in range(rolls)])

    def seq_swap(x, bits):
        return lax.ppermute(x, "seq", [(i, i ^ bits) for i in range(seqs)])

    span = jnp.stack([(seq_at * rows).astype(jnp.int32) - EDGE, lengths[0]])
    wide_rows = rows + 2 * EDGE
    codes = tokens[0] + SLOT * breaks[0]

    shard = w_out.shape[1] // 2
    shapes = [((CODES, width), BF), ((CODES, H), F32)]
    if split:
        shapes += [((shard, width), BF), ((shard, CUT_A), BF), ((shard, CUT_A), BF)]
    table, part, *parts = pl.pallas_call(
        functools.partial(first_kernel, split),
        out_shape=[jax.ShapeDtypeStruct(n, t) for n, t in shapes],
        in_specs=[HBM] * 6,
        out_specs=[VMEM] * 2 + [HBM] * (len(shapes) - 2),
        scratch_shapes=[
            pltpu.VMEM(embed_table.shape, F32),
            pltpu.VMEM((width,), F32),
            pltpu.VMEM(gain_in.shape, F32),
            pltpu.VMEM(w_in.shape[1:], BF),
            pltpu.VMEM((CODES, width), F32),
            pltpu.SemaphoreType.DMA((3,)),
        ]
        + [pltpu.VMEM(n, t) for n, t in shapes[2:]],
        cost_estimate=FREE,
        compiler_params=params(60),
    )(embed_table, break_vec, gain_in, w_in, conv_w, w_out)

    if split:
        far_a = x_swap(parts[0])
        near_out, near_in = core_swap(w_out), core_swap(w_in)
        low = roll_at % 2 == 0
        ends = codes[rows - REACH :], codes[:REACH]
        theirs = core_swap(jnp.where(low, *ends[::-1]))
        own = part + after(core_swap(part), theirs)
        other = x_swap(own.astype(BF))
        far_b = x_swap(after(parts[1], other))
        pack = jnp.stack([jnp.where(low, *ends), theirs])
        places = [(s, r) for s in range(seqs) for r in range(rolls)]
        moves = [(s * rolls + r, (s + (1, -1)[r % 2]) % seqs * rolls + r) for s, r in places]
        moved = lax.ppermute(after(pack, own), ("seq", "roll"), moves)
        other = after(other, near_out, near_in, far_a)
    else:
        own = lax.psum(part, "roll")
        other = jnp.zeros((CODES, H), BF)
        pairs = [(i, i + 1) for i in range(seqs - 1)]
        before = lax.ppermute(codes[rows - REACH :], "seq", pairs)
        behind = lax.ppermute(codes[:REACH], "seq", [(j, i) for i, j in pairs])
    wide = KERNEL * H
    shapes = [((SLOT, wide), F32), ((SLOT, wide), BF), ((1, 128), F32)] if split else [((CODES, wide), F32)]
    taps = pl.pallas_call(
        functools.partial(table_kernel, split),
        out_shape=[jax.ShapeDtypeStruct(n, t) for n, t in shapes],
        in_specs=[VMEM, VMEM, VMEM, HBM],
        out_specs=[VMEM] * len(shapes),
        scratch_shapes=[
            pltpu.VMEM(conv_w.shape[1:], BF),
            pltpu.VMEM((CODES, wide), F32),
            pltpu.SemaphoreType.DMA,
        ],
        cost_estimate=FREE,
        compiler_params=params(12),
    )(own, other, gain_mid, conv_w)
    if split:
        came = core_swap(after(moved[1], taps[2]))
        before, behind = jnp.where(low, moved[0], came), jnp.where(low, came, moved[0])
        relay = after(far_a, taps[2])
        parts_a = [far_a] + [seq_swap(relay, b) for b in (1, 2, 3)]
        sent = (taps[0] + after(core_swap(taps[1]), before, behind).astype(F32)).astype(BF)
        received = x_swap(sent)
    spare = jnp.zeros((-(rows + 2 * REACH) % 128,), jnp.int32)
    near = jnp.concatenate([before, codes, behind, spare])[None]
    if split:
        near = after(near, sent)

    shapes = [(wide_rows, KERNEL * CODES), (wide_rows, CODES)]
    operands, scratch = [], []
    if split:
        operands = [table, w_out, w_in, near_out, near_in]
        shapes += [(4 * shard + CODES, width), (8 * shard, H)]
        scratch = [pltpu.SemaphoreType.DMA]
    hot5, hot1, *chip = pl.pallas_call(
        functools.partial(hot_kernel, split),
        out_shape=[jax.ShapeDtypeStruct(n, BF) for n in shapes],
        in_specs=[SMEM, VMEM] + [ANY] * len(operands),
        out_specs=[VMEM] * len(shapes),
        scratch_shapes=scratch,
        cost_estimate=FREE,
        compiler_params=params(16),
    )(span, near, *operands)

    if split:
        near_sent = core_swap(after(sent, hot1))
        received = after(received, hot1)
        near_received = core_swap(received)
        near_a = [core_swap(after(p, hot1, far_b)) for p in parts_a]
        relay = after(far_b, received)
        parts_b = [far_b, seq_swap(relay, 1), seq_swap(relay, 2), x_swap(after(parts[2], received))]
        weights_a = [sent, received, near_sent, near_received] + chip + parts_a + near_a
        near_conv = core_swap(after(conv_w, near_received, near_sent, *near_a))
    else:
        taps = lax.psum(taps[0], "roll").astype(BF)
        gather = lambda w: lax.all_gather(w, "roll", axis=0, tiled=True)
        weights_a, weights_b = [taps, table, gather(w_out[0]), gather(w_in[1])], [gather(conv_w[1]), gather(w_out[1])]

    ci, hid = pl.pallas_call(
        functools.partial(rows_kernel, split),
        out_shape=(
            jax.ShapeDtypeStruct((wide_rows, H), BF),
            jax.ShapeDtypeStruct((rows, width), BF),
        ),
        in_specs=[SMEM] + [VMEM] * 5 + [ANY] * len(weights_a),
        out_specs=(VMEM, VMEM),
        scratch_shapes=[
            pltpu.VMEM((2, KERNEL * CODES, H), BF),
            pltpu.VMEM((H + CODES, width), BF),
            pltpu.VMEM((width, H), BF),
            pltpu.SemaphoreType.DMA((3,)),
        ],
        cost_estimate=FREE,
        compiler_params=params(30),
    )(span, hot5, hot1, gain_out, gain_in, gain_mid, *weights_a)

    if split:
        near_b = [core_swap(after(p, ci)) for p in parts_b]
        head = pl.pallas_call(
            head_kernel,
            out_shape=jax.ShapeDtypeStruct((rows, H), F32),
            in_specs=[VMEM, HBM, ANY],
            out_specs=VMEM,
            scratch_shapes=[pltpu.VMEM((KERNEL * HEAD, H), BF), pltpu.SemaphoreType.DMA],
            cost_estimate=FREE,
            compiler_params=params(16),
        )(ci, conv_w, near_conv)
        weights_b = [head, conv_w, w_out, near_conv, near_out] + parts_b + near_b
    out = pl.pallas_call(
        functools.partial(last_kernel, split),
        out_shape=jax.ShapeDtypeStruct((rows, width), BF),
        in_specs=[VMEM] * 3
        + [HBM if w is w_out or w is conv_w else VMEM if split and w is head else ANY for w in weights_b],
        out_specs=VMEM,
        scratch_shapes=[
            pltpu.VMEM((KERNEL * (TAIL if split else H), H), BF),
            pltpu.VMEM((H, width), BF),
            pltpu.SemaphoreType.DMA((2,)),
        ],
        cost_estimate=FREE,
        compiler_params=params(24),
    )(ci, hid, gain_out, *weights_b)
    return out[None]


def solution(mesh):
    placed = (
        P("roll", "seq"),
        P("roll", "seq"),
        P("roll"),
        P(),
        P(),
        P(),
        P(),
        P(),
        P(None, "roll", None),
        P(None, "roll", None),
        P(None, "roll", None),
    )
    return jax.shard_map(
        per_device, mesh=mesh, in_specs=placed, out_specs=P("roll", "seq", None), check_vma=False
    )
```

```python
import functools

import jax
import jax.numpy as jnp
from jax import lax
from jax.experimental import pallas as pl
from jax.experimental.pallas import tpu as pltpu
from jax.sharding import PartitionSpec as P

H = 640
KERNEL = 5
VOCAB = 30
SLOT = 32
CODES = 2 * SLOT
BASE_DILATION = 64
DIL0 = BASE_DILATION
DIL1 = 2 * BASE_DILATION
HALF = KERNEL // 2
EDGE = HALF * DIL1
REACH = EDGE + HALF * DIL0
BF = jnp.bfloat16
F32 = jnp.float32
VMEM = pl.BlockSpec(memory_space=pltpu.VMEM)
SMEM = pl.BlockSpec(memory_space=pltpu.SMEM)
ANY = pl.BlockSpec(memory_space=pl.ANY)
HBM = pl.BlockSpec(memory_space=pltpu.HBM)
FREE = pl.CostEstimate(flops=0, bytes_accessed=0, transcendentals=0)
CUT_A = 18 * 128
CUT_B = 17 * 128


def params(mib):
    return pltpu.CompilerParams(vmem_limit_bytes=mib * 1024 * 1024)


def gelu(x):
    return (0.5 * x) * (1.0 + lax.erf(x * 0.5**0.5))


def norm(x, gain):
    center = jnp.mean(x, axis=-1, keepdims=True)
    d = x - center
    spread = jnp.mean(d * d, axis=-1, keepdims=True)
    return d * lax.rsqrt(spread + 1e-5) * gain


def dot(a, b):
    return jnp.dot(a, b, preferred_element_type=F32)


def place():
    roll, seq = lax.axis_index("roll"), lax.axis_index("seq")
    return lax.div(roll, 2), lax.rem(roll, 2), lax.rem(seq, 2), lax.rem(lax.div(seq, 2), 2)


def start(copies):
    for c in copies:
        c.start()


def wait(copies):
    for c in copies:
        c.wait()


def stagger(stages):
    for t in range(len(stages) + 1):
        for b in range(2):
            if 0 <= t - b < len(stages):
                stages[t - b](b)


def pick(rows, columns, first):
    i = lax.broadcasted_iota(jnp.int32, (rows, columns), 0)
    j = lax.broadcasted_iota(jnp.int32, (rows, columns), 1)
    return jnp.where(i == j + first, 1.0, 0.0).astype(BF)


def part_copies(y_is_one, row_bit, w_in, conv_w, w_out, a, b, sem):
    n = b.shape[0]
    r = pl.multiple_of(row_bit * n, 16)
    r2 = pl.multiple_of(row_bit * 2 * n, 16)
    rest = conv_w.shape[2] - CUT_B
    if y_is_one:
        pairs = [
            (conv_w.at[1, pl.ds(r, n), CUT_B:], b.at[:, 0:rest]),
            (w_out.at[1, pl.ds(r, n)], b.at[:, rest:]),
        ]
        if a is not None:
            pairs += [
                (w_in.at[1, pl.ds(r2, n)], a.at[:, 0:H]),
                (w_in.at[1, pl.ds(r2 + n, n)], a.at[:, H : 2 * H]),
            ]
    else:
        pairs = [(conv_w.at[1, pl.ds(r, n), 0:CUT_A], b)]
        if a is not None:
            pairs.append((w_out.at[0, pl.ds(r, n)], a))
    return [pltpu.make_async_copy(s, d, sem) for s, d in pairs]


def first_kernel(split, embed, brk, gain, w_in, conv_w, w_out, table, part, *rest):
    count = 3 if split else 0
    parts, rest = rest[:count], rest[count:]
    emb, bv, g, w, full, sem, *held = rest
    copies = [
        pltpu.make_async_copy(s, d, sem.at[0])
        for s, d in ((embed, emb), (brk, bv), (gain, g), (w_in.at[0], w))
    ]
    start(copies)
    leaving = []
    if split:
        _, _, y, z = place()
        kinds = []
        for kind in range(2):
            kinds.append(
                part_copies(kind == 1, z, w_in, conv_w, w_out, held[0], held[1], sem.at[1])
                + part_copies(kind == 0, 1 - z, w_in, conv_w, w_out, None, held[2], sem.at[1])
            )

            @pl.when(y == kind)
            def _():
                start(kinds[kind])

        leaving = [pltpu.make_async_copy(s, d, sem.at[2]) for s, d in zip(held, parts)]

    wait(copies)
    full[...] = jnp.zeros_like(full)
    full[0:VOCAB] = emb[...]
    full[SLOT : SLOT + VOCAB] = emb[...] + bv[...][None, :]
    hidden = full[...].astype(BF)
    table[...] = hidden
    normed = gelu(norm(hidden.astype(F32), g[0:1])).astype(BF)
    if split:
        for kind in range(2):

            @pl.when(y == kind)
            def _():
                wait(kinds[kind])

        start(leaving)
    rows = w.shape[0]
    mine = dot(normed, pick(normed.shape[1], rows, lax.axis_index("roll") * rows)).astype(BF)
    part[...] = dot(mine, w[...])
    wait(leaving)


def table_kernel(split, own, other, gain, w_all, *rest):
    *outs, w, full, sem = rest
    if split:
        outs[2][...] = gain[0:1, 0:128]
    copy = pltpu.make_async_copy(w_all.at[0], w, sem)
    copy.start()
    wide = own[...] + other[...].astype(F32)
    t = gelu(norm(wide, gain[0:1])).astype(BF)
    rows = w.shape[0]
    mine = dot(t, pick(t.shape[1], rows, lax.axis_index("roll") * rows)).astype(BF)
    copy.wait()
    full[...] = dot(mine, w[...])
    if split:
        core = lax.rem(lax.axis_index("roll"), 2)
        outs[0][...] = full[pl.ds(pl.multiple_of(core * SLOT, SLOT), SLOT)]
        outs[1][...] = full[pl.ds(pl.multiple_of((1 - core) * SLOT, SLOT), SLOT)].astype(BF)
    else:
        outs[0][...] = full[...]


def chip_copies(table, w_out, w_in, near_out, near_in, chip_out, chip_in, sem):
    _, core, _, _ = place()
    n, m = w_out.shape[1], w_in.shape[1]
    copies = [pltpu.make_async_copy(table, chip_out.at[2 * n :], sem)]
    for c, o, i in ((core, w_out, w_in), (1 - core, near_out, near_in)):
        copies.append(pltpu.make_async_copy(o.at[0], chip_out.at[pl.ds(pl.multiple_of(c * n, 16), n)], sem))
        copies.append(pltpu.make_async_copy(i.at[1], chip_in.at[pl.ds(pl.multiple_of(c * m, 16), m)], sem))
    return copies


def hot_kernel(split, span, near, *rest):
    copies = []
    if split:
        *w, hot5, hot1, chip_out, chip_in, sem = rest
        copies = chip_copies(*w, chip_out, chip_in, sem)
    else:
        hot5, hot1 = rest
    start(copies)
    codes = near[...]
    count = codes.shape[1]
    rows = hot5.shape[0]
    pos = span[0] - HALF * DIL0 + lax.broadcasted_iota(jnp.int32, codes.shape, 1)
    masked = jnp.where((pos >= 0) & (pos < span[1]), codes, -1)
    lanes = lax.broadcasted_iota(jnp.int32, (CODES, count), 0)
    taps = jnp.where(lanes == masked, 1.0, 0.0).T.astype(BF)
    for k in range(KERNEL):
        hot5[:, k * CODES : (k + 1) * CODES] = taps[k * DIL0 : k * DIL0 + rows]
    center = jnp.where(lanes == codes, 1.0, 0.0).T.astype(BF)
    hot1[...] = center[HALF * DIL0 : HALF * DIL0 + rows]
    wait(copies)


def rows_kernel(split, span, hot5, hot1, gain_out, gain_in, gain_mid, *rest):
    *w, ci, hid, tw, wo, wi, sem = rest
    depth = wo.shape[0] - CODES
    if split:
        core = lax.rem(lax.axis_index("roll"), 2)
        taps = [(t, core * SLOT, SLOT, 0) for t in w[:2]] + [(t, (1 - core) * SLOT, SLOT, 0) for t in w[2:4]]
        taps = [(t, at, n, i % 2) for i, (t, at, n, _) in enumerate(taps)]
        w = w[4:]
    else:
        taps = [(w[0], 0, CODES, 0)]
        table, *w = w[1:]
    first = [
        pltpu.make_async_copy(
            t.at[:, k * H : (k + 1) * H], tw.at[i, pl.ds(pl.multiple_of(k * CODES + at, 16), n)], sem.at[0]
        )
        for t, at, n, i in taps
        for k in range(KERNEL)
    ]
    start(first)
    if not split:
        first.append(pltpu.make_async_copy(table, wo.at[depth:], sem.at[0]))
        first[-1].start()
        out_copies = [pltpu.make_async_copy(w[0], wo.at[0:depth], sem.at[1])]
        in_copies = [pltpu.make_async_copy(w[1], wi, sem.at[2])]
        start(out_copies + in_copies)
    else:
        chip_out, chip_in = w[:2]
        parts, near_parts = w[2:6], w[6:10]
        x, core, y, z = place()
        n = depth // 4
        m = 2 * n
        half = n // 2
        row = pl.multiple_of(x * 2 * n, 16)
        out_copies = [
            pltpu.make_async_copy(chip_out.at[0 : 2 * n], wo.at[pl.ds(row, 2 * n)], sem.at[1]),
            pltpu.make_async_copy(chip_out.at[2 * n :], wo.at[depth:], sem.at[1]),
        ]
        row = pl.multiple_of(x * 2 * m, 16)
        in_copies = [pltpu.make_async_copy(chip_in, wi.at[pl.ds(row, 2 * m)], sem.at[2])]

        def far(outs, ins):
            out, into = [], []
            for c, of in ((core, parts), (1 - core, near_parts)):
                at = 2 * (1 - x) + c
                for p, zz in zip(outs, (z, 1 - z)):
                    row = pl.multiple_of(at * n + zz * half, 16)
                    out.append(pltpu.make_async_copy(of[p], wo.at[pl.ds(row, half)], sem.at[1]))
                for p, zz in zip(ins, (z, 1 - z)):
                    for j in range(2):
                        row = pl.multiple_of(at * m + zz * n + j * half, 16)
                        into.append(
                            pltpu.make_async_copy(of[p].at[:, j * H : (j + 1) * H], wi.at[pl.ds(row, half)], sem.at[2])
                        )
            return out, into

        start(out_copies + in_copies)
        far0, far1 = far((0, 2), (1, 3)), far((1, 3), (0, 2))

        @pl.when(y == 0)
        def _():
            start(far0[0] + far0[1])

        @pl.when(y == 1)
        def _():
            start(far1[0] + far1[1])

        out_copies += far0[0]
        in_copies += far0[1]

    rows = hid.shape[0] + 2 * EDGE
    cuts = [0, 512, rows]
    state = [None, None]

    def once(b, copies):
        if b == 0:
            wait(copies)

    def mix(b):
        if b == 0:
            wait(first)
            if split:
                tw[0] = (tw[0].astype(F32) + tw[1].astype(F32)).astype(BF)
        state[b] = dot(hot5[cuts[b] : cuts[b + 1]], tw[0])

    def act(b):
        state[b] = gelu(norm(state[b], gain_out[0:1])).astype(BF)

    def update(b):
        once(b, out_copies)
        lhs = jnp.concatenate([state[b], hot1[cuts[b] : cuts[b + 1]]], axis=1)
        state[b] = dot(lhs, wo[...]).astype(BF)

    def enter(b):
        hidden = state[b]
        lo, hi = max(cuts[b], EDGE), min(cuts[b + 1], rows - EDGE)
        hid[lo - EDGE : hi - EDGE] = hidden[lo - cuts[b] : hi - cuts[b]]
        state[b] = gelu(norm(hidden.astype(F32), gain_in[1:2])).astype(BF)

    def widen(b):
        once(b, in_copies)
        state[b] = dot(state[b], wi[...])

    def leave(b):
        n = cuts[b + 1] - cuts[b]
        pos = span[0] + cuts[b] + lax.broadcasted_iota(jnp.int32, (n, 1), 0)
        valid = jnp.where((pos >= 0) & (pos < span[1]), 1.0, 0.0)
        ci[cuts[b] : cuts[b + 1]] = (gelu(norm(state[b], gain_mid[1:2])) * valid).astype(BF)

    stagger((mix, act, update, enter, widen, leave))


def conv_copies(src, col, width, wt, per_tap, row, n, sem):
    copies = []
    done = 0
    while done < width:
        tap, inner = divmod(col + done, H)
        step = min(H - inner, width - done)
        copies.append(
            pltpu.make_async_copy(
                src.at[:, done : done + step],
                wt.at[pl.ds(pl.multiple_of(tap * per_tap + row, 16), n), inner : inner + step],
                sem,
            )
        )
        done += step
    return copies


HEAD = 256
TAIL = H - HEAD


def windows(ci, lo, hi, first, width):
    first = pl.multiple_of(first, 128)
    return jnp.concatenate(
        [ci[lo + k * DIL1 : hi + k * DIL1, pl.ds(first, width)] for k in range(KERNEL)], axis=1
    )


def head_kernel(ci, w_conv, near_conv, out, wt, sem):
    x, core, _, _ = place()
    n = w_conv.shape[1]
    short = HEAD - n
    done = None
    for xx in range(2):
        for cc in range(2):
            copies = []
            for c, w in ((cc, w_conv), (1 - cc, near_conv)):
                if c == xx:
                    copies += conv_copies(w.at[1], 0, KERNEL * H, wt, HEAD, short * xx, n, sem)
                else:
                    part = w.at[1, (n - short) * xx : (n - short) * xx + short]
                    copies += conv_copies(part, 0, KERNEL * H, wt, HEAD, n * (1 - xx), short, sem)
            done = copies

            @pl.when((x == xx) & (core == cc))
            def _():
                start(copies)

    rows = out.shape[0]
    half = 16 * ((rows + 31) // 32)
    for b, (lo, hi) in enumerate(((0, half), (half, rows))):
        lhs = windows(ci, lo, hi, x * TAIL, HEAD)
        if b == 0:
            wait(done)
        out[lo:hi] = dot(lhs, wt[...])


def last_kernel(split, ci, hid, gain_out, *rest):
    *w, out, wt, wo, sem = rest
    if not split:
        conv_in = conv_copies(w[0], 0, KERNEL * H, wt, H, 0, H, sem.at[0])
        out_in = [pltpu.make_async_copy(w[1], wo, sem.at[1])]
        start(conv_in + out_in)
        first, width = 0, H
    else:
        head, w_conv, w_out, near_conv, near_out = w[:5]
        parts, near_parts = w[5:9], w[9:13]
        x, core, y, z = place()
        n = w_out.shape[1]
        half = n // 2
        left = 2 * n - HEAD
        rest_cols = KERNEL * H - CUT_B
        first, width = (1 - x) * HEAD, TAIL
        out_in = []
        for c, o in ((core, w_out), (1 - core, near_out)):
            row = pl.multiple_of((2 * x + c) * n, 16)
            out_in.append(pltpu.make_async_copy(o.at[1], wo.at[pl.ds(row, n)], sem.at[1]))
        from_row = pl.multiple_of((n - left) * (1 - x), 16)
        own_in, near_in = [
            conv_copies(v.at[1, pl.ds(from_row, left)], 0, KERNEL * H, wt, TAIL, 2 * n * x, left, sem.at[0])
            for v in (w_conv, near_conv)
        ]

        @pl.when(core + x == 1)
        def _():
            start(own_in)

        @pl.when(core + x != 1)
        def _():
            start(near_in)

        def far(head, tail):
            cv, out = [], []
            for c, of in ((core, parts), (1 - core, near_parts)):
                at = c * n + left * (1 - x)
                for p, zz in zip(head, (z, 1 - z)):
                    cv += conv_copies(of[p], 0, CUT_A, wt, TAIL, at + zz * half, half, sem.at[0])
                for p, zz in zip(tail, (z, 1 - z)):
                    skip = CUT_A - CUT_B
                    cv += conv_copies(
                        of[p].at[:, skip:rest_cols], CUT_A, rest_cols - skip, wt, TAIL, at + zz * half, half, sem.at[0]
                    )
                    row = pl.multiple_of((2 * (1 - x) + c) * n + zz * half, 16)
                    out.append(pltpu.make_async_copy(of[p].at[:, rest_cols:], wo.at[pl.ds(row, half)], sem.at[1]))
            return cv, out

        start(out_in)
        far0, far1 = far((0, 2), (1, 3)), far((1, 3), (0, 2))

        @pl.when(y == 0)
        def _():
            start(far0[0] + far0[1])

        @pl.when(y == 1)
        def _():
            start(far1[0] + far1[1])

        conv_in = own_in + far0[0]
        out_in += far0[1]

    rows = out.shape[0]
    cuts = [0, 16 * ((rows + 31) // 32), rows]
    state = [None, None]

    def mix(b):
        lhs = windows(ci, cuts[b], cuts[b + 1], first, width)
        if b == 0:
            wait(conv_in)
        state[b] = dot(lhs, wt[...])
        if split:
            state[b] += head[cuts[b] : cuts[b + 1]]

    def act(b):
        state[b] = gelu(norm(state[b], gain_out[1:2])).astype(BF)

    def update(b):
        if b == 0:
            wait(out_in)
        hidden = hid[cuts[b] : cuts[b + 1]].astype(F32)
        out[cuts[b] : cuts[b + 1]] = (hidden + dot(state[b], wo[...])).astype(BF)

    stagger((mix, act, update))


def after(x, *deps):
    return lax.optimization_barrier((x, *deps))[0]


def per_device(tokens, breaks, lengths, embed_table, break_vec, gain_in, gain_mid, gain_out, w_in, conv_w, w_out):
    rows = tokens.shape[1]
    width = embed_table.shape[1]
    roll_at = lax.axis_index("roll")
    seq_at = lax.axis_index("seq")
    rolls = lax.axis_size("roll")
    seqs = lax.axis_size("seq")
    split = rolls == 4 and seqs % 4 == 0

    def core_swap(x):
        return lax.ppermute(x, "roll", [(i, i ^ 1) for i in range(rolls)])

    def x_swap(x):
        return lax.ppermute(x, "roll", [(i, i ^ 2) for i in range(rolls)])

    def seq_swap(x, bits):
        return lax.ppermute(x, "seq", [(i, i ^ bits) for i in range(seqs)])

    span = jnp.stack([(seq_at * rows).astype(jnp.int32) - EDGE, lengths[0]])
    wide_rows = rows + 2 * EDGE
    codes = tokens[0] + SLOT * breaks[0]

    shard = w_out.shape[1] // 2
    shapes = [((CODES, width), BF), ((CODES, H), F32)]
    if split:
        shapes += [((shard, width), BF), ((shard, CUT_A), BF), ((shard, CUT_A), BF)]
    table, part, *parts = pl.pallas_call(
        functools.partial(first_kernel, split),
        out_shape=[jax.ShapeDtypeStruct(n, t) for n, t in shapes],
        in_specs=[HBM] * 6,
        out_specs=[VMEM] * 2 + [HBM] * (len(shapes) - 2),
        scratch_shapes=[
            pltpu.VMEM(embed_table.shape, F32),
            pltpu.VMEM((width,), F32),
            pltpu.VMEM(gain_in.shape, F32),
            pltpu.VMEM(w_in.shape[1:], BF),
            pltpu.VMEM((CODES, width), F32),
            pltpu.SemaphoreType.DMA((3,)),
        ]
        + [pltpu.VMEM(n, t) for n, t in shapes[2:]],
        cost_estimate=FREE,
        compiler_params=params(60),
    )(embed_table, break_vec, gain_in, w_in, conv_w, w_out)

    if split:
        far_a = x_swap(parts[0])
        near_out, near_in = core_swap(w_out), core_swap(w_in)
        low = roll_at % 2 == 0
        ends = codes[rows - REACH :], codes[:REACH]
        theirs = core_swap(jnp.where(low, *ends[::-1]))
        own = part + after(core_swap(part), theirs)
        other = x_swap(own.astype(BF))
        far_b = x_swap(after(parts[1], other))
        pack = jnp.stack([jnp.where(low, *ends), theirs])
        places = [(s, r) for s in range(seqs) for r in range(rolls)]
        moves = [(s * rolls + r, (s + (1, -1)[r % 2]) % seqs * rolls + r) for s, r in places]
        moved = lax.ppermute(after(pack, own), ("seq", "roll"), moves)
        other = after(other, near_out, near_in, far_a)
    else:
        own = lax.psum(part, "roll")
        other = jnp.zeros((CODES, H), BF)
        pairs = [(i, i + 1) for i in range(seqs - 1)]
        before = lax.ppermute(codes[rows - REACH :], "seq", pairs)
        behind = lax.ppermute(codes[:REACH], "seq", [(j, i) for i, j in pairs])
    wide = KERNEL * H
    shapes = [((SLOT, wide), F32), ((SLOT, wide), BF), ((1, 128), F32)] if split else [((CODES, wide), F32)]
    taps = pl.pallas_call(
        functools.partial(table_kernel, split),
        out_shape=[jax.ShapeDtypeStruct(n, t) for n, t in shapes],
        in_specs=[VMEM, VMEM, VMEM, HBM],
        out_specs=[VMEM] * len(shapes),
        scratch_shapes=[
            pltpu.VMEM(conv_w.shape[1:], BF),
            pltpu.VMEM((CODES, wide), F32),
            pltpu.SemaphoreType.DMA,
        ],
        cost_estimate=FREE,
        compiler_params=params(12),
    )(own, other, gain_mid, conv_w)
    if split:
        came = core_swap(after(moved[1], taps[2]))
        before, behind = jnp.where(low, moved[0], came), jnp.where(low, came, moved[0])
        relay = after(far_a, taps[2])
        parts_a = [far_a] + [seq_swap(relay, b) for b in (1, 2, 3)]
        sent = (taps[0] + core_swap(taps[1]).astype(F32)).astype(BF)
        received = x_swap(sent)
    spare = jnp.zeros((-(rows + 2 * REACH) % 128,), jnp.int32)
    near = jnp.concatenate([before, codes, behind, spare])[None]
    if split:
        near = after(near, sent)

    shapes = [(wide_rows, KERNEL * CODES), (wide_rows, CODES)]
    operands, scratch = [], []
    if split:
        operands = [table, w_out, w_in, near_out, near_in]
        shapes += [(4 * shard + CODES, width), (8 * shard, H)]
        scratch = [pltpu.SemaphoreType.DMA]
    hot5, hot1, *chip = pl.pallas_call(
        functools.partial(hot_kernel, split),
        out_shape=[jax.ShapeDtypeStruct(n, BF) for n in shapes],
        in_specs=[SMEM, VMEM] + [ANY] * len(operands),
        out_specs=[VMEM] * len(shapes),
        scratch_shapes=scratch,
        cost_estimate=FREE,
        compiler_params=params(16),
    )(span, near, *operands)

    if split:
        near_sent = core_swap(after(sent, hot1))
        received = after(received, hot1)
        near_received = core_swap(received)
        near_a = [core_swap(after(p, hot1, far_b)) for p in parts_a]
        relay = after(far_b, received)
        parts_b = [far_b, seq_swap(relay, 1), seq_swap(relay, 2), x_swap(after(parts[2], received))]
        weights_a = [sent, received, near_sent, near_received] + chip + parts_a + near_a
        near_conv = core_swap(after(conv_w, near_received, near_sent, *near_a))
    else:
        taps = lax.psum(taps[0], "roll").astype(BF)
        gather = lambda w: lax.all_gather(w, "roll", axis=0, tiled=True)
        weights_a, weights_b = [taps, table, gather(w_out[0]), gather(w_in[1])], [gather(conv_w[1]), gather(w_out[1])]

    ci, hid = pl.pallas_call(
        functools.partial(rows_kernel, split),
        out_shape=(
            jax.ShapeDtypeStruct((wide_rows, H), BF),
            jax.ShapeDtypeStruct((rows, width), BF),
        ),
        in_specs=[SMEM] + [VMEM] * 5 + [ANY] * len(weights_a),
        out_specs=(VMEM, VMEM),
        scratch_shapes=[
            pltpu.VMEM((2, KERNEL * CODES, H), BF),
            pltpu.VMEM((H + CODES, width), BF),
            pltpu.VMEM((width, H), BF),
            pltpu.SemaphoreType.DMA((3,)),
        ],
        cost_estimate=FREE,
        compiler_params=params(30),
    )(span, hot5, hot1, gain_out, gain_in, gain_mid, *weights_a)

    if split:
        near_b = [core_swap(after(p, ci)) for p in parts_b]
        head = pl.pallas_call(
            head_kernel,
            out_shape=jax.ShapeDtypeStruct((rows, H), F32),
            in_specs=[VMEM, HBM, ANY],
            out_specs=VMEM,
            scratch_shapes=[pltpu.VMEM((KERNEL * HEAD, H), BF), pltpu.SemaphoreType.DMA],
            cost_estimate=FREE,
            compiler_params=params(16),
        )(ci, conv_w, near_conv)
        weights_b = [head, conv_w, w_out, near_conv, near_out] + parts_b + near_b
    out = pl.pallas_call(
        functools.partial(last_kernel, split),
        out_shape=jax.ShapeDtypeStruct((rows, width), BF),
        in_specs=[VMEM] * 3
        + [HBM if w is w_out or w is conv_w else VMEM if split and w is head else ANY for w in weights_b],
        out_specs=VMEM,
        scratch_shapes=[
            pltpu.VMEM((KERNEL * (TAIL if split else H), H), BF),
            pltpu.VMEM((H, width), BF),
            pltpu.SemaphoreType.DMA((2,)),
        ],
        cost_estimate=FREE,
        compiler_params=params(24),
    )(ci, hid, gain_out, *weights_b)
    return out[None]


def solution(mesh):
    placed = (
        P("roll", "seq"),
        P("roll", "seq"),
        P("roll"),
        P(),
        P(),
        P(),
        P(),
        P(),
        P(None, "roll", None),
        P(None, "roll", None),
        P(None, "roll", None),
    )
    return jax.shard_map(
        per_device, mesh=mesh, in_specs=placed, out_specs=P("roll", "seq", None), check_vma=False
    )
```
